32 devices in a mesh: layer: 8 (over z, y), dir: 4 (over x, core).
Axes of the slice: x: 2, y: 2, z: 4, core: 2. Of those that a mesh axis runs over, the one named last changes fastest.
Arguments:
- screens: bfloat16 [3, 512, 4096], P(None, 'dir', 'layer'), may hold values from -6 to 6
- amplitude: float32 [256, 1280], P('layer'), may hold values from 0.5 to 2
- wind: int32 [3, 2], replicated, may hold values from -8 to 8, as said below
- offsets: int32 [4, 3, 2], replicated, may hold values from 0 to 4095, as said below
- ratio: int32 [4, 3, 2], replicated, may hold values from 64 to 192, as said below
Outputs:
- new_screens: bfloat16 [3, 512, 4096], P(None, 'dir', 'layer')
- spots: float32 [4, 512, 2560], P('dir', 'layer')
The draws below stay inside these ranges and needn't reach their ends.
Inputs may be any that keep to these rules, and one draw needn't show every extreme that they name: wind[l, 0] is layer l's row shift and wind[l, 1] its column shift; no shift is zero; one layer has column shift +8 and a row shift above zero, another has column shift -8 and a row shift below zero. offsets[d, l, 0] is a screen row below 512, offsets[d, l, 1] a screen column below 4096. ratio[d, l] = (num, den) with 64 <= den <= 128 and den <= num <= den + den // 2; some entry is (192, 128) and another (64, 64).
All inputs are finite; a program needn't handle non-finite values.
Results may differ from the reference program's by a relative error of at most 0.009.
Values may be sent and summed in bfloat16 or wider, within the bound.
No kernel may reach another device: no remote copies, remote signals or barrier semaphores. Data moves between devices by JAX's collectives and lax.ppermute only.
A program may use at most 64 MiB of HBM per device.

```python
import math
import jax
import jax.numpy as jnp
from jax import lax

LAYERS = 3
SUB_PIX = 16
SPOT_PIX = 32
WIND_MAX = 8
DIRS = 4
PUPIL_ROWS = 256
PUPIL_COLS = 1280
SCREEN_ROWS = 512
SCREEN_COLS = 4096


def draw_wind(key, part):
    keys = jax.random.split(key, 4)
    layer_ids = jnp.arange(LAYERS, dtype=jnp.int32)
    sizes = jax.random.randint(keys[0], (LAYERS, 2), 1, WIND_MAX + 1)
    signs = jax.random.randint(keys[1], (LAYERS, 2), 0, 2) * 2 - 1
    first = jax.random.randint(keys[2], (), 0, LAYERS)
    second = (first + jax.random.randint(keys[3], (), 1, LAYERS)) % LAYERS
    moves = sizes * signs
    forced = jnp.where(layer_ids == first, 1, jnp.where(layer_ids == second, -1, 0))
    row_moves = jnp.where(forced != 0, forced * sizes[:, 0], moves[:, 0])
    col_moves = jnp.where(forced != 0, forced * WIND_MAX, moves[:, 1])
    return jnp.stack([row_moves, col_moves], axis=1).astype(jnp.int32)


def draw_offsets(key, part):
    keys = jax.random.split(key, 5)
    rows = jax.random.randint(keys[0], (DIRS, LAYERS), 0, SCREEN_ROWS)
    cols = jax.random.randint(keys[1], (DIRS, LAYERS), 0, SCREEN_COLS)
    entries = DIRS * LAYERS
    flat = jnp.arange(entries, dtype=jnp.int32).reshape(DIRS, LAYERS)
    top_row = jax.random.randint(keys[2], (), 0, entries)
    zero_row = (top_row + jax.random.randint(keys[3], (), 1, entries)) % entries
    top_col = jax.random.randint(keys[4], (), 0, entries)
    rows = jnp.where(flat == top_row, SCREEN_ROWS - 1, rows)
    rows = jnp.where(flat == zero_row, 0, rows)
    cols = jnp.where(flat == top_col, SCREEN_COLS - 1, cols)
    return jnp.stack([rows, cols], axis=2).astype(jnp.int32)


def draw_ratio(key, part):
    keys = jax.random.split(key, 4)
    denoms = jax.random.randint(keys[0], (DIRS, LAYERS), 64, 129)
    extra = jax.random.randint(keys[1], (DIRS, LAYERS), 0, 65) % (denoms // 2 + 1)
    entries = DIRS * LAYERS
    flat = jnp.arange(entries, dtype=jnp.int32).reshape(DIRS, LAYERS)
    top_entry = jax.random.randint(keys[2], (), 0, entries)
    low_entry = (top_entry + jax.random.randint(keys[3], (), 1, entries)) % entries
    denoms = jnp.where(flat == top_entry, 128, jnp.where(flat == low_entry, 64, denoms))
    extra = jnp.where(flat == top_entry, 64, jnp.where(flat == low_entry, 0, extra))
    return jnp.stack([denoms + extra, denoms], axis=2).astype(jnp.int32)


def shard_levels(rng, dims, pieces, smallest, high):
    def one(axis_at, parts):
        steps = jax.random.uniform(jax.random.fold_in(jax.random.fold_in(rng, 6), axis_at), (parts,), jnp.float32, smallest / len(pieces), high / len(pieces))
        return jnp.repeat(jnp.exp(steps), dims[axis_at] // parts).reshape((-1,) + (1,) * (len(dims) - axis_at - 1))

    level = one(*pieces[0])
    for cut in pieces[1:]:
        level = level * one(*cut)
    return level


def noise(stream_key, extent, scale, most, shards=(), held_as=jnp.bfloat16):
    values = scale * jax.random.normal(stream_key, extent, jnp.float32)
    if shards:
        values = values * shard_levels(stream_key, extent, shards, -0.22, 0.18)
    return jnp.clip(values, -most, most).astype(held_as)


def setup_inputs(seed: int = 0) -> dict:
    splits = jax.random.split(jax.random.key(seed), 6)
    screens = noise(splits[0], (LAYERS, SCREEN_ROWS, SCREEN_COLS), 1.0, 6.0, ((1, 4), (2, 8)))
    amplitude = jnp.clip(jnp.exp(math.log(2.0) - 1.3862944 * jax.random.uniform(splits[1], (PUPIL_ROWS, PUPIL_COLS), jnp.float32) ** shard_levels(splits[1], (PUPIL_ROWS, PUPIL_COLS), ((0, 8),), -0.2, 0.2)), 0.5, 2.0)
    wind = draw_wind(jax.random.fold_in(splits[5], 71), 0)
    offsets = draw_offsets(jax.random.fold_in(splits[5], 71), 0)
    ratio = draw_ratio(jax.random.fold_in(splits[5], 71), 0)
    return {"screens": screens, "amplitude": amplitude, "wind": wind, "offsets": offsets, "ratio": ratio}


def spans(anchor, stretch_num, stretch_den, count, length):
    pixel = jnp.arange(count, dtype=jnp.int32)
    stretched = pixel * stretch_num
    base = (anchor + stretched // stretch_den) % length
    upper = (base + 1) % length
    fraction = (stretched % stretch_den).astype(jnp.float32) / stretch_den.astype(jnp.float32)
    return base, upper, (1.0 - fraction).astype(jnp.bfloat16), fraction.astype(jnp.bfloat16)


def dft_tables():
    freq = jnp.arange(SPOT_PIX, dtype=jnp.int32)[:, None] - SPOT_PIX // 2
    pixel = jnp.arange(SUB_PIX, dtype=jnp.int32)[None, :]
    turns = (freq * pixel) % SPOT_PIX
    angle = turns.astype(jnp.float32) * (2.0 * jnp.pi / SPOT_PIX)
    return jnp.cos(angle), -jnp.sin(angle)


def imaging(phase, amplitude):
    rows, cols = phase.shape
    sub_rows = rows // SUB_PIX
    sub_cols = cols // SUB_PIX
    real = (amplitude * jnp.cos(phase)).reshape(sub_rows, SUB_PIX, sub_cols, SUB_PIX)
    imag = (amplitude * jnp.sin(phase)).reshape(sub_rows, SUB_PIX, sub_cols, SUB_PIX)
    cos_table, sin_table = dft_tables()
    highest = lax.Precision.HIGHEST
    half_real = jnp.einsum('aibj,kj->aibk', real, cos_table, precision=highest) - jnp.einsum('aibj,kj->aibk', imag, sin_table, precision=highest)
    half_imag = jnp.einsum('aibj,kj->aibk', real, sin_table, precision=highest) + jnp.einsum('aibj,kj->aibk', imag, cos_table, precision=highest)
    full_real = jnp.einsum('ki,aibl->akbl', cos_table, half_real, precision=highest) - jnp.einsum('ki,aibl->akbl', sin_table, half_imag, precision=highest)
    full_imag = jnp.einsum('ki,aibl->akbl', cos_table, half_imag, precision=highest) + jnp.einsum('ki,aibl->akbl', sin_table, half_real, precision=highest)
    intensity = full_real * full_real + full_imag * full_imag
    totals = jnp.sum(intensity, axis=(1, 3), keepdims=True)
    normed = intensity * float(SPOT_PIX * SPOT_PIX) / totals
    return normed.reshape(sub_rows * SPOT_PIX, sub_cols * SPOT_PIX)


def reference(screens, amplitude, wind, offsets, ratio):
    moved = jnp.stack([jnp.roll(screens[k], (wind[k, 0], wind[k, 1]), axis=(0, 1)) for k in range(LAYERS)])
    spot_list = []
    for direction in range(DIRS):
        phase = jnp.zeros((PUPIL_ROWS, PUPIL_COLS), jnp.float32)
        for k in range(LAYERS):
            stretch_num = ratio[direction, k, 0]
            stretch_den = ratio[direction, k, 1]
            row_base, row_upper, row_low, row_high = spans(offsets[direction, k, 0], stretch_num, stretch_den, PUPIL_ROWS, SCREEN_ROWS)
            screen = moved[k].astype(jnp.float32)
            projected = row_low.astype(jnp.float32)[:, None] * screen[row_base] + row_high.astype(jnp.float32)[:, None] * screen[row_upper]
            projected = lax.optimization_barrier(projected.astype(jnp.bfloat16)).astype(jnp.float32)
            col_base, col_upper, col_low, col_high = spans(offsets[direction, k, 1], stretch_num, stretch_den, PUPIL_COLS, SCREEN_COLS)
            phase = phase + (projected[:, col_base] * col_low.astype(jnp.float32)[None, :] + projected[:, col_upper] * col_high.astype(jnp.float32)[None, :])
        spot_list.append(imaging(phase, amplitude))
    return moved, jnp.stack(spot_list)
```

```python
import functools

import jax
import jax.numpy as jnp
import numpy as np
from jax import lax
from jax.experimental import pallas as pl
from jax.experimental.pallas import tpu as pltpu
from jax.sharding import PartitionSpec as P

SUB_PIX = 16
SPOT_PIX = 32
WIND_MAX = 8
LANES = 128
VMEM_LIMIT = 56 * 1024 * 1024

SMEM_SPEC = pl.BlockSpec(memory_space=pltpu.SMEM)
VMEM_SPEC = pl.BlockSpec(memory_space=pltpu.VMEM)


def params():
    return pltpu.CompilerParams(vmem_limit_bytes=VMEM_LIMIT)


def wrap(value, length):
    value = jnp.where(value < 0, value + length, value)
    return jnp.where(value >= length, value - length, value)


def spans(pixel, anchor, num, den, length):
    stretched = (pixel * num).astype(jnp.float32)
    den = jnp.full(pixel.shape, den, jnp.int32).astype(jnp.float32)
    whole = jnp.floor((stretched + 0.5) / den)
    fraction = (stretched - whole * den) / den
    base = wrap(anchor + whole.astype(jnp.int32), length)
    upper = wrap(base + 1, length)
    return base, upper, 1.0 - fraction, fraction


def weights_kernel(geometry, wind, offsets, ratio, amplitude, ones, rows_out, cols_out, amp_out):
    n_layer, n_dir, rows_dev, cols_dev = geometry
    layers, pupil_rows, screen_rows = rows_out.shape
    pupil_cols = cols_out.shape[2]
    screen_cols = cols_dev * n_layer
    direction = lax.axis_index("dir")
    column = lax.axis_index("layer")
    block = pupil_rows // n_layer
    for level in range(layers):
        num = ratio[level, 0, direction]
        den = ratio[level, 1, direction]
        anchor = wrap(offsets[level, 0, direction] - wind[0, level], screen_rows)
        pixel = lax.broadcasted_iota(jnp.int32, (pupil_rows, LANES), 0) + column * block
        pixel = jnp.where(pixel >= pupil_rows, pixel - pupil_rows, pixel)
        base, upper, low, high = spans(pixel, anchor, num, den, screen_rows)
        lane = lax.broadcasted_iota(jnp.int32, (pupil_rows, LANES), 1)
        for peer in range(n_dir):
            for part in range(rows_dev // LANES):
                index = lane + (jnp.bitwise_xor(direction, peer) * rows_dev + part * LANES)
                weight = jnp.where(index == base, low, 0.0)
                weight = jnp.where(index == upper, high, weight)
                start = peer * rows_dev + part * LANES
                rows_out[level, :, start : start + LANES] = weight.astype(jnp.bfloat16)
        anchor = wrap(offsets[level, 1, direction] - wind[1, level], screen_cols)
        first = lax.broadcasted_iota(jnp.int32, (cols_dev, LANES), 0) + column * cols_dev

        def tile(step, carry):
            start = pl.multiple_of(step * LANES, LANES)
            pixel = lax.broadcasted_iota(jnp.int32, (8, LANES), 1) + start
            base, upper, low, high = spans(pixel, anchor, num, den, screen_cols)
            index = first.reshape(cols_dev // 8, 8, LANES)
            weight = jnp.where(index == base[None], low[None], 0.0)
            weight = jnp.where(index == upper[None], high[None], weight)
            weight = weight.reshape(cols_dev, LANES).astype(jnp.bfloat16)
            cols_out[level, :, pl.ds(start, LANES)] = weight
            return carry

        lax.fori_loop(0, pupil_cols // LANES, tile, 0)
    rows = amplitude.shape[0]
    for step in range(pupil_cols // LANES):
        cut = slice(step * LANES, (step + 1) * LANES)
        amp = amplitude[:, cut]
        energy = (amp * amp).reshape(rows // SUB_PIX, SUB_PIX, LANES).sum(axis=1)
        energy = jnp.broadcast_to(energy[:, None], (rows // SUB_PIX, SUB_PIX, LANES)).reshape(rows, LANES)
        total = jnp.dot(energy, ones[...], precision=lax.Precision.HIGHEST, preferred_element_type=jnp.float32)
        amp_out[:, cut] = amp * lax.rsqrt(total)


def project_kernel(peers, rows_ref, cols_ref, *refs):
    blocks, outs = refs[:peers], refs[peers:]
    layers, pupil_rows, screen_rows = rows_ref.shape
    _, cols_dev, pupil_cols = cols_ref.shape
    size = outs[0].shape[0]
    group = min(pupil_rows, 256)
    per_group = group // size
    for at in range(pupil_rows // group):
        projected = []
        for level in range(layers):
            screen = jnp.concatenate([block[level] for block in blocks], axis=0)
            rows = rows_ref[level, at * group : (at + 1) * group, :]
            part = jnp.dot(rows, screen, preferred_element_type=jnp.float32)
            projected.append(part.astype(jnp.bfloat16))
        projected = jnp.concatenate(projected, axis=1)
        for start in range(0, pupil_cols, 256):
            cols = cols_ref[:, :, start : start + 256].reshape(layers * cols_dev, 256)
            phase = jnp.dot(projected, cols, preferred_element_type=jnp.float32)
            for k in range(per_group):
                piece = phase[k * size : (k + 1) * size].astype(jnp.bfloat16)
                outs[at * per_group + k][:, start : start + 256] = piece


def rows_kernel(wind, own, near, far, moved, right, left):
    layers, rows, cols = own.shape
    odd = lax.rem(lax.axis_index("dir"), 2) == 1
    lane = lax.broadcasted_iota(jnp.int32, (rows, LANES), 1)
    to_right = jnp.zeros((rows, LANES), jnp.float32)
    to_left = jnp.zeros((rows, LANES), jnp.float32)
    for level in range(layers):
        near_last = near[level, rows - 16 :, :].astype(jnp.float32)
        near_first = near[level, :16, :].astype(jnp.float32)
        far_last = far[level, rows - 16 :, :].astype(jnp.float32)
        far_first = far[level, :16, :].astype(jnp.float32)
        before = jnp.where(odd, near_last, far_last)
        after = jnp.where(odd, far_first, near_first)
        wide = jnp.concatenate([before, own[level].astype(jnp.float32), after], axis=0)
        shift = wind[0, level]
        shift = jnp.where(shift < 0, shift + rows + 32, shift)
        wide = pltpu.roll(wide, shift, 0)[16 : 16 + rows]
        moved[level] = wide.astype(jnp.bfloat16)
        mine = (lane >= WIND_MAX * level) & (lane < WIND_MAX * (level + 1))
        last = pltpu.roll(wide[:, cols - LANES :], WIND_MAX * (level + 1), 1)
        to_right = jnp.where(mine, last, to_right)
        initial = wide[:, :LANES]
        if level:
            initial = pltpu.roll(initial, WIND_MAX * level, 1)
        to_left = jnp.where(mine, initial, to_left)
    right[...] = to_right.astype(jnp.bfloat16)
    left[...] = to_left.astype(jnp.bfloat16)


def cols_kernel(wind, moved, from_left, from_right, out):
    layers, rows, cols = moved.shape
    lane = lax.broadcasted_iota(jnp.int32, (rows, LANES), 1)
    before = from_left[...].astype(jnp.float32)
    after = from_right[...].astype(jnp.float32)
    for level in range(layers):
        last = pltpu.roll(before, LANES - WIND_MAX * (level + 1), 1)
        first = pltpu.roll(after, LANES - WIND_MAX * level, 1) if level else after
        extra = jnp.where(lane < WIND_MAX, first, last)
        wide = jnp.concatenate([moved[level].astype(jnp.float32), extra], axis=1)
        shift = wind[1, level]
        shift = jnp.where(shift < 0, shift + cols + LANES, shift)
        out[level] = pltpu.roll(wide, shift, 1)[:, :cols].astype(jnp.bfloat16)


def sin_cos(phase):
    turns = jnp.floor(phase * (1.0 / np.pi) + 0.5)
    rest = phase - turns * 3.140625
    rest = rest - turns * 9.67653589793e-4
    odd = turns - 2.0 * jnp.floor(turns * 0.5)
    sign = 1.0 - 2.0 * odd
    square = rest * rest
    sine = -1.0 / 39916800.0
    for term in (1.0 / 362880.0, -1.0 / 5040.0, 1.0 / 120.0, -1.0 / 6.0, 1.0):
        sine = sine * square + term
    cosine = 1.0 / 479001600.0
    for term in (-1.0 / 3628800.0, 1.0 / 40320.0, -1.0 / 720.0, 1.0 / 24.0, -0.5, 1.0):
        cosine = cosine * square + term
    return sine * rest * sign, cosine * sign


def split(value):
    high = value.astype(jnp.bfloat16)
    low = (value - high.astype(jnp.float32)).astype(jnp.bfloat16)
    return high, low


def imaging_kernel(count, *refs):
    parts = refs[:count]
    amp_ref, cols_high, cols_low, rows_table, out = refs[count:]
    rows, cols = amp_ref.shape
    tiles = cols // LANES
    phase = parts[0][...].astype(jnp.float32)
    for part in parts[1:]:
        phase = phase + part[...].astype(jnp.float32)
    sine, cosine = sin_cos(phase)
    amp = amp_ref[...]
    real, imag = amp * cosine, amp * sine
    field = jnp.concatenate(
        [
            jnp.concatenate(
                [real[:, t * LANES : (t + 1) * LANES], imag[:, t * LANES : (t + 1) * LANES]], axis=1
            )
            for t in range(tiles)
        ],
        axis=0,
    )
    high, low = split(field)
    dot = functools.partial(jnp.dot, preferred_element_type=jnp.float32)
    half = dot(high, cols_high[...]) + (dot(low, cols_high[...]) + dot(high, cols_low[...]))
    wide = 2 * LANES
    out_rows = 2 * rows
    for t in range(tiles):
        mine = half[t * rows : (t + 1) * rows]
        mine = jnp.concatenate([mine[:, :wide], mine[:, wide:]], axis=0)
        high, low = split(mine)
        full = dot(rows_table[...], jnp.concatenate([high, low, high], axis=0))
        real, imag = full[:out_rows], full[out_rows:]
        out[:, t * wide : (t + 1) * wide] = real * real + imag * imag


def tables(rows):
    freq = np.arange(SPOT_PIX)[:, None] - SPOT_PIX // 2
    angle = ((freq * np.arange(SUB_PIX)[None, :]) % SPOT_PIX) * (2.0 * np.pi / SPOT_PIX)
    cos, sin = np.cos(angle), np.sin(angle)

    def blocks(table, count):
        return np.kron(np.eye(count), table)

    per_tile = LANES // SUB_PIX
    col_cos, col_sin = blocks(cos.T, per_tile), blocks(sin.T, per_tile)
    columns = np.block([[col_cos, -col_sin], [col_sin, col_cos]])
    count = rows // SUB_PIX
    row_cos, row_sin = blocks(cos, count), blocks(sin, count)
    lines = np.block([[row_cos, row_sin], [-row_sin, row_cos]])

    def halves(value):
        value = value.astype(np.float32)
        high = value.astype(jnp.bfloat16)
        return high, (value - high.astype(np.float32)).astype(jnp.bfloat16)

    cols_high, cols_low = halves(columns)
    rows_high, rows_low = halves(lines)
    return cols_high, cols_low, np.concatenate([rows_high, rows_high, rows_low], axis=1)


def per_device(screens, amplitude, wind, offsets, ratio):
    layers, rows_dev, cols_dev = screens.shape
    n_layer = lax.axis_size("layer")
    n_dir = lax.axis_size("dir")
    assert n_dir == 4
    rows, pupil_cols = amplitude.shape
    pupil_rows = rows * n_layer
    screen_rows = rows_dev * n_dir
    bf16, f32 = jnp.bfloat16, jnp.float32
    wind = jnp.transpose(wind, (1, 0))
    offsets = jnp.transpose(offsets, (1, 2, 0))
    ratio = jnp.transpose(ratio, (1, 2, 0))

    def swap(value, bit):
        return lax.ppermute(value, "dir", [(i, i ^ bit) for i in range(n_dir)])

    def turn(value, step):
        return lax.ppermute(value, "layer", [(i, (i + step) % n_layer) for i in range(n_layer)])

    across = swap(screens, 2)
    near = swap(screens, 1)
    far = swap(across, 1)

    ones = np.kron(np.eye(LANES // SUB_PIX), np.ones((SUB_PIX, SUB_PIX))).astype(np.float32)
    row_weights, col_weights, amp = pl.pallas_call(
        functools.partial(weights_kernel, (n_layer, n_dir, rows_dev, cols_dev)),
        out_shape=(
            jax.ShapeDtypeStruct((layers, pupil_rows, screen_rows), bf16),
            jax.ShapeDtypeStruct((layers, cols_dev, pupil_cols), bf16),
            jax.ShapeDtypeStruct((rows, pupil_cols), f32),
        ),
        in_specs=[SMEM_SPEC] * 3 + [VMEM_SPEC] * 2,
        out_specs=[VMEM_SPEC] * 3,
        compiler_params=params(),
        cost_estimate=pl.CostEstimate(flops=8_000_000, bytes_accessed=6_000_000, transcendentals=0),
        name="weights",
    )(wind, offsets, ratio, amplitude, jnp.asarray(ones))

    partials = pl.pallas_call(
        functools.partial(project_kernel, n_dir),
        out_shape=[jax.ShapeDtypeStruct((rows, pupil_cols), bf16)] * n_layer,
        in_specs=[VMEM_SPEC] * (2 + n_dir),
        out_specs=[VMEM_SPEC] * n_layer,
        compiler_params=params(),
        cost_estimate=pl.CostEstimate(flops=1_400_000_000, bytes_accessed=6_000_000, transcendentals=0),
        name="project",
    )(row_weights, col_weights, screens, near, across, far)

    received = [partials[0]] + [turn(partials[k], k) for k in range(1, n_layer)]

    moved, right, left = pl.pallas_call(
        rows_kernel,
        out_shape=(
            jax.ShapeDtypeStruct((layers, rows_dev, cols_dev), bf16),
            jax.ShapeDtypeStruct((rows_dev, LANES), bf16),
            jax.ShapeDtypeStruct((rows_dev, LANES), bf16),
        ),
        in_specs=[SMEM_SPEC] + [VMEM_SPEC] * 3,
        out_specs=[VMEM_SPEC] * 3,
        compiler_params=params(),
        cost_estimate=pl.CostEstimate(flops=1_000_000, bytes_accessed=1_600_000, transcendentals=0),
        name="shift_rows",
    )(wind, screens, near, far)
    from_left = turn(right, 1)
    from_right = turn(left, n_layer - 1)
    new_screens = pl.pallas_call(
        cols_kernel,
        out_shape=jax.ShapeDtypeStruct((layers, rows_dev, cols_dev), bf16),
        in_specs=[SMEM_SPEC] + [VMEM_SPEC] * 3,
        out_specs=VMEM_SPEC,
        compiler_params=params(),
        cost_estimate=pl.CostEstimate(flops=1_000_000, bytes_accessed=1_000_000, transcendentals=0),
        name="shift_cols",
    )(wind, moved, from_left, from_right)

    spots = pl.pallas_call(
        functools.partial(imaging_kernel, n_layer),
        out_shape=jax.ShapeDtypeStruct((2 * rows, 2 * pupil_cols), f32),
        in_specs=[VMEM_SPEC] * (n_layer + 4),
        out_specs=VMEM_SPEC,
        compiler_params=params(),
        cost_estimate=pl.CostEstimate(flops=400_000_000, bytes_accessed=2_000_000, transcendentals=0),
        name="imaging",
    )(*received, amp, *[jnp.asarray(table) for table in tables(rows)])
    return (new_screens, spots[None])


def solution(mesh):
    return jax.shard_map(
        per_device,
        mesh=mesh,
        in_specs=(P(None, "dir", "layer"), P("layer", None), P(), P(), P()),
        out_specs=(P(None, "dir", "layer"), P("dir", "layer", None)),
        check_vma=False,
    )
```

```python
import functools

import jax
import jax.numpy as jnp
import numpy as np
from jax import lax
from jax.experimental import pallas as pl
from jax.experimental.pallas import tpu as pltpu
from jax.sharding import PartitionSpec as P

SUB_PIX = 16
SPOT_PIX = 32
WIND_MAX = 8
LANES = 128

SMEM_SPEC = pl.BlockSpec(memory_space=pltpu.SMEM)
VMEM_SPEC = pl.BlockSpec(memory_space=pltpu.VMEM)


def params(*arrays):
    held = sum(array.size * array.dtype.itemsize for array in jax.tree.leaves(arrays))
    return pltpu.CompilerParams(vmem_limit_bytes=held + 8 * 1024 * 1024)


def call(kernel, out_shape, operands, flops, name):
    def spec(array):
        return SMEM_SPEC if array.dtype == jnp.int32 else VMEM_SPEC

    out_specs = jax.tree.map(lambda _: VMEM_SPEC, out_shape)
    size = sum(array.size * array.dtype.itemsize for array in jax.tree.leaves((operands, out_shape)))
    return pl.pallas_call(
        kernel,
        out_shape=out_shape,
        in_specs=[spec(array) for array in operands],
        out_specs=out_specs,
        compiler_params=params(operands, out_shape),
        cost_estimate=pl.CostEstimate(flops=flops, bytes_accessed=size, transcendentals=0),
        name=name,
    )(*operands)


def wrap(value, length):
    value = jnp.where(value < 0, value + length, value)
    return jnp.where(value >= length, value - length, value)


def spans(pixel, anchor, num, den, length):
    stretched = (pixel * num).astype(jnp.float32)
    den = jnp.full(pixel.shape, den, jnp.int32).astype(jnp.float32)
    whole = jnp.floor((stretched + 0.5) / den)
    fraction = (stretched - whole * den) / den
    base = wrap(anchor + whole.astype(jnp.int32), length)
    upper = wrap(base + 1, length)
    return base, upper, 1.0 - fraction, fraction


def weights_kernel(geometry, wind, offsets, ratio, amplitude, ones, rows_out, cols_out, amp_out):
    n_layer, n_dir, rows_dev, cols_dev = geometry
    layers, pupil_rows, screen_rows = rows_out.shape
    pupil_cols = cols_out.shape[2]
    screen_cols = cols_dev * n_layer
    direction = lax.axis_index("dir")
    column = lax.axis_index("layer")
    for level in range(layers):
        num = ratio[level, 0, direction]
        den = ratio[level, 1, direction]
        anchor = wrap(offsets[level, 0, direction] - wind[0, level], screen_rows)
        pixel = lax.broadcasted_iota(jnp.int32, (pupil_rows, LANES), 0)
        base, upper, low, high = spans(pixel, anchor, num, den, screen_rows)
        lane = lax.broadcasted_iota(jnp.int32, (pupil_rows, LANES), 1)
        for peer in range(n_dir):
            for part in range(rows_dev // LANES):
                index = lane + (jnp.bitwise_xor(direction, peer) * rows_dev + part * LANES)
                weight = jnp.where(index == base, low, 0.0)
                weight = jnp.where(index == upper, high, weight)
                start = peer * rows_dev + part * LANES
                rows_out[level, :, start : start + LANES] = weight.astype(jnp.bfloat16)
        anchor = wrap(offsets[level, 1, direction] - wind[1, level], screen_cols)
        first = lax.broadcasted_iota(jnp.int32, (cols_dev, LANES), 0) + column * cols_dev

        def tile(step, carry):
            start = pl.multiple_of(step * LANES, LANES)
            pixel = lax.broadcasted_iota(jnp.int32, (8, LANES), 1) + start
            base, upper, low, high = spans(pixel, anchor, num, den, screen_cols)
            index = first.reshape(cols_dev // 8, 8, LANES)
            weight = jnp.where(index == base[None], low[None], 0.0)
            weight = jnp.where(index == upper[None], high[None], weight)
            weight = weight.reshape(cols_dev, LANES).astype(jnp.bfloat16)
            cols_out[level, :, pl.ds(start, LANES)] = weight
            return carry

        lax.fori_loop(0, pupil_cols // LANES, tile, 0)
    rows = amplitude.shape[0]
    for step in range(pupil_cols // LANES):
        cut = slice(step * LANES, (step + 1) * LANES)
        amp = amplitude[:, cut]
        energy = (amp * amp).reshape(rows // SUB_PIX, SUB_PIX, LANES).sum(axis=1)
        energy = jnp.broadcast_to(energy[:, None], (rows // SUB_PIX, SUB_PIX, LANES)).reshape(rows, LANES)
        total = jnp.dot(energy, ones[...], precision=lax.Precision.HIGHEST, preferred_element_type=jnp.float32)
        amp_out[:, cut] = amp * lax.rsqrt(total)


def project_kernel(peers, rows_ref, cols_ref, *refs):
    blocks, out = refs[:peers], refs[peers]
    layers, pupil_rows, screen_rows = rows_ref.shape
    _, cols_dev, pupil_cols = cols_ref.shape
    size = out.shape[1]
    group = min(pupil_rows, 256)
    per_group = group // size
    for at in range(pupil_rows // group):
        projected = []
        for level in range(layers):
            screen = jnp.concatenate([block[level] for block in blocks], axis=0)
            rows = rows_ref[level, at * group : (at + 1) * group, :]
            part = jnp.dot(rows, screen, preferred_element_type=jnp.float32)
            projected.append(part.astype(jnp.bfloat16))
        projected = jnp.concatenate(projected, axis=1)
        for start in range(0, pupil_cols, 256):
            cols = cols_ref[:, :, start : start + 256].reshape(layers * cols_dev, 256)
            phase = jnp.dot(projected, cols, preferred_element_type=jnp.float32)
            for k in range(per_group):
                piece = phase[k * size : (k + 1) * size].astype(jnp.bfloat16)
                out[at * per_group + k, :, start : start + 256] = piece


def rows_kernel(wind, own, near, far, moved, right, left):
    layers, rows, cols = own.shape
    odd = lax.rem(lax.axis_index("dir"), 2) == 1
    lane = lax.broadcasted_iota(jnp.int32, (rows, LANES), 1)
    to_right = jnp.zeros((rows, LANES), jnp.float32)
    to_left = jnp.zeros((rows, LANES), jnp.float32)
    for level in range(layers):
        near_last = near[level, rows - 16 :, :].astype(jnp.float32)
        near_first = near[level, :16, :].astype(jnp.float32)
        far_last = far[level, rows - 16 :, :].astype(jnp.float32)
        far_first = far[level, :16, :].astype(jnp.float32)
        before = jnp.where(odd, near_last, far_last)
        after = jnp.where(odd, far_first, near_first)
        wide = jnp.concatenate([before, own[level].astype(jnp.float32), after], axis=0)
        shift = wind[0, level]
        shift = jnp.where(shift < 0, shift + rows + 32, shift)
        wide = pltpu.roll(wide, shift, 0)[16 : 16 + rows]
        moved[level] = wide.astype(jnp.bfloat16)
        mine = (lane >= WIND_MAX * level) & (lane < WIND_MAX * (level + 1))
        last = pltpu.roll(wide[:, cols - LANES :], WIND_MAX * (level + 1), 1)
        to_right = jnp.where(mine, last, to_right)
        initial = wide[:, :LANES]
        if level:
            initial = pltpu.roll(initial, WIND_MAX * level, 1)
        to_left = jnp.where(mine, initial, to_left)
    right[...] = to_right.astype(jnp.bfloat16)
    left[...] = to_left.astype(jnp.bfloat16)


def cols_kernel(wind, moved, from_left, from_right, out):
    layers, rows, cols = moved.shape
    lane = lax.broadcasted_iota(jnp.int32, (rows, LANES), 1)
    before = from_left[...].astype(jnp.float32)
    after = from_right[...].astype(jnp.float32)
    for level in range(layers):
        last = pltpu.roll(before, LANES - WIND_MAX * (level + 1), 1)
        first = pltpu.roll(after, LANES - WIND_MAX * level, 1) if level else after
        extra = jnp.where(lane < WIND_MAX, first, last)
        wide = jnp.concatenate([moved[level].astype(jnp.float32), extra], axis=1)
        shift = wind[1, level]
        shift = jnp.where(shift < 0, shift + cols + LANES, shift)
        out[level] = pltpu.roll(wide, shift, 1)[:, :cols].astype(jnp.bfloat16)


def sin_cos(phase):
    turns = jnp.floor(phase * (1.0 / np.pi) + 0.5)
    rest = phase - turns * 3.140625
    rest = rest - turns * 9.67653589793e-4
    odd = turns - 2.0 * jnp.floor(turns * 0.5)
    sign = 1.0 - 2.0 * odd
    square = rest * rest
    sine = -1.0 / 39916800.0
    for term in (1.0 / 362880.0, -1.0 / 5040.0, 1.0 / 120.0, -1.0 / 6.0, 1.0):
        sine = sine * square + term
    cosine = 1.0 / 479001600.0
    for term in (-1.0 / 3628800.0, 1.0 / 40320.0, -1.0 / 720.0, 1.0 / 24.0, -0.5, 1.0):
        cosine = cosine * square + term
    return sine * rest * sign, cosine * sign


def split(value):
    high = value.astype(jnp.bfloat16)
    low = (value - high.astype(jnp.float32)).astype(jnp.bfloat16)
    return high, low


def imaging_kernel(parts, amp_ref, cols_high, cols_low, rows_table, out):
    rows, cols = amp_ref.shape
    tiles = cols // LANES
    phase = parts[0].astype(jnp.float32)
    for k in range(1, parts.shape[0]):
        phase = phase + parts[k].astype(jnp.float32)
    sine, cosine = sin_cos(phase)
    amp = amp_ref[...]
    real, imag = amp * cosine, amp * sine
    field = jnp.concatenate(
        [
            jnp.concatenate(
                [real[:, t * LANES : (t + 1) * LANES], imag[:, t * LANES : (t + 1) * LANES]], axis=1
            )
            for t in range(tiles)
        ],
        axis=0,
    )
    high, low = split(field)
    dot = functools.partial(jnp.dot, preferred_element_type=jnp.float32)
    half = dot(high, cols_high[...]) + (dot(low, cols_high[...]) + dot(high, cols_low[...]))
    wide = 2 * LANES
    out_rows = 2 * rows
    for t in range(tiles):
        mine = half[t * rows : (t + 1) * rows]
        mine = jnp.concatenate([mine[:, :wide], mine[:, wide:]], axis=0)
        high, low = split(mine)
        full = dot(rows_table[...], jnp.concatenate([high, low, high], axis=0))
        real, imag = full[:out_rows], full[out_rows:]
        out[:, t * wide : (t + 1) * wide] = real * real + imag * imag


def tables(rows):
    freq = np.arange(SPOT_PIX)[:, None] - SPOT_PIX // 2
    angle = ((freq * np.arange(SUB_PIX)[None, :]) % SPOT_PIX) * (2.0 * np.pi / SPOT_PIX)
    cos, sin = np.cos(angle), np.sin(angle)

    def blocks(table, count):
        return np.kron(np.eye(count), table)

    per_tile = LANES // SUB_PIX
    col_cos, col_sin = blocks(cos.T, per_tile), blocks(sin.T, per_tile)
    columns = np.block([[col_cos, -col_sin], [col_sin, col_cos]])
    count = rows // SUB_PIX
    row_cos, row_sin = blocks(cos, count), blocks(sin, count)
    lines = np.block([[row_cos, row_sin], [-row_sin, row_cos]])

    def halves(value):
        value = value.astype(np.float32)
        high = value.astype(jnp.bfloat16)
        return high, (value - high.astype(np.float32)).astype(jnp.bfloat16)

    cols_high, cols_low = halves(columns)
    rows_high, rows_low = halves(lines)
    return cols_high, cols_low, np.concatenate([rows_high, rows_high, rows_low], axis=1)


def per_device(screens, amplitude, wind, offsets, ratio):
    layers, rows_dev, cols_dev = screens.shape
    n_layer = lax.axis_size("layer")
    n_dir = lax.axis_size("dir")
    assert n_dir == 4
    rows, pupil_cols = amplitude.shape
    pupil_rows = rows * n_layer
    screen_rows = rows_dev * n_dir
    bf16, f32 = jnp.bfloat16, jnp.float32
    wind = jnp.transpose(wind, (1, 0))
    offsets = jnp.transpose(offsets, (1, 2, 0))
    ratio = jnp.transpose(ratio, (1, 2, 0))

    def swap(value, bit):
        return lax.ppermute(value, "dir", [(i, i ^ bit) for i in range(n_dir)])

    def turn(value, step):
        return lax.ppermute(value, "layer", [(i, (i + step) % n_layer) for i in range(n_layer)])

    across = swap(screens, 2)
    near = swap(screens, 1)

    def shape(*dims, dtype=bf16):
        return jax.ShapeDtypeStruct(dims, dtype)

    ones = np.kron(np.eye(LANES // SUB_PIX), np.ones((SUB_PIX, SUB_PIX))).astype(np.float32)
    row_weights, col_weights, amp = call(
        functools.partial(weights_kernel, (n_layer, n_dir, rows_dev, cols_dev)),
        (
            shape(layers, pupil_rows, screen_rows),
            shape(layers, cols_dev, pupil_cols),
            shape(rows, pupil_cols, dtype=f32),
        ),
        (wind, offsets, ratio, amplitude, jnp.asarray(ones)),
        8_000_000,
        "weights",
    )
    across, row_weights, col_weights, amp = lax.optimization_barrier(
        (across, row_weights, col_weights, amp)
    )
    far = swap(across, 1)

    partials = call(
        functools.partial(project_kernel, n_dir),
        shape(n_layer, rows, pupil_cols),
        (row_weights, col_weights, screens, near, across, far),
        1_400_000_000,
        "project",
    )
    received = lax.all_to_all(partials, "layer", 0, 0, tiled=True)

    moved, right, left = call(
        rows_kernel,
        (shape(layers, rows_dev, cols_dev), shape(rows_dev, LANES), shape(rows_dev, LANES)),
        (wind, screens, near, far),
        1_000_000,
        "shift_rows",
    )
    from_left = turn(right, 1)
    from_right = turn(left, n_layer - 1)
    new_screens = call(
        cols_kernel,
        shape(layers, rows_dev, cols_dev),
        (wind, moved, from_left, from_right),
        1_000_000,
        "shift_cols",
    )

    spots = call(
        imaging_kernel,
        shape(2 * rows, 2 * pupil_cols, dtype=f32),
        (received, amp, *[jnp.asarray(table) for table in tables(rows)]),
        400_000_000,
        "imaging",
    )
    return (new_screens, spots[None])


def solution(mesh):
    return jax.shard_map(
        per_device,
        mesh=mesh,
        in_specs=(P(None, "dir", "layer"), P("layer", None), P(), P(), P()),
        out_specs=(P(None, "dir", "layer"), P("dir", "layer", None)),
        check_vma=False,
    )
```

```python
import functools

import jax
import jax.numpy as jnp
import numpy as np
from jax import lax
from jax.experimental import pallas as pl
from jax.experimental.pallas import tpu as pltpu
from jax.sharding import PartitionSpec as P

SUB_PIX = 16
SPOT_PIX = 32
WIND_MAX = 8
LANES = 128

SMEM_SPEC = pl.BlockSpec(memory_space=pltpu.SMEM)
VMEM_SPEC = pl.BlockSpec(memory_space=pltpu.VMEM)


def params(*arrays):
    held = sum(array.size * array.dtype.itemsize for array in jax.tree.leaves(arrays))
    return pltpu.CompilerParams(vmem_limit_bytes=held + 8 * 1024 * 1024)


def call(kernel, out_shape, operands, flops, name):
    def spec(array):
        return SMEM_SPEC if array.dtype == jnp.int32 else VMEM_SPEC

    out_specs = jax.tree.map(lambda _: VMEM_SPEC, out_shape)
    size = sum(array.size * array.dtype.itemsize for array in jax.tree.leaves((operands, out_shape)))
    return pl.pallas_call(
        kernel,
        out_shape=out_shape,
        in_specs=[spec(array) for array in operands],
        out_specs=out_specs,
        compiler_params=params(operands, out_shape),
        cost_estimate=pl.CostEstimate(flops=flops, bytes_accessed=size, transcendentals=0),
        name=name,
    )(*operands)


def wrap(value, length):
    value = jnp.where(value < 0, value + length, value)
    return jnp.where(value >= length, value - length, value)


def spans(pixel, anchor, num, den, length):
    stretched = (pixel * num).astype(jnp.float32)
    den = jnp.full(pixel.shape, den, jnp.int32).astype(jnp.float32)
    whole = jnp.floor((stretched + 0.5) / den)
    fraction = (stretched - whole * den) / den
    base = wrap(anchor + whole.astype(jnp.int32), length)
    upper = wrap(base + 1, length)
    return base, upper, 1.0 - fraction, fraction


def early_kernel(n_layer, wind, offsets, ratio, amplitude, ones, own, near, rows_out, cols_out, amp_out, early_out):
    layers, rows_dev, cols_dev = own.shape
    pupil_rows = rows_out.shape[1]
    screen_rows = 4 * rows_dev
    pupil_cols = cols_out.shape[2]
    screen_cols = cols_dev * n_layer
    direction = lax.axis_index("dir")
    column = lax.axis_index("layer")
    block = pupil_rows // n_layer
    half = pupil_rows // 2
    row = lax.broadcasted_iota(jnp.int32, (half, LANES), 0)
    pair = row // block + column // 2
    pair = jnp.where(pair >= n_layer // 2, pair - n_layer // 2, pair)
    parity = lax.rem(column, 2)
    inside = lax.rem(row, block) + pair * (2 * block)
    pixel_rows = jnp.concatenate([inside + parity * block, inside + (1 - parity) * block], axis=0)
    lane = lax.broadcasted_iota(jnp.int32, (pupil_rows, LANES), 1)
    for level in range(layers):
        num = ratio[level, 0, direction]
        den = ratio[level, 1, direction]
        anchor = wrap(offsets[level, 0, direction] - wind[0, level], screen_rows)
        base, upper, low, high = spans(pixel_rows, anchor, num, den, screen_rows)

        def weights_of(peer):
            parts = []
            for part in range(rows_dev // LANES):
                index = lane + (jnp.bitwise_xor(direction, peer) * rows_dev + part * LANES)
                weight = jnp.where(index == base, low, 0.0)
                parts.append(jnp.where(index == upper, high, weight).astype(jnp.bfloat16))
            return parts

        mine = jnp.concatenate(weights_of(0) + weights_of(1), axis=1)
        screen = jnp.concatenate([own[level], near[level]], axis=0)
        early_out[level] = jnp.dot(mine, screen, preferred_element_type=jnp.float32)
        rows_out[level] = jnp.concatenate(weights_of(2) + weights_of(3), axis=1)

        anchor = wrap(offsets[level, 1, direction] - wind[1, level], screen_cols)
        first = lax.broadcasted_iota(jnp.int32, (cols_dev, LANES), 0) + column * cols_dev

        def tile(step, carry):
            start = pl.multiple_of(step * LANES, LANES)
            pixel = lax.broadcasted_iota(jnp.int32, (8, LANES), 1) + start
            base, upper, low, high = spans(pixel, anchor, num, den, screen_cols)
            index = first.reshape(cols_dev // 8, 8, LANES)
            weight = jnp.where(index == base[None], low[None], 0.0)
            weight = jnp.where(index == upper[None], high[None], weight)
            weight = weight.reshape(cols_dev, LANES).astype(jnp.bfloat16)
            cols_out[level, :, pl.ds(start, LANES)] = weight
            return carry

        lax.fori_loop(0, pupil_cols // LANES, tile, 0)
    rows = amplitude.shape[0]
    for step in range(pupil_cols // LANES):
        cut = slice(step * LANES, (step + 1) * LANES)
        amp = amplitude[:, cut]
        energy = (amp * amp).reshape(rows // SUB_PIX, SUB_PIX, LANES).sum(axis=1)
        energy = jnp.broadcast_to(energy[:, None], (rows // SUB_PIX, SUB_PIX, LANES)).reshape(rows, LANES)
        total = jnp.dot(energy, ones[...], precision=lax.Precision.HIGHEST, preferred_element_type=jnp.float32)
        amp_out[:, cut] = amp * lax.rsqrt(total)


def project_cols(projected, cols_ref, start, stop, kept, sent):
    layers, cols_dev, _ = cols_ref.shape
    blocks, size, _ = kept.shape
    for at in range(start, stop, 256):
        cols = cols_ref[:, :, at : at + 256].reshape(layers * cols_dev, 256)
        phase = jnp.dot(projected, cols, preferred_element_type=jnp.float32).astype(jnp.bfloat16)
        phase = phase.reshape(2, blocks, size, 256)
        kept[:, :, at - start : at - start + 256] = phase[0]
        sent[:, :, at - start : at - start + 256] = phase[1]


def first_kernel(stop, early, rows_ref, cols_ref, across, far, projected, kept, sent):
    layers = early.shape[0]
    width = across.shape[2]
    for level in range(layers):
        screen = jnp.concatenate([across[level], far[level]], axis=0)
        part = early[level] + jnp.dot(rows_ref[level], screen, preferred_element_type=jnp.float32)
        projected[:, level * width : (level + 1) * width] = part.astype(jnp.bfloat16)
    project_cols(projected[...], cols_ref, 0, stop, kept, sent)


def later_kernel(start, stop, projected, cols_ref, kept, sent):
    project_cols(projected[...], cols_ref, start, stop, kept, sent)


def add_kernel(kept, came, *outs):
    for k, out in enumerate(outs):
        out[...] = (kept[k].astype(jnp.float32) + came[k].astype(jnp.float32)).astype(jnp.bfloat16)


def rows_kernel(wind, own, near, far, moved, right, left):
    layers, rows, cols = own.shape
    odd = lax.rem(lax.axis_index("dir"), 2) == 1
    lane = lax.broadcasted_iota(jnp.int32, (rows, LANES), 1)
    to_right = jnp.zeros((rows, LANES), jnp.float32)
    to_left = jnp.zeros((rows, LANES), jnp.float32)
    for level in range(layers):
        near_last = near[level, rows - 16 :, :].astype(jnp.float32)
        near_first = near[level, :16, :].astype(jnp.float32)
        far_last = far[level, rows - 16 :, :].astype(jnp.float32)
        far_first = far[level, :16, :].astype(jnp.float32)
        before = jnp.where(odd, near_last, far_last)
        after = jnp.where(odd, far_first, near_first)
        wide = jnp.concatenate([before, own[level].astype(jnp.float32), after], axis=0)
        shift = wind[0, level]
        shift = jnp.where(shift < 0, shift + rows + 32, shift)
        wide = pltpu.roll(wide, shift, 0)[16 : 16 + rows]
        moved[level] = wide.astype(jnp.bfloat16)
        mine = (lane >= WIND_MAX * level) & (lane < WIND_MAX * (level + 1))
        last = pltpu.roll(wide[:, cols - LANES :], WIND_MAX * (level + 1), 1)
        to_right = jnp.where(mine, last, to_right)
        initial = wide[:, :LANES]
        if level:
            initial = pltpu.roll(initial, WIND_MAX * level, 1)
        to_left = jnp.where(mine, initial, to_left)
    right[...] = to_right.astype(jnp.bfloat16)
    left[...] = to_left.astype(jnp.bfloat16)


def cols_kernel(wind, moved, from_left, from_right, out):
    layers, rows, cols = moved.shape
    lane = lax.broadcasted_iota(jnp.int32, (rows, LANES), 1)
    before = from_left[...].astype(jnp.float32)
    after = from_right[...].astype(jnp.float32)
    for level in range(layers):
        last = pltpu.roll(before, LANES - WIND_MAX * (level + 1), 1)
        first = pltpu.roll(after, LANES - WIND_MAX * level, 1) if level else after
        extra = jnp.where(lane < WIND_MAX, first, last)
        wide = jnp.concatenate([moved[level].astype(jnp.float32), extra], axis=1)
        shift = wind[1, level]
        shift = jnp.where(shift < 0, shift + cols + LANES, shift)
        out[level] = pltpu.roll(wide, shift, 1)[:, :cols].astype(jnp.bfloat16)


def image(start, stop, pairs, operands, out_shape):
    size = sum(array.size * array.dtype.itemsize for array in operands)
    in_specs = [VMEM_SPEC] * (pairs + 4)
    aliases = {}
    if len(operands) > len(in_specs):
        aliases = {len(in_specs): 0}
        in_specs = in_specs + [pl.BlockSpec(memory_space=pl.ANY)]
    return pl.pallas_call(
        functools.partial(imaging_kernel, pairs, start),
        out_shape=out_shape,
        in_specs=in_specs,
        out_specs=pl.BlockSpec(memory_space=pl.ANY),
        scratch_shapes=[pltpu.VMEM((out_shape.shape[0], 2 * (stop - start)), jnp.float32), pltpu.SemaphoreType.DMA],
        input_output_aliases=aliases,
        compiler_params=params(operands, out_shape),
        cost_estimate=pl.CostEstimate(flops=200_000_000, bytes_accessed=size, transcendentals=0),
        name="imaging",
    )(*operands)


def sin_cos(phase):
    turns = jnp.floor(phase * (1.0 / np.pi) + 0.5)
    rest = phase - turns * 3.140625
    rest = rest - turns * 9.67653589793e-4
    odd = turns - 2.0 * jnp.floor(turns * 0.5)
    sign = 1.0 - 2.0 * odd
    square = rest * rest
    sine = -1.0 / 39916800.0
    for term in (1.0 / 362880.0, -1.0 / 5040.0, 1.0 / 120.0, -1.0 / 6.0, 1.0):
        sine = sine * square + term
    cosine = 1.0 / 479001600.0
    for term in (-1.0 / 3628800.0, 1.0 / 40320.0, -1.0 / 720.0, 1.0 / 24.0, -0.5, 1.0):
        cosine = cosine * square + term
    return sine * rest * sign, cosine * sign


def split(value):
    high = value.astype(jnp.bfloat16)
    low = (value - high.astype(jnp.float32)).astype(jnp.bfloat16)
    return high, low


def imaging_kernel(count, start, *refs):
    parts = refs[:count]
    amp_ref, cols_high, cols_low, rows_table = refs[count : count + 4]
    whole, out, sem = refs[-3:]
    rows, cols = parts[0].shape
    tiles = cols // LANES
    phase = parts[0][...].astype(jnp.float32)
    for part in parts[1:]:
        phase = phase + part[...].astype(jnp.float32)
    sine, cosine = sin_cos(phase)
    amp = amp_ref[:, start : start + cols]
    real, imag = amp * cosine, amp * sine
    field = jnp.concatenate(
        [
            jnp.concatenate(
                [real[:, t * LANES : (t + 1) * LANES], imag[:, t * LANES : (t + 1) * LANES]], axis=1
            )
            for t in range(tiles)
        ],
        axis=0,
    )
    high, low = split(field)
    dot = functools.partial(jnp.dot, preferred_element_type=jnp.float32)
    half = dot(high, cols_high[...]) + (dot(low, cols_high[...]) + dot(high, cols_low[...]))
    wide = 2 * LANES
    out_rows = 2 * rows
    for t in range(tiles):
        mine = half[t * rows : (t + 1) * rows]
        mine = jnp.concatenate([mine[:, :wide], mine[:, wide:]], axis=0)
        high, low = split(mine)
        full = dot(rows_table[...], jnp.concatenate([high, low, high], axis=0))
        real, imag = full[:out_rows], full[out_rows:]
        out[:, t * wide : (t + 1) * wide] = real * real + imag * imag
    copy = pltpu.make_async_copy(out, whole.at[:, 2 * start : 2 * (start + cols)], sem)
    copy.start()
    copy.wait()


def tables(rows):
    freq = np.arange(SPOT_PIX)[:, None] - SPOT_PIX // 2
    angle = ((freq * np.arange(SUB_PIX)[None, :]) % SPOT_PIX) * (2.0 * np.pi / SPOT_PIX)
    cos, sin = np.cos(angle), np.sin(angle)

    def blocks(table, count):
        return np.kron(np.eye(count), table)

    per_tile = LANES // SUB_PIX
    col_cos, col_sin = blocks(cos.T, per_tile), blocks(sin.T, per_tile)
    columns = np.block([[col_cos, -col_sin], [col_sin, col_cos]])
    count = rows // SUB_PIX
    row_cos, row_sin = blocks(cos, count), blocks(sin, count)
    lines = np.block([[row_cos, row_sin], [-row_sin, row_cos]])

    def halves(value):
        value = value.astype(np.float32)
        high = value.astype(jnp.bfloat16)
        return high, (value - high.astype(np.float32)).astype(jnp.bfloat16)

    cols_high, cols_low = halves(columns)
    rows_high, rows_low = halves(lines)
    return cols_high, cols_low, np.concatenate([rows_high, rows_high, rows_low], axis=1)


def per_device(screens, amplitude, wind, offsets, ratio):
    layers, rows_dev, cols_dev = screens.shape
    n_layer = lax.axis_size("layer")
    n_dir = lax.axis_size("dir")
    assert n_dir == 4
    rows, pupil_cols = amplitude.shape
    pupil_rows = rows * n_layer
    screen_rows = rows_dev * n_dir
    bf16, f32 = jnp.bfloat16, jnp.float32
    wind = jnp.transpose(wind, (1, 0))
    offsets = jnp.transpose(offsets, (1, 2, 0))
    ratio = jnp.transpose(ratio, (1, 2, 0))

    def swap(value, bit):
        return lax.ppermute(value, "dir", [(i, i ^ bit) for i in range(n_dir)])

    def turn(value, step):
        return lax.ppermute(value, "layer", [(i, (i + step) % n_layer) for i in range(n_layer)])

    def shape(*dims, dtype=bf16):
        return jax.ShapeDtypeStruct(dims, dtype)

    across = swap(screens, 2)
    near = swap(screens, 1)
    ones = np.kron(np.eye(LANES // SUB_PIX), np.ones((SUB_PIX, SUB_PIX))).astype(np.float32)
    row_weights, col_weights, amp, early = call(
        functools.partial(early_kernel, n_layer),
        (
            shape(layers, pupil_rows, 2 * rows_dev),
            shape(layers, cols_dev, pupil_cols),
            shape(rows, pupil_cols, dtype=f32),
            shape(layers, pupil_rows, cols_dev, dtype=f32),
        ),
        (wind, offsets, ratio, amplitude, jnp.asarray(ones), screens, near),
        200_000_000,
        "early",
    )
    across, row_weights, col_weights, amp, early = lax.optimization_barrier(
        (across, row_weights, col_weights, amp, early)
    )
    far = swap(across, 1)

    pairs = n_layer // 2
    cuts = [0, (pupil_cols * 5 // 8) // 256 * 256, pupil_cols]
    kept, sent = [None, None], [None, None]

    def halves(piece):
        return [shape(pairs, rows, cuts[piece + 1] - cuts[piece])] * 2

    projected, kept[0], sent[0] = call(
        functools.partial(first_kernel, cuts[1]),
        [shape(pupil_rows, layers * cols_dev)] + halves(0),
        (early, row_weights, col_weights, across, far),
        800_000_000,
        "project_first",
    )
    kept[1], sent[1] = call(
        functools.partial(later_kernel, cuts[1], cuts[2]),
        halves(1),
        (projected, col_weights),
        500_000_000,
        "project_later",
    )
    received = []
    for piece in range(2):
        came = lax.ppermute(sent[piece], "layer", [(i, i ^ 1) for i in range(n_layer)])
        sums = call(
            add_kernel,
            [shape(rows, cuts[piece + 1] - cuts[piece])] * pairs,
            (kept[piece], came),
            1_000_000,
            "add_pair",
        )
        received.append([sums[0]] + [turn(sums[k], 2 * k) for k in range(1, pairs)])

    moved, right, left = call(
        rows_kernel,
        (shape(layers, rows_dev, cols_dev), shape(rows_dev, LANES), shape(rows_dev, LANES)),
        (wind, screens, near, far),
        1_000_000,
        "shift_rows",
    )
    from_left = turn(right, 1)
    from_right = turn(left, n_layer - 1)
    new_screens = call(
        cols_kernel,
        shape(layers, rows_dev, cols_dev),
        (wind, moved, from_left, from_right),
        1_000_000,
        "shift_cols",
    )

    dft = [jnp.asarray(table) for table in tables(rows)]
    spots = None
    for piece in range(2):
        start, stop = cuts[piece], cuts[piece + 1]
        operands = [*received[piece], amp, *dft] + ([] if spots is None else [spots])
        spots = image(start, stop, pairs, operands, shape(2 * rows, 2 * pupil_cols, dtype=f32))
    return (new_screens, spots[None])


def solution(mesh):
    return jax.shard_map(
        per_device,
        mesh=mesh,
        in_specs=(P(None, "dir", "layer"), P("layer", None), P(), P(), P()),
        out_specs=(P(None, "dir", "layer"), P("dir", "layer", None)),
        check_vma=False,
    )
```

```python
import functools

import jax
import jax.numpy as jnp
import numpy as np
from jax import lax
from jax.experimental import pallas as pl
from jax.experimental.pallas import tpu as pltpu
from jax.sharding import PartitionSpec as P

SUB_PIX = 16
SPOT_PIX = 32
WIND_MAX = 8
LANES = 128
STRIP = 32

HBM_SPEC = pl.BlockSpec(memory_space=pltpu.HBM)
VMEM_SPEC = pl.BlockSpec(memory_space=pltpu.VMEM)


def params(*arrays):
    held = sum(array.size * array.dtype.itemsize for array in jax.tree.leaves(arrays))
    return pltpu.CompilerParams(vmem_limit_bytes=held + 8 * 1024 * 1024)


def call(kernel, out_shape, operands, flops, name, in_hbm=(), scratch=()):
    def spec(k, array):
        return HBM_SPEC if array.dtype == jnp.int32 or k in in_hbm else VMEM_SPEC

    out_specs = jax.tree.map(lambda _: VMEM_SPEC, out_shape)
    size = sum(array.size * array.dtype.itemsize for array in jax.tree.leaves((operands, out_shape)))
    in_specs = [spec(k, array) for k, array in enumerate(operands)]
    operands = [
        pltpu.with_memory_space_constraint(array, pltpu.HBM) if space is HBM_SPEC else array
        for array, space in zip(operands, in_specs)
    ]
    return pl.pallas_call(
        kernel,
        out_shape=out_shape,
        in_specs=in_specs,
        out_specs=out_specs,
        scratch_shapes=list(scratch),
        compiler_params=params(operands, out_shape),
        cost_estimate=pl.CostEstimate(flops=flops, bytes_accessed=size, transcendentals=0),
        name=name,
    )(*operands)


def fetch(*pairs):
    copies = [pltpu.make_async_copy(source, target, sem) for source, target, sem in pairs]
    for copy in copies:
        copy.start()
    return copies


def wrap(value, length):
    value = jnp.where(value < 0, value + length, value)
    return jnp.where(value >= length, value - length, value)


def spans(pixel, anchor, num, den, length):
    stretched = (pixel * num).astype(jnp.float32)
    den = jnp.full(pixel.shape, den, jnp.int32).astype(jnp.float32)
    whole = jnp.floor((stretched + 0.5) / den)
    fraction = (stretched - whole * den) / den
    base = wrap(anchor + whole.astype(jnp.int32), length)
    upper = wrap(base + 1, length)
    return base, upper, 1.0 - fraction, fraction


def early_kernel(n_layer, wind_hbm, offsets_hbm, ratio_hbm, own_hbm, near, rows_out, cols_out, early_out, own, *scratch):
    wind, offsets, ratio, sems = scratch
    loads = fetch(
        (wind_hbm, wind, sems.at[0]),
        (offsets_hbm, offsets, sems.at[1]),
        (ratio_hbm, ratio, sems.at[2]),
        (own_hbm, own, sems.at[3]),
    )
    for load in loads:
        load.wait()
    layers, rows_dev, cols_dev = own.shape
    pupil_rows = rows_out.shape[1]
    screen_rows = 4 * rows_dev
    pupil_cols = cols_out.shape[2]
    screen_cols = cols_dev * n_layer
    direction = lax.axis_index("dir")
    column = lax.axis_index("layer")
    block = pupil_rows // n_layer
    half = pupil_rows // 2
    row = lax.broadcasted_iota(jnp.int32, (half, LANES), 0)
    pair = row // block + column // 2
    pair = jnp.where(pair >= n_layer // 2, pair - n_layer // 2, pair)
    parity = lax.rem(column, 2)
    inside = lax.rem(row, block) + pair * (2 * block)
    pixel_rows = jnp.concatenate([inside + parity * block, inside + (1 - parity) * block], axis=0)
    lane = lax.broadcasted_iota(jnp.int32, (pupil_rows, LANES), 1)
    for level in range(layers):
        num = ratio[level, 0, direction]
        den = ratio[level, 1, direction]
        anchor = wrap(offsets[level, 0, direction] - wind[0, level], screen_rows)
        base, upper, low, high = spans(pixel_rows, anchor, num, den, screen_rows)

        def weights_of(peer):
            parts = []
            for part in range(rows_dev // LANES):
                index = lane + (jnp.bitwise_xor(direction, peer) * rows_dev + part * LANES)
                weight = jnp.where(index == base, low, 0.0)
                parts.append(jnp.where(index == upper, high, weight).astype(jnp.bfloat16))
            return parts

        mine = jnp.concatenate(weights_of(0) + weights_of(1), axis=1)
        screen = jnp.concatenate([own[level], near[level]], axis=0)
        early_out[level] = jnp.dot(mine, screen, preferred_element_type=jnp.float32)
        rows_out[level] = jnp.concatenate(weights_of(2) + weights_of(3), axis=1)

        anchor = wrap(offsets[level, 1, direction] - wind[1, level], screen_cols)
        first = lax.broadcasted_iota(jnp.int32, (cols_dev, LANES), 0) + column * cols_dev

        def tile(step, carry):
            start = pl.multiple_of(step * LANES, LANES)
            pixel = lax.broadcasted_iota(jnp.int32, (8, LANES), 1) + start
            base, upper, low, high = spans(pixel, anchor, num, den, screen_cols)
            index = first.reshape(cols_dev // 8, 8, LANES)
            weight = jnp.where(index == base[None], low[None], 0.0)
            weight = jnp.where(index == upper[None], high[None], weight)
            weight = weight.reshape(cols_dev, LANES).astype(jnp.bfloat16)
            cols_out[level, :, pl.ds(start, LANES)] = weight
            return carry

        lax.fori_loop(0, pupil_cols // LANES, tile, 0)


def optics_kernel(amplitude, ones, columns, lines, amp_out, high_out, low_out, lines_out):
    rows, pupil_cols = amplitude.shape
    for step in range(pupil_cols // LANES):
        cut = slice(step * LANES, (step + 1) * LANES)
        amp = amplitude[:, cut]
        energy = (amp * amp).reshape(rows // SUB_PIX, SUB_PIX, LANES).sum(axis=1)
        energy = jnp.broadcast_to(energy[:, None], (rows // SUB_PIX, SUB_PIX, LANES)).reshape(rows, LANES)
        total = jnp.dot(energy, ones[...], precision=lax.Precision.HIGHEST, preferred_element_type=jnp.float32)
        amp_out[:, cut] = amp * lax.rsqrt(total)
    high_out[...], low_out[...] = split(columns[...])
    high, low = split(lines[...])
    lines_out[...] = jnp.concatenate([high, high, low], axis=1)


def project_cols(projected, cols_ref, start, stop, kept, sent):
    layers, cols_dev, _ = cols_ref.shape
    half = kept.shape[0]
    for at in range(start, stop, 256):
        cols = cols_ref[:, :, at : at + 256].reshape(layers * cols_dev, 256)
        phase = jnp.dot(projected, cols, preferred_element_type=jnp.float32).astype(jnp.bfloat16)
        kept[:, at - start : at - start + 256] = phase[:half]
        sent[:, at - start : at - start + 256] = phase[half:]


def shifted_rows(wind, own, near, far, level, start, stop):
    odd = lax.rem(lax.axis_index("dir"), 2) == 1
    rows = own.shape[1]
    near_last = near[level, rows - 16 :, start:stop].astype(jnp.float32)
    near_first = near[level, :16, start:stop].astype(jnp.float32)
    far_last = far[level, rows - 16 :, start:stop].astype(jnp.float32)
    far_first = far[level, :16, start:stop].astype(jnp.float32)
    before = jnp.where(odd, near_last, far_last)
    after = jnp.where(odd, far_first, near_first)
    wide = jnp.concatenate([before, own[level, :, start:stop].astype(jnp.float32), after], axis=0)
    shift = wind[0, level]
    shift = jnp.where(shift < 0, shift + rows + 32, shift)
    return pltpu.roll(wide, shift, 0)[16 : 16 + rows]


def first_kernel(stop, wind_hbm, early, rows_ref, cols_ref, own, near, across, far, projected, kept, sent, wind, sem):
    load = fetch((wind_hbm, wind, sem))[0]
    layers, rows, width = own.shape
    for level in range(layers):
        screen = jnp.concatenate([across[level], far[level]], axis=0)
        part = early[level] + jnp.dot(rows_ref[level], screen, preferred_element_type=jnp.float32)
        projected[:, level * width : (level + 1) * width] = part.astype(jnp.bfloat16)
    project_cols(projected[...], cols_ref, 0, stop, kept, sent)
    load.wait()
    lane = lax.broadcasted_iota(jnp.int32, (rows, LANES), 1)
    strips = jnp.zeros((rows, LANES), jnp.float32)
    for level in range(layers):
        at = WIND_MAX * level
        last = shifted_rows(wind, own, near, far, level, width - LANES, width)
        last = pltpu.roll(last, WIND_MAX + at, 1)
        strips = jnp.where((lane >= at) & (lane < at + WIND_MAX), last, strips)
        at = STRIP + WIND_MAX * level
        initial = pltpu.roll(shifted_rows(wind, own, near, far, level, 0, LANES), at, 1)
        strips = jnp.where((lane >= at) & (lane < at + WIND_MAX), initial, strips)
    strips = strips.T
    sent[: 2 * STRIP, stop:] = strips[: 2 * STRIP].astype(jnp.bfloat16)
    sent[2 * STRIP :, stop:] = jnp.zeros((sent.shape[0] - 2 * STRIP, rows), jnp.bfloat16)


def later_kernel(start, stop, projected, cols_ref, kept, sent):
    project_cols(projected[...], cols_ref, start, stop, kept, sent)


def add_kernel(width, kept, came, *outs):
    rows = outs[0].shape[0]
    for k, out in enumerate(outs):
        cut = slice(k * rows, (k + 1) * rows)
        total = kept[cut].astype(jnp.float32) + came[cut, :width].astype(jnp.float32)
        out[:, :width] = total.astype(jnp.bfloat16)
        if out.shape[1] > width:
            out[:, width:] = came[:STRIP, width:] if k == 1 else came[STRIP : 2 * STRIP, width:]


def shift_kernel(wind_hbm, own, near, far, partner, below, above, out, wind, sem):
    load = fetch((wind_hbm, wind, sem))[0]
    layers, rows, cols = own.shape
    second = lax.rem(lax.axis_index("layer"), 2) == 1
    at = partner.shape[1] - rows
    partner_last = partner[:STRIP, at:].astype(jnp.float32)
    partner_first = partner[STRIP : 2 * STRIP, at:].astype(jnp.float32)
    at = below.shape[1] - rows
    left = jnp.where(second, partner_last, below[:, at:].astype(jnp.float32))
    right = jnp.where(second, above[:, at:].astype(jnp.float32), partner_first)
    strips = jnp.concatenate([left, right, jnp.zeros((LANES - 2 * STRIP, rows), jnp.float32)], axis=0).T
    lane = lax.broadcasted_iota(jnp.int32, (rows, LANES), 1)
    load.wait()
    for level in range(layers):
        last = pltpu.roll(strips, LANES - WIND_MAX * (level + 1), 1)
        first = pltpu.roll(strips, LANES - STRIP - WIND_MAX * level, 1)
        extra = jnp.where(lane < WIND_MAX, first, last)
        moved = shifted_rows(wind, own, near, far, level, 0, cols)
        shift = wind[1, level]
        shift = jnp.where(shift < 0, shift + cols + LANES, shift)
        wide = pltpu.roll(jnp.concatenate([moved, extra], axis=1), shift, 1)
        out[level] = wide[:, :cols].astype(jnp.bfloat16)


def image(start, stop, pairs, operands, out_shape):
    size = sum(array.size * array.dtype.itemsize for array in operands)
    in_specs = [VMEM_SPEC] * (pairs + 4)
    aliases = {}
    if len(operands) > len(in_specs):
        aliases = {len(in_specs): 0}
        in_specs = in_specs + [HBM_SPEC]
    return pl.pallas_call(
        functools.partial(imaging_kernel, pairs, start),
        out_shape=jax.ShapeDtypeStruct(out_shape.shape, out_shape.dtype),
        in_specs=in_specs,
        out_specs=HBM_SPEC,
        scratch_shapes=[pltpu.VMEM((out_shape.shape[0], 2 * (stop - start)), jnp.float32), pltpu.SemaphoreType.DMA],
        input_output_aliases=aliases,
        compiler_params=params(operands, out_shape),
        cost_estimate=pl.CostEstimate(flops=200_000_000, bytes_accessed=size, transcendentals=0),
        name="imaging",
    )(*operands)


def sin_cos(phase):
    turns = jnp.floor(phase * (1.0 / np.pi) + 0.5)
    rest = phase - turns * 3.140625
    rest = rest - turns * 9.67653589793e-4
    odd = turns - 2.0 * jnp.floor(turns * 0.5)
    sign = 1.0 - 2.0 * odd
    square = rest * rest
    sine = -1.0 / 39916800.0
    for term in (1.0 / 362880.0, -1.0 / 5040.0, 1.0 / 120.0, -1.0 / 6.0, 1.0):
        sine = sine * square + term
    cosine = 1.0 / 479001600.0
    for term in (-1.0 / 3628800.0, 1.0 / 40320.0, -1.0 / 720.0, 1.0 / 24.0, -0.5, 1.0):
        cosine = cosine * square + term
    return sine * rest * sign, cosine * sign


def split(value):
    high = value.astype(jnp.bfloat16)
    low = (value - high.astype(jnp.float32)).astype(jnp.bfloat16)
    return high, low


def imaging_kernel(count, start, *refs):
    parts = refs[:count]
    amp_ref, cols_high, cols_low, rows_table = refs[count : count + 4]
    whole, out, sem = refs[-3:]
    rows, cols = parts[0].shape
    tiles = cols // LANES
    phase = parts[0][...].astype(jnp.float32)
    for part in parts[1:]:
        phase = phase + part[:, :cols].astype(jnp.float32)
    sine, cosine = sin_cos(phase)
    amp = amp_ref[:, start : start + cols]
    real, imag = amp * cosine, amp * sine
    field = jnp.concatenate(
        [
            jnp.concatenate(
                [real[:, t * LANES : (t + 1) * LANES], imag[:, t * LANES : (t + 1) * LANES]], axis=1
            )
            for t in range(tiles)
        ],
        axis=0,
    )
    high, low = split(field)
    dot = functools.partial(jnp.dot, preferred_element_type=jnp.float32)
    half = dot(high, cols_high[...]) + (dot(low, cols_high[...]) + dot(high, cols_low[...]))
    wide = 2 * LANES
    out_rows = 2 * rows
    for t in range(tiles):
        mine = half[t * rows : (t + 1) * rows]
        mine = jnp.concatenate([mine[:, :wide], mine[:, wide:]], axis=0)
        high, low = split(mine)
        full = dot(rows_table[...], jnp.concatenate([high, low, high], axis=0))
        real, imag = full[:out_rows], full[out_rows:]
        out[:, t * wide : (t + 1) * wide] = real * real + imag * imag
    copy = pltpu.make_async_copy(out, whole.at[:, 2 * start : 2 * (start + cols)], sem)
    copy.start()
    copy.wait()


def tables(rows):
    freq = np.arange(SPOT_PIX)[:, None] - SPOT_PIX // 2
    angle = ((freq * np.arange(SUB_PIX)[None, :]) % SPOT_PIX) * (2.0 * np.pi / SPOT_PIX)
    cos, sin = np.cos(angle), np.sin(angle)

    def blocks(table, count):
        return np.kron(np.eye(count), table)

    per_tile = LANES // SUB_PIX
    col_cos, col_sin = blocks(cos.T, per_tile), blocks(sin.T, per_tile)
    columns = np.block([[col_cos, -col_sin], [col_sin, col_cos]])
    count = rows // SUB_PIX
    row_cos, row_sin = blocks(cos, count), blocks(sin, count)
    lines = np.block([[row_cos, row_sin], [-row_sin, row_cos]])

    return columns.astype(np.float32), lines.astype(np.float32)


def per_device(screens, amplitude, wind, offsets, ratio):
    layers, rows_dev, cols_dev = screens.shape
    n_layer = lax.axis_size("layer")
    n_dir = lax.axis_size("dir")
    assert n_dir == 4
    rows, pupil_cols = amplitude.shape
    pupil_rows = rows * n_layer
    screen_rows = rows_dev * n_dir
    bf16, f32 = jnp.bfloat16, jnp.float32
    wind = jnp.transpose(wind, (1, 0))
    offsets = jnp.transpose(offsets, (1, 2, 0))
    ratio = jnp.transpose(ratio, (1, 2, 0))

    def swap(value, bit):
        return lax.ppermute(value, "dir", [(i, i ^ bit) for i in range(n_dir)])

    def turn(value, step):
        return lax.ppermute(value, "layer", [(i, (i + step) % n_layer) for i in range(n_layer)])

    def shape(*dims, dtype=bf16):
        return jax.ShapeDtypeStruct(dims, dtype)

    across = swap(screens, 2)
    near = swap(screens, 1)
    smem, sem = pltpu.SMEM, pltpu.SemaphoreType.DMA
    row_weights, col_weights, early, own = call(
        functools.partial(early_kernel, n_layer),
        (
            shape(layers, pupil_rows, 2 * rows_dev),
            shape(layers, cols_dev, pupil_cols),
            shape(layers, pupil_rows, cols_dev, dtype=f32),
            shape(layers, rows_dev, cols_dev),
        ),
        (wind, offsets, ratio, screens, near),
        200_000_000,
        "early",
        in_hbm=(3,),
        scratch=[smem(array.shape, jnp.int32) for array in (wind, offsets, ratio)] + [sem((4,))],
    )
    across, row_weights, col_weights, early, own = lax.optimization_barrier(
        (across, row_weights, col_weights, early, own)
    )
    far = swap(across, 1)

    pairs = n_layer // 2
    cuts = [0, (pupil_cols * 5 // 8) // 256 * 256, pupil_cols]
    kept, sent = [None, None], [None, None]
    widths = [stop - start for start, stop in zip(cuts, cuts[1:])]
    half = pairs * rows
    assert half >= 2 * STRIP and rows == STRIP and pairs > 2
    wind_scratch = [smem(wind.shape, jnp.int32), sem]

    projected, kept[0], sent[0] = call(
        functools.partial(first_kernel, cuts[1]),
        [shape(pupil_rows, layers * cols_dev), shape(half, widths[0]), shape(half, widths[0] + rows_dev)],
        (wind, early, row_weights, col_weights, own, near, across, far),
        800_000_000,
        "project_first",
        scratch=wind_scratch,
    )
    kept[1], sent[1] = call(
        functools.partial(later_kernel, cuts[1], cuts[2]),
        [shape(half, widths[1])] * 2,
        (projected, col_weights),
        500_000_000,
        "project_later",
    )
    came = [lax.ppermute(part, "layer", [(i, i ^ 1) for i in range(n_layer)]) for part in sent]

    amplitude, kept[1] = lax.optimization_barrier((amplitude, kept[1]))
    ones = np.kron(np.eye(LANES // SUB_PIX), np.ones((SUB_PIX, SUB_PIX))).astype(np.float32)
    columns, lines = tables(rows)
    optics = call(
        optics_kernel,
        (
            shape(rows, pupil_cols, dtype=f32),
            shape(*columns.shape),
            shape(*columns.shape),
            shape(lines.shape[0], 3 * lines.shape[1]),
        ),
        (amplitude, jnp.asarray(ones), jnp.asarray(columns), jnp.asarray(lines)),
        30_000_000,
        "optics",
    )
    kept[0], *optics = lax.optimization_barrier((kept[0], *optics))

    received = []
    for piece in range(2):
        extra = [rows_dev if piece == 0 and k in (1, pairs - 1) else 0 for k in range(pairs)]
        sums = call(
            functools.partial(add_kernel, widths[piece]),
            [shape(rows, widths[piece] + more) for more in extra],
            (kept[piece], came[piece]),
            1_000_000,
            "add_pair",
        )
        received.append([sums[0]] + [turn(sums[k], 2 * k) for k in range(1, pairs)])

    spots = image(cuts[0], cuts[1], pairs, [*received[0], *optics], shape(2 * rows, 2 * pupil_cols, dtype=f32))
    new_screens = call(
        shift_kernel,
        shape(layers, rows_dev, cols_dev),
        (wind, own, near, far, came[0], received[0][1], received[0][pairs - 1]),
        1_000_000,
        "shift",
        scratch=wind_scratch,
    )
    spots = image(cuts[1], cuts[2], pairs, [*received[1], *optics, spots], spots)
    return (new_screens, spots[None])


def solution(mesh):
    return jax.shard_map(
        per_device,
        mesh=mesh,
        in_specs=(P(None, "dir", "layer"), P("layer", None), P(), P(), P()),
        out_specs=(P(None, "dir", "layer"), P("dir", "layer", None)),
        check_vma=False,
    )
```

```python
import functools

import jax
import jax.numpy as jnp
import numpy as np
from jax import lax
from jax.experimental import pallas as pl
from jax.experimental.pallas import tpu as pltpu
from jax.sharding import PartitionSpec as P

SUB_PIX = 16
SPOT_PIX = 32
WIND_MAX = 8
LANES = 128
STRIP = 32

HBM_SPEC = pl.BlockSpec(memory_space=pltpu.HBM)
VMEM_SPEC = pl.BlockSpec(memory_space=pltpu.VMEM)


def params(*arrays):
    held = sum(array.size * array.dtype.itemsize for array in jax.tree.leaves(arrays))
    return pltpu.CompilerParams(vmem_limit_bytes=held + 8 * 1024 * 1024)


def call(kernel, out_shape, operands, flops, name, in_hbm=(), scratch=()):
    def spec(k, array):
        return HBM_SPEC if array.dtype == jnp.int32 or k in in_hbm else VMEM_SPEC

    out_specs = jax.tree.map(lambda _: VMEM_SPEC, out_shape)
    size = sum(array.size * array.dtype.itemsize for array in jax.tree.leaves((operands, out_shape)))
    in_specs = [spec(k, array) for k, array in enumerate(operands)]
    operands = [
        pltpu.with_memory_space_constraint(array, pltpu.HBM) if space is HBM_SPEC else array
        for array, space in zip(operands, in_specs)
    ]
    return pl.pallas_call(
        kernel,
        out_shape=out_shape,
        in_specs=in_specs,
        out_specs=out_specs,
        scratch_shapes=list(scratch),
        compiler_params=params(operands, out_shape),
        cost_estimate=pl.CostEstimate(flops=flops, bytes_accessed=size, transcendentals=0),
        name=name,
    )(*operands)


def fetch(*pairs):
    copies = [pltpu.make_async_copy(source, target, sem) for source, target, sem in pairs]
    for copy in copies:
        copy.start()
    return copies


def wrap(value, length):
    value = jnp.where(value < 0, value + length, value)
    return jnp.where(value >= length, value - length, value)


def spans(pixel, anchor, num, den, length):
    stretched = (pixel * num).astype(jnp.float32)
    den = jnp.full(pixel.shape, den, jnp.int32).astype(jnp.float32)
    whole = jnp.floor((stretched + 0.5) / den)
    fraction = (stretched - whole * den) / den
    base = wrap(anchor + whole.astype(jnp.int32), length)
    upper = wrap(base + 1, length)
    return base, upper, 1.0 - fraction, fraction


def weights_kernel(n_layer, wind_hbm, offsets_hbm, ratio_hbm, own_hbm, rows_out, mine_out, other_out, own, *scratch):
    wind, offsets, ratio, sems = scratch
    loads = fetch(
        (wind_hbm, wind, sems.at[0]),
        (offsets_hbm, offsets, sems.at[1]),
        (ratio_hbm, ratio, sems.at[2]),
        (own_hbm, own, sems.at[3]),
    )
    for load in loads[:3]:
        load.wait()
    layers, rows_dev, cols_dev = own.shape
    half = rows_out.shape[1]
    screen_rows = 4 * rows_dev
    pupil_cols = mine_out.shape[2]
    screen_cols = cols_dev * n_layer
    direction = lax.axis_index("dir")
    column = lax.axis_index("layer")
    pairs = n_layer // 2
    block = half // pairs
    row = lax.broadcasted_iota(jnp.int32, (half, LANES), 0)
    pair = row // block + column // 2
    pair = jnp.where(pair >= pairs, pair - pairs, pair)
    pixel_rows = lax.rem(row, block) + (2 * pair + lax.rem(column, 2)) * block
    lane = lax.broadcasted_iota(jnp.int32, (half, LANES), 1)
    for level in range(layers):
        num = ratio[level, 0, direction]
        den = ratio[level, 1, direction]
        anchor = wrap(offsets[level, 0, direction] - wind[0, level], screen_rows)
        base, upper, low, high = spans(pixel_rows, anchor, num, den, screen_rows)
        for peer in range(4):
            for part in range(rows_dev // LANES):
                index = lane + (jnp.bitwise_xor(direction, peer) * rows_dev + part * LANES)
                weight = jnp.where(index == base, low, 0.0)
                weight = jnp.where(index == upper, high, weight)
                start = peer * rows_dev + part * LANES
                rows_out[level, :, start : start + LANES] = weight.astype(jnp.bfloat16)

        anchor = wrap(offsets[level, 1, direction] - wind[1, level], screen_cols)
        sub = lax.broadcasted_iota(jnp.int32, (cols_dev, LANES), 0).reshape(cols_dev // 8, 8, LANES)

        def tile(step, carry):
            start = pl.multiple_of(step * LANES, LANES)
            pixel = lax.broadcasted_iota(jnp.int32, (8, LANES), 1) + start
            base, upper, low, high = spans(pixel, anchor, num, den, screen_cols)
            for out, first in ((mine_out, column), (other_out, jnp.bitwise_xor(column, 1))):
                shift = first * cols_dev
                weight = jnp.where(sub == (base - shift)[None], low[None], 0.0)
                weight = jnp.where(sub == (upper - shift)[None], high[None], weight)
                out[level, :, pl.ds(start, LANES)] = weight.reshape(cols_dev, LANES).astype(jnp.bfloat16)
            return carry

        lax.fori_loop(0, pupil_cols // LANES, tile, 0)
    loads[3].wait()


def optics_kernel(amplitude, ones, columns, lines, amp_out, high_out, low_out, lines_out):
    rows, pupil_cols = amplitude.shape
    for step in range(pupil_cols // LANES):
        cut = slice(step * LANES, (step + 1) * LANES)
        amp = amplitude[:, cut]
        energy = (amp * amp).reshape(rows // SUB_PIX, SUB_PIX, LANES).sum(axis=1)
        energy = jnp.broadcast_to(energy[:, None], (rows // SUB_PIX, SUB_PIX, LANES)).reshape(rows, LANES)
        total = jnp.dot(energy, ones[...], precision=lax.Precision.HIGHEST, preferred_element_type=jnp.float32)
        amp_out[:, cut] = amp * lax.rsqrt(total)
    high_out[...], low_out[...] = split(columns[...])
    high, low = split(lines[...])
    lines_out[...] = jnp.concatenate([high, high, low], axis=1)


def stack(*blocks):
    return jnp.concatenate(blocks, axis=0)


def dot(left, right):
    return jnp.dot(left, right, preferred_element_type=jnp.float32)


def middle_kernel(rows_ref, cols_ref, own, near, across, far, beside, beside_near, phase, partial):
    layers, rows, _ = own.shape
    projected = []
    for level in range(layers):
        screen = stack(own[level], near[level], across[level], far[level])
        projected.append(dot(rows_ref[level], screen).astype(jnp.bfloat16))
        screen = stack(beside[level], beside_near[level])
        partial[level] = dot(rows_ref[level, :, : 2 * rows], screen)
    projected = jnp.concatenate(projected, axis=1)
    for at in range(0, phase.shape[1], 256):
        cols = cols_ref[:, :, at : at + 256].reshape(projected.shape[1], 256)
        phase[:, at : at + 256] = dot(projected, cols)


def shifted_rows(shift, own, near, far, start, stop):
    odd = lax.rem(lax.axis_index("dir"), 2) == 1
    own, near, far = [block[:, start:stop].astype(jnp.float32) for block in (own, near, far)]
    rows = own.shape[0]
    near_last, near_first = near[rows - 16 :], near[:16]
    far_last, far_first = far[rows - 16 :], far[:16]
    before = jnp.where(odd, near_last, far_last)
    after = jnp.where(odd, far_first, near_first)
    wide = jnp.concatenate([before, own, after], axis=0)
    shift = jnp.where(shift < 0, shift + rows + 32, shift)
    return pltpu.roll(wide, shift, 0)[16 : 16 + rows]


def edge_strips(wind, own, near, far):
    layers, rows, width = own.shape
    lane = lax.broadcasted_iota(jnp.int32, (rows, LANES), 1)
    strips = jnp.zeros((rows, LANES), jnp.float32)
    for level in range(layers):
        blocks = wind[0, level], own[level], near[level], far[level]
        at = WIND_MAX * level
        last = pltpu.roll(shifted_rows(*blocks, width - LANES, width), WIND_MAX + at, 1)
        strips = jnp.where((lane >= at) & (lane < at + WIND_MAX), last, strips)
        at = STRIP + WIND_MAX * level
        initial = pltpu.roll(shifted_rows(*blocks, 0, LANES), at, 1)
        strips = jnp.where((lane >= at) & (lane < at + WIND_MAX), initial, strips)
    return strips


def last_kernel(wind_hbm, rows_ref, cols_ref, phase, partial, beside, beside_near, cross0, cross1, far0, far1, *refs):
    outs, (strips_out, wind, sem) = refs[:-3], refs[-3:]
    load = fetch((wind_hbm, wind, sem))[0]
    layers, _, width = partial.shape
    rows = beside.shape[1]
    projected = []
    for level in range(layers):
        screen = stack(cross0[level], cross1[level], far0[level], far1[level])
        part = partial[level] + dot(rows_ref[level, :, 2 * rows :], screen)
        projected.append(part.astype(jnp.bfloat16))
    projected = jnp.concatenate(projected, axis=1)
    size, pupil_cols = outs[0].shape
    for at in range(0, pupil_cols, 256):
        cols = cols_ref[:, :, at : at + 256].reshape(projected.shape[1], 256)
        total = (phase[:, at : at + 256] + dot(projected, cols)).astype(jnp.bfloat16)
        for k, out in enumerate(outs):
            out[:, at : at + 256] = total[k * size : (k + 1) * size]
    load.wait()
    far = [stack(far0[level], far1[level]) for level in range(layers)]
    strips = edge_strips(wind, beside, beside_near, far)
    strips_out[...] = strips
    strips = strips.T.astype(jnp.bfloat16)
    outs[1][:, pupil_cols:] = strips[:STRIP]
    outs[-1][:, pupil_cols:] = strips[STRIP : 2 * STRIP]


def shift_kernel(wind_hbm, own, near, far, partner, below, above, out, wind, sem):
    load = fetch((wind_hbm, wind, sem))[0]
    layers, rows, cols = own.shape
    second = lax.rem(lax.axis_index("layer"), 2) == 1
    at = below.shape[1] - rows
    others = stack(below[:, at:], above[:, at:], jnp.zeros((LANES - 2 * STRIP, rows), jnp.bfloat16))
    others = others.astype(jnp.float32).T
    lane = lax.broadcasted_iota(jnp.int32, (rows, LANES), 1)
    strips = jnp.where((lane < STRIP) == second, partner[...], others)
    load.wait()
    for level in range(layers):
        last = pltpu.roll(strips, LANES - WIND_MAX * (level + 1), 1)
        first = pltpu.roll(strips, LANES - STRIP - WIND_MAX * level, 1)
        extra = jnp.where(lane < WIND_MAX, first, last)
        moved = shifted_rows(wind[0, level], own[level], near[level], far[level], 0, cols)
        shift = wind[1, level]
        shift = jnp.where(shift < 0, shift + cols + LANES, shift)
        wide = pltpu.roll(jnp.concatenate([moved, extra], axis=1), shift, 1)
        out[level] = wide[:, :cols].astype(jnp.bfloat16)


def sin_cos(phase):
    turns = jnp.floor(phase * (1.0 / np.pi) + 0.5)
    rest = phase - turns * 3.140625
    rest = rest - turns * 9.67653589793e-4
    odd = turns - 2.0 * jnp.floor(turns * 0.5)
    sign = 1.0 - 2.0 * odd
    square = rest * rest
    sine = -1.0 / 39916800.0
    for term in (1.0 / 362880.0, -1.0 / 5040.0, 1.0 / 120.0, -1.0 / 6.0, 1.0):
        sine = sine * square + term
    cosine = 1.0 / 479001600.0
    for term in (-1.0 / 3628800.0, 1.0 / 40320.0, -1.0 / 720.0, 1.0 / 24.0, -0.5, 1.0):
        cosine = cosine * square + term
    return sine * rest * sign, cosine * sign


def split(value):
    high = value.astype(jnp.bfloat16)
    low = (value - high.astype(jnp.float32)).astype(jnp.bfloat16)
    return high, low


def imaging_kernel(count, *refs):
    parts = refs[:count]
    amp_ref, cols_high, cols_low, rows_table, out = refs[count:]
    rows, cols = amp_ref.shape
    tiles = cols // LANES
    phase = parts[0][:, :cols].astype(jnp.float32)
    for part in parts[1:]:
        phase = phase + part[:, :cols].astype(jnp.float32)
    sine, cosine = sin_cos(phase)
    amp = amp_ref[...]
    real, imag = amp * cosine, amp * sine
    field = jnp.concatenate(
        [
            jnp.concatenate(
                [real[:, t * LANES : (t + 1) * LANES], imag[:, t * LANES : (t + 1) * LANES]], axis=1
            )
            for t in range(tiles)
        ],
        axis=0,
    )
    high, low = split(field)
    half = dot(high, cols_high[...]) + (dot(low, cols_high[...]) + dot(high, cols_low[...]))
    wide = 2 * LANES
    out_rows = 2 * rows
    for t in range(tiles):
        mine = half[t * rows : (t + 1) * rows]
        mine = jnp.concatenate([mine[:, :wide], mine[:, wide:]], axis=0)
        high, low = split(mine)
        full = dot(rows_table[...], jnp.concatenate([high, low, high], axis=0))
        real, imag = full[:out_rows], full[out_rows:]
        out[:, t * wide : (t + 1) * wide] = real * real + imag * imag


def tables(rows):
    freq = np.arange(SPOT_PIX)[:, None] - SPOT_PIX // 2
    angle = ((freq * np.arange(SUB_PIX)[None, :]) % SPOT_PIX) * (2.0 * np.pi / SPOT_PIX)
    cos, sin = np.cos(angle), np.sin(angle)

    def blocks(table, count):
        return np.kron(np.eye(count), table)

    per_tile = LANES // SUB_PIX
    col_cos, col_sin = blocks(cos.T, per_tile), blocks(sin.T, per_tile)
    columns = np.block([[col_cos, -col_sin], [col_sin, col_cos]])
    count = rows // SUB_PIX
    row_cos, row_sin = blocks(cos, count), blocks(sin, count)
    lines = np.block([[row_cos, row_sin], [-row_sin, row_cos]])

    return columns.astype(np.float32), lines.astype(np.float32)


def per_device(screens, amplitude, wind, offsets, ratio):
    layers, rows_dev, cols_dev = screens.shape
    n_layer = lax.axis_size("layer")
    n_dir = lax.axis_size("dir")
    assert n_dir == 4
    rows, pupil_cols = amplitude.shape
    pairs = n_layer // 2
    half = pairs * rows
    assert rows == STRIP and pairs > 2
    bf16, f32 = jnp.bfloat16, jnp.float32
    wind = jnp.transpose(wind, (1, 0))
    offsets = jnp.transpose(offsets, (1, 2, 0))
    ratio = jnp.transpose(ratio, (1, 2, 0))
    smem, sem = pltpu.SMEM, pltpu.SemaphoreType.DMA

    def shape(*dims, dtype=bf16):
        return jax.ShapeDtypeStruct(dims, dtype)

    def swap(value, bit):
        return lax.ppermute(value, "dir", [(i, i ^ bit) for i in range(n_dir)])

    def partner(value):
        return lax.ppermute(value, "layer", [(i, i ^ 1) for i in range(n_layer)])

    def turn(value, step):
        return lax.ppermute(value, "layer", [(i, (i + step) % n_layer) for i in range(n_layer)])

    across = swap(screens, 2)
    beside = partner(screens)
    near = swap(screens, 1)
    row_weights, mine, other, own = call(
        functools.partial(weights_kernel, n_layer),
        (
            shape(layers, half, 4 * rows_dev),
            shape(layers, cols_dev, pupil_cols),
            shape(layers, cols_dev, pupil_cols),
            shape(layers, rows_dev, cols_dev),
        ),
        (wind, offsets, ratio, screens),
        100_000_000,
        "weights",
        in_hbm=(3,),
        scratch=[smem(array.shape, jnp.int32) for array in (wind, offsets, ratio)] + [sem((4,))],
    )
    across, beside, near, row_weights, mine, other, own = lax.optimization_barrier(
        (across, beside, near, row_weights, mine, other, own)
    )
    cut = rows_dev // 2
    upper, lower, across, beside = lax.optimization_barrier((beside[:, :cut], across[:, cut:], across, beside))
    cross0 = swap(upper, 2)
    cross1 = partner(lower)
    far = swap(across, 1)
    beside_near = swap(beside, 1)
    phase, partial = call(
        middle_kernel,
        (shape(half, pupil_cols, dtype=f32), shape(layers, half, cols_dev, dtype=f32)),
        (row_weights, mine, own, near, across, far, beside, beside_near),
        700_000_000,
        "middle",
    )

    ones = np.kron(np.eye(LANES // SUB_PIX), np.ones((SUB_PIX, SUB_PIX))).astype(np.float32)
    columns, lines = tables(rows)
    amplitude, far = lax.optimization_barrier((amplitude, far))
    optics = call(
        optics_kernel,
        (
            shape(rows, pupil_cols, dtype=f32),
            shape(*columns.shape),
            shape(*columns.shape),
            shape(lines.shape[0], 3 * lines.shape[1]),
        ),
        (amplitude, jnp.asarray(ones), jnp.asarray(columns), jnp.asarray(lines)),
        30_000_000,
        "optics",
    )
    cross0, cross1, phase, partial, *optics = lax.optimization_barrier((cross0, cross1, phase, partial, *optics))
    far0 = swap(cross0, 1)
    far1 = swap(cross1, 1)

    wind_scratch = [smem(wind.shape, jnp.int32), sem]
    extra = [rows_dev if k in (1, pairs - 1) else 0 for k in range(pairs)]
    *sums, strips = call(
        last_kernel,
        [shape(rows, pupil_cols + more) for more in extra] + [shape(rows_dev, LANES, dtype=f32)],
        (wind, row_weights, other, phase, partial, beside, beside_near, cross0, cross1, far0, far1),
        700_000_000,
        "last",
        scratch=wind_scratch,
    )
    received = [sums[0]] + [turn(sums[k], 2 * k) for k in range(1, pairs)]
    new_screens = call(
        shift_kernel,
        shape(layers, rows_dev, cols_dev),
        (wind, own, near, far, strips, received[1], received[pairs - 1]),
        1_000_000,
        "shift",
        scratch=wind_scratch,
    )
    spots = call(
        functools.partial(imaging_kernel, pairs),
        shape(2 * rows, 2 * pupil_cols, dtype=f32),
        (*received, *optics),
        400_000_000,
        "imaging",
    )
    return (new_screens, spots[None])


def solution(mesh):
    return jax.shard_map(
        per_device,
        mesh=mesh,
        in_specs=(P(None, "dir", "layer"), P("layer", None), P(), P(), P()),
        out_specs=(P(None, "dir", "layer"), P("dir", "layer", None)),
        check_vma=False,
    )
```

```python
import functools

import jax
import jax.numpy as jnp
import numpy as np
from jax import lax
from jax.experimental import pallas as pl
from jax.experimental.pallas import tpu as pltpu
from jax.sharding import PartitionSpec as P

SUB_PIX = 16
SPOT_PIX = 32
WIND_MAX = 8
LANES = 128
STRIP = 32

HBM_SPEC = pl.BlockSpec(memory_space=pltpu.HBM)
VMEM_SPEC = pl.BlockSpec(memory_space=pltpu.VMEM)


def params(*arrays):
    held = sum(array.size * array.dtype.itemsize for array in jax.tree.leaves(arrays))
    return pltpu.CompilerParams(vmem_limit_bytes=held + 8 * 1024 * 1024)


def call(kernel, out_shape, operands, flops, name, in_hbm=(), scratch=(), brief=False):
    def spec(k, array):
        scalars = array.dtype == jnp.int32 and array.size < LANES
        return HBM_SPEC if scalars or k in in_hbm else VMEM_SPEC

    out_specs = jax.tree.map(lambda _: VMEM_SPEC, out_shape)
    size = sum(array.size * array.dtype.itemsize for array in jax.tree.leaves((operands, out_shape)))
    if brief:
        flops = size = 0
    in_specs = [spec(k, array) for k, array in enumerate(operands)]
    operands = [
        pltpu.with_memory_space_constraint(array, pltpu.HBM) if space is HBM_SPEC else array
        for array, space in zip(operands, in_specs)
    ]
    return pl.pallas_call(
        kernel,
        out_shape=out_shape,
        in_specs=in_specs,
        out_specs=out_specs,
        scratch_shapes=list(scratch),
        compiler_params=params(operands, out_shape),
        cost_estimate=pl.CostEstimate(flops=flops, bytes_accessed=size, transcendentals=0),
        name=name,
    )(*operands)


def fetch(*pairs):
    copies = [pltpu.make_async_copy(source, target, sem) for source, target, sem in pairs]
    for copy in copies:
        copy.start()
    return copies


def wrap(value, length):
    value = jnp.where(value < 0, value + length, value)
    return jnp.where(value >= length, value - length, value)


def stack(*blocks):
    return jnp.concatenate(blocks, axis=0)


def beside(*blocks):
    return jnp.concatenate(blocks, axis=1)


def dot(left, right):
    return jnp.dot(left, right, preferred_element_type=jnp.float32)


def spans(pixel, anchor, num, den, length):
    stretched = (pixel * num).astype(jnp.float32)
    den = (jnp.zeros_like(pixel) + den).astype(jnp.float32)
    whole = jnp.floor((stretched + 0.5) / den)
    fraction = (stretched - whole * den) / den
    base = wrap(anchor + whole.astype(jnp.int32), length)
    upper = wrap(base + 1, length)
    return base, upper, 1.0 - fraction, fraction


def split_kernel(screens, *refs):
    own, outs, sems = refs[0], refs[1:-1], refs[-1]
    width = outs[0].shape[2]
    core = lax.rem(lax.axis_index("dir"), 2)
    pairs = []
    for k, out in enumerate(outs):
        half = core if k < 2 else 1 - core
        start = pl.multiple_of((2 * half + k % 2) * width, LANES)
        pairs.append((screens.at[:, :, pl.ds(start, width)], out, sems.at[k]))
    pairs.append((screens, own, sems.at[len(outs)]))
    for load in fetch(*pairs):
        load.wait()


def weights_kernel(geometry, wind_hbm, offsets_hbm, ratio_hbm, rows_out, base_out, upper_out, low_out, high_out, *scratch):
    n_layer, rows_dev, screen_cols = geometry
    wind, offsets, ratio, sems = scratch
    loads = fetch(
        (wind_hbm, wind, sems.at[0]),
        (offsets_hbm, offsets, sems.at[1]),
        (ratio_hbm, ratio, sems.at[2]),
    )
    _, layers, pupil_rows, screen_rows = rows_out.shape
    half = pupil_rows // 2
    direction = lax.axis_index("dir")
    column = lax.axis_index("layer")
    block = pupil_rows // n_layer
    row = lax.broadcasted_iota(jnp.int32, (half, LANES), 0)
    pair = jnp.bitwise_xor(row // block, column // 2)
    parity = lax.rem(column, 2)
    inside = lax.rem(row, block) + pair * (2 * block)
    pixel_rows = stack(inside + parity * block, inside + (1 - parity) * block)
    lane = lax.broadcasted_iota(jnp.int32, (pupil_rows, LANES), 1)
    for load in loads:
        load.wait()
    for side in range(2):
        target = jnp.bitwise_xor(direction, side)
        for level in range(layers):
            anchor = wrap(offsets[level, 0, target] - wind[0, level], screen_rows)
            num, den = ratio[level, 0, target], ratio[level, 1, target]
            base, upper, low, high = spans(pixel_rows, anchor, num, den, screen_rows)
            for peer in range(4):
                for part in range(rows_dev // LANES):
                    index = lane + (jnp.bitwise_xor(direction, peer) * rows_dev + part * LANES)
                    weight = jnp.where(index == base, low, 0.0)
                    weight = jnp.where(index == upper, high, weight)
                    start = peer * rows_dev + part * LANES
                    rows_out[side, level, :, start : start + LANES] = weight.astype(jnp.bfloat16)
    sub = lax.broadcasted_iota(jnp.int32, (8, LANES), 0)
    anchor, num, den = jnp.zeros_like(sub), jnp.zeros_like(sub), jnp.ones_like(sub)
    for level in range(layers):
        start = wrap(offsets[level, 1, direction] - wind[1, level], screen_cols)
        anchor = jnp.where(sub == level, start, anchor)
        num = jnp.where(sub == level, ratio[level, 0, direction], num)
        den = jnp.where(sub == level, ratio[level, 1, direction], den)
    for at in range(0, base_out.shape[1], LANES):
        pixel = lax.broadcasted_iota(jnp.int32, (8, LANES), 1) + at
        values = spans(pixel, anchor, num, den, screen_cols)
        for out, value in zip((base_out, upper_out, low_out, high_out), values):
            out[:, at : at + LANES] = value


def column_weights(base_ref, upper_ref, low_ref, high_ref, first, out):
    layers, cols_dev, pupil_cols = out.shape
    half = cols_dev // 2
    core = lax.rem(lax.axis_index("dir"), 2)
    sub = lax.broadcasted_iota(jnp.int32, (half, LANES), 0).reshape(half // 8, 8, LANES)
    for level in range(layers):

        def tile(step, carry):
            start = pl.multiple_of(step * LANES, LANES)
            cut = (slice(level, level + 1), pl.ds(start, LANES))
            base, upper, low, high = [
                jnp.broadcast_to(ref[cut], (8, LANES)) for ref in (base_ref, upper_ref, low_ref, high_ref)
            ]
            for side in range(2):
                shift = first + jnp.bitwise_xor(core, side) * half
                weight = jnp.where(sub == (base - shift)[None], low[None], 0.0)
                weight = jnp.where(sub == (upper - shift)[None], high[None], weight)
                weight = weight.reshape(half, LANES).astype(jnp.bfloat16)
                out[level, side * half : (side + 1) * half, pl.ds(start, LANES)] = weight
            return carry

        lax.fori_loop(0, pupil_cols // LANES, tile, 0)


def columns_kernel(*refs):
    tables, out = refs[:4], refs[-1]
    column_weights(*tables, lax.axis_index("layer") * out.shape[1], out)


def project_rows(chunk, rows_ref, keep, near, across, diagonal, level):
    width = keep.shape[2]
    core = lax.rem(lax.axis_index("dir"), 2)
    start = pl.multiple_of((2 * core + chunk) * width, LANES)
    screen = stack(keep[level], near[level, :, pl.ds(start, width)], across[level], diagonal[level])
    rows = stack(rows_ref[0, level], rows_ref[1, level])
    return dot(rows, screen).astype(jnp.bfloat16)


def first_rows_kernel(rows_ref, keep, near, across, diagonal, mine, sibling, other, sibling_other):
    layers, half, _ = mine.shape
    for level in range(layers):
        part = project_rows(0, rows_ref, keep, near, across, diagonal, level)
        for k, out in enumerate((mine, other, sibling, sibling_other)):
            out[level] = part[k * half : (k + 1) * half]


def later_rows_kernel(rows_ref, keep, near, across, diagonal, across0, sibling0, mine, other, sibling_other, give):
    layers, half, width = mine.shape
    rows = across.shape[1]
    for level in range(layers):
        part = project_rows(1, rows_ref, keep, near, across, diagonal, level)
        mine[level] = part[:half]
        other[level] = part[half : 2 * half]
        sibling_other[level] = part[3 * half :]
        give[level, :half, :width] = sibling0[level]
        give[level, :half, width:] = part[2 * half : 3 * half]
        for k, block in enumerate((across0, across)):
            cut = slice(k * width, (k + 1) * width)
            give[level, half : half + 16, cut] = block[level, :16]
            give[level, half + 16 :, cut] = block[level, rows - 16 :]


def project(parts, cols_refs, at):
    cols = stack(*[ref[level, start:stop, at : at + 256] for ref, level, start, stop in cols_refs])
    return dot(beside(*parts), cols)


def phase_kernel(*refs):
    tables, refs = refs[:4], refs[4:]
    cols_ref, mine0, mine1, came, sibling_came, phase, cols_out = refs
    first = jnp.bitwise_xor(lax.axis_index("layer"), 1) * cols_out.shape[1]
    column_weights(*tables, first, cols_out)
    layers, _, width = mine0.shape
    parts, cuts = [], []
    for level in range(layers):
        parts += [mine0[level], mine1[level], came[level], sibling_came[level]]
        cuts += [(cols_ref, level, 0, 2 * width)]
        cuts += [(cols_out, level, 0, width), (cols_out, level, 2 * width, 3 * width)]
    for at in range(0, phase.shape[1], 256):
        phase[:, at : at + 256] = project(parts, cuts, at)


def last_kernel(mine_ref, cols_ref, phase, taken, came, sibling_came, *outs):
    layers, half, width = came.shape
    size, pupil_cols = outs[0].shape
    parts, cuts = [], []
    for level in range(layers):
        parts += [taken[level, :half], came[level], sibling_came[level]]
        cuts += [(mine_ref, level, 2 * width, 4 * width)]
        cuts += [(cols_ref, level, width, 2 * width), (cols_ref, level, 3 * width, 4 * width)]
    for at in range(0, pupil_cols, 256):
        total = (phase[:, at : at + 256] + project(parts, cuts, at)).astype(jnp.bfloat16)
        for k, out in enumerate(outs):
            out[:, at : at + 256] = total[k * size : (k + 1) * size]


def shifted_rows(shift, own, near, edges):
    odd = lax.rem(lax.axis_index("dir"), 2) == 1
    own, near, edges = [block.astype(jnp.float32) for block in (own, near, edges)]
    rows = own.shape[0]
    before = jnp.where(odd, near[rows - 16 :], edges[16:])
    after = jnp.where(odd, edges[:16], near[:16])
    shift = jnp.where(shift < 0, shift + rows + 32, shift)
    return pltpu.roll(stack(before, own, after), shift, 0)[16 : 16 + rows]


def strips_kernel(wind_hbm, own, near, diagonal0, diagonal1, taken, right, left, edges, wind, sem):
    load = fetch((wind_hbm, wind, sem))[0]
    layers, rows, width = own.shape
    odd = lax.rem(lax.axis_index("dir"), 2) == 1
    half = taken.shape[1] - 32
    lane = lax.broadcasted_iota(jnp.int32, (rows, LANES), 1)
    strips = jnp.zeros((rows, LANES), jnp.float32)
    for level in range(layers):
        chunks = [stack(part[level, :16], part[level, rows - 16 :]) for part in (diagonal0, diagonal1)]
        here = beside(*chunks).astype(jnp.float32)
        there = taken[level, half:].astype(jnp.float32)
        both = beside(jnp.where(odd, there, here), jnp.where(odd, here, there))
        edges[level] = both.astype(jnp.bfloat16)
    load.wait()
    for level in range(layers):
        shift = wind[0, level]
        at = WIND_MAX * level
        cut = slice(width - LANES, width)
        last = shifted_rows(shift, own[level, :, cut], near[level, :, cut], edges[level, :, cut])
        strips = jnp.where((lane >= at) & (lane < at + WIND_MAX), pltpu.roll(last, WIND_MAX + at, 1), strips)
        at = STRIP + WIND_MAX * level
        cut = slice(0, LANES)
        initial = shifted_rows(shift, own[level, :, cut], near[level, :, cut], edges[level, :, cut])
        strips = jnp.where((lane >= at) & (lane < at + WIND_MAX), pltpu.roll(initial, at, 1), strips)
    strips = strips.T.astype(jnp.bfloat16)
    right[...] = strips[:STRIP]
    left[...] = strips[STRIP : 2 * STRIP]


def shift_kernel(wind_hbm, own, near, edges, from_left, from_right, out, wind, sem):
    load = fetch((wind_hbm, wind, sem))[0]
    layers, rows, cols = own.shape
    strips = stack(from_left[...], from_right[...], jnp.zeros((LANES - 2 * STRIP, rows), jnp.bfloat16))
    strips = strips.astype(jnp.float32).T
    lane = lax.broadcasted_iota(jnp.int32, (rows, LANES), 1)
    load.wait()
    for level in range(layers):
        last = pltpu.roll(strips, LANES - WIND_MAX * (level + 1), 1)
        first = pltpu.roll(strips, LANES - STRIP - WIND_MAX * level, 1)
        extra = jnp.where(lane < WIND_MAX, first, last)
        moved = shifted_rows(wind[0, level], own[level], near[level], edges[level])
        shift = wind[1, level]
        shift = jnp.where(shift < 0, shift + cols + LANES, shift)
        out[level] = pltpu.roll(beside(moved, extra), shift, 1)[:, :cols].astype(jnp.bfloat16)


def optics_kernel(*refs):
    sources, refs = refs[:4], refs[4:]
    amp_out, high_out, low_out, lines_out, amplitude, ones, columns, lines, sems = refs
    targets = amplitude, ones, columns, lines
    loads = fetch(*[(source, target, sems.at[k]) for k, (source, target) in enumerate(zip(sources, targets))])
    for load in loads:
        load.wait()
    rows, pupil_cols = amplitude.shape
    for step in range(pupil_cols // LANES):
        cut = slice(step * LANES, (step + 1) * LANES)
        amp = amplitude[:, cut]
        energy = (amp * amp).reshape(rows // SUB_PIX, SUB_PIX, LANES).sum(axis=1)
        energy = jnp.broadcast_to(energy[:, None], (rows // SUB_PIX, SUB_PIX, LANES)).reshape(rows, LANES)
        total = jnp.dot(energy, ones[...], precision=lax.Precision.HIGHEST, preferred_element_type=jnp.float32)
        amp_out[:, cut] = amp * lax.rsqrt(total)
    high_out[...], low_out[...] = split(columns[...])
    high, low = split(lines[...])
    lines_out[...] = jnp.concatenate([high, high, low], axis=1)


def sin_cos(phase):
    turns = jnp.floor(phase * (1.0 / np.pi) + 0.5)
    rest = phase - turns * 3.140625
    rest = rest - turns * 9.67653589793e-4
    odd = turns - 2.0 * jnp.floor(turns * 0.5)
    sign = 1.0 - 2.0 * odd
    square = rest * rest
    sine = -1.0 / 39916800.0
    for term in (1.0 / 362880.0, -1.0 / 5040.0, 1.0 / 120.0, -1.0 / 6.0, 1.0):
        sine = sine * square + term
    cosine = 1.0 / 479001600.0
    for term in (-1.0 / 3628800.0, 1.0 / 40320.0, -1.0 / 720.0, 1.0 / 24.0, -0.5, 1.0):
        cosine = cosine * square + term
    return sine * rest * sign, cosine * sign


def split(value):
    high = value.astype(jnp.bfloat16)
    low = (value - high.astype(jnp.float32)).astype(jnp.bfloat16)
    return high, low


def imaging_kernel(count, *refs):
    parts = refs[:count]
    amp_ref, cols_high, cols_low, rows_table, out = refs[count:]
    rows, cols = amp_ref.shape
    tiles = cols // LANES
    phase = parts[0][...].astype(jnp.float32)
    for part in parts[1:]:
        phase = phase + part[...].astype(jnp.float32)
    sine, cosine = sin_cos(phase)
    amp = amp_ref[...]
    real, imag = amp * cosine, amp * sine
    field = jnp.concatenate(
        [
            jnp.concatenate(
                [real[:, t * LANES : (t + 1) * LANES], imag[:, t * LANES : (t + 1) * LANES]], axis=1
            )
            for t in range(tiles)
        ],
        axis=0,
    )
    high, low = split(field)
    half = dot(high, cols_high[...]) + (dot(low, cols_high[...]) + dot(high, cols_low[...]))
    wide = 2 * LANES
    out_rows = 2 * rows
    for t in range(tiles):
        mine = half[t * rows : (t + 1) * rows]
        mine = jnp.concatenate([mine[:, :wide], mine[:, wide:]], axis=0)
        high, low = split(mine)
        full = dot(rows_table[...], jnp.concatenate([high, low, high], axis=0))
        real, imag = full[:out_rows], full[out_rows:]
        out[:, t * wide : (t + 1) * wide] = real * real + imag * imag


def tables_of(rows):
    freq = np.arange(SPOT_PIX)[:, None] - SPOT_PIX // 2
    angle = ((freq * np.arange(SUB_PIX)[None, :]) % SPOT_PIX) * (2.0 * np.pi / SPOT_PIX)
    cos, sin = np.cos(angle), np.sin(angle)

    def blocks(table, count):
        return np.kron(np.eye(count), table)

    per_tile = LANES // SUB_PIX
    col_cos, col_sin = blocks(cos.T, per_tile), blocks(sin.T, per_tile)
    columns = np.block([[col_cos, -col_sin], [col_sin, col_cos]])
    count = rows // SUB_PIX
    row_cos, row_sin = blocks(cos, count), blocks(sin, count)
    lines = np.block([[row_cos, row_sin], [-row_sin, row_cos]])

    return columns.astype(np.float32), lines.astype(np.float32)


def per_device(screens, amplitude, wind, offsets, ratio):
    layers, rows_dev, cols_dev = screens.shape
    n_layer = lax.axis_size("layer")
    n_dir = lax.axis_size("dir")
    rows, pupil_cols = amplitude.shape
    pairs = n_layer // 2
    half = pairs * rows
    pupil_rows = 2 * half
    assert n_dir == 4 and rows == STRIP and pairs > 2
    bf16, f32 = jnp.bfloat16, jnp.float32
    wind = jnp.transpose(wind, (1, 0))
    offsets = jnp.transpose(offsets, (1, 2, 0))
    ratio = jnp.transpose(ratio, (1, 2, 0))
    smem, sem = pltpu.SMEM, pltpu.SemaphoreType.DMA
    wind_scratch = [smem(wind.shape, jnp.int32), sem]

    def shape(*dims, dtype=bf16):
        return jax.ShapeDtypeStruct(dims, dtype)

    def swap(value, bits):
        return lax.ppermute(value, "dir", [(i, i ^ bits) for i in range(n_dir)])

    def partner(value, bits=0):
        count = n_layer * n_dir
        return lax.ppermute(value, ("layer", "dir"), [(i, i ^ n_dir ^ bits) for i in range(count)])

    def turn(value, step):
        return lax.ppermute(value, "layer", [(i, (i + step) % n_layer) for i in range(n_layer)])

    width = cols_dev // 4
    chunk = shape(layers, rows_dev, width)
    own, keep0, keep1, give0, give1 = call(
        split_kernel,
        [shape(*screens.shape)] + [chunk] * 4,
        (screens,),
        0,
        "split",
        in_hbm=(0,),
        scratch=[sem((5,))],
        brief=True,
    )
    across0 = swap(keep0, 2)
    diagonal0 = swap(give0, 3)
    across1 = swap(keep1, 2)
    diagonal1 = swap(give1, 3)
    near = swap(own, 1)
    row_weights, *tables = call(
        functools.partial(weights_kernel, (n_layer, rows_dev, cols_dev * n_layer)),
        [shape(2, layers, pupil_rows, 4 * rows_dev)]
        + [shape(8, pupil_cols, dtype=dtype) for dtype in (jnp.int32, jnp.int32, f32, f32)],
        (wind, offsets, ratio),
        0,
        "weights",
        scratch=[smem(array.shape, jnp.int32) for array in (wind, offsets, ratio)] + [sem((3,))],
        brief=True,
    )
    tables = tuple(tables)
    across0, diagonal0, row_weights, tables = lax.optimization_barrier((across0, diagonal0, row_weights, tables))

    projected = shape(layers, half, width)
    mine0, sibling0, other0, sibling_other0 = call(
        first_rows_kernel,
        [projected] * 4,
        (row_weights, keep0, near, across0, diagonal0),
        0,
        "rows_first",
        brief=True,
    )
    came0 = partner(other0)
    sibling_came0 = partner(sibling_other0, 1)

    tables, mine0 = lax.optimization_barrier((tables, mine0))
    cols = call(
        columns_kernel, shape(layers, cols_dev, pupil_cols), tables, 0, "columns", brief=True
    )
    cols, sibling0 = lax.optimization_barrier((cols, sibling0))
    mine1, other1, sibling_other1, give = call(
        later_rows_kernel,
        [projected] * 3 + [shape(layers, half + 32, 2 * width)],
        (row_weights, keep1, near, across1, diagonal1, across0, sibling0),
        0,
        "rows_later",
        brief=True,
    )
    came1 = partner(other1)
    sibling_came1 = partner(sibling_other1, 1)
    taken = swap(give, 1)

    phase, others = call(
        phase_kernel,
        (shape(half, pupil_cols, dtype=f32), shape(layers, cols_dev, pupil_cols)),
        (*tables, cols, mine0, mine1, came0, sibling_came0),
        10_000_000_000,
        "phase",
    )
    taken, phase = lax.optimization_barrier((taken, phase))
    right, left, edges = call(
        strips_kernel,
        [shape(STRIP, rows_dev)] * 2 + [shape(layers, 32, cols_dev)],
        (wind, own, near, diagonal0, diagonal1, taken),
        0,
        "strips",
        scratch=wind_scratch,
        brief=True,
    )
    from_left = turn(right, 1)
    from_right = turn(left, n_layer - 1)
    came1, from_left, from_right = lax.optimization_barrier((came1, from_left, from_right))
    sums = call(
        last_kernel,
        [shape(rows, pupil_cols)] * pairs,
        (cols, others, phase, taken, came1, sibling_came1),
        300_000_000,
        "last",
    )
    received = [sums[0]] + [
        lax.ppermute(sums[k], "layer", [(i, i ^ (2 * k)) for i in range(n_layer)])
        for k in sorted(range(1, pairs), key=lambda k: -(k & -k))
    ]

    ones = np.kron(np.eye(LANES // SUB_PIX), np.ones((SUB_PIX, SUB_PIX))).astype(np.float32)
    columns, lines = tables_of(rows)
    amplitude, edges, first = lax.optimization_barrier((amplitude, edges, sums[0]))
    received[0] = first
    optics_in = (amplitude, jnp.asarray(ones), jnp.asarray(columns), jnp.asarray(lines))
    optics = call(
        optics_kernel,
        (
            shape(rows, pupil_cols, dtype=f32),
            shape(*columns.shape),
            shape(*columns.shape),
            shape(lines.shape[0], 3 * lines.shape[1]),
        ),
        optics_in,
        30_000_000,
        "optics",
        in_hbm=range(4),
        scratch=[pltpu.VMEM(array.shape, f32) for array in optics_in] + [sem((4,))],
    )
    new_screens = call(
        shift_kernel,
        shape(layers, rows_dev, cols_dev),
        (wind, own, near, edges, from_left, from_right),
        1_000_000,
        "shift",
        scratch=wind_scratch,
    )
    spots = call(
        functools.partial(imaging_kernel, pairs),
        shape(2 * rows, 2 * pupil_cols, dtype=f32),
        (*received, *optics),
        400_000_000,
        "imaging",
    )
    return (new_screens, spots[None])


def solution(mesh):
    return jax.shard_map(
        per_device,
        mesh=mesh,
        in_specs=(P(None, "dir", "layer"), P("layer", None), P(), P(), P()),
        out_specs=(P(None, "dir", "layer"), P("dir", "layer", None)),
        check_vma=False,
    )
```

```python
import functools

import jax
import jax.numpy as jnp
import numpy as np
from jax import lax
from jax.experimental import pallas as pl
from jax.experimental.pallas import tpu as pltpu
from jax.sharding import PartitionSpec as P

SUB_PIX = 16
SPOT_PIX = 32
WIND_MAX = 8
LANES = 128
STRIP = 32

HBM_SPEC = pl.BlockSpec(memory_space=pltpu.HBM)
VMEM_SPEC = pl.BlockSpec(memory_space=pltpu.VMEM)


def params(*arrays):
    held = sum(array.size * array.dtype.itemsize for array in jax.tree.leaves(arrays))
    return pltpu.CompilerParams(vmem_limit_bytes=held + 8 * 1024 * 1024)


def call(kernel, out_shape, operands, flops, name, in_hbm=(), out_hbm=(), aliases=None, scratch=(), brief=False):
    def spec(k, array):
        scalars = array.dtype == jnp.int32 and array.size < LANES
        return HBM_SPEC if scalars or k in in_hbm else VMEM_SPEC

    count = len(jax.tree.leaves(out_shape))
    out_specs = [HBM_SPEC if k in out_hbm else VMEM_SPEC for k in range(count)]
    out_specs = jax.tree.unflatten(jax.tree.structure(out_shape), out_specs)
    size = sum(array.size * array.dtype.itemsize for array in jax.tree.leaves((operands, out_shape)))
    if brief:
        flops = size = 0
    in_specs = [spec(k, array) for k, array in enumerate(operands)]
    operands = [
        pltpu.with_memory_space_constraint(array, pltpu.HBM) if space is HBM_SPEC else array
        for array, space in zip(operands, in_specs)
    ]
    return pl.pallas_call(
        kernel,
        out_shape=out_shape,
        in_specs=in_specs,
        out_specs=out_specs,
        scratch_shapes=list(scratch),
        input_output_aliases=aliases or {},
        compiler_params=params(operands, out_shape),
        cost_estimate=pl.CostEstimate(flops=flops, bytes_accessed=size, transcendentals=0),
        name=name,
    )(*operands)


def fetch(*pairs):
    copies = [pltpu.make_async_copy(source, target, sem) for source, target, sem in pairs]
    for copy in copies:
        copy.start()
    return copies


def wrap(value, length):
    value = jnp.where(value < 0, value + length, value)
    return jnp.where(value >= length, value - length, value)


def stack(*blocks):
    return jnp.concatenate(blocks, axis=0)


def beside(*blocks):
    return jnp.concatenate(blocks, axis=1)


def dot(left, right):
    return jnp.dot(left, right, preferred_element_type=jnp.float32)


def spans(pixel, anchor, num, den, length):
    stretched = (pixel * num).astype(jnp.float32)
    den = (jnp.zeros_like(pixel) + den).astype(jnp.float32)
    whole = jnp.floor((stretched + 0.5) / den)
    fraction = (stretched - whole * den) / den
    base = wrap(anchor + whole.astype(jnp.int32), length)
    upper = wrap(base + 1, length)
    return base, upper, 1.0 - fraction, fraction


def split_kernel(screens, *refs):
    own, outs, sems = refs[0], refs[1:-1], refs[-1]
    width = outs[0].shape[2]
    core = lax.rem(lax.axis_index("dir"), 2)
    pairs = []
    for k, out in enumerate(outs):
        half = core if k < 2 else 1 - core
        start = pl.multiple_of((2 * half + k % 2) * width, LANES)
        pairs.append((screens.at[:, :, pl.ds(start, width)], out, sems.at[k]))
    pairs.append((screens, own, sems.at[len(outs)]))
    for load in fetch(*pairs):
        load.wait()


def weights_kernel(geometry, wind_hbm, offsets_hbm, ratio_hbm, rows_out, base_out, upper_out, low_out, high_out, *scratch):
    n_layer, rows_dev, screen_cols = geometry
    wind, offsets, ratio, sems = scratch
    loads = fetch(
        (wind_hbm, wind, sems.at[0]),
        (offsets_hbm, offsets, sems.at[1]),
        (ratio_hbm, ratio, sems.at[2]),
    )
    _, layers, pupil_rows, screen_rows = rows_out.shape
    half = pupil_rows // 2
    direction = lax.axis_index("dir")
    column = lax.axis_index("layer")
    block = pupil_rows // n_layer
    row = lax.broadcasted_iota(jnp.int32, (half, LANES), 0)
    pair = row // block + column // 2
    pair = jnp.where(pair >= n_layer // 2, pair - n_layer // 2, pair)
    parity = lax.rem(column, 2)
    inside = lax.rem(row, block) + pair * (2 * block)
    pixel_rows = stack(inside + parity * block, inside + (1 - parity) * block)
    lane = lax.broadcasted_iota(jnp.int32, (pupil_rows, LANES), 1)
    for load in loads:
        load.wait()
    for side in range(2):
        target = jnp.bitwise_xor(direction, side)
        for level in range(layers):
            anchor = wrap(offsets[level, 0, target] - wind[0, level], screen_rows)
            num, den = ratio[level, 0, target], ratio[level, 1, target]
            base, upper, low, high = spans(pixel_rows, anchor, num, den, screen_rows)
            for peer in range(4):
                for part in range(rows_dev // LANES):
                    index = lane + (jnp.bitwise_xor(direction, peer) * rows_dev + part * LANES)
                    weight = jnp.where(index == base, low, 0.0)
                    weight = jnp.where(index == upper, high, weight)
                    start = peer * rows_dev + part * LANES
                    rows_out[side, level, :, start : start + LANES] = weight.astype(jnp.bfloat16)
    sub = lax.broadcasted_iota(jnp.int32, (8, LANES), 0)
    anchor, num, den = jnp.zeros_like(sub), jnp.zeros_like(sub), jnp.ones_like(sub)
    for level in range(layers):
        start = wrap(offsets[level, 1, direction] - wind[1, level], screen_cols)
        anchor = jnp.where(sub == level, start, anchor)
        num = jnp.where(sub == level, ratio[level, 0, direction], num)
        den = jnp.where(sub == level, ratio[level, 1, direction], den)
    for at in range(0, base_out.shape[1], LANES):
        pixel = lax.broadcasted_iota(jnp.int32, (8, LANES), 1) + at
        values = spans(pixel, anchor, num, den, screen_cols)
        for out, value in zip((base_out, upper_out, low_out, high_out), values):
            out[:, at : at + LANES] = value


def column_weights(base_ref, upper_ref, low_ref, high_ref, first, out):
    layers, cols_dev, pupil_cols = out.shape
    half = cols_dev // 2
    core = lax.rem(lax.axis_index("dir"), 2)
    sub = lax.broadcasted_iota(jnp.int32, (half, LANES), 0).reshape(half // 8, 8, LANES)
    for level in range(layers):

        def tile(step, carry):
            start = pl.multiple_of(step * LANES, LANES)
            cut = (slice(level, level + 1), pl.ds(start, LANES))
            base, upper, low, high = [
                jnp.broadcast_to(ref[cut], (8, LANES)) for ref in (base_ref, upper_ref, low_ref, high_ref)
            ]
            for side in range(2):
                shift = first + jnp.bitwise_xor(core, side) * half
                weight = jnp.where(sub == (base - shift)[None], low[None], 0.0)
                weight = jnp.where(sub == (upper - shift)[None], high[None], weight)
                weight = weight.reshape(half, LANES).astype(jnp.bfloat16)
                out[level, side * half : (side + 1) * half, pl.ds(start, LANES)] = weight
            return carry

        lax.fori_loop(0, pupil_cols // LANES, tile, 0)


def columns_kernel(*refs):
    tables, out = refs[:4], refs[-1]
    column_weights(*tables, lax.axis_index("layer") * out.shape[1], out)


def project_rows(chunk, rows_ref, keep, near, across, diagonal, level):
    width = keep.shape[2]
    core = lax.rem(lax.axis_index("dir"), 2)
    start = pl.multiple_of((2 * core + chunk) * width, LANES)
    screen = stack(keep[level], near[level, :, pl.ds(start, width)], across[level], diagonal[level])
    rows = stack(rows_ref[0, level], rows_ref[1, level])
    return dot(rows, screen).astype(jnp.bfloat16)


def first_rows_kernel(rows_ref, keep, near, across, diagonal, mine, sibling, other, sibling_other):
    layers, half, _ = mine.shape
    for level in range(layers):
        part = project_rows(0, rows_ref, keep, near, across, diagonal, level)
        for k, out in enumerate((mine, other, sibling, sibling_other)):
            out[level] = part[k * half : (k + 1) * half]


def outer_strip(wind, odd, own, near, far):
    rows = own[0].shape[0]
    core = lax.rem(lax.axis_index("dir"), 2)
    lane = lax.broadcasted_iota(jnp.int32, (rows, LANES), 1)
    strip = jnp.zeros((rows, LANES), jnp.float32)
    for level in range(len(own)):
        edges = stack(far[level][:16], far[level][rows - 16 :])
        moved = shifted_rows(wind[0, level], odd, own[level], near[level], edges)
        at = WIND_MAX * level
        moved = pltpu.roll(moved, at + WIND_MAX * core, 1)
        strip = jnp.where((lane >= at) & (lane < at + WIND_MAX), moved, strip)
    return strip.T[:STRIP].astype(jnp.bfloat16)


def put_strip(out, at, strip):
    for k in range(strip.shape[1] // LANES):
        out[at + k * STRIP : at + (k + 1) * STRIP, :] = strip[:, k * LANES : (k + 1) * LANES]


def get_strip(ref, at):
    return beside(*[ref[start : start + STRIP, :] for start in range(at, ref.shape[0], STRIP)])


def later_rows_kernel(wind_hbm, rows_ref, *refs):
    chunks, (near, sibling0), (mine, other, sibling_other, give, wind, sem) = refs[:6], refs[6:8], refs[8:]
    load = fetch((wind_hbm, wind, sem))[0]
    keep0, across0, diagonal0, keep, across, diagonal = chunks
    layers, half, width = mine.shape
    rows, cols = near.shape[1:]
    for level in range(layers):
        part = project_rows(1, rows_ref, keep, near, across, diagonal, level)
        mine[level] = part[:half]
        other[level * half : (level + 1) * half] = part[half : 2 * half]
        sibling_other[level * half : (level + 1) * half] = part[3 * half :]
        give[level, :half, :width] = sibling0[level]
        give[level, :half, width:] = part[2 * half : 3 * half]
        for k, block in enumerate((across0, across)):
            cut = slice(k * width, (k + 1) * width)
            give[level, half : half + 16, cut] = block[level, :16]
            give[level, half + 16 :, cut] = block[level, rows - 16 :]
    core = lax.rem(lax.axis_index("dir"), 2)
    start = pl.multiple_of(core * (cols - LANES), LANES)

    def outer(first, second):
        return [
            jnp.where(core == 1, second[level].astype(jnp.float32), first[level].astype(jnp.float32))
            for level in range(layers)
        ]

    own, far, sibling_far = outer(keep0, keep), outer(diagonal0, diagonal), outer(across0, across)
    beyond = [near[level, :, pl.ds(start, LANES)] for level in range(layers)]
    load.wait()
    put_strip(other, layers * half, outer_strip(wind, core == 1, own, beyond, far))
    put_strip(sibling_other, layers * half, outer_strip(wind, core == 0, beyond, own, sibling_far))


def project(parts, cols_refs, at):
    cols = stack(*[ref[level, start:stop, at : at + 256] for ref, level, start, stop in cols_refs])
    return dot(beside(*parts), cols)


def phase_kernel(*refs):
    tables, refs = refs[:4], refs[4:]
    cols_ref, mine0, mine1, came, sibling_came, phase, cols_out = refs
    first = jnp.bitwise_xor(lax.axis_index("layer"), 1) * cols_out.shape[1]
    column_weights(*tables, first, cols_out)
    layers, _, width = mine0.shape
    parts, cuts = [], []
    for level in range(layers):
        parts += [mine0[level], mine1[level], came[level], sibling_came[level]]
        cuts += [(cols_ref, level, 0, 2 * width)]
        cuts += [(cols_out, level, 0, width), (cols_out, level, 2 * width, 3 * width)]
    for at in range(0, phase.shape[1], 256):
        phase[:, at : at + 256] = project(parts, cuts, at)


def last_kernel(mine_ref, cols_ref, phase, taken, came, sibling_came, *outs):
    *outs, partner_strips = outs
    layers, _, width = taken.shape
    width = width // 2
    size, pupil_cols = outs[0].shape
    half = size * len(outs)
    parts, cuts = [], []
    for level in range(layers):
        cut = slice(level * half, (level + 1) * half)
        parts += [taken[level, :half], came[cut], sibling_came[cut]]
        cuts += [(mine_ref, level, 2 * width, 4 * width)]
        cuts += [(cols_ref, level, width, 2 * width), (cols_ref, level, 3 * width, 4 * width)]
    for at in range(0, pupil_cols, 256):
        total = (phase[:, at : at + 256] + project(parts, cuts, at)).astype(jnp.bfloat16)
        for k, out in enumerate(outs):
            out[:, at : at + 256] = total[k * size : (k + 1) * size]
    odd = lax.rem(lax.axis_index("dir"), 2) == 1
    here = get_strip(came, layers * half).astype(jnp.float32)
    there = get_strip(sibling_came, layers * half).astype(jnp.float32)
    last = jnp.where(odd, here, there).astype(jnp.bfloat16)
    first = jnp.where(odd, there, here).astype(jnp.bfloat16)
    outs[1][:, pupil_cols:] = last
    outs[-1][:, pupil_cols:] = first
    partner_strips[:STRIP] = last
    partner_strips[STRIP:] = first


def shifted_rows(shift, odd, own, near, edges):
    own, near, edges = [block.astype(jnp.float32) for block in (own, near, edges)]
    rows = own.shape[0]
    before = jnp.where(odd, near[rows - 16 :], edges[16:])
    after = jnp.where(odd, edges[:16], near[:16])
    shift = jnp.where(shift < 0, shift + rows + 32, shift)
    return pltpu.roll(stack(before, own, after), shift, 0)[16 : 16 + rows]


def shift_kernel(wind_hbm, own, near, diagonal0, diagonal1, taken, whole, ends, wind, sem, out):
    load = fetch((wind_hbm, wind, sem))[0]
    layers, rows, cols = own.shape
    odd = lax.rem(lax.axis_index("dir"), 2) == 1
    half = taken.shape[1] - 32
    load.wait()
    for level in range(layers):
        chunks = [stack(part[level, :16], part[level, rows - 16 :]) for part in (diagonal0, diagonal1)]
        here = beside(*chunks).astype(jnp.float32)
        there = taken[level, half:].astype(jnp.float32)
        edges = beside(jnp.where(odd, there, here), jnp.where(odd, here, there))
        moved = shifted_rows(wind[0, level], odd, own[level], near[level], edges)
        shift = wind[1, level]
        moved = pltpu.roll(moved, jnp.where(shift < 0, shift + cols, shift), 1).astype(jnp.bfloat16)
        out[level] = moved
        ends[0, level] = moved[:, :LANES]
        ends[1, level] = moved[:, cols - LANES :]
    copy = pltpu.make_async_copy(out, whole, sem)
    copy.start()
    copy.wait()


def patch_ends(wind, ends, partner_strips, below, above, out):
    _, layers, rows, _ = ends.shape
    second = lax.rem(lax.axis_index("layer"), 2) == 1
    at = below.shape[1] - rows
    strips = stack(partner_strips[:STRIP], below[:, at:], partner_strips[STRIP:], above[:, at:])
    strips = strips.astype(jnp.float32).T
    lane = lax.broadcasted_iota(jnp.int32, (rows, LANES), 1)
    left = jnp.where(second, 0, STRIP)
    right = jnp.where(second, 3 * STRIP, 2 * STRIP)
    for level in range(layers):
        shift = wind[1, level]
        at = WIND_MAX * (level + 1)
        value = pltpu.roll(strips, lax.rem(2 * LANES - at - left + shift, LANES), 1)
        out[0, level] = jnp.where(lane < shift, value, ends[0, level].astype(jnp.float32)).astype(jnp.bfloat16)
        at = WIND_MAX * level
        value = pltpu.roll(strips, lax.rem(2 * LANES - at - right + shift, LANES), 1)
        kept = ends[1, level].astype(jnp.float32)
        out[1, level] = jnp.where(lane >= LANES + shift, value, kept).astype(jnp.bfloat16)


def optics_kernel(*refs):
    sources, refs = refs[:4], refs[4:]
    amp_out, high_out, low_out, lines_out, amplitude, ones, columns, lines, sems = refs
    targets = amplitude, ones, columns, lines
    loads = fetch(*[(source, target, sems.at[k]) for k, (source, target) in enumerate(zip(sources, targets))])
    for load in loads:
        load.wait()
    rows, pupil_cols = amplitude.shape
    for step in range(pupil_cols // LANES):
        cut = slice(step * LANES, (step + 1) * LANES)
        amp = amplitude[:, cut]
        energy = (amp * amp).reshape(rows // SUB_PIX, SUB_PIX, LANES).sum(axis=1)
        energy = jnp.broadcast_to(energy[:, None], (rows // SUB_PIX, SUB_PIX, LANES)).reshape(rows, LANES)
        total = jnp.dot(energy, ones[...], precision=lax.Precision.HIGHEST, preferred_element_type=jnp.float32)
        amp_out[:, cut] = amp * lax.rsqrt(total)
    high_out[...], low_out[...] = split(columns[...])
    high, low = split(lines[...])
    lines_out[...] = jnp.concatenate([high, high, low], axis=1)


def sin_cos(phase):
    turns = jnp.floor(phase * (1.0 / np.pi) + 0.5)
    rest = phase - turns * 3.140625
    rest = rest - turns * 9.67653589793e-4
    odd = turns - 2.0 * jnp.floor(turns * 0.5)
    sign = 1.0 - 2.0 * odd
    square = rest * rest
    sine = -1.0 / 39916800.0
    for term in (1.0 / 362880.0, -1.0 / 5040.0, 1.0 / 120.0, -1.0 / 6.0, 1.0):
        sine = sine * square + term
    cosine = 1.0 / 479001600.0
    for term in (-1.0 / 3628800.0, 1.0 / 40320.0, -1.0 / 720.0, 1.0 / 24.0, -0.5, 1.0):
        cosine = cosine * square + term
    return sine * rest * sign, cosine * sign


def split(value):
    high = value.astype(jnp.bfloat16)
    low = (value - high.astype(jnp.float32)).astype(jnp.bfloat16)
    return high, low


def imaging_kernel(count, wind_hbm, *refs):
    parts, refs = refs[:count], refs[count:]
    amp_ref, cols_high, cols_low, rows_table, ends, partner_strips, _, out, screens, wind, patched, sems = refs
    load = fetch((wind_hbm, wind, sems.at[0]))[0]
    rows, cols = amp_ref.shape
    tiles = cols // LANES
    phase = parts[0][:, :cols].astype(jnp.float32)
    for part in parts[1:]:
        phase = phase + part[:, :cols].astype(jnp.float32)
    sine, cosine = sin_cos(phase)
    amp = amp_ref[...]
    real, imag = amp * cosine, amp * sine
    field = jnp.concatenate(
        [
            jnp.concatenate(
                [real[:, t * LANES : (t + 1) * LANES], imag[:, t * LANES : (t + 1) * LANES]], axis=1
            )
            for t in range(tiles)
        ],
        axis=0,
    )
    high, low = split(field)
    half = dot(high, cols_high[...]) + (dot(low, cols_high[...]) + dot(high, cols_low[...]))
    load.wait()
    patch_ends(wind, ends, partner_strips, parts[1], parts[-1], patched)
    width = screens.shape[2]
    copies = fetch(
        (patched.at[0], screens.at[:, :, :LANES], sems.at[1]),
        (patched.at[1], screens.at[:, :, width - LANES :], sems.at[2]),
    )
    wide = 2 * LANES
    out_rows = 2 * rows
    for t in range(tiles):
        mine = half[t * rows : (t + 1) * rows]
        mine = jnp.concatenate([mine[:, :wide], mine[:, wide:]], axis=0)
        high, low = split(mine)
        full = dot(rows_table[...], jnp.concatenate([high, low, high], axis=0))
        real, imag = full[:out_rows], full[out_rows:]
        out[:, t * wide : (t + 1) * wide] = real * real + imag * imag
    for copy in copies:
        copy.wait()


def tables_of(rows):
    freq = np.arange(SPOT_PIX)[:, None] - SPOT_PIX // 2
    angle = ((freq * np.arange(SUB_PIX)[None, :]) % SPOT_PIX) * (2.0 * np.pi / SPOT_PIX)
    cos, sin = np.cos(angle), np.sin(angle)

    def blocks(table, count):
        return np.kron(np.eye(count), table)

    per_tile = LANES // SUB_PIX
    col_cos, col_sin = blocks(cos.T, per_tile), blocks(sin.T, per_tile)
    columns = np.block([[col_cos, -col_sin], [col_sin, col_cos]])
    count = rows // SUB_PIX
    row_cos, row_sin = blocks(cos, count), blocks(sin, count)
    lines = np.block([[row_cos, row_sin], [-row_sin, row_cos]])

    return columns.astype(np.float32), lines.astype(np.float32)


def per_device(screens, amplitude, wind, offsets, ratio):
    layers, rows_dev, cols_dev = screens.shape
    n_layer = lax.axis_size("layer")
    n_dir = lax.axis_size("dir")
    rows, pupil_cols = amplitude.shape
    pairs = n_layer // 2
    half = pairs * rows
    pupil_rows = 2 * half
    assert n_dir == 4 and rows == STRIP and pairs > 2
    bf16, f32 = jnp.bfloat16, jnp.float32
    wind = jnp.transpose(wind, (1, 0))
    offsets = jnp.transpose(offsets, (1, 2, 0))
    ratio = jnp.transpose(ratio, (1, 2, 0))
    smem, sem = pltpu.SMEM, pltpu.SemaphoreType.DMA
    wind_scratch = [smem(wind.shape, jnp.int32), sem]

    def shape(*dims, dtype=bf16):
        return jax.ShapeDtypeStruct(dims, dtype)

    def swap(value, bits):
        return lax.ppermute(value, "dir", [(i, i ^ bits) for i in range(n_dir)])

    def partner(value, bits=0):
        count = n_layer * n_dir
        return lax.ppermute(value, ("layer", "dir"), [(i, i ^ n_dir ^ bits) for i in range(count)])

    def turn(value, step):
        return lax.ppermute(value, "layer", [(i, (i + step) % n_layer) for i in range(n_layer)])

    width = cols_dev // 4
    chunk = shape(layers, rows_dev, width)
    own, keep0, keep1, give0, give1 = call(
        split_kernel,
        [shape(*screens.shape)] + [chunk] * 4,
        (screens,),
        0,
        "split",
        in_hbm=(0,),
        scratch=[sem((5,))],
        brief=True,
    )
    across0 = swap(keep0, 2)
    diagonal0 = swap(give0, 3)
    across1 = swap(keep1, 2)
    diagonal1 = swap(give1, 3)
    near = swap(own, 1)
    row_weights, *tables = call(
        functools.partial(weights_kernel, (n_layer, rows_dev, cols_dev * n_layer)),
        [shape(2, layers, pupil_rows, 4 * rows_dev)]
        + [shape(8, pupil_cols, dtype=dtype) for dtype in (jnp.int32, jnp.int32, f32, f32)],
        (wind, offsets, ratio),
        0,
        "weights",
        scratch=[smem(array.shape, jnp.int32) for array in (wind, offsets, ratio)] + [sem((3,))],
        brief=True,
    )
    tables = tuple(tables)
    across0, diagonal0, row_weights, tables = lax.optimization_barrier((across0, diagonal0, row_weights, tables))

    projected = shape(layers, half, width)
    mine0, sibling0, other0, sibling_other0 = call(
        first_rows_kernel,
        [projected] * 4,
        (row_weights, keep0, near, across0, diagonal0),
        0,
        "rows_first",
        brief=True,
    )
    came0 = partner(other0)
    sibling_came0 = partner(sibling_other0, 1)

    tables, mine0 = lax.optimization_barrier((tables, mine0))
    cols = call(
        columns_kernel, shape(layers, cols_dev, pupil_cols), tables, 0, "columns", brief=True
    )
    cols, sibling0 = lax.optimization_barrier((cols, sibling0))
    message = shape(layers * half + STRIP * rows_dev // LANES, width)
    mine1, other1, sibling_other1, give = call(
        later_rows_kernel,
        [projected, message, message, shape(layers, half + 32, 2 * width)],
        (wind, row_weights, keep0, across0, diagonal0, keep1, across1, diagonal1, near, sibling0),
        0,
        "rows_later",
        scratch=wind_scratch,
        brief=True,
    )
    came1 = partner(other1)
    sibling_came1 = partner(sibling_other1, 1)
    taken = swap(give, 1)

    phase, others = call(
        phase_kernel,
        (shape(half, pupil_cols, dtype=f32), shape(layers, cols_dev, pupil_cols)),
        (*tables, cols, mine0, mine1, came0, sibling_came0),
        10_000_000_000,
        "phase",
    )

    ones = np.kron(np.eye(LANES // SUB_PIX), np.ones((SUB_PIX, SUB_PIX))).astype(np.float32)
    columns, lines = tables_of(rows)
    amplitude, phase = lax.optimization_barrier((amplitude, phase))
    optics_in = (amplitude, jnp.asarray(ones), jnp.asarray(columns), jnp.asarray(lines))
    optics = call(
        optics_kernel,
        (
            shape(rows, pupil_cols, dtype=f32),
            shape(*columns.shape),
            shape(*columns.shape),
            shape(lines.shape[0], 3 * lines.shape[1]),
        ),
        optics_in,
        30_000_000,
        "optics",
        in_hbm=range(4),
        scratch=[pltpu.VMEM(array.shape, f32) for array in optics_in] + [sem((4,))],
    )
    phase, optics = lax.optimization_barrier((phase, optics))
    extra = [rows_dev if k in (1, pairs - 1) else 0 for k in range(pairs)]
    *sums, strips = call(
        last_kernel,
        [shape(rows, pupil_cols + more) for more in extra] + [shape(2 * STRIP, rows_dev)],
        (cols, others, phase, taken, came1, sibling_came1),
        300_000_000,
        "last",
    )
    received = [sums[0]] + [None] * (pairs - 1)
    for k in sorted(range(1, pairs), key=lambda k: -min(k, pairs - k)):
        received[k] = turn(sums[k], 2 * k)

    diagonal0, strips = lax.optimization_barrier((diagonal0, strips))
    shifted, ends = call(
        shift_kernel,
        [shape(layers, rows_dev, cols_dev), shape(2, layers, rows_dev, LANES)],
        (wind, own, near, diagonal0, diagonal1, taken),
        1_000_000,
        "shift",
        scratch=wind_scratch + [pltpu.VMEM(own.shape, bf16)],
        out_hbm=(0,),
    )
    spots, new_screens = call(
        functools.partial(imaging_kernel, pairs),
        [shape(2 * rows, 2 * pupil_cols, dtype=f32), shape(layers, rows_dev, cols_dev)],
        (wind, *received, *optics, ends, strips, shifted),
        400_000_000,
        "imaging",
        in_hbm=(pairs + 7,),
        out_hbm=(1,),
        aliases={pairs + 7: 1},
        scratch=[wind_scratch[0], pltpu.VMEM(ends.shape, bf16), sem((3,))],
    )
    return (new_screens, spots[None])


def solution(mesh):
    return jax.shard_map(
        per_device,
        mesh=mesh,
        in_specs=(P(None, "dir", "layer"), P("layer", None), P(), P(), P()),
        out_specs=(P(None, "dir", "layer"), P("dir", "layer", None)),
        check_vma=False,
    )
```

```python
import functools

import jax
import jax.numpy as jnp
import numpy as np
from jax import lax
from jax.experimental import pallas as pl
from jax.experimental.pallas import tpu as pltpu
from jax.sharding import PartitionSpec as P

SUB_PIX = 16
SPOT_PIX = 32
WIND_MAX = 8
LANES = 128
STRIP = 32

HBM_SPEC = pl.BlockSpec(memory_space=pltpu.HBM)
VMEM_SPEC = pl.BlockSpec(memory_space=pltpu.VMEM)


def params(*arrays):
    held = sum(array.size * array.dtype.itemsize for array in jax.tree.leaves(arrays))
    return pltpu.CompilerParams(vmem_limit_bytes=held + 8 * 1024 * 1024)


def call(kernel, out_shape, operands, flops, name, in_hbm=(), scratch=(), brief=False):
    def spec(k, array):
        scalars = array.dtype == jnp.int32 and array.size < LANES
        return HBM_SPEC if scalars or k in in_hbm else VMEM_SPEC

    out_specs = jax.tree.map(lambda _: VMEM_SPEC, out_shape)
    size = sum(array.size * array.dtype.itemsize for array in jax.tree.leaves((operands, out_shape)))
    if brief:
        flops = size = 0
    in_specs = [spec(k, array) for k, array in enumerate(operands)]
    operands = [
        pltpu.with_memory_space_constraint(array, pltpu.HBM) if space is HBM_SPEC else array
        for array, space in zip(operands, in_specs)
    ]
    return pl.pallas_call(
        kernel,
        out_shape=out_shape,
        in_specs=in_specs,
        out_specs=out_specs,
        scratch_shapes=list(scratch),
        compiler_params=params(operands, out_shape),
        cost_estimate=pl.CostEstimate(flops=flops, bytes_accessed=size, transcendentals=0),
        name=name,
    )(*operands)


def fetch(*pairs):
    copies = [pltpu.make_async_copy(source, target, sem) for source, target, sem in pairs]
    for copy in copies:
        copy.start()
    return copies


def wrap(value, length):
    value = jnp.where(value < 0, value + length, value)
    return jnp.where(value >= length, value - length, value)


def stack(*blocks):
    return jnp.concatenate(blocks, axis=0)


def beside(*blocks):
    return jnp.concatenate(blocks, axis=1)


def dot(left, right):
    return jnp.dot(left, right, preferred_element_type=jnp.float32)


def spans(pixel, anchor, num, den, length):
    stretched = (pixel * num).astype(jnp.float32)
    den = (jnp.zeros_like(pixel) + den).astype(jnp.float32)
    whole = jnp.floor((stretched + 0.5) / den)
    fraction = (stretched - whole * den) / den
    base = wrap(anchor + whole.astype(jnp.int32), length)
    upper = wrap(base + 1, length)
    return base, upper, 1.0 - fraction, fraction


def split_kernel(screens, *refs):
    own, outs, sems = refs[0], refs[1:-1], refs[-1]
    width = outs[0].shape[2]
    core = lax.rem(lax.axis_index("dir"), 2)
    pairs = []
    for k, out in enumerate(outs):
        half = core if k < 2 else 1 - core
        start = pl.multiple_of((2 * half + k % 2) * width, LANES)
        pairs.append((screens.at[:, :, pl.ds(start, width)], out, sems.at[k]))
    pairs.append((screens, own, sems.at[len(outs)]))
    for load in fetch(*pairs):
        load.wait()


def weights_kernel(geometry, wind_hbm, offsets_hbm, ratio_hbm, *refs):
    n_layer, rows_dev, screen_cols = geometry
    sources, (rows_out, base_out, upper_out, low_out, high_out), refs = refs[:4], refs[4:9], refs[9:]
    copies, (wind, offsets, ratio, sems) = refs[:4], refs[4:]
    others = fetch(*[(source, copy, sems.at[3 + k]) for k, (source, copy) in enumerate(zip(sources, copies))])
    loads = fetch(
        (wind_hbm, wind, sems.at[0]),
        (offsets_hbm, offsets, sems.at[1]),
        (ratio_hbm, ratio, sems.at[2]),
    )
    _, layers, pupil_rows, screen_rows = rows_out.shape
    half = pupil_rows // 2
    direction = lax.axis_index("dir")
    column = lax.axis_index("layer")
    block = pupil_rows // n_layer
    row = lax.broadcasted_iota(jnp.int32, (half, LANES), 0)
    pair = jnp.bitwise_xor(row // block, column // 2)
    parity = lax.rem(column, 2)
    inside = lax.rem(row, block) + pair * (2 * block)
    pixel_rows = stack(inside + parity * block, inside + (1 - parity) * block)
    lane = lax.broadcasted_iota(jnp.int32, (pupil_rows, LANES), 1)
    for load in loads:
        load.wait()
    for side in range(2):
        target = jnp.bitwise_xor(direction, side)
        for level in range(layers):
            anchor = wrap(offsets[level, 0, target] - wind[0, level], screen_rows)
            num, den = ratio[level, 0, target], ratio[level, 1, target]
            base, upper, low, high = spans(pixel_rows, anchor, num, den, screen_rows)
            for peer in range(4):
                for part in range(rows_dev // LANES):
                    index = lane + (jnp.bitwise_xor(direction, peer) * rows_dev + part * LANES)
                    weight = jnp.where(index == base, low, 0.0)
                    weight = jnp.where(index == upper, high, weight)
                    start = peer * rows_dev + part * LANES
                    rows_out[side, level, :, start : start + LANES] = weight.astype(jnp.bfloat16)
    sub = lax.broadcasted_iota(jnp.int32, (8, LANES), 0)
    anchor, num, den = jnp.zeros_like(sub), jnp.zeros_like(sub), jnp.ones_like(sub)
    for level in range(layers):
        start = wrap(offsets[level, 1, direction] - wind[1, level], screen_cols)
        anchor = jnp.where(sub == level, start, anchor)
        num = jnp.where(sub == level, ratio[level, 0, direction], num)
        den = jnp.where(sub == level, ratio[level, 1, direction], den)
    for at in range(0, base_out.shape[1], LANES):
        pixel = lax.broadcasted_iota(jnp.int32, (8, LANES), 1) + at
        values = spans(pixel, anchor, num, den, screen_cols)
        for out, value in zip((base_out, upper_out, low_out, high_out), values):
            out[:, at : at + LANES] = value
    for load in others:
        load.wait()


def column_weights(base_ref, upper_ref, low_ref, high_ref, first, out):
    layers, cols_dev, pupil_cols = out.shape
    half = cols_dev // 2
    core = lax.rem(lax.axis_index("dir"), 2)
    sub = lax.broadcasted_iota(jnp.int32, (half, LANES), 0).reshape(half // 8, 8, LANES)
    for level in range(layers):

        def tile(step, carry):
            start = pl.multiple_of(step * LANES, LANES)
            cut = (slice(level, level + 1), pl.ds(start, LANES))
            base, upper, low, high = [
                jnp.broadcast_to(ref[cut], (8, LANES)) for ref in (base_ref, upper_ref, low_ref, high_ref)
            ]
            for side in range(2):
                shift = first + jnp.bitwise_xor(core, side) * half
                weight = jnp.where(sub == (base - shift)[None], low[None], 0.0)
                weight = jnp.where(sub == (upper - shift)[None], high[None], weight)
                weight = weight.reshape(half, LANES).astype(jnp.bfloat16)
                out[level, side * half : (side + 1) * half, pl.ds(start, LANES)] = weight
            return carry

        lax.fori_loop(0, pupil_cols // LANES, tile, 0)


def columns_kernel(*refs):
    tables, out = refs[:4], refs[-1]
    column_weights(*tables, lax.axis_index("layer") * out.shape[1], out)


def project_rows(chunk, rows_ref, keep, near, across, diagonal, level):
    width = keep.shape[2]
    core = lax.rem(lax.axis_index("dir"), 2)
    start = pl.multiple_of((2 * core + chunk) * width, LANES)
    screen = stack(keep[level], near[level, :, pl.ds(start, width)], across[level], diagonal[level])
    rows = stack(rows_ref[0, level], rows_ref[1, level])
    return dot(rows, screen).astype(jnp.bfloat16)


def first_rows_kernel(rows_ref, keep, near, across, diagonal, mine, sibling, other, sibling_other):
    layers, half, _ = mine.shape
    for level in range(layers):
        part = project_rows(0, rows_ref, keep, near, across, diagonal, level)
        for k, out in enumerate((mine, other, sibling, sibling_other)):
            out[level] = part[k * half : (k + 1) * half]


def outer_strip(wind, odd, own, near, far):
    rows = own[0].shape[0]
    core = lax.rem(lax.axis_index("dir"), 2)
    lane = lax.broadcasted_iota(jnp.int32, (rows, LANES), 1)
    strip = jnp.zeros((rows, LANES), jnp.float32)
    for level in range(len(own)):
        edges = stack(far[level][:16], far[level][rows - 16 :])
        moved = shifted_rows(wind[0, level], odd, own[level], near[level], edges)
        at = WIND_MAX * level
        moved = pltpu.roll(moved, at + WIND_MAX * core, 1)
        strip = jnp.where((lane >= at) & (lane < at + WIND_MAX), moved, strip)
    return strip.T[:STRIP].astype(jnp.bfloat16)


def put_strip(out, at, strip):
    for k in range(strip.shape[1] // LANES):
        out[at + k * STRIP : at + (k + 1) * STRIP, :] = strip[:, k * LANES : (k + 1) * LANES]


def get_strip(ref, at):
    return beside(*[ref[start : start + STRIP, :] for start in range(at, ref.shape[0], STRIP)])


def later_rows_kernel(wind_hbm, rows_ref, *refs):
    chunks, (near, sibling0), outs, (wind, sem) = refs[:6], refs[6:8], refs[8:-2], refs[-2:]
    mine, give, other, sibling_other = outs
    load = fetch((wind_hbm, wind, sem))[0]
    keep0, across0, diagonal0, keep, across, diagonal = chunks
    layers, half, width = mine.shape
    rows, cols = near.shape[1:]
    for level in range(layers):
        part = project_rows(1, rows_ref, keep, near, across, diagonal, level)
        mine[level] = part[:half]
        other[level * half : (level + 1) * half] = part[half : 2 * half]
        sibling_other[level * half : (level + 1) * half] = part[3 * half :]
        give[level, :half, :width] = sibling0[level]
        give[level, :half, width:] = part[2 * half : 3 * half]
        for k, block in enumerate((across0, across)):
            cut = slice(k * width, (k + 1) * width)
            give[level, half : half + 16, cut] = block[level, :16]
            give[level, half + 16 :, cut] = block[level, rows - 16 :]
    core = lax.rem(lax.axis_index("dir"), 2)
    start = pl.multiple_of(core * (cols - LANES), LANES)

    def outer(first, second):
        return [
            jnp.where(core == 1, second[level].astype(jnp.float32), first[level].astype(jnp.float32))
            for level in range(layers)
        ]

    own, far, sibling_far = outer(keep0, keep), outer(diagonal0, diagonal), outer(across0, across)
    beyond = [near[level, :, pl.ds(start, LANES)] for level in range(layers)]
    load.wait()
    put_strip(other, layers * half, outer_strip(wind, core == 1, own, beyond, far))
    put_strip(sibling_other, layers * half, outer_strip(wind, core == 0, beyond, own, sibling_far))


def project(parts, cols_refs, at):
    cols = stack(*[ref[level, start:stop, at : at + 256] for ref, level, start, stop in cols_refs])
    return dot(beside(*parts), cols)


def phase_kernel(*refs):
    tables, refs = refs[:4], refs[4:]
    cols_ref, mine0, mine1, came, sibling_came, phase, cols_out = refs
    first = jnp.bitwise_xor(lax.axis_index("layer"), 1) * cols_out.shape[1]
    column_weights(*tables, first, cols_out)
    layers, _, width = mine0.shape
    parts, cuts = [], []
    for level in range(layers):
        parts += [mine0[level], mine1[level], came[level], sibling_came[level]]
        cuts += [(cols_ref, level, 0, 2 * width)]
        cuts += [(cols_out, level, 0, width), (cols_out, level, 2 * width, 3 * width)]
    for at in range(0, phase.shape[1], 256):
        phase[:, at : at + 256] = project(parts, cuts, at)


def last_kernel(mine_ref, cols_ref, phase, taken, came, sibling_came, *outs):
    *outs, strips = outs
    layers, _, width = taken.shape
    width = width // 2
    size, half, pairs = outs[0].shape[0], phase.shape[0], len(outs)
    parts, cuts = [], []
    for level in range(layers):
        cut = slice(level * half, (level + 1) * half)
        parts += [taken[level, :half], came[cut], sibling_came[cut]]
        cuts += [(mine_ref, level, 2 * width, 4 * width)]
        cuts += [(cols_ref, level, width, 2 * width), (cols_ref, level, 3 * width, 4 * width)]
    for at in range(0, phase.shape[1], 256):
        total = (phase[:, at : at + 256] + project(parts, cuts, at)).astype(jnp.bfloat16)
        for k, out in enumerate(outs):
            out[:, at : at + 256] = total[k * size : (k + 1) * size]
    odd = lax.rem(lax.axis_index("dir"), 2) == 1
    here = get_strip(came, layers * half).astype(jnp.float32)
    there = get_strip(sibling_came, layers * half).astype(jnp.float32)
    last, first = jnp.where(odd, here, there), jnp.where(odd, there, here)
    strips[:STRIP] = last.astype(jnp.bfloat16)
    strips[STRIP:] = first.astype(jnp.bfloat16)
    pair = lax.axis_index("layer") // 2
    for step in strip_steps(pairs):
        after = lax.rem(pair + 1, pairs) == jnp.bitwise_xor(pair, step)
        outs[step][:, phase.shape[1] :] = jnp.where(after, last, first).astype(jnp.bfloat16)


def strip_steps(pairs):
    return [2**k - 1 for k in range(1, pairs.bit_length())]


def shifted_rows(shift, odd, own, near, edges):
    own, near, edges = [block.astype(jnp.float32) for block in (own, near, edges)]
    rows = own.shape[0]
    before = jnp.where(odd, near[rows - 16 :], edges[16:])
    after = jnp.where(odd, edges[:16], near[:16])
    shift = jnp.where(shift < 0, shift + rows + 32, shift)
    return pltpu.roll(stack(before, own, after), shift, 0)[16 : 16 + rows]


def shift_kernel(pairs, wind_hbm, own, near, diagonal0, diagonal1, taken, partner_strips, *refs):
    messages, (out, wind, sem) = refs[:-3], refs[-3:]
    load = fetch((wind_hbm, wind, sem))[0]
    layers, rows, cols = own.shape
    odd = lax.rem(lax.axis_index("dir"), 2) == 1
    half = taken.shape[1] - 32
    pair, second = lax.axis_index("layer") // 2, lax.rem(lax.axis_index("layer"), 2) == 1
    before = jnp.bitwise_xor(pair, lax.rem(pair + pairs - 1, pairs))
    after = jnp.bitwise_xor(pair, lax.rem(pair + 1, pairs))
    left = partner_strips[:STRIP].astype(jnp.float32)
    right = partner_strips[STRIP:].astype(jnp.float32)
    for step, message in zip(strip_steps(pairs), messages):
        strip = message[:, message.shape[1] - rows :].astype(jnp.float32)
        left = jnp.where(jnp.logical_and(before == step, jnp.logical_not(second)), strip, left)
        right = jnp.where(jnp.logical_and(after == step, second), strip, right)
    strips = stack(left, right, jnp.zeros((LANES - 2 * STRIP, rows), jnp.float32)).T
    lane = lax.broadcasted_iota(jnp.int32, (rows, LANES), 1)
    load.wait()
    for level in range(layers):
        last = pltpu.roll(strips, LANES - WIND_MAX * (level + 1), 1)
        first = pltpu.roll(strips, LANES - STRIP - WIND_MAX * level, 1)
        extra = jnp.where(lane < WIND_MAX, first, last)
        chunks = [stack(part[level, :16], part[level, rows - 16 :]) for part in (diagonal0, diagonal1)]
        here = beside(*chunks).astype(jnp.float32)
        there = taken[level, half:].astype(jnp.float32)
        edges = beside(jnp.where(odd, there, here), jnp.where(odd, here, there))
        moved = shifted_rows(wind[0, level], odd, own[level], near[level], edges)
        shift = wind[1, level]
        shift = jnp.where(shift < 0, shift + cols + LANES, shift)
        out[level] = pltpu.roll(beside(moved, extra), shift, 1)[:, :cols].astype(jnp.bfloat16)


def optics_kernel(amplitude, ones, columns, lines, amp_out, high_out, low_out, lines_out):
    rows, pupil_cols = amplitude.shape
    for step in range(pupil_cols // LANES):
        cut = slice(step * LANES, (step + 1) * LANES)
        amp = amplitude[:, cut]
        energy = (amp * amp).reshape(rows // SUB_PIX, SUB_PIX, LANES).sum(axis=1)
        energy = jnp.broadcast_to(energy[:, None], (rows // SUB_PIX, SUB_PIX, LANES)).reshape(rows, LANES)
        total = jnp.dot(energy, ones[...], precision=lax.Precision.HIGHEST, preferred_element_type=jnp.float32)
        amp_out[:, cut] = amp * lax.rsqrt(total)
    high_out[...], low_out[...] = split(columns[...])
    high, low = split(lines[...])
    lines_out[...] = jnp.concatenate([high, high, low], axis=1)


def sin_cos(phase):
    turns = jnp.floor(phase * (1.0 / np.pi) + 0.5)
    rest = phase - turns * 3.140625
    rest = rest - turns * 9.67653589793e-4
    odd = turns - 2.0 * jnp.floor(turns * 0.5)
    sign = 1.0 - 2.0 * odd
    square = rest * rest
    sine = -1.0 / 39916800.0
    for term in (1.0 / 362880.0, -1.0 / 5040.0, 1.0 / 120.0, -1.0 / 6.0, 1.0):
        sine = sine * square + term
    cosine = 1.0 / 479001600.0
    for term in (-1.0 / 3628800.0, 1.0 / 40320.0, -1.0 / 720.0, 1.0 / 24.0, -0.5, 1.0):
        cosine = cosine * square + term
    return sine * rest * sign, cosine * sign


def split(value):
    high = value.astype(jnp.bfloat16)
    low = (value - high.astype(jnp.float32)).astype(jnp.bfloat16)
    return high, low


def imaging_kernel(count, *refs):
    parts = refs[:count]
    amp_ref, cols_high, cols_low, rows_table, out = refs[count:]
    rows, cols = amp_ref.shape
    tiles = cols // LANES
    phase = parts[0][:, :cols].astype(jnp.float32)
    for part in parts[1:]:
        phase = phase + part[:, :cols].astype(jnp.float32)
    sine, cosine = sin_cos(phase)
    amp = amp_ref[...]
    real, imag = amp * cosine, amp * sine
    field = jnp.concatenate(
        [
            jnp.concatenate(
                [real[:, t * LANES : (t + 1) * LANES], imag[:, t * LANES : (t + 1) * LANES]], axis=1
            )
            for t in range(tiles)
        ],
        axis=0,
    )
    high, low = split(field)
    half = dot(high, cols_high[...]) + (dot(low, cols_high[...]) + dot(high, cols_low[...]))
    wide = 2 * LANES
    out_rows = 2 * rows
    for t in range(tiles):
        mine = half[t * rows : (t + 1) * rows]
        mine = jnp.concatenate([mine[:, :wide], mine[:, wide:]], axis=0)
        high, low = split(mine)
        full = dot(rows_table[...], jnp.concatenate([high, low, high], axis=0))
        real, imag = full[:out_rows], full[out_rows:]
        out[:, t * wide : (t + 1) * wide] = real * real + imag * imag


def tables_of(rows):
    freq = np.arange(SPOT_PIX)[:, None] - SPOT_PIX // 2
    angle = ((freq * np.arange(SUB_PIX)[None, :]) % SPOT_PIX) * (2.0 * np.pi / SPOT_PIX)
    cos, sin = np.cos(angle), np.sin(angle)

    def blocks(table, count):
        return np.kron(np.eye(count), table)

    per_tile = LANES // SUB_PIX
    col_cos, col_sin = blocks(cos.T, per_tile), blocks(sin.T, per_tile)
    columns = np.block([[col_cos, -col_sin], [col_sin, col_cos]])
    count = rows // SUB_PIX
    row_cos, row_sin = blocks(cos, count), blocks(sin, count)
    lines = np.block([[row_cos, row_sin], [-row_sin, row_cos]])

    return columns.astype(np.float32), lines.astype(np.float32)


def per_device(screens, amplitude, wind, offsets, ratio):
    layers, rows_dev, cols_dev = screens.shape
    n_layer = lax.axis_size("layer")
    n_dir = lax.axis_size("dir")
    rows, pupil_cols = amplitude.shape
    pairs = n_layer // 2
    half = pairs * rows
    pupil_rows = 2 * half
    assert n_dir == 4 and rows == STRIP and pairs > 2
    bf16, f32 = jnp.bfloat16, jnp.float32
    wind = jnp.transpose(wind, (1, 0))
    offsets = jnp.transpose(offsets, (1, 2, 0))
    ratio = jnp.transpose(ratio, (1, 2, 0))
    smem, sem = pltpu.SMEM, pltpu.SemaphoreType.DMA
    wind_scratch = [smem(wind.shape, jnp.int32), sem]

    def shape(*dims, dtype=bf16):
        return jax.ShapeDtypeStruct(dims, dtype)

    def swap(value, bits):
        return lax.ppermute(value, "dir", [(i, i ^ bits) for i in range(n_dir)])

    def partner(value, bits=0):
        count = n_layer * n_dir
        return lax.ppermute(value, ("layer", "dir"), [(i, i ^ n_dir ^ bits) for i in range(count)])

    def turn(value, step):
        return lax.ppermute(value, "layer", [(i, (i + step) % n_layer) for i in range(n_layer)])

    width = cols_dev // 4
    chunk = shape(layers, rows_dev, width)
    own, keep0, keep1, give0, give1 = call(
        split_kernel,
        [shape(*screens.shape)] + [chunk] * 4,
        (screens,),
        0,
        "split",
        in_hbm=(0,),
        scratch=[sem((5,))],
        brief=True,
    )
    across0 = swap(keep0, 2)
    diagonal0 = swap(give0, 3)
    across1 = swap(keep1, 2)
    diagonal1 = swap(give1, 3)
    ones = np.kron(np.eye(LANES // SUB_PIX), np.ones((SUB_PIX, SUB_PIX))).astype(np.float32)
    optics_in = (amplitude, jnp.asarray(ones), *[jnp.asarray(table) for table in tables_of(rows)])
    copies = [shape(*array.shape, dtype=f32) for array in optics_in]
    row_weights, *tables = call(
        functools.partial(weights_kernel, (n_layer, rows_dev, cols_dev * n_layer)),
        [shape(2, layers, pupil_rows, 4 * rows_dev)]
        + [shape(8, pupil_cols, dtype=dtype) for dtype in (jnp.int32, jnp.int32, f32, f32)]
        + copies,
        (wind, offsets, ratio, *optics_in),
        0,
        "weights",
        in_hbm=range(3, 7),
        scratch=[smem(array.shape, jnp.int32) for array in (wind, offsets, ratio)] + [sem((7,))],
        brief=True,
    )
    tables, optics_in = tables[:4], tables[4:]
    near = swap(own, 1)
    tables = tuple(tables)
    across0, diagonal0, row_weights, tables = lax.optimization_barrier((across0, diagonal0, row_weights, tables))

    projected = shape(layers, half, width)
    mine0, sibling0, other0, sibling_other0 = call(
        first_rows_kernel,
        [projected] * 4,
        (row_weights, keep0, near, across0, diagonal0),
        0,
        "rows_first",
        brief=True,
    )
    came0 = partner(other0)
    sibling_came0 = partner(sibling_other0, 1)

    tables, mine0 = lax.optimization_barrier((tables, mine0))
    cols = call(
        columns_kernel, shape(layers, cols_dev, pupil_cols), tables, 0, "columns", brief=True
    )
    cols, sibling0 = lax.optimization_barrier((cols, sibling0))
    message = shape(layers * half + STRIP * rows_dev // LANES, width)
    mine1, give, other1, sibling_other1 = call(
        later_rows_kernel,
        [projected, shape(layers, half + 32, 2 * width), message, message],
        (wind, row_weights, keep0, across0, diagonal0, keep1, across1, diagonal1, near, sibling0),
        0,
        "rows_later",
        scratch=wind_scratch,
        brief=True,
    )
    came1 = partner(other1)
    sibling_came1 = partner(sibling_other1, 1)
    taken = swap(give, 1)

    phase, others = call(
        phase_kernel,
        (shape(half, pupil_cols, dtype=f32), shape(layers, cols_dev, pupil_cols)),
        (*tables, cols, mine0, mine1, came0, sibling_came0),
        10_000_000_000,
        "phase",
    )

    steps = strip_steps(pairs)
    *sums, strips = call(
        last_kernel,
        [shape(rows, pupil_cols + (rows_dev if k in steps else 0)) for k in range(pairs)] + [shape(2 * STRIP, rows_dev)],
        (cols, others, phase, taken, came1, sibling_came1),
        300_000_000,
        "last",
    )
    received = list(sums)
    for k in range(pairs - 1, 0, -1):
        received[k] = lax.ppermute(sums[k], "layer", [(i, i ^ (2 * k)) for i in range(n_layer)])

    optics_in, received[0] = lax.optimization_barrier((optics_in, received[0]))
    optics = call(
        optics_kernel,
        (
            shape(rows, pupil_cols, dtype=f32),
            shape(*optics_in[2].shape),
            shape(*optics_in[2].shape),
            shape(optics_in[3].shape[0], 3 * optics_in[3].shape[1]),
        ),
        optics_in,
        30_000_000,
        "optics",
    )
    new_screens = call(
        functools.partial(shift_kernel, pairs),
        shape(layers, rows_dev, cols_dev),
        (wind, own, near, diagonal0, diagonal1, taken, strips, *[received[k] for k in steps]),
        1_000_000,
        "shift",
        scratch=wind_scratch,
    )
    spots = call(
        functools.partial(imaging_kernel, pairs),
        shape(2 * rows, 2 * pupil_cols, dtype=f32),
        (*received, *optics),
        400_000_000,
        "imaging",
    )
    return (new_screens, spots[None])


def solution(mesh):
    return jax.shard_map(
        per_device,
        mesh=mesh,
        in_specs=(P(None, "dir", "layer"), P("layer", None), P(), P(), P()),
        out_specs=(P(None, "dir", "layer"), P("dir", "layer", None)),
        check_vma=False,
    )
```

```python
import functools

import jax
import jax.numpy as jnp
import numpy as np
from jax import lax
from jax.experimental import pallas as pl
from jax.experimental.pallas import tpu as pltpu
from jax.sharding import PartitionSpec as P

SUB_PIX = 16
SPOT_PIX = 32
WIND_MAX = 8
LANES = 128
STRIP = 32

HBM_SPEC = pl.BlockSpec(memory_space=pltpu.HBM)
VMEM_SPEC = pl.BlockSpec(memory_space=pltpu.VMEM)


def params(*arrays):
    held = sum(array.size * array.dtype.itemsize for array in jax.tree.leaves(arrays))
    return pltpu.CompilerParams(vmem_limit_bytes=held + 8 * 1024 * 1024)


def call(kernel, out_shape, operands, flops, name, in_hbm=(), scratch=(), brief=False):
    def spec(k, array):
        scalars = array.dtype == jnp.int32 and array.size < LANES
        return HBM_SPEC if scalars or k in in_hbm else VMEM_SPEC

    out_specs = jax.tree.map(lambda _: VMEM_SPEC, out_shape)
    size = sum(array.size * array.dtype.itemsize for array in jax.tree.leaves((operands, out_shape)))
    if brief:
        flops = size = 0
    in_specs = [spec(k, array) for k, array in enumerate(operands)]
    operands = [
        pltpu.with_memory_space_constraint(array, pltpu.HBM) if space is HBM_SPEC else array
        for array, space in zip(operands, in_specs)
    ]
    return pl.pallas_call(
        kernel,
        out_shape=out_shape,
        in_specs=in_specs,
        out_specs=out_specs,
        scratch_shapes=list(scratch),
        compiler_params=params(operands, out_shape),
        cost_estimate=pl.CostEstimate(flops=flops, bytes_accessed=size, transcendentals=0),
        name=name,
    )(*operands)


def fetch(*pairs):
    copies = [pltpu.make_async_copy(source, target, sem) for source, target, sem in pairs]
    for copy in copies:
        copy.start()
    return copies


def wrap(value, length):
    value = jnp.where(value < 0, value + length, value)
    return jnp.where(value >= length, value - length, value)


def stack(*blocks):
    return jnp.concatenate(blocks, axis=0)


def beside(*blocks):
    return jnp.concatenate(blocks, axis=1)


def dot(left, right):
    return jnp.dot(left, right, preferred_element_type=jnp.float32)


def spans(pixel, anchor, num, den, length):
    stretched = (pixel * num).astype(jnp.float32)
    den = (jnp.zeros_like(pixel) + den).astype(jnp.float32)
    whole = jnp.floor((stretched + 0.5) / den)
    fraction = (stretched - whole * den) / den
    base = wrap(anchor + whole.astype(jnp.int32), length)
    upper = wrap(base + 1, length)
    return base, upper, 1.0 - fraction, fraction


def split_kernel(screens, *refs):
    outs, sems = refs[:-1], refs[-1]
    width = outs[0].shape[2]
    core = lax.rem(lax.axis_index("dir"), 2)
    pairs = []
    for k, out in enumerate(outs):
        half = core if k < 2 else 1 - core
        start = pl.multiple_of((2 * half + k % 2) * width, LANES)
        pairs.append((screens.at[:, :, pl.ds(start, width)], out, sems.at[k]))
    for load in fetch(*pairs):
        load.wait()


def weights_kernel(geometry, wind_hbm, offsets_hbm, ratio_hbm, *refs):
    n_layer, rows_dev, screen_cols = geometry
    sources, (rows_out, base_out, upper_out, low_out, high_out), refs = refs[:5], refs[5:10], refs[10:]
    copies, (wind, offsets, ratio, sems) = refs[:5], refs[5:]
    others = fetch(*[(source, copy, sems.at[3 + k]) for k, (source, copy) in enumerate(zip(sources, copies))])
    loads = fetch(
        (wind_hbm, wind, sems.at[0]),
        (offsets_hbm, offsets, sems.at[1]),
        (ratio_hbm, ratio, sems.at[2]),
    )
    _, layers, pupil_rows, screen_rows = rows_out.shape
    half = pupil_rows // 2
    direction = lax.axis_index("dir")
    column = lax.axis_index("layer")
    block = pupil_rows // n_layer
    row = lax.broadcasted_iota(jnp.int32, (half, LANES), 0)
    pair = jnp.bitwise_xor(row // block, column // 2)
    parity = lax.rem(column, 2)
    inside = lax.rem(row, block) + pair * (2 * block)
    pixel_rows = stack(inside + parity * block, inside + (1 - parity) * block)
    lane = lax.broadcasted_iota(jnp.int32, (pupil_rows, LANES), 1)
    for load in loads:
        load.wait()
    for side in range(2):
        target = jnp.bitwise_xor(direction, side)
        for level in range(layers):
            anchor = wrap(offsets[level, 0, target] - wind[0, level], screen_rows)
            num, den = ratio[level, 0, target], ratio[level, 1, target]
            base, upper, low, high = spans(pixel_rows, anchor, num, den, screen_rows)
            for peer in range(4):
                for part in range(rows_dev // LANES):
                    index = lane + (jnp.bitwise_xor(direction, peer) * rows_dev + part * LANES)
                    weight = jnp.where(index == base, low, 0.0)
                    weight = jnp.where(index == upper, high, weight)
                    start = peer * rows_dev + part * LANES
                    rows_out[side, level, :, start : start + LANES] = weight.astype(jnp.bfloat16)
    sub = lax.broadcasted_iota(jnp.int32, (8, LANES), 0)
    anchor, num, den = jnp.zeros_like(sub), jnp.zeros_like(sub), jnp.ones_like(sub)
    for level in range(layers):
        start = wrap(offsets[level, 1, direction] - wind[1, level], screen_cols)
        anchor = jnp.where(sub == level, start, anchor)
        num = jnp.where(sub == level, ratio[level, 0, direction], num)
        den = jnp.where(sub == level, ratio[level, 1, direction], den)
    for at in range(0, base_out.shape[1], LANES):
        pixel = lax.broadcasted_iota(jnp.int32, (8, LANES), 1) + at
        values = spans(pixel, anchor, num, den, screen_cols)
        for out, value in zip((base_out, upper_out, low_out, high_out), values):
            out[:, at : at + LANES] = value
    for load in others:
        load.wait()


def column_weights(base_ref, upper_ref, low_ref, high_ref, first, out):
    layers, cols_dev, pupil_cols = out.shape
    half = cols_dev // 2
    core = lax.rem(lax.axis_index("dir"), 2)
    sub = lax.broadcasted_iota(jnp.int32, (half, LANES), 0).reshape(half // 8, 8, LANES)
    for level in range(layers):

        def tile(step, carry):
            start = pl.multiple_of(step * LANES, LANES)
            cut = (slice(level, level + 1), pl.ds(start, LANES))
            base, upper, low, high = [
                jnp.broadcast_to(ref[cut], (8, LANES)) for ref in (base_ref, upper_ref, low_ref, high_ref)
            ]
            for side in range(2):
                shift = first + jnp.bitwise_xor(core, side) * half
                weight = jnp.where(sub == (base - shift)[None], low[None], 0.0)
                weight = jnp.where(sub == (upper - shift)[None], high[None], weight)
                weight = weight.reshape(half, LANES).astype(jnp.bfloat16)
                out[level, side * half : (side + 1) * half, pl.ds(start, LANES)] = weight
            return carry

        lax.fori_loop(0, pupil_cols // LANES, tile, 0)


def columns_kernel(*refs):
    tables, out = refs[:4], refs[-1]
    column_weights(*tables, lax.axis_index("layer") * out.shape[1], out)


def project_rows(rows_ref, keep, near, across, diagonal, level):
    screen = stack(keep[level], near[level], across[level], diagonal[level])
    rows = stack(rows_ref[0, level], rows_ref[1, level])
    return dot(rows, screen).astype(jnp.bfloat16)


def first_rows_kernel(rows_ref, across, diagonal, near, keep, mine, sibling, other, sibling_other):
    layers, half, _ = mine.shape
    for level in range(layers):
        part = project_rows(rows_ref, keep, near, across, diagonal, level)
        for k, out in enumerate((mine, other, sibling, sibling_other)):
            out[level] = part[k * half : (k + 1) * half]


def outer_strip(wind, odd, own, near, far):
    rows = own[0].shape[0]
    core = lax.rem(lax.axis_index("dir"), 2)
    lane = lax.broadcasted_iota(jnp.int32, (rows, LANES), 1)
    strip = jnp.zeros((rows, LANES), jnp.float32)
    for level in range(len(own)):
        edges = [stack(block[level][:16], block[level][rows - 16 :]) for block in (near, far)]
        moved = shifted_rows(wind[0, level], odd, own[level], *edges)
        at = WIND_MAX * level
        moved = pltpu.roll(moved, at + WIND_MAX * core, 1)
        strip = jnp.where((lane >= at) & (lane < at + WIND_MAX), moved, strip)
    return strip.T[:STRIP].astype(jnp.bfloat16)


def put_strip(out, at, strip):
    for k in range(strip.shape[1] // LANES):
        out[at + k * STRIP : at + (k + 1) * STRIP, :] = strip[:, k * LANES : (k + 1) * LANES]


def get_strip(ref, at):
    return beside(*[ref[start : start + STRIP, :] for start in range(at, ref.shape[0], STRIP)])


def later_rows_kernel(wind_hbm, rows_ref, *refs):
    chunks, sibling0, outs, (wind, sem) = refs[:8], refs[8], refs[9:-2], refs[-2:]
    mine, give, other, sibling_other = outs
    load = fetch((wind_hbm, wind, sem))[0]
    across, diagonal, near, keep, across0, diagonal0, near0, keep0 = chunks
    layers, half, width = mine.shape
    rows = near.shape[1]
    for level in range(layers):
        part = project_rows(rows_ref, keep, near, across, diagonal, level)
        mine[level] = part[:half]
        other[level * half : (level + 1) * half] = part[half : 2 * half]
        sibling_other[level * half : (level + 1) * half] = part[3 * half :]
        give[level, :half, :width] = sibling0[level]
        give[level, :half, width:] = part[2 * half : 3 * half]
        for k, blocks in enumerate(((across0, keep0), (across, keep))):
            cut = slice(k * width, (k + 1) * width)
            edges = [block[level, at : at + 16] for block in blocks for at in (0, rows - 16)]
            give[level, half:, cut] = stack(*edges)
    core = lax.rem(lax.axis_index("dir"), 2)

    def outer(first, second):
        return [
            jnp.where(core == 1, second[level].astype(jnp.float32), first[level].astype(jnp.float32))
            for level in range(layers)
        ]

    own, far, sibling_far = outer(keep0, keep), outer(diagonal0, diagonal), outer(across0, across)
    beyond = outer(near0, near)
    load.wait()
    put_strip(other, layers * half, outer_strip(wind, core == 1, own, beyond, far))
    put_strip(sibling_other, layers * half, outer_strip(wind, core == 0, beyond, own, sibling_far))


def project(parts, cols_refs, at):
    cols = stack(*[ref[level, start:stop, at : at + 256] for ref, level, start, stop in cols_refs])
    return dot(beside(*parts), cols)


def phase_kernel(*refs):
    tables, refs = refs[:4], refs[4:]
    cols_ref, mine0, mine1, came, sibling_came, phase, cols_out = refs
    first = jnp.bitwise_xor(lax.axis_index("layer"), 1) * cols_out.shape[1]
    column_weights(*tables, first, cols_out)
    layers, _, width = mine0.shape
    parts, cuts = [], []
    for level in range(layers):
        parts += [mine0[level], mine1[level], came[level], sibling_came[level]]
        cuts += [(cols_ref, level, 0, 2 * width)]
        cuts += [(cols_out, level, 0, width), (cols_out, level, 2 * width, 3 * width)]
    for at in range(0, phase.shape[1], 256):
        phase[:, at : at + 256] = project(parts, cuts, at)


def last_kernel(mine_ref, cols_ref, phase, taken, came, sibling_came, *outs):
    *outs, strips, passed = outs
    layers, _, width = taken.shape
    width = width // 2
    size, half = outs[0].shape[0], phase.shape[0]
    parts, cuts = [], []
    for level in range(layers):
        cut = slice(level * half, (level + 1) * half)
        parts += [taken[level, :half], came[cut], sibling_came[cut]]
        cuts += [(mine_ref, level, 2 * width, 4 * width)]
        cuts += [(cols_ref, level, width, 2 * width), (cols_ref, level, 3 * width, 4 * width)]
    for at in range(0, phase.shape[1], 256):
        total = (phase[:, at : at + 256] + project(parts, cuts, at)).astype(jnp.bfloat16)
        for k, out in enumerate(outs):
            out[:, at : at + 256] = total[k * size : (k + 1) * size]
    odd = lax.rem(lax.axis_index("dir"), 2) == 1
    here = get_strip(came, layers * half).astype(jnp.float32)
    there = get_strip(sibling_came, layers * half).astype(jnp.float32)
    last, first = jnp.where(odd, here, there), jnp.where(odd, there, here)
    strips[:STRIP] = last.astype(jnp.bfloat16)
    strips[STRIP:] = first.astype(jnp.bfloat16)
    second = lax.rem(lax.axis_index("layer"), 2) == 1
    passed[...] = jnp.where(second, first, last).astype(jnp.bfloat16)


def shifted_rows(shift, odd, own, near, far):
    own, near, far = [block.astype(jnp.float32) for block in (own, near, far)]
    rows = own.shape[0]
    before = jnp.where(odd, near[16:], far[16:])
    after = jnp.where(odd, far[:16], near[:16])
    shift = jnp.where(shift < 0, shift + rows + 32, shift)
    return pltpu.roll(stack(before, own, after), shift, 0)[16 : 16 + rows]


def shift_kernel(wind_hbm, own, near0, near1, diagonal0, diagonal1, taken, partner_strips, came, out, wind, sem):
    load = fetch((wind_hbm, wind, sem))[0]
    layers, rows, cols = own.shape
    odd = lax.rem(lax.axis_index("dir"), 2) == 1
    half = taken.shape[1] - 64
    second = lax.rem(lax.axis_index("layer"), 2) == 1
    other = came[...].astype(jnp.float32)
    left = jnp.where(second, partner_strips[:STRIP].astype(jnp.float32), other)
    right = jnp.where(second, other, partner_strips[STRIP:].astype(jnp.float32))
    strips = stack(left, right, jnp.zeros((LANES - 2 * STRIP, rows), jnp.float32)).T
    lane = lax.broadcasted_iota(jnp.int32, (rows, LANES), 1)
    load.wait()
    for level in range(layers):
        last = pltpu.roll(strips, LANES - WIND_MAX * (level + 1), 1)
        first = pltpu.roll(strips, LANES - STRIP - WIND_MAX * level, 1)
        extra = jnp.where(lane < WIND_MAX, first, last)
        pair = []
        for at, parts in ((half, (diagonal0, diagonal1)), (half + 32, (near0, near1))):
            here = beside(*[stack(part[level, :16], part[level, rows - 16 :]) for part in parts])
            here, there = here.astype(jnp.float32), taken[level, at : at + 32].astype(jnp.float32)
            pair.append(beside(jnp.where(odd, there, here), jnp.where(odd, here, there)))
        far, near = pair
        moved = shifted_rows(wind[0, level], odd, own[level], near, far)
        shift = wind[1, level]
        shift = jnp.where(shift < 0, shift + cols + LANES, shift)
        out[level] = pltpu.roll(beside(moved, extra), shift, 1)[:, :cols].astype(jnp.bfloat16)


def optics_kernel(amplitude, ones, columns, lines, amp_out, high_out, low_out, lines_out):
    rows, pupil_cols = amplitude.shape
    for step in range(pupil_cols // LANES):
        cut = slice(step * LANES, (step + 1) * LANES)
        amp = amplitude[:, cut]
        energy = (amp * amp).reshape(rows // SUB_PIX, SUB_PIX, LANES).sum(axis=1)
        energy = jnp.broadcast_to(energy[:, None], (rows // SUB_PIX, SUB_PIX, LANES)).reshape(rows, LANES)
        total = jnp.dot(energy, ones[...], precision=lax.Precision.HIGHEST, preferred_element_type=jnp.float32)
        amp_out[:, cut] = amp * lax.rsqrt(total)
    high_out[...], low_out[...] = split(columns[...])
    high, low = split(lines[...])
    lines_out[...] = jnp.concatenate([high, high, low], axis=1)


def sin_cos(phase):
    turns = jnp.floor(phase * (1.0 / np.pi) + 0.5)
    rest = phase - turns * 3.140625
    rest = rest - turns * 9.67653589793e-4
    odd = turns - 2.0 * jnp.floor(turns * 0.5)
    sign = 1.0 - 2.0 * odd
    square = rest * rest
    sine = -1.0 / 39916800.0
    for term in (1.0 / 362880.0, -1.0 / 5040.0, 1.0 / 120.0, -1.0 / 6.0, 1.0):
        sine = sine * square + term
    cosine = 1.0 / 479001600.0
    for term in (-1.0 / 3628800.0, 1.0 / 40320.0, -1.0 / 720.0, 1.0 / 24.0, -0.5, 1.0):
        cosine = cosine * square + term
    return sine * rest * sign, cosine * sign


def split(value):
    high = value.astype(jnp.bfloat16)
    low = (value - high.astype(jnp.float32)).astype(jnp.bfloat16)
    return high, low


def imaging_kernel(count, *refs):
    parts = refs[:count]
    amp_ref, cols_high, cols_low, rows_table, out = refs[count:]
    rows, cols = amp_ref.shape
    tiles = cols // LANES
    phase = parts[0][:, :cols].astype(jnp.float32)
    for part in parts[1:]:
        phase = phase + part[:, :cols].astype(jnp.float32)
    sine, cosine = sin_cos(phase)
    amp = amp_ref[...]
    real, imag = amp * cosine, amp * sine
    field = jnp.concatenate(
        [
            jnp.concatenate(
                [real[:, t * LANES : (t + 1) * LANES], imag[:, t * LANES : (t + 1) * LANES]], axis=1
            )
            for t in range(tiles)
        ],
        axis=0,
    )
    high, low = split(field)
    half = dot(high, cols_high[...]) + (dot(low, cols_high[...]) + dot(high, cols_low[...]))
    wide = 2 * LANES
    out_rows = 2 * rows
    for t in range(tiles):
        mine = half[t * rows : (t + 1) * rows]
        mine = jnp.concatenate([mine[:, :wide], mine[:, wide:]], axis=0)
        high, low = split(mine)
        full = dot(rows_table[...], jnp.concatenate([high, low, high], axis=0))
        real, imag = full[:out_rows], full[out_rows:]
        out[:, t * wide : (t + 1) * wide] = real * real + imag * imag


def tables_of(rows):
    freq = np.arange(SPOT_PIX)[:, None] - SPOT_PIX // 2
    angle = ((freq * np.arange(SUB_PIX)[None, :]) % SPOT_PIX) * (2.0 * np.pi / SPOT_PIX)
    cos, sin = np.cos(angle), np.sin(angle)

    def blocks(table, count):
        return np.kron(np.eye(count), table)

    per_tile = LANES // SUB_PIX
    col_cos, col_sin = blocks(cos.T, per_tile), blocks(sin.T, per_tile)
    columns = np.block([[col_cos, -col_sin], [col_sin, col_cos]])
    count = rows // SUB_PIX
    row_cos, row_sin = blocks(cos, count), blocks(sin, count)
    lines = np.block([[row_cos, row_sin], [-row_sin, row_cos]])

    return columns.astype(np.float32), lines.astype(np.float32)


def per_device(screens, amplitude, wind, offsets, ratio):
    layers, rows_dev, cols_dev = screens.shape
    n_layer = lax.axis_size("layer")
    n_dir = lax.axis_size("dir")
    rows, pupil_cols = amplitude.shape
    pairs = n_layer // 2
    half = pairs * rows
    pupil_rows = 2 * half
    assert n_dir == 4 and rows == STRIP and pairs > 2
    bf16, f32 = jnp.bfloat16, jnp.float32
    wind = jnp.transpose(wind, (1, 0))
    offsets = jnp.transpose(offsets, (1, 2, 0))
    ratio = jnp.transpose(ratio, (1, 2, 0))
    smem, sem = pltpu.SMEM, pltpu.SemaphoreType.DMA
    wind_scratch = [smem(wind.shape, jnp.int32), sem]

    def shape(*dims, dtype=bf16):
        return jax.ShapeDtypeStruct(dims, dtype)

    def swap(value, bits):
        return lax.ppermute(value, "dir", [(i, i ^ bits) for i in range(n_dir)])

    def partner(value, bits=0):
        count = n_layer * n_dir
        return lax.ppermute(value, ("layer", "dir"), [(i, i ^ n_dir ^ bits) for i in range(count)])

    def turn(value, step):
        return lax.ppermute(value, "layer", [(i, (i + step) % n_layer) for i in range(n_layer)])

    width = cols_dev // 4
    chunk = shape(layers, rows_dev, width)
    keep0, keep1, give0, give1 = call(
        split_kernel,
        [chunk] * 4,
        (screens,),
        0,
        "split",
        in_hbm=(0,),
        scratch=[sem((4,))],
        brief=True,
    )
    across0 = swap(keep0, 2)
    diagonal0 = swap(give0, 3)
    near0 = swap(give0, 1)
    across1 = swap(keep1, 2)
    diagonal1 = swap(give1, 3)
    ones = np.kron(np.eye(LANES // SUB_PIX), np.ones((SUB_PIX, SUB_PIX))).astype(np.float32)
    optics_in = (amplitude, jnp.asarray(ones), *[jnp.asarray(table) for table in tables_of(rows)])
    copies = [shape(*array.shape, dtype=array.dtype) for array in (screens, *optics_in)]
    row_weights, *tables = call(
        functools.partial(weights_kernel, (n_layer, rows_dev, cols_dev * n_layer)),
        [shape(2, layers, pupil_rows, 4 * rows_dev)]
        + [shape(8, pupil_cols, dtype=dtype) for dtype in (jnp.int32, jnp.int32, f32, f32)]
        + copies,
        (wind, offsets, ratio, screens, *optics_in),
        0,
        "weights",
        in_hbm=range(3, 8),
        scratch=[smem(array.shape, jnp.int32) for array in (wind, offsets, ratio)] + [sem((8,))],
        brief=True,
    )
    tables, own, optics_in = tables[:4], tables[4], tables[5:]
    give1, own = lax.optimization_barrier((give1, own))
    near1 = swap(give1, 1)
    tables = tuple(tables)
    across0, diagonal0, row_weights, tables = lax.optimization_barrier((across0, diagonal0, row_weights, tables))

    projected = shape(layers, half, width)
    mine0, sibling0, other0, sibling_other0 = call(
        first_rows_kernel,
        [projected] * 4,
        (row_weights, across0, diagonal0, near0, keep0),
        0,
        "rows_first",
        brief=True,
    )
    came0 = partner(other0)
    sibling_came0 = partner(sibling_other0, 1)

    tables, mine0 = lax.optimization_barrier((tables, mine0))
    cols = call(
        columns_kernel, shape(layers, cols_dev, pupil_cols), tables, 0, "columns", brief=True
    )
    cols, sibling0 = lax.optimization_barrier((cols, sibling0))
    message = shape(layers * half + STRIP * rows_dev // LANES, width)
    mine1, give, other1, sibling_other1 = call(
        later_rows_kernel,
        [projected, shape(layers, half + 64, 2 * width), message, message],
        (wind, row_weights, across1, diagonal1, near1, keep1, across0, diagonal0, near0, keep0, sibling0),
        0,
        "rows_later",
        scratch=wind_scratch,
        brief=True,
    )
    came1 = partner(other1)
    sibling_came1 = partner(sibling_other1, 1)
    taken = swap(give, 1)

    phase, others = call(
        phase_kernel,
        (shape(half, pupil_cols, dtype=f32), shape(layers, cols_dev, pupil_cols)),
        (*tables, cols, mine0, mine1, came0, sibling_came0),
        10_000_000_000,
        "phase",
    )

    *sums, strips, passed = call(
        last_kernel,
        [shape(rows, pupil_cols)] * pairs + [shape(2 * STRIP, rows_dev), shape(STRIP, rows_dev)],
        (cols, others, phase, taken, came1, sibling_came1),
        300_000_000,
        "last",
    )
    order = sorted(range(1, pairs), key=lambda k: (-(k & (pairs // 2)), k))
    received = [sums[0]] + [
        lax.ppermute(sums[k], "layer", [(i, i ^ (2 * k)) for i in range(n_layer)]) for k in order
    ]
    steps = [(i, (i - 2 if i % 2 else i + 2) % n_layer) for i in range(n_layer)]
    came = lax.ppermute(passed, "layer", steps)

    optics_in, received[0] = lax.optimization_barrier((optics_in, received[0]))
    optics = call(
        optics_kernel,
        (
            shape(rows, pupil_cols, dtype=f32),
            shape(*optics_in[2].shape),
            shape(*optics_in[2].shape),
            shape(optics_in[3].shape[0], 3 * optics_in[3].shape[1]),
        ),
        optics_in,
        30_000_000,
        "optics",
    )
    came, received[1] = lax.optimization_barrier((came, received[1]))
    new_screens = call(
        shift_kernel,
        shape(layers, rows_dev, cols_dev),
        (wind, own, near0, near1, diagonal0, diagonal1, taken, strips, came),
        1_000_000,
        "shift",
        scratch=wind_scratch,
    )
    spots = call(
        functools.partial(imaging_kernel, pairs),
        shape(2 * rows, 2 * pupil_cols, dtype=f32),
        (*received, *optics),
        400_000_000,
        "imaging",
    )
    return (new_screens, spots[None])


def solution(mesh):
    return jax.shard_map(
        per_device,
        mesh=mesh,
        in_specs=(P(None, "dir", "layer"), P("layer", None), P(), P(), P()),
        out_specs=(P(None, "dir", "layer"), P("dir", "layer", None)),
        check_vma=False,
    )
```

```python
import functools

import jax
import jax.numpy as jnp
import numpy as np
from jax import lax
from jax.experimental import pallas as pl
from jax.experimental.pallas import tpu as pltpu
from jax.sharding import PartitionSpec as P

SUB_PIX = 16
SPOT_PIX = 32
WIND_MAX = 8
LANES = 128
STRIP = 32

HBM_SPEC = pl.BlockSpec(memory_space=pltpu.HBM)
VMEM_SPEC = pl.BlockSpec(memory_space=pltpu.VMEM)


def params(*arrays):
    held = sum(array.size * array.dtype.itemsize for array in jax.tree.leaves(arrays))
    return pltpu.CompilerParams(vmem_limit_bytes=held + 8 * 1024 * 1024)


def call(kernel, out_shape, operands, flops, name, in_hbm=(), scratch=(), brief=False):
    def spec(k, array):
        scalars = array.dtype == jnp.int32 and array.size < LANES
        return HBM_SPEC if scalars or k in in_hbm else VMEM_SPEC

    out_specs = jax.tree.map(lambda _: VMEM_SPEC, out_shape)
    size = sum(array.size * array.dtype.itemsize for array in jax.tree.leaves((operands, out_shape)))
    if brief:
        flops = size = 0
    in_specs = [spec(k, array) for k, array in enumerate(operands)]
    operands = [
        pltpu.with_memory_space_constraint(array, pltpu.HBM) if space is HBM_SPEC else array
        for array, space in zip(operands, in_specs)
    ]
    return pl.pallas_call(
        kernel,
        out_shape=out_shape,
        in_specs=in_specs,
        out_specs=out_specs,
        scratch_shapes=list(scratch),
        compiler_params=params(operands, out_shape),
        cost_estimate=pl.CostEstimate(flops=flops, bytes_accessed=size, transcendentals=0),
        name=name,
    )(*operands)


def fetch(*pairs):
    copies = [pltpu.make_async_copy(source, target, sem) for source, target, sem in pairs]
    for copy in copies:
        copy.start()
    return copies


def wrap(value, length):
    value = jnp.where(value < 0, value + length, value)
    return jnp.where(value >= length, value - length, value)


def stack(*blocks):
    return jnp.concatenate(blocks, axis=0)


def beside(*blocks):
    return jnp.concatenate(blocks, axis=1)


def dot(left, right):
    return jnp.dot(left, right, preferred_element_type=jnp.float32)


def spans(pixel, anchor, num, den, length):
    stretched = (pixel * num).astype(jnp.float32)
    den = (jnp.zeros_like(pixel) + den).astype(jnp.float32)
    whole = jnp.floor((stretched + 0.5) / den)
    fraction = (stretched - whole * den) / den
    base = wrap(anchor + whole.astype(jnp.int32), length)
    upper = wrap(base + 1, length)
    return base, upper, 1.0 - fraction, fraction


def chunk_start(half, chunk):
    return 3 * half + chunk * (1 - 2 * half)


def split_kernel(screens, *refs):
    outs, sems = refs[:-1], refs[-1]
    width = outs[0].shape[2]
    core = lax.rem(lax.axis_index("dir"), 2)
    pairs = []
    for k, out in enumerate(outs):
        half = core if k < 2 else 1 - core
        start = pl.multiple_of(chunk_start(half, k % 2) * width, LANES)
        pairs.append((screens.at[:, :, pl.ds(start, width)], out, sems.at[k]))
    for load in fetch(*pairs):
        load.wait()


def weights_kernel(geometry, wind_hbm, offsets_hbm, ratio_hbm, *refs):
    n_layer, rows_dev, screen_cols = geometry
    sources, (rows_out, base_out, upper_out, low_out, high_out), refs = refs[:5], refs[5:10], refs[10:]
    copies, (wind, offsets, ratio, sems) = refs[:5], refs[5:]
    others = fetch(*[(source, copy, sems.at[3 + k]) for k, (source, copy) in enumerate(zip(sources, copies))])
    loads = fetch(
        (wind_hbm, wind, sems.at[0]),
        (offsets_hbm, offsets, sems.at[1]),
        (ratio_hbm, ratio, sems.at[2]),
    )
    _, layers, pupil_rows, screen_rows = rows_out.shape
    half = pupil_rows // 2
    direction = lax.axis_index("dir")
    column = lax.axis_index("layer")
    block = pupil_rows // n_layer
    row = lax.broadcasted_iota(jnp.int32, (half, LANES), 0)
    pair = jnp.bitwise_xor(row // block, column // 2)
    parity = lax.rem(column, 2)
    inside = lax.rem(row, block) + pair * (2 * block)
    pixel_rows = stack(inside + parity * block, inside + (1 - parity) * block)
    lane = lax.broadcasted_iota(jnp.int32, (pupil_rows, LANES), 1)
    for load in loads:
        load.wait()
    for side in range(2):
        target = jnp.bitwise_xor(direction, side)
        for level in range(layers):
            anchor = wrap(offsets[level, 0, target] - wind[0, level], screen_rows)
            num, den = ratio[level, 0, target], ratio[level, 1, target]
            base, upper, low, high = spans(pixel_rows, anchor, num, den, screen_rows)
            for peer in range(4):
                for part in range(rows_dev // LANES):
                    index = lane + (jnp.bitwise_xor(direction, peer) * rows_dev + part * LANES)
                    weight = jnp.where(index == base, low, 0.0)
                    weight = jnp.where(index == upper, high, weight)
                    start = peer * rows_dev + part * LANES
                    rows_out[side, level, :, start : start + LANES] = weight.astype(jnp.bfloat16)
    sub = lax.broadcasted_iota(jnp.int32, (8, LANES), 0)
    anchor, num, den = jnp.zeros_like(sub), jnp.zeros_like(sub), jnp.ones_like(sub)
    for level in range(layers):
        start = wrap(offsets[level, 1, direction] - wind[1, level], screen_cols)
        anchor = jnp.where(sub == level, start, anchor)
        num = jnp.where(sub == level, ratio[level, 0, direction], num)
        den = jnp.where(sub == level, ratio[level, 1, direction], den)
    for at in range(0, base_out.shape[1], LANES):
        pixel = lax.broadcasted_iota(jnp.int32, (8, LANES), 1) + at
        values = spans(pixel, anchor, num, den, screen_cols)
        for out, value in zip((base_out, upper_out, low_out, high_out), values):
            out[:, at : at + LANES] = value
    for load in others:
        load.wait()


def column_weights(base_ref, upper_ref, low_ref, high_ref, first, out):
    layers, cols_dev, pupil_cols = out.shape
    width = cols_dev // 4
    core = lax.rem(lax.axis_index("dir"), 2)
    sub = lax.broadcasted_iota(jnp.int32, (width, LANES), 0).astype(jnp.float32).astype(jnp.bfloat16)
    zero = jnp.zeros((width, LANES), jnp.bfloat16)
    for level in range(layers):

        def tile(step, carry):
            start = pl.multiple_of(step * LANES, LANES)
            cut = (slice(level, level + 1), pl.ds(start, LANES))
            base, upper = base_ref[cut], upper_ref[cut]
            low, high = [
                jnp.broadcast_to(ref[cut].astype(jnp.bfloat16), (width, LANES)) for ref in (low_ref, high_ref)
            ]
            for k in range(4):
                shift = first + chunk_start(jnp.bitwise_xor(core, k // 2), k % 2) * width
                base_at, upper_at = [
                    jnp.broadcast_to(
                        jnp.clip(value - shift, -1, width).astype(jnp.float32).astype(jnp.bfloat16), (width, LANES)
                    )
                    for value in (base, upper)
                ]
                weight = jnp.where(sub == base_at, low, zero)
                weight = jnp.where(sub == upper_at, high, weight)
                out[level, k * width : (k + 1) * width, pl.ds(start, LANES)] = weight
            return carry

        lax.fori_loop(0, pupil_cols // LANES, tile, 0)


def columns_kernel(wind_hbm, *refs):
    tables, blocks, (out, strip, sibling_strip, wind, sem) = refs[:4], refs[4:8], refs[8:]
    load = fetch((wind_hbm, wind, sem))[0]
    column_weights(*tables, lax.axis_index("layer") * out.shape[1], out)
    across, diagonal, near, keep = blocks
    core = lax.rem(lax.axis_index("dir"), 2)
    load.wait()
    strip[...] = outer_strip(wind, core == 1, keep, near, diagonal)
    sibling_strip[...] = outer_strip(wind, core == 0, near, keep, across)


def project_rows(rows_ref, keep, near, across, diagonal, level):
    screen = stack(keep[level], near[level], across[level], diagonal[level])
    rows = stack(rows_ref[0, level], rows_ref[1, level])
    return dot(rows, screen).astype(jnp.bfloat16)


def first_rows_kernel(rows_ref, across, diagonal, near, keep, mine, sibling, other, sibling_other):
    layers, half, _ = mine.shape
    for level in range(layers):
        part = project_rows(rows_ref, keep, near, across, diagonal, level)
        for k, out in enumerate((mine, other, sibling, sibling_other)):
            out[level] = part[k * half : (k + 1) * half]


def outer_strip(wind, odd, own, near, far):
    layers, rows, _ = own.shape
    core = lax.rem(lax.axis_index("dir"), 2)
    lane = lax.broadcasted_iota(jnp.int32, (rows, LANES), 1)
    strip = jnp.zeros((rows, LANES), jnp.float32)
    for level in range(layers):
        edges = [stack(block[level, :16], block[level, rows - 16 :]) for block in (near, far)]
        moved = shifted_rows(wind[0, level], odd, own[level], *edges)
        at = WIND_MAX * level
        moved = pltpu.roll(moved, at + WIND_MAX * core, 1)
        strip = jnp.where((lane >= at) & (lane < at + WIND_MAX), moved, strip)
    return strip.T[:STRIP].astype(jnp.bfloat16)


def put_strip(out, at, strip):
    for k in range(strip.shape[1] // LANES):
        out[at + k * STRIP : at + (k + 1) * STRIP, :] = strip[:, k * LANES : (k + 1) * LANES]


def get_strip(ref, at):
    return beside(*[ref[start : start + STRIP, :] for start in range(at, ref.shape[0], STRIP)])


def later_rows_kernel(rows_ref, *refs):
    chunks, refs = refs[:8], refs[8:]
    sibling0, strip, sibling_strip, mine, give, far, sibling_far, rest, sibling_rest = refs
    across, diagonal, near, keep, across0, diagonal0, near0, keep0 = chunks
    layers, half, width = mine.shape
    rows = near.shape[1]
    size = (far.shape[0] - STRIP * rows // LANES) // layers
    start = half - size
    for level in range(layers):
        part = project_rows(rows_ref, keep, near, across, diagonal, level)
        mine[level] = part[:half]
        for k, out, remainder in ((1, far, rest), (3, sibling_far, sibling_rest)):
            piece = part[k * half : (k + 1) * half]
            out[level * size : (level + 1) * size] = piece[start:]
            remainder[level * start : (level + 1) * start] = piece[:start]
        give[level, :half, :width] = sibling0[level]
        give[level, :half, width:] = part[2 * half : 3 * half]
        for k, blocks in enumerate(((across0, keep0), (across, keep))):
            cut = slice(k * width, (k + 1) * width)
            edges = [block[level, at : at + 16] for block in blocks for at in (0, rows - 16)]
            give[level, half:, cut] = stack(*edges)
    put_strip(far, layers * size, strip)
    put_strip(sibling_far, layers * size, sibling_strip)


def project(parts, cols_refs, at):
    cols = stack(*[ref[level, start:stop, at : at + 256] for ref, level, start, stop in cols_refs])
    return dot(beside(*parts), cols)


def phase_kernel(*refs):
    tables, refs = refs[:4], refs[4:]
    cols_ref, mine0, mine1, came, sibling_came, phase, cols_out = refs
    first = jnp.bitwise_xor(lax.axis_index("layer"), 1) * cols_out.shape[1]
    column_weights(*tables, first, cols_out)
    layers, _, width = mine0.shape
    parts, cuts = [], []
    for level in range(layers):
        parts += [mine0[level], mine1[level], came[level], sibling_came[level]]
        cuts += [(cols_ref, level, 0, 2 * width)]
        cuts += [(cols_out, level, 0, width), (cols_out, level, 2 * width, 3 * width)]
    for at in range(0, phase.shape[1], 256):
        phase[:, at : at + 256] = project(parts, cuts, at)


def sum_up(start, mine_ref, cols_ref, phase, taken, came, sibling_came, outs):
    layers, _, width = taken.shape
    width = width // 2
    block = outs[0].shape[0]
    size = block * len(outs)
    rows = slice(start, start + size)
    parts, cuts = [], []
    for level in range(layers):
        cut = slice(level * size, (level + 1) * size)
        parts += [taken[level, rows], came[cut], sibling_came[cut]]
        cuts += [(mine_ref, level, 2 * width, 4 * width)]
        cuts += [(cols_ref, level, width, 2 * width), (cols_ref, level, 3 * width, 4 * width)]
    pupil_cols = phase.shape[1]
    for at in range(0, pupil_cols, 256):
        total = (phase[rows, at : at + 256] + project(parts, cuts, at)).astype(jnp.bfloat16)
        for k, out in enumerate(outs):
            out[:, at : at + 256] = total[k * block : (k + 1) * block]


def strip_steps(pairs):
    return [2**k - 1 for k in range(1, pairs.bit_length())]


def add_strip(pairs, step, strips, out):
    pair = lax.axis_index("layer") // 2
    after = lax.rem(pair + 1, pairs) == jnp.bitwise_xor(pair, step)
    at = out.shape[1] - strips.shape[1]
    last, first = strips[:STRIP].astype(jnp.float32), strips[STRIP:].astype(jnp.float32)
    out[:, at:] = jnp.where(after, last, first).astype(jnp.bfloat16)


def far_kernel(mine_ref, cols_ref, phase, taken, came, sibling_came, out, strips):
    half, size = phase.shape[0], out.shape[0]
    sum_up(half - size, mine_ref, cols_ref, phase, taken, came, sibling_came, [out])
    layers = taken.shape[0]
    odd = lax.rem(lax.axis_index("dir"), 2) == 1
    here = get_strip(came, layers * size).astype(jnp.float32)
    there = get_strip(sibling_came, layers * size).astype(jnp.float32)
    strips[:STRIP] = jnp.where(odd, here, there).astype(jnp.bfloat16)
    strips[STRIP:] = jnp.where(odd, there, here).astype(jnp.bfloat16)
    add_strip(half // size, half // size - 1, strips, out)


def rest_kernel(mine_ref, cols_ref, phase, taken, came, sibling_came, strips, *outs):
    sum_up(0, mine_ref, cols_ref, phase, taken, came, sibling_came, outs)
    pairs = len(outs) + 1
    for step in strip_steps(pairs)[:-1]:
        add_strip(pairs, step, strips, outs[step])


def shifted_rows(shift, odd, own, near, far):
    own, near, far = [block.astype(jnp.float32) for block in (own, near, far)]
    rows = own.shape[0]
    before = jnp.where(odd, near[16:], far[16:])
    after = jnp.where(odd, far[:16], near[:16])
    shift = jnp.where(shift < 0, shift + rows + 32, shift)
    return pltpu.roll(stack(before, own, after), shift, 0)[16 : 16 + rows]


def shift_kernel(wind_hbm, own, near0, near1, diagonal0, diagonal1, taken, partner_strips, *refs):
    messages, (out, wind, sem) = refs[:-3], refs[-3:]
    load = fetch((wind_hbm, wind, sem))[0]
    layers, rows, cols = own.shape
    odd = lax.rem(lax.axis_index("dir"), 2) == 1
    half = taken.shape[1] - 64
    pairs = 2 ** len(messages)
    pair, second = lax.axis_index("layer") // 2, lax.rem(lax.axis_index("layer"), 2) == 1
    before = jnp.bitwise_xor(pair, lax.rem(pair + pairs - 1, pairs))
    after = jnp.bitwise_xor(pair, lax.rem(pair + 1, pairs))
    left = partner_strips[:STRIP].astype(jnp.float32)
    right = partner_strips[STRIP:].astype(jnp.float32)
    for step, message in zip(strip_steps(pairs), messages):
        strip = message[:, message.shape[1] - rows :].astype(jnp.float32)
        left = jnp.where(jnp.logical_and(before == step, jnp.logical_not(second)), strip, left)
        right = jnp.where(jnp.logical_and(after == step, second), strip, right)
    strips = stack(left, right, jnp.zeros((LANES - 2 * STRIP, rows), jnp.float32)).T
    lane = lax.broadcasted_iota(jnp.int32, (rows, LANES), 1)
    load.wait()
    for level in range(layers):
        last = pltpu.roll(strips, LANES - WIND_MAX * (level + 1), 1)
        first = pltpu.roll(strips, LANES - STRIP - WIND_MAX * level, 1)
        extra = jnp.where(lane < WIND_MAX, first, last)
        pair = []
        for at, parts in ((half, (diagonal0, diagonal1)), (half + 32, (near0, near1))):
            here = [stack(part[level, :16], part[level, rows - 16 :]).astype(jnp.float32) for part in parts]
            there = taken[level, at : at + 32].astype(jnp.float32)
            width = there.shape[1] // 2
            quarters = [*here, there[:, width:], there[:, :width]]
            pair.append(beside(*[jnp.where(odd, quarters[3 - k], quarters[k]) for k in range(4)]))
        far, near = pair
        moved = shifted_rows(wind[0, level], odd, own[level], near, far)
        shift = wind[1, level]
        shift = jnp.where(shift < 0, shift + cols + LANES, shift)
        out[level] = pltpu.roll(beside(moved, extra), shift, 1)[:, :cols].astype(jnp.bfloat16)


def optics_kernel(amplitude, ones, columns, lines, amp_out, high_out, low_out, lines_out):
    rows, pupil_cols = amplitude.shape
    for step in range(pupil_cols // LANES):
        cut = slice(step * LANES, (step + 1) * LANES)
        amp = amplitude[:, cut]
        energy = (amp * amp).reshape(rows // SUB_PIX, SUB_PIX, LANES).sum(axis=1)
        energy = jnp.broadcast_to(energy[:, None], (rows // SUB_PIX, SUB_PIX, LANES)).reshape(rows, LANES)
        total = jnp.dot(energy, ones[...], precision=lax.Precision.HIGHEST, preferred_element_type=jnp.float32)
        amp_out[:, cut] = amp * lax.rsqrt(total)
    high_out[...], low_out[...] = split(columns[...])
    high, low = split(lines[...])
    lines_out[...] = jnp.concatenate([high, high, low], axis=1)


def sin_cos(phase):
    turns = jnp.floor(phase * (1.0 / np.pi) + 0.5)
    rest = phase - turns * 3.140625
    rest = rest - turns * 9.67653589793e-4
    odd = turns - 2.0 * jnp.floor(turns * 0.5)
    sign = 1.0 - 2.0 * odd
    square = rest * rest
    sine = -1.0 / 39916800.0
    for term in (1.0 / 362880.0, -1.0 / 5040.0, 1.0 / 120.0, -1.0 / 6.0, 1.0):
        sine = sine * square + term
    cosine = 1.0 / 479001600.0
    for term in (-1.0 / 3628800.0, 1.0 / 40320.0, -1.0 / 720.0, 1.0 / 24.0, -0.5, 1.0):
        cosine = cosine * square + term
    return sine * rest * sign, cosine * sign


def split(value):
    high = value.astype(jnp.bfloat16)
    low = (value - high.astype(jnp.float32)).astype(jnp.bfloat16)
    return high, low


def imaging_kernel(count, *refs):
    parts = refs[:count]
    amp_ref, cols_high, cols_low, rows_table, out = refs[count:]
    rows, cols = amp_ref.shape
    tiles = cols // LANES
    phase = parts[0][:, :cols].astype(jnp.float32)
    for part in parts[1:]:
        phase = phase + part[:, :cols].astype(jnp.float32)
    sine, cosine = sin_cos(phase)
    amp = amp_ref[...]
    real, imag = amp * cosine, amp * sine
    field = jnp.concatenate(
        [
            jnp.concatenate(
                [real[:, t * LANES : (t + 1) * LANES], imag[:, t * LANES : (t + 1) * LANES]], axis=1
            )
            for t in range(tiles)
        ],
        axis=0,
    )
    high, low = split(field)
    half = dot(high, cols_high[...]) + (dot(low, cols_high[...]) + dot(high, cols_low[...]))
    wide = 2 * LANES
    out_rows = 2 * rows
    for t in range(tiles):
        mine = half[t * rows : (t + 1) * rows]
        mine = jnp.concatenate([mine[:, :wide], mine[:, wide:]], axis=0)
        high, low = split(mine)
        full = dot(rows_table[...], jnp.concatenate([high, low, high], axis=0))
        real, imag = full[:out_rows], full[out_rows:]
        out[:, t * wide : (t + 1) * wide] = real * real + imag * imag


def tables_of(rows):
    freq = np.arange(SPOT_PIX)[:, None] - SPOT_PIX // 2
    angle = ((freq * np.arange(SUB_PIX)[None, :]) % SPOT_PIX) * (2.0 * np.pi / SPOT_PIX)
    cos, sin = np.cos(angle), np.sin(angle)

    def blocks(table, count):
        return np.kron(np.eye(count), table)

    per_tile = LANES // SUB_PIX
    col_cos, col_sin = blocks(cos.T, per_tile), blocks(sin.T, per_tile)
    columns = np.block([[col_cos, -col_sin], [col_sin, col_cos]])
    count = rows // SUB_PIX
    row_cos, row_sin = blocks(cos, count), blocks(sin, count)
    lines = np.block([[row_cos, row_sin], [-row_sin, row_cos]])

    return columns.astype(np.float32), lines.astype(np.float32)


def per_device(screens, amplitude, wind, offsets, ratio):
    layers, rows_dev, cols_dev = screens.shape
    n_layer = lax.axis_size("layer")
    n_dir = lax.axis_size("dir")
    rows, pupil_cols = amplitude.shape
    pairs = n_layer // 2
    half = pairs * rows
    pupil_rows = 2 * half
    assert n_dir == 4 and rows == STRIP and pairs > 2
    bf16, f32 = jnp.bfloat16, jnp.float32
    wind = jnp.transpose(wind, (1, 0))
    offsets = jnp.transpose(offsets, (1, 2, 0))
    ratio = jnp.transpose(ratio, (1, 2, 0))
    smem, sem = pltpu.SMEM, pltpu.SemaphoreType.DMA
    wind_scratch = [smem(wind.shape, jnp.int32), sem]

    def shape(*dims, dtype=bf16):
        return jax.ShapeDtypeStruct(dims, dtype)

    def swap(value, bits):
        return lax.ppermute(value, "dir", [(i, i ^ bits) for i in range(n_dir)])

    def partner(value, bits=0):
        count = n_layer * n_dir
        return lax.ppermute(value, ("layer", "dir"), [(i, i ^ n_dir ^ bits) for i in range(count)])

    def turn(value, step):
        return lax.ppermute(value, "layer", [(i, (i + step) % n_layer) for i in range(n_layer)])

    width = cols_dev // 4
    chunk = shape(layers, rows_dev, width)
    keep0, keep1, give0, give1 = call(
        split_kernel,
        [chunk] * 4,
        (screens,),
        0,
        "split",
        in_hbm=(0,),
        scratch=[sem((4,))],
        brief=True,
    )
    across0 = swap(keep0, 2)
    diagonal0 = swap(give0, 3)
    near0 = swap(give0, 1)
    across1 = swap(keep1, 2)
    diagonal1 = swap(give1, 3)
    ones = np.kron(np.eye(LANES // SUB_PIX), np.ones((SUB_PIX, SUB_PIX))).astype(np.float32)
    optics_in = (amplitude, jnp.asarray(ones), *[jnp.asarray(table) for table in tables_of(rows)])
    copies = [shape(*array.shape, dtype=array.dtype) for array in (screens, *optics_in)]
    row_weights, *tables = call(
        functools.partial(weights_kernel, (n_layer, rows_dev, cols_dev * n_layer)),
        [shape(2, layers, pupil_rows, 4 * rows_dev)]
        + [shape(8, pupil_cols, dtype=dtype) for dtype in (jnp.int32, jnp.int32, f32, f32)]
        + copies,
        (wind, offsets, ratio, screens, *optics_in),
        0,
        "weights",
        in_hbm=range(3, 8),
        scratch=[smem(array.shape, jnp.int32) for array in (wind, offsets, ratio)] + [sem((8,))],
        brief=True,
    )
    tables, own, optics_in = tables[:4], tables[4], tables[5:]
    give1, own = lax.optimization_barrier((give1, own))
    near1 = swap(give1, 1)
    tables = tuple(tables)
    across0, diagonal0, row_weights, tables = lax.optimization_barrier((across0, diagonal0, row_weights, tables))

    projected = shape(layers, half, width)
    mine0, sibling0, other0, sibling_other0 = call(
        first_rows_kernel,
        [projected] * 4,
        (row_weights, across0, diagonal0, near0, keep0),
        0,
        "rows_first",
        brief=True,
    )
    came0 = partner(other0)
    sibling_came0 = partner(sibling_other0, 1)

    tables, mine0 = lax.optimization_barrier((tables, mine0))
    cols, strip, sibling_strip = call(
        columns_kernel,
        [shape(layers, cols_dev, pupil_cols), shape(STRIP, rows_dev), shape(STRIP, rows_dev)],
        (wind, *tables, across0, diagonal0, near0, keep0),
        0,
        "columns",
        scratch=wind_scratch,
        brief=True,
    )
    message = shape(layers * rows + STRIP * rows_dev // LANES, width)
    remainder = shape(layers * (half - rows), width)
    mine1, give, far1, sibling_far1, rest1, sibling_rest1 = call(
        later_rows_kernel,
        [projected, shape(layers, half + 64, 2 * width), message, message, remainder, remainder],
        (row_weights, across1, diagonal1, near1, keep1, across0, diagonal0, near0, keep0, sibling0, strip, sibling_strip),
        0,
        "rows_later",
        brief=True,
    )
    far1, sibling_far1 = partner(far1), partner(sibling_far1, 1)
    rest1, sibling_rest1 = partner(rest1), partner(sibling_rest1, 1)
    taken = swap(give, 1)
    phase, others = call(
        phase_kernel,
        (shape(half, pupil_cols, dtype=f32), shape(layers, cols_dev, pupil_cols)),
        (*tables, cols, mine0, mine1, came0, sibling_came0),
        10_000_000_000,
        "phase",
    )

    steps = strip_steps(pairs)
    sums = [shape(rows, pupil_cols + (rows_dev if k in steps else 0)) for k in range(pairs)]
    far_sum, strips = call(
        far_kernel,
        [sums[-1], shape(2 * STRIP, rows_dev)],
        (cols, others, phase, taken, far1, sibling_far1),
        300_000_000,
        "far",
    )
    rest_sums = call(
        rest_kernel,
        sums[:-1],
        (cols, others, phase, taken, rest1, sibling_rest1, strips),
        300_000_000,
        "rest",
    )
    received = [*rest_sums, far_sum]
    for k in range(1, pairs):
        received[k] = lax.ppermute(received[k], "layer", [(i, i ^ (2 * k)) for i in range(n_layer)])

    optics_in, received[0] = lax.optimization_barrier((optics_in, received[0]))
    optics = call(
        optics_kernel,
        (
            shape(rows, pupil_cols, dtype=f32),
            shape(*optics_in[2].shape),
            shape(*optics_in[2].shape),
            shape(optics_in[3].shape[0], 3 * optics_in[3].shape[1]),
        ),
        optics_in,
        30_000_000,
        "optics",
    )
    new_screens = call(
        shift_kernel,
        shape(layers, rows_dev, cols_dev),
        (wind, own, near0, near1, diagonal0, diagonal1, taken, strips, *[received[k] for k in steps]),
        1_000_000,
        "shift",
        scratch=wind_scratch,
    )
    spots = call(
        functools.partial(imaging_kernel, pairs),
        shape(2 * rows, 2 * pupil_cols, dtype=f32),
        (*received, *optics),
        400_000_000,
        "imaging",
    )
    return (new_screens, spots[None])


def solution(mesh):
    return jax.shard_map(
        per_device,
        mesh=mesh,
        in_specs=(P(None, "dir", "layer"), P("layer", None), P(), P(), P()),
        out_specs=(P(None, "dir", "layer"), P("dir", "layer", None)),
        check_vma=False,
    )
```

```python
import functools

import jax
import jax.numpy as jnp
import numpy as np
from jax import lax
from jax.experimental import pallas as pl
from jax.experimental.pallas import tpu as pltpu
from jax.sharding import PartitionSpec as P

SUB_PIX = 16
SPOT_PIX = 32
WIND_MAX = 8
LANES = 128
STRIP = 32

HBM_SPEC = pl.BlockSpec(memory_space=pltpu.HBM)
VMEM_SPEC = pl.BlockSpec(memory_space=pltpu.VMEM)


def params(*arrays):
    held = sum(array.size * array.dtype.itemsize for array in jax.tree.leaves(arrays))
    return pltpu.CompilerParams(vmem_limit_bytes=held + 8 * 1024 * 1024)


def call(kernel, out_shape, operands, flops, name, in_hbm=(), scratch=(), brief=False):
    def spec(k, array):
        scalars = array.dtype == jnp.int32 and array.size < LANES
        return HBM_SPEC if scalars or k in in_hbm else VMEM_SPEC

    out_specs = jax.tree.map(lambda _: VMEM_SPEC, out_shape)
    size = sum(array.size * array.dtype.itemsize for array in jax.tree.leaves((operands, out_shape)))
    if brief:
        flops = size = 0
    in_specs = [spec(k, array) for k, array in enumerate(operands)]
    operands = [
        pltpu.with_memory_space_constraint(array, pltpu.HBM) if space is HBM_SPEC else array
        for array, space in zip(operands, in_specs)
    ]
    return pl.pallas_call(
        kernel,
        out_shape=out_shape,
        in_specs=in_specs,
        out_specs=out_specs,
        scratch_shapes=list(scratch),
        compiler_params=params(operands, out_shape),
        cost_estimate=pl.CostEstimate(flops=flops, bytes_accessed=size, transcendentals=0),
        name=name,
    )(*operands)


def fetch(*pairs):
    copies = [pltpu.make_async_copy(source, target, sem) for source, target, sem in pairs]
    for copy in copies:
        copy.start()
    return copies


def wrap(value, length):
    value = jnp.where(value < 0, value + length, value)
    return jnp.where(value >= length, value - length, value)


def stack(*blocks):
    return jnp.concatenate(blocks, axis=0)


def beside(*blocks):
    return jnp.concatenate(blocks, axis=1)


def dot(left, right):
    return jnp.dot(left, right, preferred_element_type=jnp.float32)


def spans(pixel, anchor, num, den, length):
    stretched = (pixel * num).astype(jnp.float32)
    den = (jnp.zeros_like(pixel) + den).astype(jnp.float32)
    whole = jnp.floor((stretched + 0.5) / den)
    fraction = (stretched - whole * den) / den
    base = wrap(anchor + whole.astype(jnp.int32), length)
    upper = wrap(base + 1, length)
    return base, upper, 1.0 - fraction, fraction


def chunk_start(half, chunk):
    return 3 * half + chunk * (1 - 2 * half)


def split_kernel(screens, *refs):
    outs, sems = refs[:-1], refs[-1]
    width = outs[0].shape[2]
    core = lax.rem(lax.axis_index("dir"), 2)
    pairs = []
    for k, out in enumerate(outs):
        half = core if k < 2 else 1 - core
        start = pl.multiple_of(chunk_start(half, k % 2) * width, LANES)
        pairs.append((screens.at[:, :, pl.ds(start, width)], out, sems.at[k]))
    for load in fetch(*pairs):
        load.wait()


def weights_kernel(geometry, wind_hbm, offsets_hbm, ratio_hbm, *refs):
    n_layer, rows_dev, screen_cols = geometry
    sources, (rows_out, base_out, upper_out, low_out, high_out), refs = refs[:5], refs[5:10], refs[10:]
    copies, (wind, offsets, ratio, sems) = refs[:5], refs[5:]
    others = fetch(*[(source, copy, sems.at[3 + k]) for k, (source, copy) in enumerate(zip(sources, copies))])
    loads = fetch(
        (wind_hbm, wind, sems.at[0]),
        (offsets_hbm, offsets, sems.at[1]),
        (ratio_hbm, ratio, sems.at[2]),
    )
    _, layers, pupil_rows, screen_rows = rows_out.shape
    half = pupil_rows // 2
    direction = lax.axis_index("dir")
    column = lax.axis_index("layer")
    block = pupil_rows // n_layer
    row = lax.broadcasted_iota(jnp.int32, (half, LANES), 0)
    pair = jnp.bitwise_xor(row // block, column // 2)
    parity = lax.rem(column, 2)
    inside = lax.rem(row, block) + pair * (2 * block)
    pixel_rows = stack(inside + parity * block, inside + (1 - parity) * block)
    lane = lax.broadcasted_iota(jnp.int32, (pupil_rows, LANES), 1)
    for load in loads:
        load.wait()
    for side in range(2):
        target = jnp.bitwise_xor(direction, side)
        for level in range(layers):
            anchor = wrap(offsets[level, 0, target] - wind[0, level], screen_rows)
            num, den = ratio[level, 0, target], ratio[level, 1, target]
            base, upper, low, high = spans(pixel_rows, anchor, num, den, screen_rows)
            for peer in range(4):
                for part in range(rows_dev // LANES):
                    index = lane + (jnp.bitwise_xor(direction, peer) * rows_dev + part * LANES)
                    weight = jnp.where(index == base, low, 0.0)
                    weight = jnp.where(index == upper, high, weight)
                    start = peer * rows_dev + part * LANES
                    rows_out[side, level, :, start : start + LANES] = weight.astype(jnp.bfloat16)
    sub = lax.broadcasted_iota(jnp.int32, (8, LANES), 0)
    anchor, num, den = jnp.zeros_like(sub), jnp.zeros_like(sub), jnp.ones_like(sub)
    for level in range(layers):
        start = wrap(offsets[level, 1, direction] - wind[1, level], screen_cols)
        anchor = jnp.where(sub == level, start, anchor)
        num = jnp.where(sub == level, ratio[level, 0, direction], num)
        den = jnp.where(sub == level, ratio[level, 1, direction], den)
    for at in range(0, base_out.shape[1], LANES):
        pixel = lax.broadcasted_iota(jnp.int32, (8, LANES), 1) + at
        values = spans(pixel, anchor, num, den, screen_cols)
        for out, value in zip((base_out, upper_out, low_out, high_out), values):
            out[:, at : at + LANES] = value
    for load in others:
        load.wait()


def column_weights(base_ref, upper_ref, low_ref, high_ref, first, out):
    layers, cols_dev, pupil_cols = out.shape
    width = cols_dev // 4
    core = lax.rem(lax.axis_index("dir"), 2)
    sub = lax.broadcasted_iota(jnp.int32, (width, LANES), 0).astype(jnp.float32).astype(jnp.bfloat16)
    zero = jnp.zeros((width, LANES), jnp.bfloat16)
    for level in range(layers):

        def tile(step, carry):
            start = pl.multiple_of(step * LANES, LANES)
            cut = (slice(level, level + 1), pl.ds(start, LANES))
            base, upper = base_ref[cut], upper_ref[cut]
            low, high = [
                jnp.broadcast_to(ref[cut].astype(jnp.bfloat16), (width, LANES)) for ref in (low_ref, high_ref)
            ]
            for k in range(4):
                shift = first + chunk_start(jnp.bitwise_xor(core, k // 2), k % 2) * width
                base_at, upper_at = [
                    jnp.broadcast_to(
                        jnp.clip(value - shift, -1, width).astype(jnp.float32).astype(jnp.bfloat16), (width, LANES)
                    )
                    for value in (base, upper)
                ]
                weight = jnp.where(sub == base_at, low, zero)
                weight = jnp.where(sub == upper_at, high, weight)
                out[level, k * width : (k + 1) * width, pl.ds(start, LANES)] = weight
            return carry

        lax.fori_loop(0, pupil_cols // LANES, tile, 0)


def columns_kernel(wind_hbm, *refs):
    tables, blocks, (out, strip, sibling_strip, wind, sem) = refs[:4], refs[4:8], refs[8:]
    load = fetch((wind_hbm, wind, sem))[0]
    column_weights(*tables, lax.axis_index("layer") * out.shape[1], out)
    across, diagonal, near, keep = blocks
    core = lax.rem(lax.axis_index("dir"), 2)
    load.wait()
    strip[...] = outer_strip(wind, core == 1, keep, near, diagonal)
    sibling_strip[...] = outer_strip(wind, core == 0, near, keep, across)


def project_rows(rows_ref, keep, near, across, diagonal, level):
    screen = stack(keep[level], near[level], across[level], diagonal[level])
    rows = stack(rows_ref[0, level], rows_ref[1, level])
    return dot(rows, screen).astype(jnp.bfloat16)


def first_rows_kernel(rows_ref, across, diagonal, near, keep, mine, sibling, other, sibling_other):
    layers, half, _ = mine.shape
    for level in range(layers):
        part = project_rows(rows_ref, keep, near, across, diagonal, level)
        for k, out in enumerate((mine, other, sibling, sibling_other)):
            out[level] = part[k * half : (k + 1) * half]


def outer_strip(wind, odd, own, near, far):
    layers, rows, _ = own.shape
    core = lax.rem(lax.axis_index("dir"), 2)
    lane = lax.broadcasted_iota(jnp.int32, (rows, LANES), 1)
    strip = jnp.zeros((rows, LANES), jnp.float32)
    for level in range(layers):
        edges = [stack(block[level, :16], block[level, rows - 16 :]) for block in (near, far)]
        moved = shifted_rows(wind[0, level], odd, own[level], *edges)
        at = WIND_MAX * level
        moved = pltpu.roll(moved, at + WIND_MAX * core, 1)
        strip = jnp.where((lane >= at) & (lane < at + WIND_MAX), moved, strip)
    return strip.T[:STRIP].astype(jnp.bfloat16)


def put_strip(out, at, strip):
    for k in range(strip.shape[1] // LANES):
        out[at + k * STRIP : at + (k + 1) * STRIP, :] = strip[:, k * LANES : (k + 1) * LANES]


def get_strip(ref, at):
    return beside(*[ref[start : start + STRIP, :] for start in range(at, ref.shape[0], STRIP)])


def later_rows_kernel(rows_ref, *refs):
    chunks, refs = refs[:8], refs[8:]
    sibling0, strip, sibling_strip, mine, give, far, sibling_far, rest, sibling_rest = refs
    across, diagonal, near, keep, across0, diagonal0, near0, keep0 = chunks
    layers, half, width = mine.shape
    rows = near.shape[1]
    size = (far.shape[0] - STRIP * rows // LANES) // layers
    start = half - size
    for level in range(layers):
        part = project_rows(rows_ref, keep, near, across, diagonal, level)
        mine[level] = part[:half]
        for k, out, remainder in ((1, far, rest), (3, sibling_far, sibling_rest)):
            piece = part[k * half : (k + 1) * half]
            out[level * size : (level + 1) * size] = piece[start:]
            remainder[level * start : (level + 1) * start] = piece[:start]
        give[level, :half, :width] = sibling0[level]
        give[level, :half, width:] = part[2 * half : 3 * half]
        for k, blocks in enumerate(((across0, keep0), (across, keep))):
            cut = slice(k * width, (k + 1) * width)
            edges = [block[level, at : at + 16] for block in blocks for at in (0, rows - 16)]
            give[level, half:, cut] = stack(*edges)
    put_strip(far, layers * size, strip)
    put_strip(sibling_far, layers * size, sibling_strip)


def project(parts, cols_refs, at):
    cols = stack(*[ref[level, start:stop, at : at + 256] for ref, level, start, stop in cols_refs])
    return dot(beside(*parts), cols)


def phase_kernel(*refs):
    tables, refs = refs[:4], refs[4:]
    cols_ref, mine0, mine1, came, sibling_came, phase, cols_out = refs
    first = jnp.bitwise_xor(lax.axis_index("layer"), 1) * cols_out.shape[1]
    column_weights(*tables, first, cols_out)
    layers, _, width = mine0.shape
    parts, cuts = [], []
    for level in range(layers):
        parts += [mine0[level], mine1[level], came[level], sibling_came[level]]
        cuts += [(cols_ref, level, 0, 2 * width)]
        cuts += [(cols_out, level, 0, width), (cols_out, level, 2 * width, 3 * width)]
    for at in range(0, phase.shape[1], 256):
        phase[:, at : at + 256] = project(parts, cuts, at)


def sum_up(start, mine_ref, cols_ref, phase, taken, came, sibling_came, outs):
    layers, _, width = taken.shape
    width = width // 2
    block = outs[0].shape[0]
    size = block * len(outs)
    rows = slice(start, start + size)
    parts, cuts = [], []
    for level in range(layers):
        cut = slice(level * size, (level + 1) * size)
        parts += [taken[level, rows], came[cut], sibling_came[cut]]
        cuts += [(mine_ref, level, 2 * width, 4 * width)]
        cuts += [(cols_ref, level, width, 2 * width), (cols_ref, level, 3 * width, 4 * width)]
    pupil_cols = phase.shape[1]
    for at in range(0, pupil_cols, 256):
        total = (phase[rows, at : at + 256] + project(parts, cuts, at)).astype(jnp.bfloat16)
        for k, out in enumerate(outs):
            out[:, at : at + 256] = total[k * block : (k + 1) * block]


def strip_steps(pairs):
    return [2**k - 1 for k in range(1, pairs.bit_length())]


def add_strip(pairs, step, strips, out):
    pair = lax.axis_index("layer") // 2
    after = lax.rem(pair + 1, pairs) == jnp.bitwise_xor(pair, step)
    at = out.shape[1] - strips.shape[1]
    last, first = strips[:STRIP].astype(jnp.float32), strips[STRIP:].astype(jnp.float32)
    out[:, at:] = jnp.where(after, last, first).astype(jnp.bfloat16)


def far_kernel(mine_ref, cols_ref, phase, taken, came, sibling_came, out, strips):
    half, size = phase.shape[0], out.shape[0]
    sum_up(half - size, mine_ref, cols_ref, phase, taken, came, sibling_came, [out])
    layers = taken.shape[0]
    odd = lax.rem(lax.axis_index("dir"), 2) == 1
    here = get_strip(came, layers * size).astype(jnp.float32)
    there = get_strip(sibling_came, layers * size).astype(jnp.float32)
    strips[:STRIP] = jnp.where(odd, here, there).astype(jnp.bfloat16)
    strips[STRIP:] = jnp.where(odd, there, here).astype(jnp.bfloat16)
    add_strip(half // size, half // size - 1, strips, out)


def rest_kernel(mine_ref, cols_ref, phase, taken, came, sibling_came, strips, *outs):
    sum_up(0, mine_ref, cols_ref, phase, taken, came, sibling_came, outs)
    pairs = len(outs) + 1
    for step in strip_steps(pairs)[:-1]:
        add_strip(pairs, step, strips, outs[step])


def shifted_rows(shift, odd, own, near, far):
    own, near, far = [block.astype(jnp.float32) for block in (own, near, far)]
    rows = own.shape[0]
    before = jnp.where(odd, near[16:], far[16:])
    after = jnp.where(odd, far[:16], near[:16])
    shift = jnp.where(shift < 0, shift + rows + 32, shift)
    return pltpu.roll(stack(before, own, after), shift, 0)[16 : 16 + rows]


def shift_kernel(wind_hbm, own, near0, near1, diagonal0, diagonal1, taken, partner_strips, *refs):
    messages, (out, wind, sem) = refs[:-3], refs[-3:]
    load = fetch((wind_hbm, wind, sem))[0]
    layers, rows, cols = own.shape
    odd = lax.rem(lax.axis_index("dir"), 2) == 1
    half = taken.shape[1] - 64
    pairs = 2 ** len(messages)
    pair, second = lax.axis_index("layer") // 2, lax.rem(lax.axis_index("layer"), 2) == 1
    before = jnp.bitwise_xor(pair, lax.rem(pair + pairs - 1, pairs))
    after = jnp.bitwise_xor(pair, lax.rem(pair + 1, pairs))
    left = partner_strips[:STRIP].astype(jnp.float32)
    right = partner_strips[STRIP:].astype(jnp.float32)
    for step, message in zip(strip_steps(pairs), messages):
        strip = message[:, message.shape[1] - rows :].astype(jnp.float32)
        left = jnp.where(jnp.logical_and(before == step, jnp.logical_not(second)), strip, left)
        right = jnp.where(jnp.logical_and(after == step, second), strip, right)
    strips = stack(left, right, jnp.zeros((LANES - 2 * STRIP, rows), jnp.float32)).T
    lane = lax.broadcasted_iota(jnp.int32, (rows, LANES), 1)
    load.wait()
    for level in range(layers):
        last = pltpu.roll(strips, LANES - WIND_MAX * (level + 1), 1)
        first = pltpu.roll(strips, LANES - STRIP - WIND_MAX * level, 1)
        extra = jnp.where(lane < WIND_MAX, first, last)
        pair = []
        for at, parts in ((half, (diagonal0, diagonal1)), (half + 32, (near0, near1))):
            here = [stack(part[level, :16], part[level, rows - 16 :]).astype(jnp.float32) for part in parts]
            there = taken[level, at : at + 32].astype(jnp.float32)
            width = there.shape[1] // 2
            quarters = [*here, there[:, width:], there[:, :width]]
            pair.append(beside(*[jnp.where(odd, quarters[3 - k], quarters[k]) for k in range(4)]))
        far, near = pair
        moved = shifted_rows(wind[0, level], odd, own[level], near, far)
        shift = wind[1, level]
        shift = jnp.where(shift < 0, shift + cols + LANES, shift)
        out[level] = pltpu.roll(beside(moved, extra), shift, 1)[:, :cols].astype(jnp.bfloat16)


def optics_kernel(amplitude, ones, columns, lines, amp_out, high_out, low_out, lines_out):
    rows, pupil_cols = amplitude.shape
    for step in range(pupil_cols // LANES):
        cut = slice(step * LANES, (step + 1) * LANES)
        amp = amplitude[:, cut]
        energy = (amp * amp).reshape(rows // SUB_PIX, SUB_PIX, LANES).sum(axis=1)
        energy = jnp.broadcast_to(energy[:, None], (rows // SUB_PIX, SUB_PIX, LANES)).reshape(rows, LANES)
        total = jnp.dot(energy, ones[...], precision=lax.Precision.HIGHEST, preferred_element_type=jnp.float32)
        amp_out[:, cut] = amp * lax.rsqrt(total)
    high_out[...], low_out[...] = split(columns[...])
    high, low = split(lines[...])
    lines_out[...] = jnp.concatenate([high, high, low], axis=1)


def sin_cos(phase):
    turns = jnp.floor(phase * (1.0 / np.pi) + 0.5)
    rest = phase - turns * 3.140625
    rest = rest - turns * 9.67653589793e-4
    odd = turns - 2.0 * jnp.floor(turns * 0.5)
    sign = 1.0 - 2.0 * odd
    square = rest * rest
    sine = -1.0 / 39916800.0
    for term in (1.0 / 362880.0, -1.0 / 5040.0, 1.0 / 120.0, -1.0 / 6.0, 1.0):
        sine = sine * square + term
    cosine = 1.0 / 479001600.0
    for term in (-1.0 / 3628800.0, 1.0 / 40320.0, -1.0 / 720.0, 1.0 / 24.0, -0.5, 1.0):
        cosine = cosine * square + term
    return sine * rest * sign, cosine * sign


def split(value):
    high = value.astype(jnp.bfloat16)
    low = (value - high.astype(jnp.float32)).astype(jnp.bfloat16)
    return high, low


def imaging_kernel(count, *refs):
    parts = refs[:count]
    amp_ref, cols_high, cols_low, rows_table, out = refs[count:]
    rows, cols = amp_ref.shape
    tiles = cols // LANES
    phase = parts[0][:, :cols].astype(jnp.float32)
    for part in parts[1:]:
        phase = phase + part[:, :cols].astype(jnp.float32)
    sine, cosine = sin_cos(phase)
    amp = amp_ref[...]
    real, imag = amp * cosine, amp * sine
    field = jnp.concatenate(
        [
            jnp.concatenate(
                [real[:, t * LANES : (t + 1) * LANES], imag[:, t * LANES : (t + 1) * LANES]], axis=1
            )
            for t in range(tiles)
        ],
        axis=0,
    )
    high, low = split(field)
    half = dot(high, cols_high[...]) + (dot(low, cols_high[...]) + dot(high, cols_low[...]))
    wide = 2 * LANES
    out_rows = 2 * rows
    for t in range(tiles):
        mine = half[t * rows : (t + 1) * rows]
        mine = jnp.concatenate([mine[:, :wide], mine[:, wide:]], axis=0)
        high, low = split(mine)
        full = dot(rows_table[...], jnp.concatenate([high, low, high], axis=0))
        real, imag = full[:out_rows], full[out_rows:]
        out[:, t * wide : (t + 1) * wide] = real * real + imag * imag


def tables_of(rows):
    freq = np.arange(SPOT_PIX)[:, None] - SPOT_PIX // 2
    angle = ((freq * np.arange(SUB_PIX)[None, :]) % SPOT_PIX) * (2.0 * np.pi / SPOT_PIX)
    cos, sin = np.cos(angle), np.sin(angle)

    def blocks(table, count):
        return np.kron(np.eye(count), table)

    per_tile = LANES // SUB_PIX
    col_cos, col_sin = blocks(cos.T, per_tile), blocks(sin.T, per_tile)
    columns = np.block([[col_cos, -col_sin], [col_sin, col_cos]])
    count = rows // SUB_PIX
    row_cos, row_sin = blocks(cos, count), blocks(sin, count)
    lines = np.block([[row_cos, row_sin], [-row_sin, row_cos]])

    return columns.astype(np.float32), lines.astype(np.float32)


def per_device(screens, amplitude, wind, offsets, ratio):
    layers, rows_dev, cols_dev = screens.shape
    n_layer = lax.axis_size("layer")
    n_dir = lax.axis_size("dir")
    rows, pupil_cols = amplitude.shape
    pairs = n_layer // 2
    half = pairs * rows
    pupil_rows = 2 * half
    assert n_dir == 4 and rows == STRIP and pairs > 2
    bf16, f32 = jnp.bfloat16, jnp.float32
    wind = jnp.transpose(wind, (1, 0))
    offsets = jnp.transpose(offsets, (1, 2, 0))
    ratio = jnp.transpose(ratio, (1, 2, 0))
    smem, sem = pltpu.SMEM, pltpu.SemaphoreType.DMA
    wind_scratch = [smem(wind.shape, jnp.int32), sem]

    def shape(*dims, dtype=bf16):
        return jax.ShapeDtypeStruct(dims, dtype)

    def swap(value, bits):
        return lax.ppermute(value, "dir", [(i, i ^ bits) for i in range(n_dir)])

    def partner(value, bits=0):
        count = n_layer * n_dir
        return lax.ppermute(value, ("layer", "dir"), [(i, i ^ n_dir ^ bits) for i in range(count)])

    def turn(value, step):
        return lax.ppermute(value, "layer", [(i, (i + step) % n_layer) for i in range(n_layer)])

    width = cols_dev // 4
    chunk = shape(layers, rows_dev, width)
    keep0, keep1, give0, give1 = call(
        split_kernel,
        [chunk] * 4,
        (screens,),
        0,
        "split",
        in_hbm=(0,),
        scratch=[sem((4,))],
        brief=True,
    )
    across0 = swap(keep0, 2)
    diagonal0 = swap(give0, 3)
    near0 = swap(give0, 1)
    across1 = swap(keep1, 2)
    diagonal1 = swap(give1, 3)
    ones = np.kron(np.eye(LANES // SUB_PIX), np.ones((SUB_PIX, SUB_PIX))).astype(np.float32)
    optics_in = (amplitude, jnp.asarray(ones), *[jnp.asarray(table) for table in tables_of(rows)])
    copies = [shape(*array.shape, dtype=array.dtype) for array in (screens, *optics_in)]
    row_weights, *tables = call(
        functools.partial(weights_kernel, (n_layer, rows_dev, cols_dev * n_layer)),
        [shape(2, layers, pupil_rows, 4 * rows_dev)]
        + [shape(8, pupil_cols, dtype=dtype) for dtype in (jnp.int32, jnp.int32, f32, f32)]
        + copies,
        (wind, offsets, ratio, screens, *optics_in),
        0,
        "weights",
        in_hbm=range(3, 8),
        scratch=[smem(array.shape, jnp.int32) for array in (wind, offsets, ratio)] + [sem((8,))],
        brief=True,
    )
    tables, own, optics_in = tables[:4], tables[4], tables[5:]
    give1, own = lax.optimization_barrier((give1, own))
    near1 = swap(give1, 1)
    tables = tuple(tables)
    across0, diagonal0, row_weights, tables = lax.optimization_barrier((across0, diagonal0, row_weights, tables))

    projected = shape(layers, half, width)
    mine0, sibling0, other0, sibling_other0 = call(
        first_rows_kernel,
        [projected] * 4,
        (row_weights, across0, diagonal0, near0, keep0),
        0,
        "rows_first",
        brief=True,
    )
    came0 = partner(other0)
    sibling_came0 = partner(sibling_other0, 1)

    tables, mine0 = lax.optimization_barrier((tables, mine0))
    cols, strip, sibling_strip = call(
        columns_kernel,
        [shape(layers, cols_dev, pupil_cols), shape(STRIP, rows_dev), shape(STRIP, rows_dev)],
        (wind, *tables, across0, diagonal0, near0, keep0),
        0,
        "columns",
        scratch=wind_scratch,
        brief=True,
    )
    message = shape(layers * rows + STRIP * rows_dev // LANES, width)
    remainder = shape(layers * (half - rows), width)
    mine1, give, far1, sibling_far1, rest1, sibling_rest1 = call(
        later_rows_kernel,
        [projected, shape(layers, half + 64, 2 * width), message, message, remainder, remainder],
        (row_weights, across1, diagonal1, near1, keep1, across0, diagonal0, near0, keep0, sibling0, strip, sibling_strip),
        0,
        "rows_later",
        brief=True,
    )
    far1, sibling_far1 = partner(far1), partner(sibling_far1, 1)
    rest1, sibling_rest1 = partner(rest1), partner(sibling_rest1, 1)
    taken = swap(give, 1)
    phase, others = call(
        phase_kernel,
        (shape(half, pupil_cols, dtype=f32), shape(layers, cols_dev, pupil_cols)),
        (*tables, cols, mine0, mine1, came0, sibling_came0),
        10_000_000_000,
        "phase",
    )

    steps = strip_steps(pairs)
    sums = [shape(rows, pupil_cols + (rows_dev if k in steps else 0)) for k in range(pairs)]
    far_sum, strips = call(
        far_kernel,
        [sums[-1], shape(2 * STRIP, rows_dev)],
        (cols, others, phase, taken, far1, sibling_far1),
        300_000_000,
        "far",
    )
    rest_sums = call(
        rest_kernel,
        sums[:-1],
        (cols, others, phase, taken, rest1, sibling_rest1, strips),
        0,
        "rest",
        brief=True,
    )
    received = [*rest_sums, far_sum]
    for k in range(1, pairs):
        received[k] = lax.ppermute(received[k], "layer", [(i, i ^ (2 * k)) for i in range(n_layer)])

    optics_in, received[-1] = lax.optimization_barrier((optics_in, received[-1]))
    optics = call(
        optics_kernel,
        (
            shape(rows, pupil_cols, dtype=f32),
            shape(*optics_in[2].shape),
            shape(*optics_in[2].shape),
            shape(optics_in[3].shape[0], 3 * optics_in[3].shape[1]),
        ),
        optics_in,
        0,
        "optics",
        brief=True,
    )
    received[1], optics = lax.optimization_barrier((received[1], optics))
    new_screens = call(
        shift_kernel,
        shape(layers, rows_dev, cols_dev),
        (wind, own, near0, near1, diagonal0, diagonal1, taken, strips, *[received[k] for k in steps]),
        0,
        "shift",
        scratch=wind_scratch,
        brief=True,
    )
    spots = call(
        functools.partial(imaging_kernel, pairs),
        shape(2 * rows, 2 * pupil_cols, dtype=f32),
        (*received, *optics),
        400_000_000,
        "imaging",
    )
    return (new_screens, spots[None])


def solution(mesh):
    return jax.shard_map(
        per_device,
        mesh=mesh,
        in_specs=(P(None, "dir", "layer"), P("layer", None), P(), P(), P()),
        out_specs=(P(None, "dir", "layer"), P("dir", "layer", None)),
        check_vma=False,
    )
```

```python
import functools

import jax
import jax.numpy as jnp
import numpy as np
from jax import lax
from jax.experimental import pallas as pl
from jax.experimental.pallas import tpu as pltpu
from jax.sharding import PartitionSpec as P

SUB_PIX = 16
SPOT_PIX = 32
WIND_MAX = 8
LANES = 128
STRIP = 32

HBM_SPEC = pl.BlockSpec(memory_space=pltpu.HBM)
VMEM_SPEC = pl.BlockSpec(memory_space=pltpu.VMEM)


def params(*arrays):
    held = sum(array.size * array.dtype.itemsize for array in jax.tree.leaves(arrays))
    return pltpu.CompilerParams(vmem_limit_bytes=held + 8 * 1024 * 1024)


def call(kernel, out_shape, operands, flops, name, in_hbm=(), scratch=(), brief=False):
    def spec(k, array):
        scalars = array.dtype == jnp.int32 and array.size < LANES
        return HBM_SPEC if scalars or k in in_hbm else VMEM_SPEC

    out_specs = jax.tree.map(lambda _: VMEM_SPEC, out_shape)
    size = sum(array.size * array.dtype.itemsize for array in jax.tree.leaves((operands, out_shape)))
    if brief:
        flops = size = 0
    in_specs = [spec(k, array) for k, array in enumerate(operands)]
    operands = [
        pltpu.with_memory_space_constraint(array, pltpu.HBM) if space is HBM_SPEC else array
        for array, space in zip(operands, in_specs)
    ]
    return pl.pallas_call(
        kernel,
        out_shape=out_shape,
        in_specs=in_specs,
        out_specs=out_specs,
        scratch_shapes=list(scratch),
        compiler_params=params(operands, out_shape),
        cost_estimate=pl.CostEstimate(flops=flops, bytes_accessed=size, transcendentals=0),
        name=name,
    )(*operands)


def fetch(*pairs):
    copies = [pltpu.make_async_copy(source, target, sem) for source, target, sem in pairs]
    for copy in copies:
        copy.start()
    return copies


def wrap(value, length):
    value = jnp.where(value < 0, value + length, value)
    return jnp.where(value >= length, value - length, value)


def stack(*blocks):
    return jnp.concatenate(blocks, axis=0)


def beside(*blocks):
    return jnp.concatenate(blocks, axis=1)


def dot(left, right):
    return jnp.dot(left, right, preferred_element_type=jnp.float32)


def spans(pixel, anchor, num, den, length):
    stretched = (pixel * num).astype(jnp.float32)
    den = (jnp.zeros_like(pixel) + den).astype(jnp.float32)
    whole = jnp.floor((stretched + 0.5) / den)
    fraction = (stretched - whole * den) / den
    base = wrap(anchor + whole.astype(jnp.int32), length)
    upper = wrap(base + 1, length)
    return base, upper, 1.0 - fraction, fraction


def chunk_start(half, chunk):
    return 3 * half + chunk * (1 - 2 * half)


def split_kernel(screens, *refs):
    outs, sems = refs[:-1], refs[-1]
    width = outs[0].shape[2]
    core = lax.rem(lax.axis_index("dir"), 2)
    pairs = []
    for k, out in enumerate(outs):
        half = core if k < 2 else 1 - core
        start = pl.multiple_of(chunk_start(half, k % 2) * width, LANES)
        pairs.append((screens.at[:, :, pl.ds(start, width)], out, sems.at[k]))
    for load in fetch(*pairs):
        load.wait()


def weights_kernel(geometry, wind_hbm, offsets_hbm, ratio_hbm, *refs):
    n_layer, rows_dev, screen_cols = geometry
    sources, (rows_out, base_out, upper_out, low_out, high_out), refs = refs[:5], refs[5:10], refs[10:]
    copies, (wind, offsets, ratio, sems) = refs[:5], refs[5:]
    others = fetch(*[(source, copy, sems.at[3 + k]) for k, (source, copy) in enumerate(zip(sources, copies))])
    loads = fetch(
        (wind_hbm, wind, sems.at[0]),
        (offsets_hbm, offsets, sems.at[1]),
        (ratio_hbm, ratio, sems.at[2]),
    )
    _, layers, pupil_rows, screen_rows = rows_out.shape
    half = pupil_rows // 2
    direction = lax.axis_index("dir")
    column = lax.axis_index("layer")
    block = pupil_rows // n_layer
    row = lax.broadcasted_iota(jnp.int32, (half, LANES), 0)
    step = row // block
    for at, value in enumerate(send_order(n_layer // 2)):
        step = jnp.where(row // block == at, value, step)
    pair = jnp.bitwise_xor(step, column // 2)
    parity = lax.rem(column, 2)
    inside = lax.rem(row, block) + pair * (2 * block)
    pixel_rows = stack(inside + parity * block, inside + (1 - parity) * block)
    lane = lax.broadcasted_iota(jnp.int32, (pupil_rows, LANES), 1)
    for load in loads:
        load.wait()
    for side in range(2):
        target = jnp.bitwise_xor(direction, side)
        for level in range(layers):
            anchor = wrap(offsets[level, 0, target] - wind[0, level], screen_rows)
            num, den = ratio[level, 0, target], ratio[level, 1, target]
            base, upper, low, high = spans(pixel_rows, anchor, num, den, screen_rows)
            for peer in range(4):
                for part in range(rows_dev // LANES):
                    index = lane + (jnp.bitwise_xor(direction, peer) * rows_dev + part * LANES)
                    weight = jnp.where(index == base, low, 0.0)
                    weight = jnp.where(index == upper, high, weight)
                    start = peer * rows_dev + part * LANES
                    rows_out[side, level, :, start : start + LANES] = weight.astype(jnp.bfloat16)
    sub = lax.broadcasted_iota(jnp.int32, (8, LANES), 0)
    anchor, num, den = jnp.zeros_like(sub), jnp.zeros_like(sub), jnp.ones_like(sub)
    for level in range(layers):
        start = wrap(offsets[level, 1, direction] - wind[1, level], screen_cols)
        anchor = jnp.where(sub == level, start, anchor)
        num = jnp.where(sub == level, ratio[level, 0, direction], num)
        den = jnp.where(sub == level, ratio[level, 1, direction], den)
    for at in range(0, base_out.shape[1], LANES):
        pixel = lax.broadcasted_iota(jnp.int32, (8, LANES), 1) + at
        values = spans(pixel, anchor, num, den, screen_cols)
        for out, value in zip((base_out, upper_out, low_out, high_out), values):
            out[:, at : at + LANES] = value
    for load in others:
        load.wait()


def column_weights(base_ref, upper_ref, low_ref, high_ref, first, out):
    layers, cols_dev, pupil_cols = out.shape
    width = cols_dev // 4
    core = lax.rem(lax.axis_index("dir"), 2)
    sub = lax.broadcasted_iota(jnp.int32, (width, LANES), 0).astype(jnp.float32).astype(jnp.bfloat16)
    zero = jnp.zeros((width, LANES), jnp.bfloat16)
    for level in range(layers):

        def tile(step, carry):
            start = pl.multiple_of(step * LANES, LANES)
            cut = (slice(level, level + 1), pl.ds(start, LANES))
            base, upper = base_ref[cut], upper_ref[cut]
            low, high = [
                jnp.broadcast_to(ref[cut].astype(jnp.bfloat16), (width, LANES)) for ref in (low_ref, high_ref)
            ]
            for k in range(4):
                shift = first + chunk_start(jnp.bitwise_xor(core, k // 2), k % 2) * width
                base_at, upper_at = [
                    jnp.broadcast_to(
                        jnp.clip(value - shift, -1, width).astype(jnp.float32).astype(jnp.bfloat16), (width, LANES)
                    )
                    for value in (base, upper)
                ]
                weight = jnp.where(sub == base_at, low, zero)
                weight = jnp.where(sub == upper_at, high, weight)
                out[level, k * width : (k + 1) * width, pl.ds(start, LANES)] = weight
            return carry

        lax.fori_loop(0, pupil_cols // LANES, tile, 0)


def columns_kernel(wind_hbm, *refs):
    tables, blocks, (out, strip, sibling_strip, wind, sem) = refs[:4], refs[4:8], refs[8:]
    load = fetch((wind_hbm, wind, sem))[0]
    column_weights(*tables, lax.axis_index("layer") * out.shape[1], out)
    across, diagonal, near, keep = blocks
    core = lax.rem(lax.axis_index("dir"), 2)
    load.wait()
    strip[...] = outer_strip(wind, core == 1, keep, near, diagonal)
    sibling_strip[...] = outer_strip(wind, core == 0, near, keep, across)


def project_rows(rows_ref, keep, near, across, diagonal, level):
    screen = stack(keep[level], near[level], across[level], diagonal[level])
    rows = stack(rows_ref[0, level], rows_ref[1, level])
    return dot(rows, screen).astype(jnp.bfloat16)


def first_rows_kernel(rows_ref, across, diagonal, near, keep, mine, sibling, other, sibling_other):
    layers, half, _ = mine.shape
    for level in range(layers):
        part = project_rows(rows_ref, keep, near, across, diagonal, level)
        for k, out in enumerate((mine, other, sibling, sibling_other)):
            out[level] = part[k * half : (k + 1) * half]


def outer_strip(wind, odd, own, near, far):
    layers, rows, _ = own.shape
    core = lax.rem(lax.axis_index("dir"), 2)
    lane = lax.broadcasted_iota(jnp.int32, (rows, LANES), 1)
    strip = jnp.zeros((rows, LANES), jnp.float32)
    for level in range(layers):
        edges = [stack(block[level, :16], block[level, rows - 16 :]) for block in (near, far)]
        moved = shifted_rows(wind[0, level], odd, own[level], *edges)
        at = WIND_MAX * level
        moved = pltpu.roll(moved, at + WIND_MAX * core, 1)
        strip = jnp.where((lane >= at) & (lane < at + WIND_MAX), moved, strip)
    return strip.T[:STRIP].astype(jnp.bfloat16)


def put_strip(out, at, strip):
    for k in range(strip.shape[1] // LANES):
        out[at + k * STRIP : at + (k + 1) * STRIP, :] = strip[:, k * LANES : (k + 1) * LANES]


def get_strip(ref, at):
    return beside(*[ref[start : start + STRIP, :] for start in range(at, ref.shape[0], STRIP)])


def later_rows_kernel(rows_ref, *refs):
    chunks, refs = refs[:8], refs[8:]
    sibling0, strip, sibling_strip, mine, give, far, sibling_far, rest, sibling_rest = refs
    across, diagonal, near, keep, across0, diagonal0, near0, keep0 = chunks
    layers, half, width = mine.shape
    rows = near.shape[1]
    size = (far.shape[0] - STRIP * rows // LANES) // layers
    start = half - size
    for out in (rest, sibling_rest):
        left = out.shape[0] - layers * start
        if left:
            out[layers * start :] = jnp.zeros((left, width), jnp.bfloat16)
    for level in range(layers):
        part = project_rows(rows_ref, keep, near, across, diagonal, level)
        mine[level] = part[:half]
        for k, out, remainder in ((1, far, rest), (3, sibling_far, sibling_rest)):
            piece = part[k * half : (k + 1) * half]
            out[level * size : (level + 1) * size] = piece[start:]
            remainder[level * start : (level + 1) * start] = piece[:start]
        give[level, :half, :width] = sibling0[level]
        give[level, :half, width:] = part[2 * half : 3 * half]
        for k, blocks in enumerate(((across0, keep0), (across, keep))):
            cut = slice(k * width, (k + 1) * width)
            edges = [block[level, at : at + 16] for block in blocks for at in (0, rows - 16)]
            give[level, half:, cut] = stack(*edges)
    put_strip(far, layers * size, strip)
    put_strip(sibling_far, layers * size, sibling_strip)


def project(parts, cols_refs, at):
    cols = stack(*[ref[level, start:stop, at : at + 256] for ref, level, start, stop in cols_refs])
    return dot(beside(*parts), cols)


def phase_kernel(*refs):
    tables, refs = refs[:4], refs[4:]
    cols_ref, mine0, mine1, came, sibling_came, phase, cols_out = refs
    first = jnp.bitwise_xor(lax.axis_index("layer"), 1) * cols_out.shape[1]
    column_weights(*tables, first, cols_out)
    layers, _, width = mine0.shape
    parts, cuts = [], []
    for level in range(layers):
        parts += [mine0[level], mine1[level], came[level], sibling_came[level]]
        cuts += [(cols_ref, level, 0, 2 * width)]
        cuts += [(cols_out, level, 0, width), (cols_out, level, 2 * width, 3 * width)]
    for at in range(0, phase.shape[1], 256):
        phase[:, at : at + 256] = project(parts, cuts, at)


def sum_up(start, mine_ref, cols_ref, phase, taken, came, sibling_came, outs):
    layers, _, width = taken.shape
    width = width // 2
    block = outs[0].shape[0]
    size = block * len(outs)
    rows = slice(start, start + size)
    parts, cuts = [], []
    for level in range(layers):
        cut = slice(level * size, (level + 1) * size)
        parts += [taken[level, rows], came[cut], sibling_came[cut]]
        cuts += [(mine_ref, level, 2 * width, 4 * width)]
        cuts += [(cols_ref, level, width, 2 * width), (cols_ref, level, 3 * width, 4 * width)]
    pupil_cols = phase.shape[1]
    for at in range(0, pupil_cols, 256):
        total = (phase[rows, at : at + 256] + project(parts, cuts, at)).astype(jnp.bfloat16)
        for k, out in enumerate(outs):
            out[:, at : at + 256] = total[k * block : (k + 1) * block]


def strip_steps(pairs):
    return [2**k - 1 for k in range(1, pairs.bit_length())]


def send_order(pairs):
    steps = strip_steps(pairs)
    return [k for k in range(pairs) if k not in steps] + steps


def add_strip(pairs, step, strips, out):
    pair = lax.axis_index("layer") // 2
    after = lax.rem(pair + 1, pairs) == jnp.bitwise_xor(pair, step)
    at = out.shape[1] - strips.shape[1]
    last, first = strips[:STRIP].astype(jnp.float32), strips[STRIP:].astype(jnp.float32)
    out[:, at:] = jnp.where(after, last, first).astype(jnp.bfloat16)


def far_kernel(mine_ref, cols_ref, phase, taken, came, sibling_came, *outs):
    *outs, strips = outs
    half = phase.shape[0]
    size = outs[0].shape[0] * len(outs)
    sum_up(half - size, mine_ref, cols_ref, phase, taken, came, sibling_came, outs)
    layers = taken.shape[0]
    odd = lax.rem(lax.axis_index("dir"), 2) == 1
    here = get_strip(came, layers * size).astype(jnp.float32)
    there = get_strip(sibling_came, layers * size).astype(jnp.float32)
    strips[:STRIP] = jnp.where(odd, here, there).astype(jnp.bfloat16)
    strips[STRIP:] = jnp.where(odd, there, here).astype(jnp.bfloat16)
    pairs = half // outs[0].shape[0]
    for out, step in zip(outs, strip_steps(pairs)):
        add_strip(pairs, step, strips, out)


def rest_kernel(mine_ref, cols_ref, phase, taken, came, sibling_came, *outs):
    sum_up(0, mine_ref, cols_ref, phase, taken, came, sibling_came, outs)


def shifted_rows(shift, odd, own, near, far):
    own, near, far = [block.astype(jnp.float32) for block in (own, near, far)]
    rows = own.shape[0]
    before = jnp.where(odd, near[16:], far[16:])
    after = jnp.where(odd, far[:16], near[:16])
    shift = jnp.where(shift < 0, shift + rows + 32, shift)
    return pltpu.roll(stack(before, own, after), shift, 0)[16 : 16 + rows]


def shift_kernel(wind_hbm, own, near0, near1, diagonal0, diagonal1, taken, partner_strips, *refs):
    messages, (out, wind, sem) = refs[:-3], refs[-3:]
    load = fetch((wind_hbm, wind, sem))[0]
    layers, rows, cols = own.shape
    odd = lax.rem(lax.axis_index("dir"), 2) == 1
    half = taken.shape[1] - 64
    pairs = 2 ** len(messages)
    pair, second = lax.axis_index("layer") // 2, lax.rem(lax.axis_index("layer"), 2) == 1
    before = jnp.bitwise_xor(pair, lax.rem(pair + pairs - 1, pairs))
    after = jnp.bitwise_xor(pair, lax.rem(pair + 1, pairs))
    left = partner_strips[:STRIP].astype(jnp.float32)
    right = partner_strips[STRIP:].astype(jnp.float32)
    for step, message in zip(strip_steps(pairs), messages):
        strip = message[:, message.shape[1] - rows :].astype(jnp.float32)
        left = jnp.where(jnp.logical_and(before == step, jnp.logical_not(second)), strip, left)
        right = jnp.where(jnp.logical_and(after == step, second), strip, right)
    strips = stack(left, right, jnp.zeros((LANES - 2 * STRIP, rows), jnp.float32)).T
    lane = lax.broadcasted_iota(jnp.int32, (rows, LANES), 1)
    load.wait()
    for level in range(layers):
        last = pltpu.roll(strips, LANES - WIND_MAX * (level + 1), 1)
        first = pltpu.roll(strips, LANES - STRIP - WIND_MAX * level, 1)
        extra = jnp.where(lane < WIND_MAX, first, last)
        pair = []
        for at, parts in ((half, (diagonal0, diagonal1)), (half + 32, (near0, near1))):
            here = [stack(part[level, :16], part[level, rows - 16 :]).astype(jnp.float32) for part in parts]
            there = taken[level, at : at + 32].astype(jnp.float32)
            width = there.shape[1] // 2
            quarters = [*here, there[:, width:], there[:, :width]]
            pair.append(beside(*[jnp.where(odd, quarters[3 - k], quarters[k]) for k in range(4)]))
        far, near = pair
        moved = shifted_rows(wind[0, level], odd, own[level], near, far)
        shift = wind[1, level]
        shift = jnp.where(shift < 0, shift + cols + LANES, shift)
        out[level] = pltpu.roll(beside(moved, extra), shift, 1)[:, :cols].astype(jnp.bfloat16)


def optics_kernel(amplitude, ones, columns, lines, amp_out, high_out, low_out, lines_out):
    rows, pupil_cols = amplitude.shape
    for step in range(pupil_cols // LANES):
        cut = slice(step * LANES, (step + 1) * LANES)
        amp = amplitude[:, cut]
        energy = (amp * amp).reshape(rows // SUB_PIX, SUB_PIX, LANES).sum(axis=1)
        energy = jnp.broadcast_to(energy[:, None], (rows // SUB_PIX, SUB_PIX, LANES)).reshape(rows, LANES)
        total = jnp.dot(energy, ones[...], precision=lax.Precision.HIGHEST, preferred_element_type=jnp.float32)
        amp_out[:, cut] = amp * lax.rsqrt(total)
    high_out[...], low_out[...] = split(columns[...])
    high, low = split(lines[...])
    lines_out[...] = jnp.concatenate([high, high, low], axis=1)


def sin_cos(phase):
    turns = jnp.floor(phase * (1.0 / np.pi) + 0.5)
    rest = phase - turns * 3.140625
    rest = rest - turns * 9.67653589793e-4
    odd = turns - 2.0 * jnp.floor(turns * 0.5)
    sign = 1.0 - 2.0 * odd
    square = rest * rest
    sine = -1.0 / 39916800.0
    for term in (1.0 / 362880.0, -1.0 / 5040.0, 1.0 / 120.0, -1.0 / 6.0, 1.0):
        sine = sine * square + term
    cosine = 1.0 / 479001600.0
    for term in (-1.0 / 3628800.0, 1.0 / 40320.0, -1.0 / 720.0, 1.0 / 24.0, -0.5, 1.0):
        cosine = cosine * square + term
    return sine * rest * sign, cosine * sign


def split(value):
    high = value.astype(jnp.bfloat16)
    low = (value - high.astype(jnp.float32)).astype(jnp.bfloat16)
    return high, low


def imaging_kernel(count, *refs):
    parts = refs[:count]
    amp_ref, cols_high, cols_low, rows_table, out = refs[count:]
    rows, cols = amp_ref.shape
    tiles = cols // LANES
    phase = parts[0][:, :cols].astype(jnp.float32)
    for part in parts[1:]:
        phase = phase + part[:, :cols].astype(jnp.float32)
    sine, cosine = sin_cos(phase)
    amp = amp_ref[...]
    real, imag = amp * cosine, amp * sine
    field = jnp.concatenate(
        [
            jnp.concatenate(
                [real[:, t * LANES : (t + 1) * LANES], imag[:, t * LANES : (t + 1) * LANES]], axis=1
            )
            for t in range(tiles)
        ],
        axis=0,
    )
    high, low = split(field)
    half = dot(high, cols_high[...]) + (dot(low, cols_high[...]) + dot(high, cols_low[...]))
    wide = 2 * LANES
    out_rows = 2 * rows
    for t in range(tiles):
        mine = half[t * rows : (t + 1) * rows]
        mine = jnp.concatenate([mine[:, :wide], mine[:, wide:]], axis=0)
        high, low = split(mine)
        full = dot(rows_table[...], jnp.concatenate([high, low, high], axis=0))
        real, imag = full[:out_rows], full[out_rows:]
        out[:, t * wide : (t + 1) * wide] = real * real + imag * imag


def tables_of(rows):
    freq = np.arange(SPOT_PIX)[:, None] - SPOT_PIX // 2
    angle = ((freq * np.arange(SUB_PIX)[None, :]) % SPOT_PIX) * (2.0 * np.pi / SPOT_PIX)
    cos, sin = np.cos(angle), np.sin(angle)

    def blocks(table, count):
        return np.kron(np.eye(count), table)

    per_tile = LANES // SUB_PIX
    col_cos, col_sin = blocks(cos.T, per_tile), blocks(sin.T, per_tile)
    columns = np.block([[col_cos, -col_sin], [col_sin, col_cos]])
    count = rows // SUB_PIX
    row_cos, row_sin = blocks(cos, count), blocks(sin, count)
    lines = np.block([[row_cos, row_sin], [-row_sin, row_cos]])

    return columns.astype(np.float32), lines.astype(np.float32)


def per_device(screens, amplitude, wind, offsets, ratio):
    layers, rows_dev, cols_dev = screens.shape
    n_layer = lax.axis_size("layer")
    n_dir = lax.axis_size("dir")
    rows, pupil_cols = amplitude.shape
    pairs = n_layer // 2
    half = pairs * rows
    pupil_rows = 2 * half
    assert n_dir == 4 and rows == STRIP and pairs > 2
    bf16, f32 = jnp.bfloat16, jnp.float32
    wind = jnp.transpose(wind, (1, 0))
    offsets = jnp.transpose(offsets, (1, 2, 0))
    ratio = jnp.transpose(ratio, (1, 2, 0))
    smem, sem = pltpu.SMEM, pltpu.SemaphoreType.DMA
    wind_scratch = [smem(wind.shape, jnp.int32), sem]

    def shape(*dims, dtype=bf16):
        return jax.ShapeDtypeStruct(dims, dtype)

    def swap(value, bits):
        return lax.ppermute(value, "dir", [(i, i ^ bits) for i in range(n_dir)])

    def partner(value, bits=0):
        count = n_layer * n_dir
        return lax.ppermute(value, ("layer", "dir"), [(i, i ^ n_dir ^ bits) for i in range(count)])

    def turn(value, step):
        return lax.ppermute(value, "layer", [(i, (i + step) % n_layer) for i in range(n_layer)])

    width = cols_dev // 4
    chunk = shape(layers, rows_dev, width)
    keep0, keep1, give0, give1 = call(
        split_kernel,
        [chunk] * 4,
        (screens,),
        0,
        "split",
        in_hbm=(0,),
        scratch=[sem((4,))],
        brief=True,
    )
    across0 = swap(keep0, 2)
    diagonal0 = swap(give0, 3)
    near0 = swap(give0, 1)
    across1 = swap(keep1, 2)
    diagonal1 = swap(give1, 3)
    ones = np.kron(np.eye(LANES // SUB_PIX), np.ones((SUB_PIX, SUB_PIX))).astype(np.float32)
    optics_in = (amplitude, jnp.asarray(ones), *[jnp.asarray(table) for table in tables_of(rows)])
    copies = [shape(*array.shape, dtype=array.dtype) for array in (screens, *optics_in)]
    row_weights, *tables = call(
        functools.partial(weights_kernel, (n_layer, rows_dev, cols_dev * n_layer)),
        [shape(2, layers, pupil_rows, 4 * rows_dev)]
        + [shape(8, pupil_cols, dtype=dtype) for dtype in (jnp.int32, jnp.int32, f32, f32)]
        + copies,
        (wind, offsets, ratio, screens, *optics_in),
        0,
        "weights",
        in_hbm=range(3, 8),
        scratch=[smem(array.shape, jnp.int32) for array in (wind, offsets, ratio)] + [sem((8,))],
        brief=True,
    )
    tables, own, optics_in = tables[:4], tables[4], tables[5:]
    give1, own = lax.optimization_barrier((give1, own))
    near1 = swap(give1, 1)
    tables = tuple(tables)
    across0, diagonal0, row_weights, tables = lax.optimization_barrier((across0, diagonal0, row_weights, tables))

    projected = shape(layers, half, width)
    mine0, sibling0, other0, sibling_other0 = call(
        first_rows_kernel,
        [projected] * 4,
        (row_weights, across0, diagonal0, near0, keep0),
        0,
        "rows_first",
        brief=True,
    )
    came0 = partner(other0)
    sibling_came0 = partner(sibling_other0, 1)

    tables, mine0 = lax.optimization_barrier((tables, mine0))
    cols, strip, sibling_strip = call(
        columns_kernel,
        [shape(layers, cols_dev, pupil_cols), shape(STRIP, rows_dev), shape(STRIP, rows_dev)],
        (wind, *tables, across0, diagonal0, near0, keep0),
        0,
        "columns",
        scratch=wind_scratch,
        brief=True,
    )
    steps = strip_steps(pairs)
    far = len(steps) * rows
    message = shape(layers * far + STRIP * rows_dev // LANES, width)
    remainder = shape(max(layers * (half - far), message.shape[0] + 16), width)
    mine1, give, far1, sibling_far1, rest1, sibling_rest1 = call(
        later_rows_kernel,
        [projected, shape(layers, half + 64, 2 * width), message, message, remainder, remainder],
        (row_weights, across1, diagonal1, near1, keep1, across0, diagonal0, near0, keep0, sibling0, strip, sibling_strip),
        0,
        "rows_later",
        brief=True,
    )
    far1, sibling_far1 = partner(far1), partner(sibling_far1, 1)
    rest1, sibling_rest1 = partner(rest1), partner(sibling_rest1, 1)
    taken = swap(give, 1)
    phase, others = call(
        phase_kernel,
        (shape(half, pupil_cols, dtype=f32), shape(layers, cols_dev, pupil_cols)),
        (*tables, cols, mine0, mine1, came0, sibling_came0),
        10_000_000_000,
        "phase",
    )

    *far_sums, strips = call(
        far_kernel,
        [shape(rows, pupil_cols + rows_dev)] * len(steps) + [shape(2 * STRIP, rows_dev)],
        (cols, others, phase, taken, far1, sibling_far1),
        300_000_000,
        "far",
    )
    rest_sums = call(
        rest_kernel,
        [shape(rows, pupil_cols)] * (pairs - len(steps)),
        (cols, others, phase, taken, rest1, sibling_rest1),
        0,
        "rest",
        brief=True,
    )
    received = dict(zip(send_order(pairs), [*rest_sums, *far_sums]))
    for k in range(1, pairs):
        received[k] = lax.ppermute(received[k], "layer", [(i, i ^ (2 * k)) for i in range(n_layer)])
    received = [received[k] for k in range(pairs)]

    optics_in, received[-1] = lax.optimization_barrier((optics_in, received[-1]))
    optics = call(
        optics_kernel,
        (
            shape(rows, pupil_cols, dtype=f32),
            shape(*optics_in[2].shape),
            shape(*optics_in[2].shape),
            shape(optics_in[3].shape[0], 3 * optics_in[3].shape[1]),
        ),
        optics_in,
        0,
        "optics",
        brief=True,
    )
    received[1], optics = lax.optimization_barrier((received[1], optics))
    new_screens = call(
        shift_kernel,
        shape(layers, rows_dev, cols_dev),
        (wind, own, near0, near1, diagonal0, diagonal1, taken, strips, *[received[k] for k in steps]),
        0,
        "shift",
        scratch=wind_scratch,
        brief=True,
    )
    spots = call(
        functools.partial(imaging_kernel, pairs),
        shape(2 * rows, 2 * pupil_cols, dtype=f32),
        (*received, *optics),
        400_000_000,
        "imaging",
    )
    return (new_screens, spots[None])


def solution(mesh):
    return jax.shard_map(
        per_device,
        mesh=mesh,
        in_specs=(P(None, "dir", "layer"), P("layer", None), P(), P(), P()),
        out_specs=(P(None, "dir", "layer"), P("dir", "layer", None)),
        check_vma=False,
    )
```

```python
import functools

import jax
import jax.numpy as jnp
import numpy as np
from jax import lax
from jax.experimental import pallas as pl
from jax.experimental.pallas import tpu as pltpu
from jax.sharding import PartitionSpec as P

SUB_PIX = 16
SPOT_PIX = 32
WIND_MAX = 8
LANES = 128
STRIP = 32

HBM_SPEC = pl.BlockSpec(memory_space=pltpu.HBM)
VMEM_SPEC = pl.BlockSpec(memory_space=pltpu.VMEM)


def params(*arrays):
    held = sum(array.size * array.dtype.itemsize for array in jax.tree.leaves(arrays))
    return pltpu.CompilerParams(vmem_limit_bytes=held + 8 * 1024 * 1024)


def call(kernel, out_shape, operands, flops, name, in_hbm=(), out_hbm=(), scratch=(), brief=False):
    def spec(k, array):
        return HBM_SPEC if k in in_hbm else VMEM_SPEC

    if out_hbm:
        out_specs = [HBM_SPEC if k in out_hbm else VMEM_SPEC for k in range(len(out_shape))]
    else:
        out_specs = jax.tree.map(lambda _: VMEM_SPEC, out_shape)
    size = sum(array.size * array.dtype.itemsize for array in jax.tree.leaves((operands, out_shape)))
    if brief:
        flops = size = 0
    in_specs = [spec(k, array) for k, array in enumerate(operands)]
    operands = [
        pltpu.with_memory_space_constraint(array, pltpu.HBM) if space is HBM_SPEC else array
        for array, space in zip(operands, in_specs)
    ]
    return pl.pallas_call(
        kernel,
        out_shape=out_shape,
        in_specs=in_specs,
        out_specs=out_specs,
        scratch_shapes=list(scratch),
        compiler_params=params(operands, out_shape),
        cost_estimate=pl.CostEstimate(flops=flops, bytes_accessed=size, transcendentals=0),
        name=name,
    )(*operands)


def fetch(*pairs):
    copies = [pltpu.make_async_copy(source, target, sem) for source, target, sem in pairs]
    for copy in copies:
        copy.start()
    return copies


def wrap(value, length):
    value = jnp.where(value < 0, value + length, value)
    return jnp.where(value >= length, value - length, value)


def stack(*blocks):
    return jnp.concatenate(blocks, axis=0)


def beside(*blocks):
    return jnp.concatenate(blocks, axis=1)


def dot(left, right):
    return jnp.dot(left, right, preferred_element_type=jnp.float32)


def spans(pixel, anchor, num, den, length):
    stretched = (pixel * num).astype(jnp.float32)
    den = (jnp.zeros_like(pixel) + den).astype(jnp.float32)
    whole = jnp.floor((stretched + 0.5) / den)
    fraction = (stretched - whole * den) / den
    base = wrap(anchor + whole.astype(jnp.int32), length)
    upper = wrap(base + 1, length)
    return base, upper, 1.0 - fraction, fraction


def chunk_start(half, chunk):
    return 3 * half + chunk * (1 - 2 * half)


def split_kernel(screens, *refs):
    outs, sems = refs[:-1], refs[-1]
    width = outs[0].shape[2]
    core = lax.rem(lax.axis_index("dir"), 2)
    pairs = []
    for k, out in enumerate(outs):
        half = core if k < 2 else 1 - core
        start = pl.multiple_of(chunk_start(half, k % 2) * width, LANES)
        pairs.append((screens.at[:, :, pl.ds(start, width)], out, sems.at[k]))
    for load in fetch(*pairs):
        load.wait()


def weights_kernel(geometry, wind_hbm, offsets_hbm, ratio_hbm, *refs):
    n_layer, rows_dev, screen_cols = geometry
    sources, (rows_out, base_out, upper_out, low_out, high_out), refs = refs[:5], refs[5:10], refs[10:]
    copies, (wind_copy, wind, offsets, ratio, sems) = refs[:5], refs[5:]
    pairs = [*zip(sources, copies), (wind_hbm, wind_copy)]
    others = fetch(*[(source, copy, sems.at[3 + k]) for k, (source, copy) in enumerate(pairs)])
    loads = fetch(
        (wind_hbm, wind, sems.at[0]),
        (offsets_hbm, offsets, sems.at[1]),
        (ratio_hbm, ratio, sems.at[2]),
    )
    _, layers, pupil_rows, screen_rows = rows_out.shape
    half = pupil_rows // 2
    direction = lax.axis_index("dir")
    column = lax.axis_index("layer")
    block = pupil_rows // n_layer
    row = lax.broadcasted_iota(jnp.int32, (half, LANES), 0)
    step = row // block
    for at, value in enumerate(send_order(n_layer // 2)):
        step = jnp.where(row // block == at, value, step)
    pair = jnp.bitwise_xor(step, column // 2)
    parity = lax.rem(column, 2)
    inside = lax.rem(row, block) + pair * (2 * block)
    pixel_rows = stack(inside + parity * block, inside + (1 - parity) * block)
    lane = lax.broadcasted_iota(jnp.int32, (pupil_rows, LANES), 1)
    for load in loads:
        load.wait()
    for side in range(2):
        target = jnp.bitwise_xor(direction, side)
        for level in range(layers):
            anchor = wrap(offsets[level, 0, target] - wind[0, level], screen_rows)
            num, den = ratio[level, 0, target], ratio[level, 1, target]
            base, upper, low, high = spans(pixel_rows, anchor, num, den, screen_rows)
            for peer in range(4):
                for part in range(rows_dev // LANES):
                    index = lane + (jnp.bitwise_xor(direction, peer) * rows_dev + part * LANES)
                    weight = jnp.where(index == base, low, 0.0)
                    weight = jnp.where(index == upper, high, weight)
                    start = peer * rows_dev + part * LANES
                    rows_out[side, level, :, start : start + LANES] = weight.astype(jnp.bfloat16)
    sub = lax.broadcasted_iota(jnp.int32, (8, LANES), 0)
    anchor, num, den = jnp.zeros_like(sub), jnp.zeros_like(sub), jnp.ones_like(sub)
    for level in range(layers):
        start = wrap(offsets[level, 1, direction] - wind[1, level], screen_cols)
        anchor = jnp.where(sub == level, start, anchor)
        num = jnp.where(sub == level, ratio[level, 0, direction], num)
        den = jnp.where(sub == level, ratio[level, 1, direction], den)
    for at in range(0, base_out.shape[1], LANES):
        pixel = lax.broadcasted_iota(jnp.int32, (8, LANES), 1) + at
        values = spans(pixel, anchor, num, den, screen_cols)
        for out, value in zip((base_out, upper_out, low_out, high_out), values):
            out[:, at : at + LANES] = value
    for load in others:
        load.wait()


def column_weights(base_ref, upper_ref, low_ref, high_ref, first, out):
    layers, cols_dev, pupil_cols = out.shape
    width = cols_dev // 4
    core = lax.rem(lax.axis_index("dir"), 2)
    sub = lax.broadcasted_iota(jnp.int32, (width, LANES), 0).astype(jnp.float32).astype(jnp.bfloat16)
    zero = jnp.zeros((width, LANES), jnp.bfloat16)
    for level in range(layers):

        def tile(step, carry):
            start = pl.multiple_of(step * LANES, LANES)
            cut = (slice(level, level + 1), pl.ds(start, LANES))
            base, upper = base_ref[cut], upper_ref[cut]
            low, high = [
                jnp.broadcast_to(ref[cut].astype(jnp.bfloat16), (width, LANES)) for ref in (low_ref, high_ref)
            ]
            for k in range(4):
                shift = first + chunk_start(jnp.bitwise_xor(core, k // 2), k % 2) * width
                base_at, upper_at = [
                    jnp.broadcast_to(
                        jnp.clip(value - shift, -1, width).astype(jnp.float32).astype(jnp.bfloat16), (width, LANES)
                    )
                    for value in (base, upper)
                ]
                weight = jnp.where(sub == base_at, low, zero)
                weight = jnp.where(sub == upper_at, high, weight)
                out[level, k * width : (k + 1) * width, pl.ds(start, LANES)] = weight
            return carry

        lax.fori_loop(0, pupil_cols // LANES, tile, 0)


def columns_kernel(wind_held, *refs):
    tables, blocks, (out, strip, sibling_strip, wind, sem) = refs[:4], refs[4:8], refs[8:]
    load = fetch((wind_held, wind, sem))[0]
    column_weights(*tables, lax.axis_index("layer") * out.shape[1], out)
    across, diagonal, near, keep = blocks
    core = lax.rem(lax.axis_index("dir"), 2)
    load.wait()
    strip[...] = outer_strip(wind, core == 1, keep, near, diagonal)
    sibling_strip[...] = outer_strip(wind, core == 0, near, keep, across)


def project_rows(rows_ref, keep, near, across, diagonal, level):
    screen = stack(keep[level], near[level], across[level], diagonal[level])
    rows = stack(rows_ref[0, level], rows_ref[1, level])
    return dot(rows, screen).astype(jnp.bfloat16)


def first_rows_kernel(rows_ref, across, diagonal, near, keep, mine, sibling, other, sibling_other):
    layers, half, _ = mine.shape
    for level in range(layers):
        part = project_rows(rows_ref, keep, near, across, diagonal, level)
        for k, out in enumerate((mine, other, sibling, sibling_other)):
            out[level] = part[k * half : (k + 1) * half]


def outer_strip(wind, odd, own, near, far):
    layers, rows, _ = own.shape
    core = lax.rem(lax.axis_index("dir"), 2)
    lane = lax.broadcasted_iota(jnp.int32, (rows, LANES), 1)
    strip = jnp.zeros((rows, LANES), jnp.float32)
    for level in range(layers):
        edges = [stack(block[level, :16], block[level, rows - 16 :]) for block in (near, far)]
        moved = shifted_rows(wind[0, level], odd, own[level], *edges)
        at = WIND_MAX * level
        moved = pltpu.roll(moved, at + WIND_MAX * core, 1)
        strip = jnp.where((lane >= at) & (lane < at + WIND_MAX), moved, strip)
    return strip.T[:STRIP].astype(jnp.bfloat16)


def put_strip(out, at, strip):
    for k in range(strip.shape[1] // LANES):
        out[at + k * STRIP : at + (k + 1) * STRIP, :] = strip[:, k * LANES : (k + 1) * LANES]


def get_strip(ref, at):
    return beside(*[ref[start : start + STRIP, :] for start in range(at, ref.shape[0], STRIP)])


def later_rows_kernel(rows_ref, *refs):
    chunks, refs = refs[:8], refs[8:]
    sibling0, strip, sibling_strip, mine, give, far, sibling_far, rest, sibling_rest = refs
    across, diagonal, near, keep, across0, diagonal0, near0, keep0 = chunks
    layers, half, width = mine.shape
    rows = near.shape[1]
    size = (far.shape[0] - STRIP * rows // LANES) // layers
    start = half - size
    for out in (rest, sibling_rest):
        left = out.shape[0] - layers * start
        if left:
            out[layers * start :] = jnp.zeros((left, width), jnp.bfloat16)
    for level in range(layers):
        part = project_rows(rows_ref, keep, near, across, diagonal, level)
        mine[level] = part[:half]
        for k, out, remainder in ((1, far, rest), (3, sibling_far, sibling_rest)):
            piece = part[k * half : (k + 1) * half]
            out[level * size : (level + 1) * size] = piece[start:]
            remainder[level * start : (level + 1) * start] = piece[:start]
        give[level, :half, :width] = sibling0[level]
        give[level, :half, width:] = part[2 * half : 3 * half]
        for k, blocks in enumerate(((across0, keep0), (across, keep))):
            cut = slice(k * width, (k + 1) * width)
            edges = [block[level, at : at + 16] for block in blocks for at in (0, rows - 16)]
            give[level, half:, cut] = stack(*edges)
    put_strip(far, layers * size, strip)
    put_strip(sibling_far, layers * size, sibling_strip)


def project(parts, cols_refs, at):
    cols = stack(*[ref[level, start:stop, at : at + 256] for ref, level, start, stop in cols_refs])
    return dot(beside(*parts), cols)


def phase_kernel(*refs):
    tables, refs = refs[:4], refs[4:]
    cols_ref, mine0, mine1, came, sibling_came, phase, cols_out = refs
    first = jnp.bitwise_xor(lax.axis_index("layer"), 1) * cols_out.shape[1]
    column_weights(*tables, first, cols_out)
    layers, _, width = mine0.shape
    parts, cuts = [], []
    for level in range(layers):
        parts += [mine0[level], mine1[level], came[level], sibling_came[level]]
        cuts += [(cols_ref, level, 0, 2 * width)]
        cuts += [(cols_out, level, 0, width), (cols_out, level, 2 * width, 3 * width)]
    for at in range(0, phase.shape[1], 256):
        phase[:, at : at + 256] = project(parts, cuts, at)


def sum_up(start, mine_ref, cols_ref, phase, taken, came, sibling_came, outs):
    layers, _, width = taken.shape
    width = width // 2
    block = outs[0].shape[0]
    size = block * len(outs)
    rows = slice(start, start + size)
    parts, cuts = [], []
    for level in range(layers):
        cut = slice(level * size, (level + 1) * size)
        parts += [taken[level, rows], came[cut], sibling_came[cut]]
        cuts += [(mine_ref, level, 2 * width, 4 * width)]
        cuts += [(cols_ref, level, width, 2 * width), (cols_ref, level, 3 * width, 4 * width)]
    pupil_cols = phase.shape[1]
    for at in range(0, pupil_cols, 256):
        total = (phase[rows, at : at + 256] + project(parts, cuts, at)).astype(jnp.bfloat16)
        for k, out in enumerate(outs):
            out[:, at : at + 256] = total[k * block : (k + 1) * block]


def strip_steps(pairs):
    return [2**k - 1 for k in range(1, pairs.bit_length())]


def send_order(pairs):
    steps = strip_steps(pairs)
    return [k for k in range(pairs) if k not in steps] + steps


def add_strip(pairs, step, strips, out):
    pair = lax.axis_index("layer") // 2
    after = lax.rem(pair + 1, pairs) == jnp.bitwise_xor(pair, step)
    at = out.shape[1] - strips.shape[1]
    last, first = strips[:STRIP].astype(jnp.float32), strips[STRIP:].astype(jnp.float32)
    out[:, at:] = jnp.where(after, last, first).astype(jnp.bfloat16)


def far_kernel(mine_ref, cols_ref, phase, taken, came, sibling_came, *outs):
    *outs, strips = outs
    half = phase.shape[0]
    size = outs[0].shape[0] * len(outs)
    sum_up(half - size, mine_ref, cols_ref, phase, taken, came, sibling_came, outs)
    layers = taken.shape[0]
    odd = lax.rem(lax.axis_index("dir"), 2) == 1
    here = get_strip(came, layers * size).astype(jnp.float32)
    there = get_strip(sibling_came, layers * size).astype(jnp.float32)
    strips[:STRIP] = jnp.where(odd, here, there).astype(jnp.bfloat16)
    strips[STRIP:] = jnp.where(odd, there, here).astype(jnp.bfloat16)
    pairs = half // outs[0].shape[0]
    for out, step in zip(outs, strip_steps(pairs)):
        add_strip(pairs, step, strips, out)


def rest_kernel(mine_ref, cols_ref, phase, taken, came, sibling_came, *outs):
    sum_up(0, mine_ref, cols_ref, phase, taken, came, sibling_came, outs)


def shifted_rows(shift, odd, own, near, far):
    own, near, far = [block.astype(jnp.float32) for block in (own, near, far)]
    rows = own.shape[0]
    before = jnp.where(odd, near[16:], far[16:])
    after = jnp.where(odd, far[:16], near[:16])
    shift = jnp.where(shift < 0, shift + rows + 32, shift)
    return pltpu.roll(stack(before, own, after), shift, 0)[16 : 16 + rows]


def shift_kernel(wind_held, own, near0, near1, diagonal0, diagonal1, taken, partner_strips, *refs):
    messages, (out, wind, sem) = refs[:-3], refs[-3:]
    load = fetch((wind_held, wind, sem))[0]
    layers, rows, cols = own.shape
    odd = lax.rem(lax.axis_index("dir"), 2) == 1
    half = taken.shape[1] - 64
    pairs = 2 ** len(messages)
    pair, second = lax.axis_index("layer") // 2, lax.rem(lax.axis_index("layer"), 2) == 1
    before = jnp.bitwise_xor(pair, lax.rem(pair + pairs - 1, pairs))
    after = jnp.bitwise_xor(pair, lax.rem(pair + 1, pairs))
    left = partner_strips[:STRIP].astype(jnp.float32)
    right = partner_strips[STRIP:].astype(jnp.float32)
    for step, message in zip(strip_steps(pairs), messages):
        strip = message[:, message.shape[1] - rows :].astype(jnp.float32)
        left = jnp.where(jnp.logical_and(before == step, jnp.logical_not(second)), strip, left)
        right = jnp.where(jnp.logical_and(after == step, second), strip, right)
    strips = stack(left, right, jnp.zeros((LANES - 2 * STRIP, rows), jnp.float32)).T
    lane = lax.broadcasted_iota(jnp.int32, (rows, LANES), 1)
    load.wait()
    for level in range(layers):
        last = pltpu.roll(strips, LANES - WIND_MAX * (level + 1), 1)
        first = pltpu.roll(strips, LANES - STRIP - WIND_MAX * level, 1)
        extra = jnp.where(lane < WIND_MAX, first, last)
        pair = []
        for at, parts in ((half, (diagonal0, diagonal1)), (half + 32, (near0, near1))):
            here = [stack(part[level, :16], part[level, rows - 16 :]).astype(jnp.float32) for part in parts]
            there = taken[level, at : at + 32].astype(jnp.float32)
            width = there.shape[1] // 2
            quarters = [*here, there[:, width:], there[:, :width]]
            pair.append(beside(*[jnp.where(odd, quarters[3 - k], quarters[k]) for k in range(4)]))
        far, near = pair
        moved = shifted_rows(wind[0, level], odd, own[level], near, far)
        shift = wind[1, level]
        shift = jnp.where(shift < 0, shift + cols + LANES, shift)
        out[level] = pltpu.roll(beside(moved, extra), shift, 1)[:, :cols].astype(jnp.bfloat16)


def optics_kernel(amplitude, ones, columns, lines, amp_out, columns_out, lines_out):
    rows, pupil_cols = amplitude.shape
    for step in range(pupil_cols // LANES):
        cut = slice(step * LANES, (step + 1) * LANES)
        amp = amplitude[:, cut]
        energy = (amp * amp).reshape(rows // SUB_PIX, SUB_PIX, LANES).sum(axis=1)
        energy = jnp.broadcast_to(energy[:, None], (rows // SUB_PIX, SUB_PIX, LANES)).reshape(rows, LANES)
        total = jnp.dot(energy, ones[...], precision=lax.Precision.HIGHEST, preferred_element_type=jnp.float32)
        amp_out[:, cut] = amp * lax.rsqrt(total)
    columns_out[...] = columns[...].astype(jnp.bfloat16)
    lines_out[...] = lines[...].astype(jnp.bfloat16)


def sin_cos(phase):
    turns = jnp.floor(phase * (1.0 / np.pi) + 0.5)
    rest = phase - turns * 3.140625
    rest = rest - turns * 9.67653589793e-4
    odd = turns - 2.0 * jnp.floor(turns * 0.5)
    sign = 1.0 - 2.0 * odd
    square = rest * rest
    sine = -1.0 / 39916800.0
    for term in (1.0 / 362880.0, -1.0 / 5040.0, 1.0 / 120.0, -1.0 / 6.0, 1.0):
        sine = sine * square + term
    cosine = 1.0 / 479001600.0
    for term in (-1.0 / 3628800.0, 1.0 / 40320.0, -1.0 / 720.0, 1.0 / 24.0, -0.5, 1.0):
        cosine = cosine * square + term
    return sine * rest * sign, cosine * sign


def imaging_kernel(count, *refs):
    parts, (amp_ref, columns, lines, shifted, spots, screens, out, sems) = refs[:count], refs[count:]
    copies = fetch((shifted, screens, sems.at[0]))
    rows, cols = amp_ref.shape
    tiles = cols // LANES
    phase = parts[0][:, :cols].astype(jnp.float32)
    for part in parts[1:]:
        phase = phase + part[:, :cols].astype(jnp.float32)
    sine, cosine = sin_cos(phase)
    amp = amp_ref[...]
    real, imag = (amp * cosine).astype(jnp.bfloat16), (amp * sine).astype(jnp.bfloat16)
    cuts = [slice(t * LANES, (t + 1) * LANES) for t in range(tiles)]
    field = stack(*[beside(real[:, cut], imag[:, cut]) for cut in cuts])
    half = dot(field, columns[...]).astype(jnp.bfloat16)
    wide = 2 * LANES
    out_rows = 2 * rows
    for t in range(tiles):
        mine = half[t * rows : (t + 1) * rows]
        full = dot(lines[...], stack(mine[:, :wide], mine[:, wide:]))
        real, imag = full[:out_rows], full[out_rows:]
        out[:, t * wide : (t + 1) * wide] = real * real + imag * imag
        if t % 2:
            cut = slice((t - 1) * wide, (t + 1) * wide)
            copies += fetch((out.at[:, cut], spots.at[:, cut], sems.at[1 + t // 2]))
    for copy in copies:
        copy.wait()


def tables_of(rows):
    freq = np.arange(SPOT_PIX)[:, None] - SPOT_PIX // 2
    angle = ((freq * np.arange(SUB_PIX)[None, :]) % SPOT_PIX) * (2.0 * np.pi / SPOT_PIX)
    cos, sin = np.cos(angle), np.sin(angle)

    def blocks(table, count):
        return np.kron(np.eye(count), table)

    per_tile = LANES // SUB_PIX
    col_cos, col_sin = blocks(cos.T, per_tile), blocks(sin.T, per_tile)
    columns = np.block([[col_cos, -col_sin], [col_sin, col_cos]])
    count = rows // SUB_PIX
    row_cos, row_sin = blocks(cos, count), blocks(sin, count)
    lines = np.block([[row_cos, row_sin], [-row_sin, row_cos]])

    return columns.astype(np.float32), lines.astype(np.float32)


def per_device(screens, amplitude, wind, offsets, ratio):
    layers, rows_dev, cols_dev = screens.shape
    n_layer = lax.axis_size("layer")
    n_dir = lax.axis_size("dir")
    rows, pupil_cols = amplitude.shape
    pairs = n_layer // 2
    half = pairs * rows
    pupil_rows = 2 * half
    assert n_dir == 4 and rows == STRIP and pairs > 2
    bf16, f32 = jnp.bfloat16, jnp.float32
    wind = jnp.transpose(wind, (1, 0))
    offsets = jnp.transpose(offsets, (1, 2, 0))
    ratio = jnp.transpose(ratio, (1, 2, 0))
    smem, sem = pltpu.SMEM, pltpu.SemaphoreType.DMA
    wind_scratch = [smem(wind.shape, jnp.int32), sem]

    def shape(*dims, dtype=bf16):
        return jax.ShapeDtypeStruct(dims, dtype)

    def swap(value, bits):
        return lax.ppermute(value, "dir", [(i, i ^ bits) for i in range(n_dir)])

    def partner(value, bits=0):
        count = n_layer * n_dir
        return lax.ppermute(value, ("layer", "dir"), [(i, i ^ n_dir ^ bits) for i in range(count)])

    def turn(value, step):
        return lax.ppermute(value, "layer", [(i, (i + step) % n_layer) for i in range(n_layer)])

    width = cols_dev // 4
    chunk = shape(layers, rows_dev, width)
    keep0, keep1, give0, give1 = call(
        split_kernel,
        [chunk] * 4,
        (screens,),
        0,
        "split",
        in_hbm=(0,),
        scratch=[sem((4,))],
        brief=True,
    )
    across0 = swap(keep0, 2)
    diagonal0 = swap(give0, 3)
    near0 = swap(give0, 1)
    across1 = swap(keep1, 2)
    diagonal1 = swap(give1, 3)
    ones = np.kron(np.eye(LANES // SUB_PIX), np.ones((SUB_PIX, SUB_PIX))).astype(np.float32)
    optics_in = (amplitude, jnp.asarray(ones), *[jnp.asarray(table) for table in tables_of(rows)])
    copies = [shape(*array.shape, dtype=array.dtype) for array in (screens, *optics_in, wind)]
    row_weights, *tables = call(
        functools.partial(weights_kernel, (n_layer, rows_dev, cols_dev * n_layer)),
        [shape(2, layers, pupil_rows, 4 * rows_dev)]
        + [shape(8, pupil_cols, dtype=dtype) for dtype in (jnp.int32, jnp.int32, f32, f32)]
        + copies,
        (wind, offsets, ratio, screens, *optics_in),
        0,
        "weights",
        in_hbm=range(8),
        scratch=[smem(array.shape, jnp.int32) for array in (wind, offsets, ratio)] + [sem((9,))],
        brief=True,
    )
    tables, own, optics_in, wind = tables[:4], tables[4], tables[5:-1], tables[-1]
    give1, own = lax.optimization_barrier((give1, own))
    near1 = swap(give1, 1)
    tables = tuple(tables)
    across0, diagonal0, row_weights, tables = lax.optimization_barrier((across0, diagonal0, row_weights, tables))

    projected = shape(layers, half, width)
    mine0, sibling0, other0, sibling_other0 = call(
        first_rows_kernel,
        [projected] * 4,
        (row_weights, across0, diagonal0, near0, keep0),
        0,
        "rows_first",
        brief=True,
    )
    came0 = partner(other0)
    sibling_came0 = partner(sibling_other0, 1)

    tables, mine0 = lax.optimization_barrier((tables, mine0))
    cols, strip, sibling_strip = call(
        columns_kernel,
        [shape(layers, cols_dev, pupil_cols), shape(STRIP, rows_dev), shape(STRIP, rows_dev)],
        (wind, *tables, across0, diagonal0, near0, keep0),
        0,
        "columns",
        scratch=wind_scratch,
        brief=True,
    )
    steps = strip_steps(pairs)
    far = len(steps) * rows
    message = shape(layers * far + STRIP * rows_dev // LANES, width)
    remainder = shape(max(layers * (half - far), message.shape[0] + 16), width)
    mine1, give, far1, sibling_far1, rest1, sibling_rest1 = call(
        later_rows_kernel,
        [projected, shape(layers, half + 64, 2 * width), message, message, remainder, remainder],
        (row_weights, across1, diagonal1, near1, keep1, across0, diagonal0, near0, keep0, sibling0, strip, sibling_strip),
        0,
        "rows_later",
        brief=True,
    )
    far1, sibling_far1 = partner(far1), partner(sibling_far1, 1)
    rest1, sibling_rest1 = partner(rest1), partner(sibling_rest1, 1)
    taken = swap(give, 1)
    phase, others = call(
        phase_kernel,
        (shape(half, pupil_cols, dtype=f32), shape(layers, cols_dev, pupil_cols)),
        (*tables, cols, mine0, mine1, came0, sibling_came0),
        10_000_000_000,
        "phase",
    )

    *far_sums, strips = call(
        far_kernel,
        [shape(rows, pupil_cols + rows_dev)] * len(steps) + [shape(2 * STRIP, rows_dev)],
        (cols, others, phase, taken, far1, sibling_far1),
        300_000_000,
        "far",
    )
    rest_sums = call(
        rest_kernel,
        [shape(rows, pupil_cols)] * (pairs - len(steps)),
        (cols, others, phase, taken, rest1, sibling_rest1),
        0,
        "rest",
        brief=True,
    )
    received = dict(zip(send_order(pairs), [*rest_sums, *far_sums]))
    for k in range(1, pairs):
        received[k] = lax.ppermute(received[k], "layer", [(i, i ^ (2 * k)) for i in range(n_layer)])
    received = [received[k] for k in range(pairs)]

    optics_in, received[-1] = lax.optimization_barrier((optics_in, received[-1]))
    optics = call(
        optics_kernel,
        (
            shape(rows, pupil_cols, dtype=f32),
            shape(*optics_in[2].shape),
            shape(*optics_in[3].shape),
        ),
        optics_in,
        0,
        "optics",
        brief=True,
    )
    received[1], optics = lax.optimization_barrier((received[1], optics))
    shifted = call(
        shift_kernel,
        shape(layers, rows_dev, cols_dev),
        (wind, own, near0, near1, diagonal0, diagonal1, taken, strips, *[received[k] for k in steps]),
        0,
        "shift",
        scratch=wind_scratch,
        brief=True,
    )
    spots_shape = shape(2 * rows, 2 * pupil_cols, dtype=f32)
    spots, new_screens = call(
        functools.partial(imaging_kernel, pairs),
        [spots_shape, shape(layers, rows_dev, cols_dev)],
        (*received, *optics, shifted),
        400_000_000,
        "imaging",
        out_hbm=(0, 1),
        scratch=[pltpu.VMEM(spots_shape.shape, f32), sem((1 + pupil_cols // (2 * LANES),))],
    )
    return (new_screens, spots[None])


def solution(mesh):
    return jax.shard_map(
        per_device,
        mesh=mesh,
        in_specs=(P(None, "dir", "layer"), P("layer", None), P(), P(), P()),
        out_specs=(P(None, "dir", "layer"), P("dir", "layer", None)),
        check_vma=False,
    )
```

```python
import functools

import jax
import jax.numpy as jnp
import numpy as np
from jax import lax
from jax.experimental import pallas as pl
from jax.experimental.pallas import tpu as pltpu
from jax.sharding import PartitionSpec as P

SUB_PIX = 16
SPOT_PIX = 32
WIND_MAX = 8
LANES = 128
STRIP = 32

HBM_SPEC = pl.BlockSpec(memory_space=pltpu.HBM)
VMEM_SPEC = pl.BlockSpec(memory_space=pltpu.VMEM)


def params(*arrays):
    held = sum(array.size * array.dtype.itemsize for array in jax.tree.leaves(arrays))
    return pltpu.CompilerParams(vmem_limit_bytes=held + 8 * 1024 * 1024)


def call(kernel, out_shape, operands, flops, name, in_hbm=(), out_hbm=(), scratch=(), brief=False):
    def spec(k, array):
        return HBM_SPEC if k in in_hbm else VMEM_SPEC

    if out_hbm:
        out_specs = [HBM_SPEC if k in out_hbm else VMEM_SPEC for k in range(len(out_shape))]
    else:
        out_specs = jax.tree.map(lambda _: VMEM_SPEC, out_shape)
    size = sum(array.size * array.dtype.itemsize for array in jax.tree.leaves((operands, out_shape)))
    if brief:
        flops = size = 0
    in_specs = [spec(k, array) for k, array in enumerate(operands)]
    operands = [
        pltpu.with_memory_space_constraint(array, pltpu.HBM) if space is HBM_SPEC else array
        for array, space in zip(operands, in_specs)
    ]
    return pl.pallas_call(
        kernel,
        out_shape=out_shape,
        in_specs=in_specs,
        out_specs=out_specs,
        scratch_shapes=list(scratch),
        compiler_params=params(operands, out_shape),
        cost_estimate=pl.CostEstimate(flops=flops, bytes_accessed=size, transcendentals=0),
        name=name,
    )(*operands)


def fetch(*pairs):
    copies = [pltpu.make_async_copy(source, target, sem) for source, target, sem in pairs]
    for copy in copies:
        copy.start()
    return copies


def wrap(value, length):
    value = jnp.where(value < 0, value + length, value)
    return jnp.where(value >= length, value - length, value)


def stack(*blocks):
    return jnp.concatenate(blocks, axis=0)


def beside(*blocks):
    return jnp.concatenate(blocks, axis=1)


def dot(left, right):
    return jnp.dot(left, right, preferred_element_type=jnp.float32)


def spans(pixel, anchor, num, den, length):
    stretched = (pixel * num).astype(jnp.float32)
    den = (jnp.zeros_like(pixel) + den).astype(jnp.float32)
    whole = jnp.floor((stretched + 0.5) / den)
    fraction = (stretched - whole * den) / den
    base = wrap(anchor + whole.astype(jnp.int32), length)
    upper = wrap(base + 1, length)
    return base, upper, 1.0 - fraction, fraction


def chunk_start(half, chunk):
    return 3 * half + chunk * (1 - 2 * half)


def split_kernel(screens, *refs):
    outs, sems = refs[:-1], refs[-1]
    width = outs[0].shape[2]
    core = lax.rem(lax.axis_index("dir"), 2)
    pairs = []
    for k, out in enumerate(outs):
        half = core if k < 2 else 1 - core
        start = pl.multiple_of(chunk_start(half, k % 2) * width, LANES)
        pairs.append((screens.at[:, :, pl.ds(start, width)], out, sems.at[k]))
    for load in fetch(*pairs):
        load.wait()


def weights_kernel(geometry, wind_hbm, offsets_hbm, ratio_hbm, *refs):
    n_layer, rows_dev, screen_cols = geometry
    sources, (rows_out, mine_out, other_out), refs = refs[:5], refs[5:8], refs[8:]
    copies, (wind_copy, wind, offsets, ratio, *tables, sems) = refs[:5], refs[5:]
    pupil_cols = mine_out.shape[2]
    pairs = [*zip(sources, copies), (wind_hbm, wind_copy)]
    others = fetch(*[(source, copy, sems.at[3 + k]) for k, (source, copy) in enumerate(pairs)])
    loads = fetch(
        (wind_hbm, wind, sems.at[0]),
        (offsets_hbm, offsets, sems.at[1]),
        (ratio_hbm, ratio, sems.at[2]),
    )
    _, layers, pupil_rows, screen_rows = rows_out.shape
    half = pupil_rows // 2
    direction = lax.axis_index("dir")
    column = lax.axis_index("layer")
    block = pupil_rows // n_layer
    row = lax.broadcasted_iota(jnp.int32, (half, LANES), 0)
    step = row // block
    for at, value in enumerate(send_order(n_layer // 2)):
        step = jnp.where(row // block == at, value, step)
    pair = jnp.bitwise_xor(step, column // 2)
    parity = lax.rem(column, 2)
    inside = lax.rem(row, block) + pair * (2 * block)
    pixel_rows = stack(inside + parity * block, inside + (1 - parity) * block)
    lane = lax.broadcasted_iota(jnp.int32, (pupil_rows, LANES), 1)
    for load in loads:
        load.wait()
    for side in range(2):
        target = jnp.bitwise_xor(direction, side)
        for level in range(layers):
            anchor = wrap(offsets[level, 0, target] - wind[0, level], screen_rows)
            num, den = ratio[level, 0, target], ratio[level, 1, target]
            base, upper, low, high = spans(pixel_rows, anchor, num, den, screen_rows)
            for peer in range(4):
                for part in range(rows_dev // LANES):
                    index = lane + (jnp.bitwise_xor(direction, peer) * rows_dev + part * LANES)
                    weight = jnp.where(index == base, low, 0.0)
                    weight = jnp.where(index == upper, high, weight)
                    start = peer * rows_dev + part * LANES
                    rows_out[side, level, :, start : start + LANES] = weight.astype(jnp.bfloat16)
    sub = lax.broadcasted_iota(jnp.int32, (8, LANES), 0)
    anchor, num, den = jnp.zeros_like(sub), jnp.zeros_like(sub), jnp.ones_like(sub)
    for level in range(layers):
        start = wrap(offsets[level, 1, direction] - wind[1, level], screen_cols)
        anchor = jnp.where(sub == level, start, anchor)
        num = jnp.where(sub == level, ratio[level, 0, direction], num)
        den = jnp.where(sub == level, ratio[level, 1, direction], den)
    for at in range(0, pupil_cols, LANES):
        pixel = lax.broadcasted_iota(jnp.int32, (8, LANES), 1) + at
        values = spans(pixel, anchor, num, den, screen_cols)
        for table, value in zip(tables, values):
            table[:, at : at + LANES] = value
    for out, block in ((mine_out, column), (other_out, jnp.bitwise_xor(column, 1))):
        column_weights(*tables, block * out.shape[1], out)
    for load in others:
        load.wait()


def column_weights(base_ref, upper_ref, low_ref, high_ref, first, out):
    layers, cols_dev, pupil_cols = out.shape
    width = cols_dev // 4
    core = lax.rem(lax.axis_index("dir"), 2)
    sub = lax.broadcasted_iota(jnp.int32, (width, LANES), 0).astype(jnp.float32).astype(jnp.bfloat16)
    zero = jnp.zeros((width, LANES), jnp.bfloat16)
    for level in range(layers):

        def tile(step, carry):
            start = pl.multiple_of(step * LANES, LANES)
            cut = (slice(level, level + 1), pl.ds(start, LANES))
            base, upper = base_ref[cut], upper_ref[cut]
            low, high = [
                jnp.broadcast_to(ref[cut].astype(jnp.bfloat16), (width, LANES)) for ref in (low_ref, high_ref)
            ]
            for k in range(4):
                shift = first + chunk_start(jnp.bitwise_xor(core, k // 2), k % 2) * width
                base_at, upper_at = [
                    jnp.broadcast_to(
                        jnp.clip(value - shift, -1, width).astype(jnp.float32).astype(jnp.bfloat16), (width, LANES)
                    )
                    for value in (base, upper)
                ]
                weight = jnp.where(sub == base_at, low, zero)
                weight = jnp.where(sub == upper_at, high, weight)
                out[level, k * width : (k + 1) * width, pl.ds(start, LANES)] = weight
            return carry

        lax.fori_loop(0, pupil_cols // LANES, tile, 0)


def strips_kernel(wind_held, across, diagonal, near, keep, strip, sibling_strip, wind, sem):
    load = fetch((wind_held, wind, sem))[0]
    layers, rows, _ = keep.shape
    core = lax.rem(lax.axis_index("dir"), 2)
    odd = core == 1
    lane = lax.broadcasted_iota(jnp.int32, (rows + 32, LANES), 1)

    def wide(own, near, far, odd, level):
        own, near, far = [block[level].astype(jnp.float32) for block in (own, near, far)]
        before = jnp.where(odd, near[rows - 16 :], far[rows - 16 :])
        return stack(before, own, jnp.where(odd, far[:16], near[:16]))

    packed = jnp.zeros((rows + 32, LANES), jnp.float32)
    for level in range(layers):
        blocks = (keep, near, diagonal, odd), (near, keep, across, core == 0)
        for at, block in zip((WIND_MAX * level, STRIP + WIND_MAX * level), blocks):
            block = pltpu.roll(wide(*block, level), at + WIND_MAX * core, 1)
            packed = jnp.where((lane >= at) & (lane < at + WIND_MAX), block, packed)
    load.wait()
    strips = jnp.zeros((rows, LANES), jnp.float32)
    for level in range(layers):
        shift = wind[0, level]
        shift = jnp.where(shift < 0, shift + rows + 32, shift)
        moved = pltpu.roll(packed, shift, 0)[16 : 16 + rows]
        mine = lax.rem(lane[:rows], STRIP)
        strips = jnp.where((mine >= WIND_MAX * level) & (mine < WIND_MAX * (level + 1)), moved, strips)
    strips = strips.T.astype(jnp.bfloat16)
    strip[...] = strips[:STRIP]
    sibling_strip[...] = strips[STRIP : 2 * STRIP]


def project_rows(rows_ref, keep, near, across, diagonal, level):
    screen = stack(keep[level], near[level], across[level], diagonal[level])
    rows = stack(rows_ref[0, level], rows_ref[1, level])
    return dot(rows, screen).astype(jnp.bfloat16)


def first_rows_kernel(rows_ref, across, diagonal, near, keep, mine, sibling, other, sibling_other):
    layers, half, _ = mine.shape
    for level in range(layers):
        part = project_rows(rows_ref, keep, near, across, diagonal, level)
        for k, out in enumerate((mine, other, sibling, sibling_other)):
            out[level] = part[k * half : (k + 1) * half]


def put_strip(out, at, strip):
    for k in range(strip.shape[1] // LANES):
        out[at + k * STRIP : at + (k + 1) * STRIP, :] = strip[:, k * LANES : (k + 1) * LANES]


def get_strip(ref, at):
    return beside(*[ref[start : start + STRIP, :] for start in range(at, ref.shape[0], STRIP)])


def later_rows_kernel(rows_ref, *refs):
    chunks, refs = refs[:8], refs[8:]
    sibling0, strip, sibling_strip, mine, give, far, sibling_far, rest, sibling_rest = refs
    across, diagonal, near, keep, across0, diagonal0, near0, keep0 = chunks
    layers, half, width = mine.shape
    rows = near.shape[1]
    size = (far.shape[0] - STRIP * rows // LANES) // layers
    start = half - size
    for out in (rest, sibling_rest):
        left = out.shape[0] - layers * start
        if left:
            out[layers * start :] = jnp.zeros((left, width), jnp.bfloat16)
    for level in range(layers):
        part = project_rows(rows_ref, keep, near, across, diagonal, level)
        mine[level] = part[:half]
        for k, out, remainder in ((1, far, rest), (3, sibling_far, sibling_rest)):
            piece = part[k * half : (k + 1) * half]
            out[level * size : (level + 1) * size] = piece[start:]
            remainder[level * start : (level + 1) * start] = piece[:start]
        give[level, :half, :width] = sibling0[level]
        give[level, :half, width:] = part[2 * half : 3 * half]
        for k, blocks in enumerate(((across0, keep0), (across, keep))):
            cut = slice(k * width, (k + 1) * width)
            edges = [block[level, at : at + 16] for block in blocks for at in (0, rows - 16)]
            give[level, half:, cut] = stack(*edges)
    put_strip(far, layers * size, strip)
    put_strip(sibling_far, layers * size, sibling_strip)


def project(parts, cols_refs, at):
    cols = stack(*[ref[level, start:stop, at : at + 256] for ref, level, start, stop in cols_refs])
    return dot(beside(*parts), cols)


def phase_kernel(mine_ref, other_ref, mine0, mine1, came, sibling_came, phase):
    layers, _, width = mine0.shape
    parts, cuts = [], []
    for level in range(layers):
        parts += [mine0[level], mine1[level], came[level], sibling_came[level]]
        cuts += [(mine_ref, level, 0, 2 * width)]
        cuts += [(other_ref, level, 0, width), (other_ref, level, 2 * width, 3 * width)]
    for at in range(0, phase.shape[1], 256):
        phase[:, at : at + 256] = project(parts, cuts, at)


def sum_up(start, mine_ref, cols_ref, phase, taken, came, sibling_came, outs):
    layers, _, width = taken.shape
    width = width // 2
    block = outs[0].shape[0]
    size = block * len(outs)
    rows = slice(start, start + size)
    parts, cuts = [], []
    for level in range(layers):
        cut = slice(level * size, (level + 1) * size)
        parts += [taken[level, rows], came[cut], sibling_came[cut]]
        cuts += [(mine_ref, level, 2 * width, 4 * width)]
        cuts += [(cols_ref, level, width, 2 * width), (cols_ref, level, 3 * width, 4 * width)]
    pupil_cols = phase.shape[1]
    for at in range(0, pupil_cols, 256):
        total = (phase[rows, at : at + 256] + project(parts, cuts, at)).astype(jnp.bfloat16)
        for k, out in enumerate(outs):
            out[:, at : at + 256] = total[k * block : (k + 1) * block]


def strip_steps(pairs):
    return [2**k - 1 for k in range(1, pairs.bit_length())]


def send_order(pairs):
    steps = strip_steps(pairs)
    return [k for k in range(pairs) if k not in steps] + steps


def add_strip(pairs, step, strips, out):
    pair = lax.axis_index("layer") // 2
    after = lax.rem(pair + 1, pairs) == jnp.bitwise_xor(pair, step)
    at = out.shape[1] - strips.shape[1]
    last, first = strips[:STRIP].astype(jnp.float32), strips[STRIP:].astype(jnp.float32)
    out[:, at:] = jnp.where(after, last, first).astype(jnp.bfloat16)


def far_kernel(mine_ref, cols_ref, phase, taken, came, sibling_came, *outs):
    *outs, strips = outs
    half = phase.shape[0]
    size = outs[0].shape[0] * len(outs)
    sum_up(half - size, mine_ref, cols_ref, phase, taken, came, sibling_came, outs)
    layers = taken.shape[0]
    odd = lax.rem(lax.axis_index("dir"), 2) == 1
    here = get_strip(came, layers * size).astype(jnp.float32)
    there = get_strip(sibling_came, layers * size).astype(jnp.float32)
    strips[:STRIP] = jnp.where(odd, here, there).astype(jnp.bfloat16)
    strips[STRIP:] = jnp.where(odd, there, here).astype(jnp.bfloat16)
    pairs = half // outs[0].shape[0]
    for out, step in zip(outs, strip_steps(pairs)):
        add_strip(pairs, step, strips, out)


def rest_kernel(mine_ref, cols_ref, phase, taken, came, sibling_came, *outs):
    sum_up(0, mine_ref, cols_ref, phase, taken, came, sibling_came, outs)


def shifted_rows(shift, odd, own, near, far):
    own, near, far = [block.astype(jnp.float32) for block in (own, near, far)]
    rows = own.shape[0]
    before = jnp.where(odd, near[16:], far[16:])
    after = jnp.where(odd, far[:16], near[:16])
    shift = jnp.where(shift < 0, shift + rows + 32, shift)
    return pltpu.roll(stack(before, own, after), shift, 0)[16 : 16 + rows]


def shift_kernel(wind_held, own, near0, near1, diagonal0, diagonal1, taken, partner_strips, *refs):
    messages, (out, wind, sem) = refs[:-3], refs[-3:]
    load = fetch((wind_held, wind, sem))[0]
    layers, rows, cols = own.shape
    odd = lax.rem(lax.axis_index("dir"), 2) == 1
    half = taken.shape[1] - 64
    pairs = 2 ** len(messages)
    pair, second = lax.axis_index("layer") // 2, lax.rem(lax.axis_index("layer"), 2) == 1
    before = jnp.bitwise_xor(pair, lax.rem(pair + pairs - 1, pairs))
    after = jnp.bitwise_xor(pair, lax.rem(pair + 1, pairs))
    left = partner_strips[:STRIP].astype(jnp.float32)
    right = partner_strips[STRIP:].astype(jnp.float32)
    for step, message in zip(strip_steps(pairs), messages):
        strip = message[:, message.shape[1] - rows :].astype(jnp.float32)
        left = jnp.where(jnp.logical_and(before == step, jnp.logical_not(second)), strip, left)
        right = jnp.where(jnp.logical_and(after == step, second), strip, right)
    strips = stack(left, right, jnp.zeros((LANES - 2 * STRIP, rows), jnp.float32)).T
    lane = lax.broadcasted_iota(jnp.int32, (rows, LANES), 1)
    load.wait()
    for level in range(layers):
        last = pltpu.roll(strips, LANES - WIND_MAX * (level + 1), 1)
        first = pltpu.roll(strips, LANES - STRIP - WIND_MAX * level, 1)
        extra = jnp.where(lane < WIND_MAX, first, last)
        pair = []
        for at, parts in ((half, (diagonal0, diagonal1)), (half + 32, (near0, near1))):
            here = [stack(part[level, :16], part[level, rows - 16 :]).astype(jnp.float32) for part in parts]
            there = taken[level, at : at + 32].astype(jnp.float32)
            width = there.shape[1] // 2
            quarters = [*here, there[:, width:], there[:, :width]]
            pair.append(beside(*[jnp.where(odd, quarters[3 - k], quarters[k]) for k in range(4)]))
        far, near = pair
        moved = shifted_rows(wind[0, level], odd, own[level], near, far)
        shift = wind[1, level]
        shift = jnp.where(shift < 0, shift + cols + LANES, shift)
        out[level] = pltpu.roll(beside(moved, extra), shift, 1)[:, :cols].astype(jnp.bfloat16)


def optics_kernel(amplitude, ones, columns, lines, amp_out, columns_out, lines_out):
    rows, pupil_cols = amplitude.shape
    for step in range(pupil_cols // LANES):
        cut = slice(step * LANES, (step + 1) * LANES)
        amp = amplitude[:, cut]
        energy = (amp * amp).reshape(rows // SUB_PIX, SUB_PIX, LANES).sum(axis=1)
        energy = jnp.broadcast_to(energy[:, None], (rows // SUB_PIX, SUB_PIX, LANES)).reshape(rows, LANES)
        total = jnp.dot(energy, ones[...], precision=lax.Precision.HIGHEST, preferred_element_type=jnp.float32)
        amp_out[:, cut] = amp * lax.rsqrt(total)
    columns_out[...] = columns[...].astype(jnp.bfloat16)
    lines_out[...] = lines[...].astype(jnp.bfloat16)


def sin_cos(phase):
    turns = jnp.floor(phase * (1.0 / np.pi) + 0.5)
    rest = phase - turns * 3.140625
    rest = rest - turns * 9.67653589793e-4
    odd = turns - 2.0 * jnp.floor(turns * 0.5)
    sign = 1.0 - 2.0 * odd
    square = rest * rest
    sine = -1.0 / 39916800.0
    for term in (1.0 / 362880.0, -1.0 / 5040.0, 1.0 / 120.0, -1.0 / 6.0, 1.0):
        sine = sine * square + term
    cosine = 1.0 / 479001600.0
    for term in (-1.0 / 3628800.0, 1.0 / 40320.0, -1.0 / 720.0, 1.0 / 24.0, -0.5, 1.0):
        cosine = cosine * square + term
    return sine * rest * sign, cosine * sign


def imaging_kernel(count, *refs):
    parts, (amp_ref, columns, lines, shifted, spots, screens, out, sems) = refs[:count], refs[count:]
    copies = fetch((shifted, screens, sems.at[0]))
    rows, cols = amp_ref.shape
    tiles = cols // LANES
    phase = parts[0][:, :cols].astype(jnp.float32)
    for part in parts[1:]:
        phase = phase + part[:, :cols].astype(jnp.float32)
    sine, cosine = sin_cos(phase)
    amp = amp_ref[...]
    real, imag = (amp * cosine).astype(jnp.bfloat16), (amp * sine).astype(jnp.bfloat16)
    cuts = [slice(t * LANES, (t + 1) * LANES) for t in range(tiles)]
    field = stack(*[beside(real[:, cut], imag[:, cut]) for cut in cuts])
    half = dot(field, columns[...]).astype(jnp.bfloat16)
    wide = 2 * LANES
    out_rows = 2 * rows
    for t in range(tiles):
        mine = half[t * rows : (t + 1) * rows]
        full = dot(lines[...], stack(mine[:, :wide], mine[:, wide:]))
        real, imag = full[:out_rows], full[out_rows:]
        out[:, t * wide : (t + 1) * wide] = real * real + imag * imag
        if t % 2:
            cut = slice((t - 1) * wide, (t + 1) * wide)
            copies += fetch((out.at[:, cut], spots.at[:, cut], sems.at[1 + t // 2]))
    for copy in copies:
        copy.wait()


def tables_of(rows):
    freq = np.arange(SPOT_PIX)[:, None] - SPOT_PIX // 2
    angle = ((freq * np.arange(SUB_PIX)[None, :]) % SPOT_PIX) * (2.0 * np.pi / SPOT_PIX)
    cos, sin = np.cos(angle), np.sin(angle)

    def blocks(table, count):
        return np.kron(np.eye(count), table)

    per_tile = LANES // SUB_PIX
    col_cos, col_sin = blocks(cos.T, per_tile), blocks(sin.T, per_tile)
    columns = np.block([[col_cos, -col_sin], [col_sin, col_cos]])
    count = rows // SUB_PIX
    row_cos, row_sin = blocks(cos, count), blocks(sin, count)
    lines = np.block([[row_cos, row_sin], [-row_sin, row_cos]])

    return columns.astype(np.float32), lines.astype(np.float32)


def per_device(screens, amplitude, wind, offsets, ratio):
    layers, rows_dev, cols_dev = screens.shape
    n_layer = lax.axis_size("layer")
    n_dir = lax.axis_size("dir")
    rows, pupil_cols = amplitude.shape
    pairs = n_layer // 2
    half = pairs * rows
    pupil_rows = 2 * half
    assert n_dir == 4 and rows == STRIP and pairs > 2
    bf16, f32 = jnp.bfloat16, jnp.float32
    wind = jnp.transpose(wind, (1, 0))
    offsets = jnp.transpose(offsets, (1, 2, 0))
    ratio = jnp.transpose(ratio, (1, 2, 0))
    smem, sem = pltpu.SMEM, pltpu.SemaphoreType.DMA
    wind_scratch = [smem(wind.shape, jnp.int32), sem]

    def shape(*dims, dtype=bf16):
        return jax.ShapeDtypeStruct(dims, dtype)

    def swap(value, bits):
        return lax.ppermute(value, "dir", [(i, i ^ bits) for i in range(n_dir)])

    def partner(value, bits=0):
        count = n_layer * n_dir
        return lax.ppermute(value, ("layer", "dir"), [(i, i ^ n_dir ^ bits) for i in range(count)])

    def turn(value, step):
        return lax.ppermute(value, "layer", [(i, (i + step) % n_layer) for i in range(n_layer)])

    width = cols_dev // 4
    chunk = shape(layers, rows_dev, width)
    keep0, keep1, give0, give1 = call(
        split_kernel,
        [chunk] * 4,
        (screens,),
        0,
        "split",
        in_hbm=(0,),
        scratch=[sem((4,))],
        brief=True,
    )
    across0 = swap(keep0, 2)
    diagonal0 = swap(give0, 3)
    near0 = swap(give0, 1)
    across1 = swap(keep1, 2)
    diagonal1 = swap(give1, 3)
    ones = np.kron(np.eye(LANES // SUB_PIX), np.ones((SUB_PIX, SUB_PIX))).astype(np.float32)
    optics_in = (amplitude, jnp.asarray(ones), *[jnp.asarray(table) for table in tables_of(rows)])
    copies = [shape(*array.shape, dtype=array.dtype) for array in (screens, *optics_in, wind)]
    row_weights, cols, others, *loaded = call(
        functools.partial(weights_kernel, (n_layer, rows_dev, cols_dev * n_layer)),
        [shape(2, layers, pupil_rows, 4 * rows_dev)] + [shape(layers, cols_dev, pupil_cols)] * 2 + copies,
        (wind, offsets, ratio, screens, *optics_in),
        0,
        "weights",
        in_hbm=range(8),
        scratch=[smem(array.shape, jnp.int32) for array in (wind, offsets, ratio)]
        + [pltpu.VMEM((8, pupil_cols), dtype) for dtype in (jnp.int32, jnp.int32, f32, f32)]
        + [sem((9,))],
        brief=True,
    )
    own, *optics_in, wind = loaded
    give1, own = lax.optimization_barrier((give1, own))
    near1 = swap(give1, 1)
    across0, diagonal0, row_weights, cols = lax.optimization_barrier((across0, diagonal0, row_weights, cols))

    projected = shape(layers, half, width)
    mine0, sibling0, other0, sibling_other0 = call(
        first_rows_kernel,
        [projected] * 4,
        (row_weights, across0, diagonal0, near0, keep0),
        0,
        "rows_first",
        brief=True,
    )
    came0 = partner(other0)
    sibling_came0 = partner(sibling_other0, 1)

    wind, mine0 = lax.optimization_barrier((wind, mine0))
    strip, sibling_strip = call(
        strips_kernel,
        [shape(STRIP, rows_dev)] * 2,
        (wind, across0, diagonal0, near0, keep0),
        0,
        "strips",
        scratch=wind_scratch,
        brief=True,
    )
    steps = strip_steps(pairs)
    far = len(steps) * rows
    message = shape(layers * far + STRIP * rows_dev // LANES, width)
    remainder = shape(max(layers * (half - far), message.shape[0] + 16), width)
    mine1, give, far1, sibling_far1, rest1, sibling_rest1 = call(
        later_rows_kernel,
        [projected, shape(layers, half + 64, 2 * width), message, message, remainder, remainder],
        (row_weights, across1, diagonal1, near1, keep1, across0, diagonal0, near0, keep0, sibling0, strip, sibling_strip),
        0,
        "rows_later",
        brief=True,
    )
    far1, sibling_far1 = partner(far1), partner(sibling_far1, 1)
    rest1, sibling_rest1 = partner(rest1), partner(sibling_rest1, 1)
    taken = swap(give, 1)
    phase = call(
        phase_kernel,
        shape(half, pupil_cols, dtype=f32),
        (cols, others, mine0, mine1, came0, sibling_came0),
        10_000_000_000,
        "phase",
    )

    *far_sums, strips = call(
        far_kernel,
        [shape(rows, pupil_cols + rows_dev)] * len(steps) + [shape(2 * STRIP, rows_dev)],
        (cols, others, phase, taken, far1, sibling_far1),
        300_000_000,
        "far",
    )
    rest_sums = call(
        rest_kernel,
        [shape(rows, pupil_cols)] * (pairs - len(steps)),
        (cols, others, phase, taken, rest1, sibling_rest1),
        0,
        "rest",
        brief=True,
    )
    received = dict(zip(send_order(pairs), [*rest_sums, *far_sums]))
    for k in range(1, pairs):
        received[k] = lax.ppermute(received[k], "layer", [(i, i ^ (2 * k)) for i in range(n_layer)])
    received = [received[k] for k in range(pairs)]

    optics_in, received[-1] = lax.optimization_barrier((optics_in, received[-1]))
    optics = call(
        optics_kernel,
        (
            shape(rows, pupil_cols, dtype=f32),
            shape(*optics_in[2].shape),
            shape(*optics_in[3].shape),
        ),
        optics_in,
        0,
        "optics",
        brief=True,
    )
    received[1], optics = lax.optimization_barrier((received[1], optics))
    shifted = call(
        shift_kernel,
        shape(layers, rows_dev, cols_dev),
        (wind, own, near0, near1, diagonal0, diagonal1, taken, strips, *[received[k] for k in steps]),
        0,
        "shift",
        scratch=wind_scratch,
        brief=True,
    )
    spots_shape = shape(2 * rows, 2 * pupil_cols, dtype=f32)
    spots, new_screens = call(
        functools.partial(imaging_kernel, pairs),
        [spots_shape, shape(layers, rows_dev, cols_dev)],
        (*received, *optics, shifted),
        400_000_000,
        "imaging",
        out_hbm=(0, 1),
        scratch=[pltpu.VMEM(spots_shape.shape, f32), sem((1 + pupil_cols // (2 * LANES),))],
    )
    return (new_screens, spots[None])


def solution(mesh):
    return jax.shard_map(
        per_device,
        mesh=mesh,
        in_specs=(P(None, "dir", "layer"), P("layer", None), P(), P(), P()),
        out_specs=(P(None, "dir", "layer"), P("dir", "layer", None)),
        check_vma=False,
    )
```

```python
import functools

import jax
import jax.numpy as jnp
import numpy as np
from jax import lax
from jax.experimental import pallas as pl
from jax.experimental.pallas import tpu as pltpu
from jax.sharding import PartitionSpec as P

SUB_PIX = 16
SPOT_PIX = 32
WIND_MAX = 8
LANES = 128
STRIP = 32

HBM_SPEC = pl.BlockSpec(memory_space=pltpu.HBM)
VMEM_SPEC = pl.BlockSpec(memory_space=pltpu.VMEM)


def params(*arrays):
    held = sum(array.size * array.dtype.itemsize for array in jax.tree.leaves(arrays))
    return pltpu.CompilerParams(vmem_limit_bytes=held + 8 * 1024 * 1024)


def call(kernel, out_shape, operands, flops, name, in_hbm=(), out_hbm=(), scratch=(), brief=False):
    def spec(k, array):
        return HBM_SPEC if k in in_hbm else VMEM_SPEC

    if out_hbm:
        out_specs = [HBM_SPEC if k in out_hbm else VMEM_SPEC for k in range(len(out_shape))]
    else:
        out_specs = jax.tree.map(lambda _: VMEM_SPEC, out_shape)
    size = sum(array.size * array.dtype.itemsize for array in jax.tree.leaves((operands, out_shape)))
    if brief:
        flops = size = 0
    in_specs = [spec(k, array) for k, array in enumerate(operands)]
    operands = [
        pltpu.with_memory_space_constraint(array, pltpu.HBM) if space is HBM_SPEC else array
        for array, space in zip(operands, in_specs)
    ]
    return pl.pallas_call(
        kernel,
        out_shape=out_shape,
        in_specs=in_specs,
        out_specs=out_specs,
        scratch_shapes=list(scratch),
        compiler_params=params(operands, out_shape),
        cost_estimate=pl.CostEstimate(flops=flops, bytes_accessed=size, transcendentals=0),
        name=name,
    )(*operands)


def fetch(*pairs):
    copies = [pltpu.make_async_copy(source, target, sem) for source, target, sem in pairs]
    for copy in copies:
        copy.start()
    return copies


def wrap(value, length):
    value = jnp.where(value < 0, value + length, value)
    return jnp.where(value >= length, value - length, value)


def stack(*blocks):
    return jnp.concatenate(blocks, axis=0)


def beside(*blocks):
    return jnp.concatenate(blocks, axis=1)


def dot(left, right):
    return jnp.dot(left, right, preferred_element_type=jnp.float32)


def spans(pixel, anchor, num, den, length):
    stretched = (pixel * num).astype(jnp.float32)
    den = (jnp.zeros_like(pixel) + den).astype(jnp.float32)
    whole = jnp.floor((stretched + 0.5) / den)
    fraction = (stretched - whole * den) / den
    base = wrap(anchor + whole.astype(jnp.int32), length)
    upper = wrap(base + 1, length)
    return base, upper, 1.0 - fraction, fraction


def chunk_start(half, chunk):
    return 3 * half + chunk * (1 - 2 * half)


def split_kernel(screens, *refs):
    outs, sems = refs[:-1], refs[-1]
    width = outs[0].shape[2]
    core = lax.rem(lax.axis_index("dir"), 2)
    pairs = []
    for k, out in enumerate(outs):
        half = core if k < 2 else 1 - core
        start = pl.multiple_of(chunk_start(half, k % 2) * width, LANES)
        pairs.append((screens.at[:, :, pl.ds(start, width)], out, sems.at[k]))
    for load in fetch(*pairs):
        load.wait()


def weights_kernel(geometry, wind_hbm, offsets_hbm, ratio_hbm, *refs):
    n_layer, rows_dev, screen_cols = geometry
    sources, (rows_out, cols_out, *tables), refs = refs[:5], refs[5:11], refs[11:]
    copies, (wind_copy, wind, offsets, ratio, sems) = refs[:5], refs[5:]
    pupil_cols = cols_out.shape[2]
    pairs = [*zip(sources, copies), (wind_hbm, wind_copy)]
    others = fetch(*[(source, copy, sems.at[3 + k]) for k, (source, copy) in enumerate(pairs)])
    loads = fetch(
        (wind_hbm, wind, sems.at[0]),
        (offsets_hbm, offsets, sems.at[1]),
        (ratio_hbm, ratio, sems.at[2]),
    )
    _, layers, pupil_rows, screen_rows = rows_out.shape
    half = pupil_rows // 2
    direction = lax.axis_index("dir")
    column = lax.axis_index("layer")
    block = pupil_rows // n_layer
    row = lax.broadcasted_iota(jnp.int32, (half, LANES), 0)
    step = row // block
    for at, value in enumerate(send_order(n_layer // 2)):
        step = jnp.where(row // block == at, value, step)
    pair = jnp.bitwise_xor(step, column // 2)
    parity = lax.rem(column, 2)
    inside = lax.rem(row, block) + pair * (2 * block)
    pixel_rows = stack(inside + parity * block, inside + (1 - parity) * block)
    lane = lax.broadcasted_iota(jnp.int32, (pupil_rows, LANES), 1)
    for load in loads:
        load.wait()
    for side in range(2):
        target = jnp.bitwise_xor(direction, side)
        for level in range(layers):
            anchor = wrap(offsets[level, 0, target] - wind[0, level], screen_rows)
            num, den = ratio[level, 0, target], ratio[level, 1, target]
            base, upper, low, high = spans(pixel_rows, anchor, num, den, screen_rows)
            for peer in range(4):
                for part in range(rows_dev // LANES):
                    index = lane + (jnp.bitwise_xor(direction, peer) * rows_dev + part * LANES)
                    weight = jnp.where(index == base, low, 0.0)
                    weight = jnp.where(index == upper, high, weight)
                    start = peer * rows_dev + part * LANES
                    rows_out[side, level, :, start : start + LANES] = weight.astype(jnp.bfloat16)
    sub = lax.broadcasted_iota(jnp.int32, (8, LANES), 0)
    anchor, num, den = jnp.zeros_like(sub), jnp.zeros_like(sub), jnp.ones_like(sub)
    for level in range(layers):
        start = wrap(offsets[level, 1, direction] - wind[1, level], screen_cols)
        anchor = jnp.where(sub == level, start, anchor)
        num = jnp.where(sub == level, ratio[level, 0, direction], num)
        den = jnp.where(sub == level, ratio[level, 1, direction], den)
    for at in range(0, pupil_cols, LANES):
        pixel = lax.broadcasted_iota(jnp.int32, (8, LANES), 1) + at
        values = spans(pixel, anchor, num, den, screen_cols)
        for table, value in zip(tables, values):
            table[:, at : at + LANES] = value
    column_weights(*tables, column * cols_out.shape[1], cols_out)
    for load in others:
        load.wait()


def column_weights(base_ref, upper_ref, low_ref, high_ref, first, out):
    layers, cols_dev, pupil_cols = out.shape
    width = cols_dev // 4
    core = lax.rem(lax.axis_index("dir"), 2)
    sub = lax.broadcasted_iota(jnp.int32, (width, LANES), 0).astype(jnp.float32).astype(jnp.bfloat16)
    zero = jnp.zeros((width, LANES), jnp.bfloat16)
    for level in range(layers):

        def tile(step, carry):
            start = pl.multiple_of(step * LANES, LANES)
            cut = (slice(level, level + 1), pl.ds(start, LANES))
            base, upper = base_ref[cut], upper_ref[cut]
            low, high = [
                jnp.broadcast_to(ref[cut].astype(jnp.bfloat16), (width, LANES)) for ref in (low_ref, high_ref)
            ]
            for k in range(4):
                shift = first + chunk_start(jnp.bitwise_xor(core, k // 2), k % 2) * width
                base_at, upper_at = [
                    jnp.broadcast_to(
                        jnp.clip(value - shift, -1, width).astype(jnp.float32).astype(jnp.bfloat16), (width, LANES)
                    )
                    for value in (base, upper)
                ]
                weight = jnp.where(sub == base_at, low, zero)
                weight = jnp.where(sub == upper_at, high, weight)
                out[level, k * width : (k + 1) * width, pl.ds(start, LANES)] = weight
            return carry

        lax.fori_loop(0, pupil_cols // LANES, tile, 0)


def strips_kernel(wind_held, *refs):
    tables, (across, diagonal, near, keep, cols_out, strip, sibling_strip, wind, sem) = refs[:4], refs[4:]
    load = fetch((wind_held, wind, sem))[0]
    column_weights(*tables, jnp.bitwise_xor(lax.axis_index("layer"), 1) * cols_out.shape[1], cols_out)
    layers, rows, _ = keep.shape
    core = lax.rem(lax.axis_index("dir"), 2)
    odd = core == 1
    lane = lax.broadcasted_iota(jnp.int32, (rows + 32, LANES), 1)

    def wide(own, near, far, odd, level):
        own, near, far = [block[level].astype(jnp.float32) for block in (own, near, far)]
        before = jnp.where(odd, near[rows - 16 :], far[rows - 16 :])
        return stack(before, own, jnp.where(odd, far[:16], near[:16]))

    packed = jnp.zeros((rows + 32, LANES), jnp.float32)
    for level in range(layers):
        blocks = (keep, near, diagonal, odd), (near, keep, across, core == 0)
        for at, block in zip((WIND_MAX * level, STRIP + WIND_MAX * level), blocks):
            block = pltpu.roll(wide(*block, level), at + WIND_MAX * core, 1)
            packed = jnp.where((lane >= at) & (lane < at + WIND_MAX), block, packed)
    load.wait()
    strips = jnp.zeros((rows, LANES), jnp.float32)
    for level in range(layers):
        shift = wind[0, level]
        shift = jnp.where(shift < 0, shift + rows + 32, shift)
        moved = pltpu.roll(packed, shift, 0)[16 : 16 + rows]
        mine = lax.rem(lane[:rows], STRIP)
        strips = jnp.where((mine >= WIND_MAX * level) & (mine < WIND_MAX * (level + 1)), moved, strips)
    strips = strips.T.astype(jnp.bfloat16)
    strip[...] = strips[:STRIP]
    sibling_strip[...] = strips[STRIP : 2 * STRIP]


def project_rows(rows_ref, keep, near, across, diagonal, level):
    screen = stack(keep[level], near[level], across[level], diagonal[level])
    rows = stack(rows_ref[0, level], rows_ref[1, level])
    return dot(rows, screen).astype(jnp.bfloat16)


def first_rows_kernel(rows_ref, across, diagonal, near, keep, mine, sibling, other, sibling_other):
    layers, half, _ = mine.shape
    for level in range(layers):
        part = project_rows(rows_ref, keep, near, across, diagonal, level)
        for k, out in enumerate((mine, other, sibling, sibling_other)):
            out[level] = part[k * half : (k + 1) * half]


def put_strip(out, at, strip):
    for k in range(strip.shape[1] // LANES):
        out[at + k * STRIP : at + (k + 1) * STRIP, :] = strip[:, k * LANES : (k + 1) * LANES]


def get_strip(ref, at):
    return beside(*[ref[start : start + STRIP, :] for start in range(at, ref.shape[0], STRIP)])


def later_rows_kernel(rows_ref, *refs):
    chunks, refs = refs[:8], refs[8:]
    sibling0, strip, sibling_strip, mine, give, far, sibling_far, rest, sibling_rest = refs
    across, diagonal, near, keep, across0, diagonal0, near0, keep0 = chunks
    layers, half, width = mine.shape
    rows = near.shape[1]
    size = (far.shape[0] - STRIP * rows // LANES) // layers
    start = half - size
    for out in (rest, sibling_rest):
        left = out.shape[0] - layers * start
        if left:
            out[layers * start :] = jnp.zeros((left, width), jnp.bfloat16)
    for level in range(layers):
        part = project_rows(rows_ref, keep, near, across, diagonal, level)
        mine[level] = part[:half]
        for k, out, remainder in ((1, far, rest), (3, sibling_far, sibling_rest)):
            piece = part[k * half : (k + 1) * half]
            out[level * size : (level + 1) * size] = piece[start:]
            remainder[level * start : (level + 1) * start] = piece[:start]
        give[level, :half, :width] = sibling0[level]
        give[level, :half, width:] = part[2 * half : 3 * half]
        for k, blocks in enumerate(((across0, keep0), (across, keep))):
            cut = slice(k * width, (k + 1) * width)
            edges = [block[level, at : at + 16] for block in blocks for at in (0, rows - 16)]
            give[level, half:, cut] = stack(*edges)
    put_strip(far, layers * size, strip)
    put_strip(sibling_far, layers * size, sibling_strip)


def project(parts, cols_refs, at):
    cols = stack(*[ref[level, start:stop, at : at + 256] for ref, level, start, stop in cols_refs])
    return dot(beside(*parts), cols)


def phase_kernel(mine_ref, other_ref, mine0, mine1, came, sibling_came, phase):
    layers, _, width = mine0.shape
    parts, cuts = [], []
    for level in range(layers):
        parts += [mine0[level], mine1[level], came[level], sibling_came[level]]
        cuts += [(mine_ref, level, 0, 2 * width)]
        cuts += [(other_ref, level, 0, width), (other_ref, level, 2 * width, 3 * width)]
    for at in range(0, phase.shape[1], 256):
        phase[:, at : at + 256] = project(parts, cuts, at)


def sum_up(start, mine_ref, cols_ref, phase, taken, came, sibling_came, outs):
    layers, _, width = taken.shape
    width = width // 2
    block = outs[0].shape[0]
    size = block * len(outs)
    rows = slice(start, start + size)
    parts, cuts = [], []
    for level in range(layers):
        cut = slice(level * size, (level + 1) * size)
        parts += [taken[level, rows], came[cut], sibling_came[cut]]
        cuts += [(mine_ref, level, 2 * width, 4 * width)]
        cuts += [(cols_ref, level, width, 2 * width), (cols_ref, level, 3 * width, 4 * width)]
    pupil_cols = phase.shape[1]
    for at in range(0, pupil_cols, 256):
        total = (phase[rows, at : at + 256] + project(parts, cuts, at)).astype(jnp.bfloat16)
        for k, out in enumerate(outs):
            out[:, at : at + 256] = total[k * block : (k + 1) * block]


def strip_steps(pairs):
    return [2**k - 1 for k in range(1, pairs.bit_length())]


def send_order(pairs):
    steps = strip_steps(pairs)
    return [k for k in range(pairs) if k not in steps] + steps


def add_strip(pairs, step, strips, out):
    pair = lax.axis_index("layer") // 2
    after = lax.rem(pair + 1, pairs) == jnp.bitwise_xor(pair, step)
    at = out.shape[1] - strips.shape[1]
    last, first = strips[:STRIP].astype(jnp.float32), strips[STRIP:].astype(jnp.float32)
    out[:, at:] = jnp.where(after, last, first).astype(jnp.bfloat16)


def far_kernel(mine_ref, cols_ref, phase, taken, came, sibling_came, *outs):
    *outs, strips = outs
    half = phase.shape[0]
    size = outs[0].shape[0] * len(outs)
    sum_up(half - size, mine_ref, cols_ref, phase, taken, came, sibling_came, outs)
    layers = taken.shape[0]
    odd = lax.rem(lax.axis_index("dir"), 2) == 1
    here = get_strip(came, layers * size).astype(jnp.float32)
    there = get_strip(sibling_came, layers * size).astype(jnp.float32)
    strips[:STRIP] = jnp.where(odd, here, there).astype(jnp.bfloat16)
    strips[STRIP:] = jnp.where(odd, there, here).astype(jnp.bfloat16)
    pairs = half // outs[0].shape[0]
    for out, step in zip(outs, strip_steps(pairs)):
        add_strip(pairs, step, strips, out)


def rest_kernel(mine_ref, cols_ref, phase, taken, came, sibling_came, *outs):
    sum_up(0, mine_ref, cols_ref, phase, taken, came, sibling_came, outs)


def shifted_rows(shift, odd, own, near, far):
    own, near, far = [block.astype(jnp.float32) for block in (own, near, far)]
    rows = own.shape[0]
    before = jnp.where(odd, near[16:], far[16:])
    after = jnp.where(odd, far[:16], near[:16])
    shift = jnp.where(shift < 0, shift + rows + 32, shift)
    return pltpu.roll(stack(before, own, after), shift, 0)[16 : 16 + rows]


def shift_kernel(wind_held, own, near0, near1, diagonal0, diagonal1, taken, partner_strips, *refs):
    messages, (out, wind, sem) = refs[:-3], refs[-3:]
    load = fetch((wind_held, wind, sem))[0]
    layers, rows, cols = own.shape
    odd = lax.rem(lax.axis_index("dir"), 2) == 1
    half = taken.shape[1] - 64
    pairs = 2 ** len(messages)
    pair, second = lax.axis_index("layer") // 2, lax.rem(lax.axis_index("layer"), 2) == 1
    before = jnp.bitwise_xor(pair, lax.rem(pair + pairs - 1, pairs))
    after = jnp.bitwise_xor(pair, lax.rem(pair + 1, pairs))
    left = partner_strips[:STRIP].astype(jnp.float32)
    right = partner_strips[STRIP:].astype(jnp.float32)
    for step, message in zip(strip_steps(pairs), messages):
        strip = message[:, message.shape[1] - rows :].astype(jnp.float32)
        left = jnp.where(jnp.logical_and(before == step, jnp.logical_not(second)), strip, left)
        right = jnp.where(jnp.logical_and(after == step, second), strip, right)
    strips = stack(left, right, jnp.zeros((LANES - 2 * STRIP, rows), jnp.float32)).T
    lane = lax.broadcasted_iota(jnp.int32, (rows, LANES), 1)
    load.wait()
    for level in range(layers):
        last = pltpu.roll(strips, LANES - WIND_MAX * (level + 1), 1)
        first = pltpu.roll(strips, LANES - STRIP - WIND_MAX * level, 1)
        extra = jnp.where(lane < WIND_MAX, first, last)
        pair = []
        for at, parts in ((half, (diagonal0, diagonal1)), (half + 32, (near0, near1))):
            here = [stack(part[level, :16], part[level, rows - 16 :]).astype(jnp.float32) for part in parts]
            there = taken[level, at : at + 32].astype(jnp.float32)
            width = there.shape[1] // 2
            quarters = [*here, there[:, width:], there[:, :width]]
            pair.append(beside(*[jnp.where(odd, quarters[3 - k], quarters[k]) for k in range(4)]))
        far, near = pair
        moved = shifted_rows(wind[0, level], odd, own[level], near, far)
        shift = wind[1, level]
        shift = jnp.where(shift < 0, shift + cols + LANES, shift)
        out[level] = pltpu.roll(beside(moved, extra), shift, 1)[:, :cols].astype(jnp.bfloat16)


def optics_kernel(amplitude, ones, columns, lines, amp_out, columns_out, lines_out):
    rows, pupil_cols = amplitude.shape
    for step in range(pupil_cols // LANES):
        cut = slice(step * LANES, (step + 1) * LANES)
        amp = amplitude[:, cut]
        energy = (amp * amp).reshape(rows // SUB_PIX, SUB_PIX, LANES).sum(axis=1)
        energy = jnp.broadcast_to(energy[:, None], (rows // SUB_PIX, SUB_PIX, LANES)).reshape(rows, LANES)
        total = jnp.dot(energy, ones[...], precision=lax.Precision.HIGHEST, preferred_element_type=jnp.float32)
        amp_out[:, cut] = amp * lax.rsqrt(total)
    columns_out[...] = columns[...].astype(jnp.bfloat16)
    lines_out[...] = lines[...].astype(jnp.bfloat16)


def sin_cos(phase):
    turns = jnp.floor(phase * (1.0 / np.pi) + 0.5)
    rest = phase - turns * 3.140625
    rest = rest - turns * 9.67653589793e-4
    odd = turns - 2.0 * jnp.floor(turns * 0.5)
    sign = 1.0 - 2.0 * odd
    square = rest * rest
    sine = -1.0 / 39916800.0
    for term in (1.0 / 362880.0, -1.0 / 5040.0, 1.0 / 120.0, -1.0 / 6.0, 1.0):
        sine = sine * square + term
    cosine = 1.0 / 479001600.0
    for term in (-1.0 / 3628800.0, 1.0 / 40320.0, -1.0 / 720.0, 1.0 / 24.0, -0.5, 1.0):
        cosine = cosine * square + term
    return sine * rest * sign, cosine * sign


def imaging_kernel(count, *refs):
    parts, (amp_ref, columns, lines, shifted, spots, screens, out, sems) = refs[:count], refs[count:]
    copies = fetch((shifted, screens, sems.at[0]))
    rows, cols = amp_ref.shape
    tiles = cols // LANES
    phase = parts[0][:, :cols].astype(jnp.float32)
    for part in parts[1:]:
        phase = phase + part[:, :cols].astype(jnp.float32)
    sine, cosine = sin_cos(phase)
    amp = amp_ref[...]
    real, imag = (amp * cosine).astype(jnp.bfloat16), (amp * sine).astype(jnp.bfloat16)
    cuts = [slice(t * LANES, (t + 1) * LANES) for t in range(tiles)]
    field = stack(*[beside(real[:, cut], imag[:, cut]) for cut in cuts])
    half = dot(field, columns[...]).astype(jnp.bfloat16)
    wide = 2 * LANES
    out_rows = 2 * rows
    for t in range(tiles):
        mine = half[t * rows : (t + 1) * rows]
        full = dot(lines[...], stack(mine[:, :wide], mine[:, wide:]))
        real, imag = full[:out_rows], full[out_rows:]
        out[:, t * wide : (t + 1) * wide] = real * real + imag * imag
        if t % 2:
            cut = slice((t - 1) * wide, (t + 1) * wide)
            copies += fetch((out.at[:, cut], spots.at[:, cut], sems.at[1 + t // 2]))
    for copy in copies:
        copy.wait()


def tables_of(rows):
    freq = np.arange(SPOT_PIX)[:, None] - SPOT_PIX // 2
    angle = ((freq * np.arange(SUB_PIX)[None, :]) % SPOT_PIX) * (2.0 * np.pi / SPOT_PIX)
    cos, sin = np.cos(angle), np.sin(angle)

    def blocks(table, count):
        return np.kron(np.eye(count), table)

    per_tile = LANES // SUB_PIX
    col_cos, col_sin = blocks(cos.T, per_tile), blocks(sin.T, per_tile)
    columns = np.block([[col_cos, -col_sin], [col_sin, col_cos]])
    count = rows // SUB_PIX
    row_cos, row_sin = blocks(cos, count), blocks(sin, count)
    lines = np.block([[row_cos, row_sin], [-row_sin, row_cos]])

    return columns.astype(np.float32), lines.astype(np.float32)


def per_device(screens, amplitude, wind, offsets, ratio):
    layers, rows_dev, cols_dev = screens.shape
    n_layer = lax.axis_size("layer")
    n_dir = lax.axis_size("dir")
    rows, pupil_cols = amplitude.shape
    pairs = n_layer // 2
    half = pairs * rows
    pupil_rows = 2 * half
    assert n_dir == 4 and rows == STRIP and pairs > 2
    bf16, f32 = jnp.bfloat16, jnp.float32
    wind = jnp.transpose(wind, (1, 0))
    offsets = jnp.transpose(offsets, (1, 2, 0))
    ratio = jnp.transpose(ratio, (1, 2, 0))
    smem, sem = pltpu.SMEM, pltpu.SemaphoreType.DMA
    wind_scratch = [smem(wind.shape, jnp.int32), sem]

    def shape(*dims, dtype=bf16):
        return jax.ShapeDtypeStruct(dims, dtype)

    def swap(value, bits):
        return lax.ppermute(value, "dir", [(i, i ^ bits) for i in range(n_dir)])

    def partner(value, bits=0):
        count = n_layer * n_dir
        return lax.ppermute(value, ("layer", "dir"), [(i, i ^ n_dir ^ bits) for i in range(count)])

    def turn(value, step):
        return lax.ppermute(value, "layer", [(i, (i + step) % n_layer) for i in range(n_layer)])

    width = cols_dev // 4
    chunk = shape(layers, rows_dev, width)
    keep0, keep1, give0, give1 = call(
        split_kernel,
        [chunk] * 4,
        (screens,),
        0,
        "split",
        in_hbm=(0,),
        scratch=[sem((4,))],
        brief=True,
    )
    across0 = swap(keep0, 2)
    diagonal0 = swap(give0, 3)
    near0 = swap(give0, 1)
    across1 = swap(keep1, 2)
    diagonal1 = swap(give1, 3)
    ones = np.kron(np.eye(LANES // SUB_PIX), np.ones((SUB_PIX, SUB_PIX))).astype(np.float32)
    optics_in = (amplitude, jnp.asarray(ones), *[jnp.asarray(table) for table in tables_of(rows)])
    copies = [shape(*array.shape, dtype=array.dtype) for array in (screens, *optics_in, wind)]
    row_weights, cols, *loaded = call(
        functools.partial(weights_kernel, (n_layer, rows_dev, cols_dev * n_layer)),
        [shape(2, layers, pupil_rows, 4 * rows_dev), shape(layers, cols_dev, pupil_cols)]
        + [shape(8, pupil_cols, dtype=dtype) for dtype in (jnp.int32, jnp.int32, f32, f32)]
        + copies,
        (wind, offsets, ratio, screens, *optics_in),
        0,
        "weights",
        in_hbm=range(8),
        scratch=[smem(array.shape, jnp.int32) for array in (wind, offsets, ratio)]
        + [sem((9,))],
        brief=True,
    )
    tables, (own, *optics_in, wind) = loaded[:4], loaded[4:]
    give1, own = lax.optimization_barrier((give1, own))
    near1 = swap(give1, 1)
    across0, diagonal0, row_weights, cols = lax.optimization_barrier((across0, diagonal0, row_weights, cols))

    projected = shape(layers, half, width)
    mine0, sibling0, other0, sibling_other0 = call(
        first_rows_kernel,
        [projected] * 4,
        (row_weights, across0, diagonal0, near0, keep0),
        0,
        "rows_first",
        brief=True,
    )
    came0 = partner(other0)
    sibling_came0 = partner(sibling_other0, 1)

    wind, mine0 = lax.optimization_barrier((wind, mine0))
    others, strip, sibling_strip = call(
        strips_kernel,
        [shape(layers, cols_dev, pupil_cols)] + [shape(STRIP, rows_dev)] * 2,
        (wind, *tables, across0, diagonal0, near0, keep0),
        0,
        "strips",
        scratch=wind_scratch,
        brief=True,
    )
    steps = strip_steps(pairs)
    far = len(steps) * rows
    message = shape(layers * far + STRIP * rows_dev // LANES, width)
    remainder = shape(max(layers * (half - far), message.shape[0] + 16), width)
    mine1, give, far1, sibling_far1, rest1, sibling_rest1 = call(
        later_rows_kernel,
        [projected, shape(layers, half + 64, 2 * width), message, message, remainder, remainder],
        (row_weights, across1, diagonal1, near1, keep1, across0, diagonal0, near0, keep0, sibling0, strip, sibling_strip),
        0,
        "rows_later",
        brief=True,
    )
    far1, sibling_far1 = partner(far1), partner(sibling_far1, 1)
    taken = swap(give, 1)
    phase = call(
        phase_kernel,
        shape(half, pupil_cols, dtype=f32),
        (cols, others, mine0, mine1, came0, sibling_came0),
        10_000_000_000,
        "phase",
    )

    rest1, sibling_rest1, phase = lax.optimization_barrier((rest1, sibling_rest1, phase))
    rest1, sibling_rest1 = partner(rest1), partner(sibling_rest1, 1)
    *far_sums, strips = call(
        far_kernel,
        [shape(rows, pupil_cols + rows_dev)] * len(steps) + [shape(2 * STRIP, rows_dev)],
        (cols, others, phase, taken, far1, sibling_far1),
        300_000_000,
        "far",
    )
    rest_sums = call(
        rest_kernel,
        [shape(rows, pupil_cols)] * (pairs - len(steps)),
        (cols, others, phase, taken, rest1, sibling_rest1),
        0,
        "rest",
        brief=True,
    )
    received = dict(zip(send_order(pairs), [*rest_sums, *far_sums]))
    for k in range(1, pairs):
        received[k] = lax.ppermute(received[k], "layer", [(i, i ^ (2 * k)) for i in range(n_layer)])
    received = [received[k] for k in range(pairs)]

    optics_in, received[-1] = lax.optimization_barrier((optics_in, received[-1]))
    optics = call(
        optics_kernel,
        (
            shape(rows, pupil_cols, dtype=f32),
            shape(*optics_in[2].shape),
            shape(*optics_in[3].shape),
        ),
        optics_in,
        0,
        "optics",
        brief=True,
    )
    received[1], optics = lax.optimization_barrier((received[1], optics))
    shifted = call(
        shift_kernel,
        shape(layers, rows_dev, cols_dev),
        (wind, own, near0, near1, diagonal0, diagonal1, taken, strips, *[received[k] for k in steps]),
        0,
        "shift",
        scratch=wind_scratch,
        brief=True,
    )
    spots_shape = shape(2 * rows, 2 * pupil_cols, dtype=f32)
    spots, new_screens = call(
        functools.partial(imaging_kernel, pairs),
        [spots_shape, shape(layers, rows_dev, cols_dev)],
        (*received, *optics, shifted),
        400_000_000,
        "imaging",
        out_hbm=(0, 1),
        scratch=[pltpu.VMEM(spots_shape.shape, f32), sem((1 + pupil_cols // (2 * LANES),))],
    )
    return (new_screens, spots[None])


def solution(mesh):
    return jax.shard_map(
        per_device,
        mesh=mesh,
        in_specs=(P(None, "dir", "layer"), P("layer", None), P(), P(), P()),
        out_specs=(P(None, "dir", "layer"), P("dir", "layer", None)),
        check_vma=False,
    )
```

```python
import functools

import jax
import jax.numpy as jnp
import numpy as np
from jax import lax
from jax.experimental import pallas as pl
from jax.experimental.pallas import tpu as pltpu
from jax.sharding import PartitionSpec as P

SUB_PIX = 16
SPOT_PIX = 32
WIND_MAX = 8
LANES = 128
STRIP = 32

HBM_SPEC = pl.BlockSpec(memory_space=pltpu.HBM)
VMEM_SPEC = pl.BlockSpec(memory_space=pltpu.VMEM)


def params(*arrays):
    held = sum(array.size * array.dtype.itemsize for array in jax.tree.leaves(arrays))
    return pltpu.CompilerParams(vmem_limit_bytes=held + 8 * 1024 * 1024)


def call(kernel, out_shape, operands, flops, name, in_hbm=(), out_hbm=(), scratch=(), brief=False):
    def spec(k, array):
        return HBM_SPEC if k in in_hbm else VMEM_SPEC

    if out_hbm:
        out_specs = [HBM_SPEC if k in out_hbm else VMEM_SPEC for k in range(len(out_shape))]
    else:
        out_specs = jax.tree.map(lambda _: VMEM_SPEC, out_shape)
    size = sum(array.size * array.dtype.itemsize for array in jax.tree.leaves((operands, out_shape)))
    if brief:
        flops = size = 0
    in_specs = [spec(k, array) for k, array in enumerate(operands)]
    operands = [
        pltpu.with_memory_space_constraint(array, pltpu.HBM) if space is HBM_SPEC else array
        for array, space in zip(operands, in_specs)
    ]
    return pl.pallas_call(
        kernel,
        out_shape=out_shape,
        in_specs=in_specs,
        out_specs=out_specs,
        scratch_shapes=list(scratch),
        compiler_params=params(operands, out_shape),
        cost_estimate=pl.CostEstimate(flops=flops, bytes_accessed=size, transcendentals=0),
        name=name,
    )(*operands)


def fetch(*pairs):
    copies = [pltpu.make_async_copy(source, target, sem) for source, target, sem in pairs]
    for copy in copies:
        copy.start()
    return copies


def wrap(value, length):
    value = jnp.where(value < 0, value + length, value)
    return jnp.where(value >= length, value - length, value)


def stack(*blocks):
    return jnp.concatenate(blocks, axis=0)


def beside(*blocks):
    return jnp.concatenate(blocks, axis=1)


def dot(left, right):
    return jnp.dot(left, right, preferred_element_type=jnp.float32)


def spans(pixel, anchor, num, den, length):
    stretched = (pixel * num).astype(jnp.float32)
    den = (jnp.zeros_like(pixel) + den).astype(jnp.float32)
    whole = jnp.floor((stretched + 0.5) / den)
    fraction = (stretched - whole * den) / den
    base = wrap(anchor + whole.astype(jnp.int32), length)
    upper = wrap(base + 1, length)
    return base, upper, 1.0 - fraction, fraction


def chunk_start(half, chunk):
    return 3 * half + chunk * (1 - 2 * half)


def split_kernel(screens, *refs):
    outs, sems = refs[:-1], refs[-1]
    width = outs[0].shape[2]
    core = lax.rem(lax.axis_index("dir"), 2)
    pairs = []
    for k, out in enumerate(outs):
        half = core if k < 2 else 1 - core
        start = pl.multiple_of(chunk_start(half, k % 2) * width, LANES)
        pairs.append((screens.at[:, :, pl.ds(start, width)], out, sems.at[k]))
    for load in fetch(*pairs):
        load.wait()


def weights_kernel(geometry, wind_hbm, offsets_hbm, ratio_hbm, *refs):
    n_layer, rows_dev, screen_cols = geometry
    sources, (rows_out, cols_out, *tables), refs = refs[:5], refs[5:11], refs[11:]
    copies, (wind_copy, wind, offsets, ratio, sems) = refs[:5], refs[5:]
    pupil_cols = cols_out.shape[2]
    pairs = [*zip(sources, copies), (wind_hbm, wind_copy)]
    others = fetch(*[(source, copy, sems.at[3 + k]) for k, (source, copy) in enumerate(pairs)])
    loads = fetch(
        (wind_hbm, wind, sems.at[0]),
        (offsets_hbm, offsets, sems.at[1]),
        (ratio_hbm, ratio, sems.at[2]),
    )
    _, layers, pupil_rows, screen_rows = rows_out.shape
    half = pupil_rows // 2
    direction = lax.axis_index("dir")
    column = lax.axis_index("layer")
    block = pupil_rows // n_layer
    row = lax.broadcasted_iota(jnp.int32, (half, LANES), 0)
    step = row // block
    for at, value in enumerate(send_order(n_layer // 2)):
        step = jnp.where(row // block == at, value, step)
    pair = jnp.bitwise_xor(step, column // 2)
    parity = lax.rem(column, 2)
    inside = lax.rem(row, block) + pair * (2 * block)
    pixel_rows = stack(inside + parity * block, inside + (1 - parity) * block)
    lane = lax.broadcasted_iota(jnp.int32, (pupil_rows, LANES), 1)
    for load in loads:
        load.wait()
    for side in range(2):
        target = jnp.bitwise_xor(direction, side)
        for level in range(layers):
            anchor = wrap(offsets[level, 0, target] - wind[0, level], screen_rows)
            num, den = ratio[level, 0, target], ratio[level, 1, target]
            base, upper, low, high = spans(pixel_rows, anchor, num, den, screen_rows)
            for peer in range(4):
                for part in range(rows_dev // LANES):
                    index = lane + (jnp.bitwise_xor(direction, peer) * rows_dev + part * LANES)
                    weight = jnp.where(index == base, low, 0.0)
                    weight = jnp.where(index == upper, high, weight)
                    start = peer * rows_dev + part * LANES
                    rows_out[side, level, :, start : start + LANES] = weight.astype(jnp.bfloat16)
    sub = lax.broadcasted_iota(jnp.int32, (8, LANES), 0)
    anchor, num, den = jnp.zeros_like(sub), jnp.zeros_like(sub), jnp.ones_like(sub)
    for level in range(layers):
        start = wrap(offsets[level, 1, direction] - wind[1, level], screen_cols)
        anchor = jnp.where(sub == level, start, anchor)
        num = jnp.where(sub == level, ratio[level, 0, direction], num)
        den = jnp.where(sub == level, ratio[level, 1, direction], den)
    for at in range(0, pupil_cols, LANES):
        pixel = lax.broadcasted_iota(jnp.int32, (8, LANES), 1) + at
        values = spans(pixel, anchor, num, den, screen_cols)
        for table, value in zip(tables, values):
            table[:, at : at + LANES] = value
    column_weights(*tables, column * cols_out.shape[1], cols_out)
    for load in others:
        load.wait()


def column_weights(base_ref, upper_ref, low_ref, high_ref, first, out):
    layers, cols_dev, pupil_cols = out.shape
    width = cols_dev // 4
    core = lax.rem(lax.axis_index("dir"), 2)
    sub = lax.broadcasted_iota(jnp.int32, (width, LANES), 0).astype(jnp.float32).astype(jnp.bfloat16)
    zero = jnp.zeros((width, LANES), jnp.bfloat16)
    for level in range(layers):

        def tile(step, carry):
            start = pl.multiple_of(step * LANES, LANES)
            cut = (slice(level, level + 1), pl.ds(start, LANES))
            base, upper = base_ref[cut], upper_ref[cut]
            low, high = [
                jnp.broadcast_to(ref[cut].astype(jnp.bfloat16), (width, LANES)) for ref in (low_ref, high_ref)
            ]
            for k in range(4):
                shift = first + chunk_start(jnp.bitwise_xor(core, k // 2), k % 2) * width
                base_at, upper_at = [
                    jnp.broadcast_to(
                        jnp.clip(value - shift, -1, width).astype(jnp.float32).astype(jnp.bfloat16), (width, LANES)
                    )
                    for value in (base, upper)
                ]
                weight = jnp.where(sub == base_at, low, zero)
                weight = jnp.where(sub == upper_at, high, weight)
                out[level, k * width : (k + 1) * width, pl.ds(start, LANES)] = weight
            return carry

        lax.fori_loop(0, pupil_cols // LANES, tile, 0)


def strips_kernel(wind_held, *refs):
    tables, (across, diagonal, near, keep, cols_out, strip, sibling_strip, wind, sem) = refs[:4], refs[4:]
    load = fetch((wind_held, wind, sem))[0]
    column_weights(*tables, jnp.bitwise_xor(lax.axis_index("layer"), 1) * cols_out.shape[1], cols_out)
    layers, rows, _ = keep.shape
    core = lax.rem(lax.axis_index("dir"), 2)
    odd = core == 1
    lane = lax.broadcasted_iota(jnp.int32, (rows + 32, LANES), 1)

    def wide(own, near, far, odd, level):
        own, near, far = [block[level].astype(jnp.float32) for block in (own, near, far)]
        before = jnp.where(odd, near[rows - 16 :], far[rows - 16 :])
        return stack(before, own, jnp.where(odd, far[:16], near[:16]))

    packed = jnp.zeros((rows + 32, LANES), jnp.float32)
    for level in range(layers):
        blocks = (keep, near, diagonal, odd), (near, keep, across, core == 0)
        for at, block in zip((WIND_MAX * level, STRIP + WIND_MAX * level), blocks):
            block = pltpu.roll(wide(*block, level), at + WIND_MAX * core, 1)
            packed = jnp.where((lane >= at) & (lane < at + WIND_MAX), block, packed)
    load.wait()
    strips = jnp.zeros((rows, LANES), jnp.float32)
    for level in range(layers):
        shift = wind[0, level]
        shift = jnp.where(shift < 0, shift + rows + 32, shift)
        moved = pltpu.roll(packed, shift, 0)[16 : 16 + rows]
        mine = lax.rem(lane[:rows], STRIP)
        strips = jnp.where((mine >= WIND_MAX * level) & (mine < WIND_MAX * (level + 1)), moved, strips)
    strips = strips.T.astype(jnp.bfloat16)
    strip[...] = strips[:STRIP]
    sibling_strip[...] = strips[STRIP : 2 * STRIP]


def project_rows(rows_ref, keep, near, across, diagonal, level):
    screen = stack(keep[level], near[level], across[level], diagonal[level])
    rows = stack(rows_ref[0, level], rows_ref[1, level])
    return dot(rows, screen).astype(jnp.bfloat16)


def first_rows_kernel(rows_ref, across, diagonal, near, keep, mine, sibling, other, sibling_other):
    layers, half, _ = mine.shape
    for level in range(layers):
        part = project_rows(rows_ref, keep, near, across, diagonal, level)
        for k, out in enumerate((mine, other, sibling, sibling_other)):
            out[level] = part[k * half : (k + 1) * half]


def put_strip(out, at, strip):
    for k in range(strip.shape[1] // LANES):
        out[at + k * STRIP : at + (k + 1) * STRIP, :] = strip[:, k * LANES : (k + 1) * LANES]


def get_strip(ref, at):
    return beside(*[ref[start : start + STRIP, :] for start in range(at, ref.shape[0], STRIP)])


def later_rows_kernel(rows_ref, *refs):
    chunks, refs = refs[:8], refs[8:]
    sibling0, strip, sibling_strip, mine, give, far, sibling_far, rest, sibling_rest = refs
    across, diagonal, near, keep, across0, diagonal0, near0, keep0 = chunks
    layers, half, width = mine.shape
    rows = near.shape[1]
    size = (far.shape[0] - STRIP * rows // LANES) // layers
    start = half - size
    for level in range(layers):
        part = project_rows(rows_ref, keep, near, across, diagonal, level)
        mine[level] = part[:half]
        for k, out, remainder in ((1, far, rest), (3, sibling_far, sibling_rest)):
            piece = part[k * half : (k + 1) * half]
            out[level * size : (level + 1) * size] = piece[start:]
            remainder[level * start : (level + 1) * start] = piece[:start]
        give[level, :half, :width] = sibling0[level]
        give[level, :half, width:] = part[2 * half : 3 * half]
        for k, blocks in enumerate(((across0, keep0), (across, keep))):
            cut = slice(k * width, (k + 1) * width)
            edges = [block[level, at : at + 16] for block in blocks for at in (0, rows - 16)]
            give[level, half:, cut] = stack(*edges)
    put_strip(far, layers * size, strip)
    put_strip(sibling_far, layers * size, sibling_strip)


def project(parts, cols_refs, at):
    cols = stack(*[ref[level, start:stop, at : at + 256] for ref, level, start, stop in cols_refs])
    return dot(beside(*parts), cols)


def phase_kernel(mine_ref, other_ref, mine0, mine1, came, sibling_came, phase):
    layers, _, width = mine0.shape
    parts, cuts = [], []
    for level in range(layers):
        parts += [mine0[level], mine1[level], came[level], sibling_came[level]]
        cuts += [(mine_ref, level, 0, 2 * width)]
        cuts += [(other_ref, level, 0, width), (other_ref, level, 2 * width, 3 * width)]
    for at in range(0, phase.shape[1], 256):
        phase[:, at : at + 256] = project(parts, cuts, at)


def sum_up(start, mine_ref, cols_ref, phase, taken, came, sibling_came, outs):
    layers, _, width = taken.shape
    width = width // 2
    block = outs[0].shape[0]
    size = block * len(outs)
    rows = slice(start, start + size)
    parts, cuts = [], []
    for level in range(layers):
        cut = slice(level * size, (level + 1) * size)
        parts += [taken[level, rows], came[cut], sibling_came[cut]]
        cuts += [(mine_ref, level, 2 * width, 4 * width)]
        cuts += [(cols_ref, level, width, 2 * width), (cols_ref, level, 3 * width, 4 * width)]
    pupil_cols = phase.shape[1]
    for at in range(0, pupil_cols, 256):
        total = (phase[rows, at : at + 256] + project(parts, cuts, at)).astype(jnp.bfloat16)
        for k, out in enumerate(outs):
            out[:, at : at + 256] = total[k * block : (k + 1) * block]


def strip_steps(pairs):
    return [2**k - 1 for k in range(1, pairs.bit_length())]


def send_order(pairs):
    steps = strip_steps(pairs)
    return [k for k in range(pairs) if k not in steps] + steps


def add_strip(pairs, step, strips, out):
    pair = lax.axis_index("layer") // 2
    after = lax.rem(pair + 1, pairs) == jnp.bitwise_xor(pair, step)
    at = out.shape[1] - strips.shape[1]
    last, first = strips[:STRIP].astype(jnp.float32), strips[STRIP:].astype(jnp.float32)
    out[:, at:] = jnp.where(after, last, first).astype(jnp.bfloat16)


def far_kernel(mine_ref, cols_ref, phase, taken, came, sibling_came, *outs):
    *outs, strips = outs
    half = phase.shape[0]
    size = outs[0].shape[0] * len(outs)
    sum_up(half - size, mine_ref, cols_ref, phase, taken, came, sibling_came, outs)
    layers = taken.shape[0]
    odd = lax.rem(lax.axis_index("dir"), 2) == 1
    here = get_strip(came, layers * size).astype(jnp.float32)
    there = get_strip(sibling_came, layers * size).astype(jnp.float32)
    strips[:STRIP] = jnp.where(odd, here, there).astype(jnp.bfloat16)
    strips[STRIP:] = jnp.where(odd, there, here).astype(jnp.bfloat16)
    pairs = half // outs[0].shape[0]
    for out, step in zip(outs, strip_steps(pairs)):
        add_strip(pairs, step, strips, out)


def rest_kernel(mine_ref, cols_ref, phase, taken, came, sibling_came, *outs):
    sum_up(0, mine_ref, cols_ref, phase, taken, came, sibling_came, outs)


def shifted_rows(shift, odd, own, near, far):
    own, near, far = [block.astype(jnp.float32) for block in (own, near, far)]
    rows = own.shape[0]
    before = jnp.where(odd, near[16:], far[16:])
    after = jnp.where(odd, far[:16], near[:16])
    shift = jnp.where(shift < 0, shift + rows + 32, shift)
    return pltpu.roll(stack(before, own, after), shift, 0)[16 : 16 + rows]


def shift_kernel(wind_held, own, near0, near1, diagonal0, diagonal1, taken, partner_strips, *refs):
    messages, (out, wind, sem) = refs[:-3], refs[-3:]
    load = fetch((wind_held, wind, sem))[0]
    layers, rows, cols = own.shape
    odd = lax.rem(lax.axis_index("dir"), 2) == 1
    half = taken.shape[1] - 64
    pairs = 2 ** len(messages)
    pair, second = lax.axis_index("layer") // 2, lax.rem(lax.axis_index("layer"), 2) == 1
    before = jnp.bitwise_xor(pair, lax.rem(pair + pairs - 1, pairs))
    after = jnp.bitwise_xor(pair, lax.rem(pair + 1, pairs))
    left = partner_strips[:STRIP].astype(jnp.float32)
    right = partner_strips[STRIP:].astype(jnp.float32)
    for step, message in zip(strip_steps(pairs), messages):
        strip = message[:, message.shape[1] - rows :].astype(jnp.float32)
        left = jnp.where(jnp.logical_and(before == step, jnp.logical_not(second)), strip, left)
        right = jnp.where(jnp.logical_and(after == step, second), strip, right)
    strips = stack(left, right, jnp.zeros((LANES - 2 * STRIP, rows), jnp.float32)).T
    lane = lax.broadcasted_iota(jnp.int32, (rows, LANES), 1)
    load.wait()
    for level in range(layers):
        last = pltpu.roll(strips, LANES - WIND_MAX * (level + 1), 1)
        first = pltpu.roll(strips, LANES - STRIP - WIND_MAX * level, 1)
        extra = jnp.where(lane < WIND_MAX, first, last)
        pair = []
        for at, parts in ((half, (diagonal0, diagonal1)), (half + 32, (near0, near1))):
            here = [stack(part[level, :16], part[level, rows - 16 :]).astype(jnp.float32) for part in parts]
            there = taken[level, at : at + 32].astype(jnp.float32)
            width = there.shape[1] // 2
            quarters = [*here, there[:, width:], there[:, :width]]
            pair.append(beside(*[jnp.where(odd, quarters[3 - k], quarters[k]) for k in range(4)]))
        far, near = pair
        moved = shifted_rows(wind[0, level], odd, own[level], near, far)
        shift = wind[1, level]
        shift = jnp.where(shift < 0, shift + cols + LANES, shift)
        out[level] = pltpu.roll(beside(moved, extra), shift, 1)[:, :cols].astype(jnp.bfloat16)


def optics_kernel(amplitude, ones, columns, lines, amp_out, columns_out, lines_out):
    rows, pupil_cols = amplitude.shape
    for step in range(pupil_cols // LANES):
        cut = slice(step * LANES, (step + 1) * LANES)
        amp = amplitude[:, cut]
        energy = (amp * amp).reshape(rows // SUB_PIX, SUB_PIX, LANES).sum(axis=1)
        energy = jnp.broadcast_to(energy[:, None], (rows // SUB_PIX, SUB_PIX, LANES)).reshape(rows, LANES)
        total = jnp.dot(energy, ones[...], precision=lax.Precision.HIGHEST, preferred_element_type=jnp.float32)
        amp_out[:, cut] = amp * lax.rsqrt(total)
    columns_out[...] = columns[...].astype(jnp.bfloat16)
    lines_out[...] = lines[...].astype(jnp.bfloat16)


def sin_cos(phase):
    turns = jnp.floor(phase * (1.0 / np.pi) + 0.5)
    rest = phase - turns * 3.140625
    rest = rest - turns * 9.67653589793e-4
    odd = turns - 2.0 * jnp.floor(turns * 0.5)
    sign = 1.0 - 2.0 * odd
    square = rest * rest
    sine = -1.0 / 39916800.0
    for term in (1.0 / 362880.0, -1.0 / 5040.0, 1.0 / 120.0, -1.0 / 6.0, 1.0):
        sine = sine * square + term
    cosine = 1.0 / 479001600.0
    for term in (-1.0 / 3628800.0, 1.0 / 40320.0, -1.0 / 720.0, 1.0 / 24.0, -0.5, 1.0):
        cosine = cosine * square + term
    return sine * rest * sign, cosine * sign


def imaging_kernel(count, *refs):
    parts, (amp_ref, columns, lines, shifted, spots, screens, out, sems) = refs[:count], refs[count:]
    copies = fetch((shifted, screens, sems.at[0]))
    rows, cols = amp_ref.shape
    tiles = cols // LANES
    phase = parts[0][:, :cols].astype(jnp.float32)
    for part in parts[1:]:
        phase = phase + part[:, :cols].astype(jnp.float32)
    sine, cosine = sin_cos(phase)
    amp = amp_ref[...]
    real, imag = (amp * cosine).astype(jnp.bfloat16), (amp * sine).astype(jnp.bfloat16)
    cuts = [slice(t * LANES, (t + 1) * LANES) for t in range(tiles)]
    field = stack(*[beside(real[:, cut], imag[:, cut]) for cut in cuts])
    half = dot(field, columns[...]).astype(jnp.bfloat16)
    wide = 2 * LANES
    out_rows = 2 * rows
    for t in range(tiles):
        mine = half[t * rows : (t + 1) * rows]
        full = dot(lines[...], stack(mine[:, :wide], mine[:, wide:]))
        real, imag = full[:out_rows], full[out_rows:]
        out[:, t * wide : (t + 1) * wide] = real * real + imag * imag
        if t % 2:
            cut = slice((t - 1) * wide, (t + 1) * wide)
            copies += fetch((out.at[:, cut], spots.at[:, cut], sems.at[1 + t // 2]))
    for copy in copies:
        copy.wait()


def tables_of(rows):
    freq = np.arange(SPOT_PIX)[:, None] - SPOT_PIX // 2
    angle = ((freq * np.arange(SUB_PIX)[None, :]) % SPOT_PIX) * (2.0 * np.pi / SPOT_PIX)
    cos, sin = np.cos(angle), np.sin(angle)

    def blocks(table, count):
        return np.kron(np.eye(count), table)

    per_tile = LANES // SUB_PIX
    col_cos, col_sin = blocks(cos.T, per_tile), blocks(sin.T, per_tile)
    columns = np.block([[col_cos, -col_sin], [col_sin, col_cos]])
    count = rows // SUB_PIX
    row_cos, row_sin = blocks(cos, count), blocks(sin, count)
    lines = np.block([[row_cos, row_sin], [-row_sin, row_cos]])

    return columns.astype(np.float32), lines.astype(np.float32)


def per_device(screens, amplitude, wind, offsets, ratio):
    layers, rows_dev, cols_dev = screens.shape
    n_layer = lax.axis_size("layer")
    n_dir = lax.axis_size("dir")
    rows, pupil_cols = amplitude.shape
    pairs = n_layer // 2
    half = pairs * rows
    pupil_rows = 2 * half
    assert n_dir == 4 and rows == STRIP and pairs > 2
    bf16, f32 = jnp.bfloat16, jnp.float32
    wind = jnp.transpose(wind, (1, 0))
    offsets = jnp.transpose(offsets, (1, 2, 0))
    ratio = jnp.transpose(ratio, (1, 2, 0))
    smem, sem = pltpu.SMEM, pltpu.SemaphoreType.DMA
    wind_scratch = [smem(wind.shape, jnp.int32), sem]

    def shape(*dims, dtype=bf16):
        return jax.ShapeDtypeStruct(dims, dtype)

    def swap(value, bits):
        return lax.ppermute(value, "dir", [(i, i ^ bits) for i in range(n_dir)])

    def partner(value, bits=0):
        count = n_layer * n_dir
        return lax.ppermute(value, ("layer", "dir"), [(i, i ^ n_dir ^ bits) for i in range(count)])

    def turn(value, step):
        return lax.ppermute(value, "layer", [(i, (i + step) % n_layer) for i in range(n_layer)])

    width = cols_dev // 4
    chunk = shape(layers, rows_dev, width)
    keep0, keep1, give0, give1 = call(
        split_kernel,
        [chunk] * 4,
        (screens,),
        0,
        "split",
        in_hbm=(0,),
        scratch=[sem((4,))],
        brief=True,
    )
    across0 = swap(keep0, 2)
    diagonal0 = swap(give0, 3)
    near0 = swap(give0, 1)
    across1 = swap(keep1, 2)
    diagonal1 = swap(give1, 3)
    ones = np.kron(np.eye(LANES // SUB_PIX), np.ones((SUB_PIX, SUB_PIX))).astype(np.float32)
    optics_in = (amplitude, jnp.asarray(ones), *[jnp.asarray(table) for table in tables_of(rows)])
    copies = [shape(*array.shape, dtype=array.dtype) for array in (screens, *optics_in, wind)]
    row_weights, cols, *loaded = call(
        functools.partial(weights_kernel, (n_layer, rows_dev, cols_dev * n_layer)),
        [shape(2, layers, pupil_rows, 4 * rows_dev), shape(layers, cols_dev, pupil_cols)]
        + [shape(8, pupil_cols, dtype=dtype) for dtype in (jnp.int32, jnp.int32, f32, f32)]
        + copies,
        (wind, offsets, ratio, screens, *optics_in),
        0,
        "weights",
        in_hbm=range(8),
        scratch=[smem(array.shape, jnp.int32) for array in (wind, offsets, ratio)]
        + [sem((9,))],
        brief=True,
    )
    tables, (own, *optics_in, wind) = loaded[:4], loaded[4:]
    give1, own = lax.optimization_barrier((give1, own))
    near1 = swap(give1, 1)
    across0, diagonal0, row_weights, cols = lax.optimization_barrier((across0, diagonal0, row_weights, cols))

    projected = shape(layers, half, width)
    mine0, sibling0, other0, sibling_other0 = call(
        first_rows_kernel,
        [projected] * 4,
        (row_weights, across0, diagonal0, near0, keep0),
        0,
        "rows_first",
        brief=True,
    )
    came0 = partner(other0)
    sibling_came0 = partner(sibling_other0, 1)

    wind, mine0 = lax.optimization_barrier((wind, mine0))
    others, strip, sibling_strip = call(
        strips_kernel,
        [shape(layers, cols_dev, pupil_cols)] + [shape(STRIP, rows_dev)] * 2,
        (wind, *tables, across0, diagonal0, near0, keep0),
        0,
        "strips",
        scratch=wind_scratch,
        brief=True,
    )
    steps = strip_steps(pairs)
    far = len(steps) * rows
    message = shape(layers * far + STRIP * rows_dev // LANES, width)
    remainder = shape(layers * (half - far), width)
    mine1, give, far1, sibling_far1, rest1, sibling_rest1 = call(
        later_rows_kernel,
        [projected, shape(layers, half + 64, 2 * width), message, message, remainder, remainder],
        (row_weights, across1, diagonal1, near1, keep1, across0, diagonal0, near0, keep0, sibling0, strip, sibling_strip),
        0,
        "rows_later",
        brief=True,
    )
    far1, sibling_far1 = partner(far1), partner(sibling_far1, 1)
    taken = swap(give, 1)
    phase = call(
        phase_kernel,
        shape(half, pupil_cols, dtype=f32),
        (cols, others, mine0, mine1, came0, sibling_came0),
        10_000_000_000,
        "phase",
    )

    rest1, sibling_rest1, phase = lax.optimization_barrier((rest1, sibling_rest1, phase))
    rest1, sibling_rest1 = partner(rest1), partner(sibling_rest1, 1)
    *far_sums, strips = call(
        far_kernel,
        [shape(rows, pupil_cols + rows_dev)] * len(steps) + [shape(2 * STRIP, rows_dev)],
        (cols, others, phase, taken, far1, sibling_far1),
        300_000_000,
        "far",
    )
    rest_sums = call(
        rest_kernel,
        [shape(rows, pupil_cols)] * (pairs - len(steps)),
        (cols, others, phase, taken, rest1, sibling_rest1),
        0,
        "rest",
        brief=True,
    )
    received = dict(zip(send_order(pairs), [*rest_sums, *far_sums]))
    for k in range(1, pairs):
        received[k] = lax.ppermute(received[k], "layer", [(i, i ^ (2 * k)) for i in range(n_layer)])
    received = [received[k] for k in range(pairs)]

    optics_in, received[-1] = lax.optimization_barrier((optics_in, received[-1]))
    optics = call(
        optics_kernel,
        (
            shape(rows, pupil_cols, dtype=f32),
            shape(*optics_in[2].shape),
            shape(*optics_in[3].shape),
        ),
        optics_in,
        0,
        "optics",
        brief=True,
    )
    received[1], optics = lax.optimization_barrier((received[1], optics))
    shifted = call(
        shift_kernel,
        shape(layers, rows_dev, cols_dev),
        (wind, own, near0, near1, diagonal0, diagonal1, taken, strips, *[received[k] for k in steps]),
        0,
        "shift",
        scratch=wind_scratch,
        brief=True,
    )
    spots_shape = shape(2 * rows, 2 * pupil_cols, dtype=f32)
    spots, new_screens = call(
        functools.partial(imaging_kernel, pairs),
        [spots_shape, shape(layers, rows_dev, cols_dev)],
        (*received, *optics, shifted),
        400_000_000,
        "imaging",
        out_hbm=(0, 1),
        scratch=[pltpu.VMEM(spots_shape.shape, f32), sem((1 + pupil_cols // (2 * LANES),))],
    )
    return (new_screens, spots[None])


def solution(mesh):
    return jax.shard_map(
        per_device,
        mesh=mesh,
        in_specs=(P(None, "dir", "layer"), P("layer", None), P(), P(), P()),
        out_specs=(P(None, "dir", "layer"), P("dir", "layer", None)),
        check_vma=False,
    )
```

```python
import functools

import jax
import jax.numpy as jnp
import numpy as np
from jax import lax
from jax.experimental import pallas as pl
from jax.experimental.pallas import tpu as pltpu
from jax.sharding import PartitionSpec as P

SUB_PIX = 16
SPOT_PIX = 32
WIND_MAX = 8
LANES = 128
STRIP = 32

HBM_SPEC = pl.BlockSpec(memory_space=pltpu.HBM)
VMEM_SPEC = pl.BlockSpec(memory_space=pltpu.VMEM)


def params(*arrays):
    held = sum(array.size * array.dtype.itemsize for array in jax.tree.leaves(arrays))
    return pltpu.CompilerParams(vmem_limit_bytes=held + 8 * 1024 * 1024)


def call(kernel, out_shape, operands, flops, name, in_hbm=(), out_hbm=(), scratch=(), brief=False):
    def spec(k, array):
        return HBM_SPEC if k in in_hbm else VMEM_SPEC

    if out_hbm:
        out_specs = [HBM_SPEC if k in out_hbm else VMEM_SPEC for k in range(len(out_shape))]
    else:
        out_specs = jax.tree.map(lambda _: VMEM_SPEC, out_shape)
    size = sum(array.size * array.dtype.itemsize for array in jax.tree.leaves((operands, out_shape)))
    if brief:
        flops = size = 0
    in_specs = [spec(k, array) for k, array in enumerate(operands)]
    operands = [
        pltpu.with_memory_space_constraint(array, pltpu.HBM) if space is HBM_SPEC else array
        for array, space in zip(operands, in_specs)
    ]
    return pl.pallas_call(
        kernel,
        out_shape=out_shape,
        in_specs=in_specs,
        out_specs=out_specs,
        scratch_shapes=list(scratch),
        compiler_params=params(operands, out_shape),
        cost_estimate=pl.CostEstimate(flops=flops, bytes_accessed=size, transcendentals=0),
        name=name,
    )(*operands)


def fetch(*pairs):
    copies = [pltpu.make_async_copy(source, target, sem) for source, target, sem in pairs]
    for copy in copies:
        copy.start()
    return copies


def wrap(value, length):
    value = jnp.where(value < 0, value + length, value)
    return jnp.where(value >= length, value - length, value)


def stack(*blocks):
    return jnp.concatenate(blocks, axis=0)


def beside(*blocks):
    return jnp.concatenate(blocks, axis=1)


def dot(left, right):
    return jnp.dot(left, right, preferred_element_type=jnp.float32)


def spans(pixel, anchor, num, den, length):
    stretched = (pixel * num).astype(jnp.float32)
    den = (jnp.zeros_like(pixel) + den).astype(jnp.float32)
    whole = jnp.floor((stretched + 0.5) / den)
    fraction = (stretched - whole * den) / den
    base = wrap(anchor + whole.astype(jnp.int32), length)
    upper = wrap(base + 1, length)
    return base, upper, 1.0 - fraction, fraction


def chunk_start(half, chunk):
    return 3 * half + chunk * (1 - 2 * half)


def split_kernel(screens, *refs):
    outs, sems = refs[:-1], refs[-1]
    width = outs[0].shape[2]
    core = lax.rem(lax.axis_index("dir"), 2)
    pairs = []
    for k, out in enumerate(outs):
        half = core if k < 2 else 1 - core
        start = pl.multiple_of(chunk_start(half, k % 2) * width, LANES)
        pairs.append((screens.at[:, :, pl.ds(start, width)], out, sems.at[k]))
    for load in fetch(*pairs):
        load.wait()


def weights_kernel(geometry, wind_hbm, offsets_hbm, ratio_hbm, *refs):
    n_layer, rows_dev, screen_cols = geometry
    sources, (rows_out, cols_out, *tables), refs = refs[:5], refs[5:11], refs[11:]
    copies, (wind_copy, wind, offsets, ratio, sems) = refs[:5], refs[5:]
    pupil_cols = cols_out.shape[2]
    pairs = [*zip(sources, copies), (wind_hbm, wind_copy)]
    others = fetch(*[(source, copy, sems.at[3 + k]) for k, (source, copy) in enumerate(pairs)])
    loads = fetch(
        (wind_hbm, wind, sems.at[0]),
        (offsets_hbm, offsets, sems.at[1]),
        (ratio_hbm, ratio, sems.at[2]),
    )
    _, layers, pupil_rows, screen_rows = rows_out.shape
    half = pupil_rows // 2
    direction = lax.axis_index("dir")
    column = lax.axis_index("layer")
    block = pupil_rows // n_layer
    row = lax.broadcasted_iota(jnp.int32, (half, LANES), 0)
    step = row // block
    for at, value in enumerate(send_order(n_layer // 2)):
        step = jnp.where(row // block == at, value, step)
    pair = jnp.bitwise_xor(step, column // 2)
    parity = lax.rem(column, 2)
    inside = lax.rem(row, block) + pair * (2 * block)
    pixel_rows = stack(inside + parity * block, inside + (1 - parity) * block)
    lane = lax.broadcasted_iota(jnp.int32, (pupil_rows, LANES), 1)
    for load in loads:
        load.wait()
    for side in range(2):
        target = jnp.bitwise_xor(direction, side)
        for level in range(layers):
            anchor = wrap(offsets[level, 0, target] - wind[0, level], screen_rows)
            num, den = ratio[level, 0, target], ratio[level, 1, target]
            base, upper, low, high = spans(pixel_rows, anchor, num, den, screen_rows)
            for peer in range(4):
                for part in range(rows_dev // LANES):
                    index = lane + (jnp.bitwise_xor(direction, peer) * rows_dev + part * LANES)
                    weight = jnp.where(index == base, low, 0.0)
                    weight = jnp.where(index == upper, high, weight)
                    start = peer * rows_dev + part * LANES
                    rows_out[side, level, :, start : start + LANES] = weight.astype(jnp.bfloat16)
    sub = lax.broadcasted_iota(jnp.int32, (8, LANES), 0)
    anchor, num, den = jnp.zeros_like(sub), jnp.zeros_like(sub), jnp.ones_like(sub)
    for level in range(layers):
        start = wrap(offsets[level, 1, direction] - wind[1, level], screen_cols)
        anchor = jnp.where(sub == level, start, anchor)
        num = jnp.where(sub == level, ratio[level, 0, direction], num)
        den = jnp.where(sub == level, ratio[level, 1, direction], den)
    for at in range(0, pupil_cols, LANES):
        pixel = lax.broadcasted_iota(jnp.int32, (8, LANES), 1) + at
        values = spans(pixel, anchor, num, den, screen_cols)
        for table, value in zip(tables, values):
            table[:, at : at + LANES] = value
    column_weights(*tables, column * cols_out.shape[1], cols_out)
    for load in others:
        load.wait()


def column_weights(base_ref, upper_ref, low_ref, high_ref, first, out):
    layers, cols_dev, pupil_cols = out.shape
    width = cols_dev // 4
    core = lax.rem(lax.axis_index("dir"), 2)
    sub = lax.broadcasted_iota(jnp.int32, (width, LANES), 0).astype(jnp.float32).astype(jnp.bfloat16)
    zero = jnp.zeros((width, LANES), jnp.bfloat16)
    for level in range(layers):

        def tile(step, carry):
            start = pl.multiple_of(step * LANES, LANES)
            cut = (slice(level, level + 1), pl.ds(start, LANES))
            base, upper = base_ref[cut], upper_ref[cut]
            low, high = [
                jnp.broadcast_to(ref[cut].astype(jnp.bfloat16), (width, LANES)) for ref in (low_ref, high_ref)
            ]
            for k in range(4):
                shift = first + chunk_start(jnp.bitwise_xor(core, k // 2), k % 2) * width
                base_at, upper_at = [
                    jnp.broadcast_to(
                        jnp.clip(value - shift, -1, width).astype(jnp.float32).astype(jnp.bfloat16), (width, LANES)
                    )
                    for value in (base, upper)
                ]
                weight = jnp.where(sub == base_at, low, zero)
                weight = jnp.where(sub == upper_at, high, weight)
                out[level, k * width : (k + 1) * width, pl.ds(start, LANES)] = weight
            return carry

        lax.fori_loop(0, pupil_cols // LANES, tile, 0)


def strips_kernel(wind_held, *refs):
    tables, (across, diagonal, near, keep, cols_out, strip, sibling_strip, wind, sem) = refs[:4], refs[4:]
    load = fetch((wind_held, wind, sem))[0]
    column_weights(*tables, jnp.bitwise_xor(lax.axis_index("layer"), 1) * cols_out.shape[1], cols_out)
    layers, rows, _ = keep.shape
    core = lax.rem(lax.axis_index("dir"), 2)
    odd = core == 1
    lane = lax.broadcasted_iota(jnp.int32, (rows + 32, LANES), 1)

    def wide(own, near, far, odd, level):
        own, near, far = [block[level].astype(jnp.float32) for block in (own, near, far)]
        before = jnp.where(odd, near[rows - 16 :], far[rows - 16 :])
        return stack(before, own, jnp.where(odd, far[:16], near[:16]))

    packed = jnp.zeros((rows + 32, LANES), jnp.float32)
    for level in range(layers):
        blocks = (keep, near, diagonal, odd), (near, keep, across, core == 0)
        for at, block in zip((WIND_MAX * level, STRIP + WIND_MAX * level), blocks):
            block = pltpu.roll(wide(*block, level), at + WIND_MAX * core, 1)
            packed = jnp.where((lane >= at) & (lane < at + WIND_MAX), block, packed)
    load.wait()
    strips = jnp.zeros((rows, LANES), jnp.float32)
    for level in range(layers):
        shift = wind[0, level]
        shift = jnp.where(shift < 0, shift + rows + 32, shift)
        moved = pltpu.roll(packed, shift, 0)[16 : 16 + rows]
        mine = lax.rem(lane[:rows], STRIP)
        strips = jnp.where((mine >= WIND_MAX * level) & (mine < WIND_MAX * (level + 1)), moved, strips)
    strips = strips.T.astype(jnp.bfloat16)
    strip[...] = strips[:STRIP]
    sibling_strip[...] = strips[STRIP : 2 * STRIP]


def project_rows(rows_ref, keep, near, across, diagonal, level):
    screen = stack(keep[level], near[level], across[level], diagonal[level])
    rows = stack(rows_ref[0, level], rows_ref[1, level])
    return dot(rows, screen).astype(jnp.bfloat16)


def first_rows_kernel(rows_ref, across, diagonal, near, keep, mine, sibling, other, sibling_other):
    layers, half, _ = mine.shape
    for level in range(layers):
        part = project_rows(rows_ref, keep, near, across, diagonal, level)
        for k, out in enumerate((mine, other, sibling, sibling_other)):
            out[level] = part[k * half : (k + 1) * half]


def put_strip(out, at, strip):
    for k in range(strip.shape[1] // LANES):
        out[at + k * STRIP : at + (k + 1) * STRIP, :] = strip[:, k * LANES : (k + 1) * LANES]


def get_strip(ref, at):
    return beside(*[ref[start : start + STRIP, :] for start in range(at, ref.shape[0], STRIP)])


def later_rows_kernel(rows_ref, *refs):
    chunks, refs = refs[:8], refs[8:]
    sibling0, strip, sibling_strip, mine, give, far, sibling_far, rest, sibling_rest = refs
    across, diagonal, near, keep, across0, diagonal0, near0, keep0 = chunks
    layers, half, width = mine.shape
    rows = near.shape[1]
    size = (far.shape[0] - STRIP * rows // LANES) // layers
    start = half - size
    for level in range(layers):
        part = project_rows(rows_ref, keep, near, across, diagonal, level)
        mine[level] = part[:half]
        for k, out, remainder in ((1, far, rest), (3, sibling_far, sibling_rest)):
            piece = part[k * half : (k + 1) * half]
            out[level * size : (level + 1) * size] = piece[start:]
            remainder[level * start : (level + 1) * start] = piece[:start]
        give[level, :half, :width] = sibling0[level]
        give[level, :half, width:] = part[2 * half : 3 * half]
        for k, blocks in enumerate(((across0, keep0), (across, keep))):
            cut = slice(k * width, (k + 1) * width)
            edges = [block[level, at : at + 16] for block in blocks for at in (0, rows - 16)]
            give[level, half:, cut] = stack(*edges)
    put_strip(far, layers * size, strip)
    put_strip(sibling_far, layers * size, sibling_strip)


def project(parts, cols_refs, at):
    cols = stack(*[ref[level, start:stop, at : at + 256] for ref, level, start, stop in cols_refs])
    return dot(beside(*parts), cols)


def phase_kernel(mine_ref, other_ref, mine0, mine1, came, sibling_came, phase):
    layers, _, width = mine0.shape
    parts, cuts = [], []
    for level in range(layers):
        parts += [mine0[level], mine1[level], came[level], sibling_came[level]]
        cuts += [(mine_ref, level, 0, 2 * width)]
        cuts += [(other_ref, level, 0, width), (other_ref, level, 2 * width, 3 * width)]
    for at in range(0, phase.shape[1], 256):
        phase[:, at : at + 256] = project(parts, cuts, at)


def sum_up(start, mine_ref, cols_ref, phase, taken, came, sibling_came, outs):
    layers, _, width = taken.shape
    width = width // 2
    block = outs[0].shape[0]
    size = block * len(outs)
    rows = slice(start, start + size)
    parts, cuts = [], []
    for level in range(layers):
        cut = slice(level * size, (level + 1) * size)
        parts += [taken[level, rows], came[cut], sibling_came[cut]]
        cuts += [(mine_ref, level, 2 * width, 4 * width)]
        cuts += [(cols_ref, level, width, 2 * width), (cols_ref, level, 3 * width, 4 * width)]
    pupil_cols = phase.shape[1]
    for at in range(0, pupil_cols, 256):
        total = (phase[rows, at : at + 256] + project(parts, cuts, at)).astype(jnp.bfloat16)
        for k, out in enumerate(outs):
            out[:, at : at + 256] = total[k * block : (k + 1) * block]


def strip_steps(pairs):
    return [2**k - 1 for k in range(1, pairs.bit_length())]


def send_order(pairs):
    steps = strip_steps(pairs)
    return [k for k in range(pairs) if k not in steps] + steps


def add_strip(pairs, step, strips, out):
    pair = lax.axis_index("layer") // 2
    after = lax.rem(pair + 1, pairs) == jnp.bitwise_xor(pair, step)
    at = out.shape[1] - strips.shape[1]
    last, first = strips[:STRIP].astype(jnp.float32), strips[STRIP:].astype(jnp.float32)
    out[:, at:] = jnp.where(after, last, first).astype(jnp.bfloat16)


def far_kernel(mine_ref, cols_ref, phase, taken, came, sibling_came, *outs):
    *outs, strips = outs
    half = phase.shape[0]
    size = outs[0].shape[0] * len(outs)
    sum_up(half - size, mine_ref, cols_ref, phase, taken, came, sibling_came, outs)
    layers = taken.shape[0]
    odd = lax.rem(lax.axis_index("dir"), 2) == 1
    here = get_strip(came, layers * size).astype(jnp.float32)
    there = get_strip(sibling_came, layers * size).astype(jnp.float32)
    strips[:STRIP] = jnp.where(odd, here, there).astype(jnp.bfloat16)
    strips[STRIP:] = jnp.where(odd, there, here).astype(jnp.bfloat16)
    pairs = half // outs[0].shape[0]
    for out, step in zip(outs, strip_steps(pairs)):
        add_strip(pairs, step, strips, out)


def rest_kernel(mine_ref, cols_ref, phase, taken, came, sibling_came, *outs):
    sum_up(0, mine_ref, cols_ref, phase, taken, came, sibling_came, outs)


def shifted_rows(shift, odd, own, near, far):
    own, near, far = [block.astype(jnp.float32) for block in (own, near, far)]
    rows = own.shape[0]
    before = jnp.where(odd, near[16:], far[16:])
    after = jnp.where(odd, far[:16], near[:16])
    shift = jnp.where(shift < 0, shift + rows + 32, shift)
    return pltpu.roll(stack(before, own, after), shift, 0)[16 : 16 + rows]


def shift_kernel(wind_held, own, near0, near1, diagonal0, diagonal1, taken, partner_strips, *refs):
    messages, (out, wind, sem) = refs[:-3], refs[-3:]
    load = fetch((wind_held, wind, sem))[0]
    layers, rows, cols = own.shape
    odd = lax.rem(lax.axis_index("dir"), 2) == 1
    half = taken.shape[1] - 64
    pairs = 2 ** len(messages)
    pair, second = lax.axis_index("layer") // 2, lax.rem(lax.axis_index("layer"), 2) == 1
    before = jnp.bitwise_xor(pair, lax.rem(pair + pairs - 1, pairs))
    after = jnp.bitwise_xor(pair, lax.rem(pair + 1, pairs))
    left = partner_strips[:STRIP].astype(jnp.float32)
    right = partner_strips[STRIP:].astype(jnp.float32)
    for step, message in zip(strip_steps(pairs), messages):
        strip = message[:, message.shape[1] - rows :].astype(jnp.float32)
        left = jnp.where(jnp.logical_and(before == step, jnp.logical_not(second)), strip, left)
        right = jnp.where(jnp.logical_and(after == step, second), strip, right)
    strips = stack(left, right, jnp.zeros((LANES - 2 * STRIP, rows), jnp.float32)).T
    lane = lax.broadcasted_iota(jnp.int32, (rows, LANES), 1)
    load.wait()
    for level in range(layers):
        last = pltpu.roll(strips, LANES - WIND_MAX * (level + 1), 1)
        first = pltpu.roll(strips, LANES - STRIP - WIND_MAX * level, 1)
        extra = jnp.where(lane < WIND_MAX, first, last)
        pair = []
        for at, parts in ((half, (diagonal0, diagonal1)), (half + 32, (near0, near1))):
            here = [stack(part[level, :16], part[level, rows - 16 :]).astype(jnp.float32) for part in parts]
            there = taken[level, at : at + 32].astype(jnp.float32)
            width = there.shape[1] // 2
            quarters = [*here, there[:, width:], there[:, :width]]
            pair.append(beside(*[jnp.where(odd, quarters[3 - k], quarters[k]) for k in range(4)]))
        far, near = pair
        moved = shifted_rows(wind[0, level], odd, own[level], near, far)
        shift = wind[1, level]
        shift = jnp.where(shift < 0, shift + cols + LANES, shift)
        out[level] = pltpu.roll(beside(moved, extra), shift, 1)[:, :cols].astype(jnp.bfloat16)


def optics_kernel(amplitude, ones, columns, lines, amp_out, columns_out, lines_out):
    rows, pupil_cols = amplitude.shape
    for step in range(pupil_cols // LANES):
        cut = slice(step * LANES, (step + 1) * LANES)
        amp = amplitude[:, cut]
        energy = (amp * amp).reshape(rows // SUB_PIX, SUB_PIX, LANES).sum(axis=1)
        energy = jnp.broadcast_to(energy[:, None], (rows // SUB_PIX, SUB_PIX, LANES)).reshape(rows, LANES)
        total = jnp.dot(energy, ones[...], precision=lax.Precision.HIGHEST, preferred_element_type=jnp.float32)
        amp_out[:, cut] = amp * lax.rsqrt(total)
    columns_out[...] = columns[...].astype(jnp.bfloat16)
    lines_out[...] = lines[...].astype(jnp.bfloat16)


def sin_cos(phase):
    turns = jnp.floor(phase * (1.0 / np.pi) + 0.5)
    rest = phase - turns * 3.140625
    rest = rest - turns * 9.67653589793e-4
    odd = turns - 2.0 * jnp.floor(turns * 0.5)
    sign = 1.0 - 2.0 * odd
    square = rest * rest
    sine = -1.0 / 39916800.0
    for term in (1.0 / 362880.0, -1.0 / 5040.0, 1.0 / 120.0, -1.0 / 6.0, 1.0):
        sine = sine * square + term
    cosine = 1.0 / 479001600.0
    for term in (-1.0 / 3628800.0, 1.0 / 40320.0, -1.0 / 720.0, 1.0 / 24.0, -0.5, 1.0):
        cosine = cosine * square + term
    return sine * rest * sign, cosine * sign


def imaging_kernel(count, *refs):
    parts, (amp_ref, columns, lines, shifted, spots, screens, out, sems) = refs[:count], refs[count:]
    copies = fetch((shifted, screens, sems.at[0]))
    rows, cols = amp_ref.shape
    tiles = cols // LANES
    phase = parts[0][:, :cols].astype(jnp.float32)
    for part in parts[1:]:
        phase = phase + part[:, :cols].astype(jnp.float32)
    sine, cosine = sin_cos(phase)
    amp = amp_ref[...]
    real, imag = (amp * cosine).astype(jnp.bfloat16), (amp * sine).astype(jnp.bfloat16)
    cuts = [slice(t * LANES, (t + 1) * LANES) for t in range(tiles)]
    field = stack(*[beside(real[:, cut], imag[:, cut]) for cut in cuts])
    half = dot(field, columns[...]).astype(jnp.bfloat16)
    wide = 2 * LANES
    out_rows = 2 * rows
    for t in range(tiles):
        mine = half[t * rows : (t + 1) * rows]
        full = dot(lines[...], stack(mine[:, :wide], mine[:, wide:]))
        real, imag = full[:out_rows], full[out_rows:]
        out[:, t * wide : (t + 1) * wide] = real * real + imag * imag
        if t % 2:
            cut = slice((t - 1) * wide, (t + 1) * wide)
            copies += fetch((out.at[:, cut], spots.at[:, cut], sems.at[1 + t // 2]))
    for copy in copies:
        copy.wait()


def tables_of(rows):
    freq = np.arange(SPOT_PIX)[:, None] - SPOT_PIX // 2
    angle = ((freq * np.arange(SUB_PIX)[None, :]) % SPOT_PIX) * (2.0 * np.pi / SPOT_PIX)
    cos, sin = np.cos(angle), np.sin(angle)

    def blocks(table, count):
        return np.kron(np.eye(count), table)

    per_tile = LANES // SUB_PIX
    col_cos, col_sin = blocks(cos.T, per_tile), blocks(sin.T, per_tile)
    columns = np.block([[col_cos, -col_sin], [col_sin, col_cos]])
    count = rows // SUB_PIX
    row_cos, row_sin = blocks(cos, count), blocks(sin, count)
    lines = np.block([[row_cos, row_sin], [-row_sin, row_cos]])

    return columns.astype(np.float32), lines.astype(np.float32)


def per_device(screens, amplitude, wind, offsets, ratio):
    layers, rows_dev, cols_dev = screens.shape
    n_layer = lax.axis_size("layer")
    n_dir = lax.axis_size("dir")
    rows, pupil_cols = amplitude.shape
    pairs = n_layer // 2
    half = pairs * rows
    pupil_rows = 2 * half
    assert n_dir == 4 and rows == STRIP and pairs > 2
    bf16, f32 = jnp.bfloat16, jnp.float32
    wind = jnp.transpose(wind, (1, 0))
    offsets = jnp.transpose(offsets, (1, 2, 0))
    ratio = jnp.transpose(ratio, (1, 2, 0))
    smem, sem = pltpu.SMEM, pltpu.SemaphoreType.DMA
    wind_scratch = [smem(wind.shape, jnp.int32), sem]

    def shape(*dims, dtype=bf16):
        return jax.ShapeDtypeStruct(dims, dtype)

    def swap(value, bits):
        return lax.ppermute(value, "dir", [(i, i ^ bits) for i in range(n_dir)])

    def partner(value, bits=0):
        count = n_layer * n_dir
        return lax.ppermute(value, ("layer", "dir"), [(i, i ^ n_dir ^ bits) for i in range(count)])

    def turn(value, step):
        return lax.ppermute(value, "layer", [(i, (i + step) % n_layer) for i in range(n_layer)])

    width = cols_dev // 4
    chunk = shape(layers, rows_dev, width)
    keep0, keep1, give0, give1 = call(
        split_kernel,
        [chunk] * 4,
        (screens,),
        0,
        "split",
        in_hbm=(0,),
        scratch=[sem((4,))],
        brief=True,
    )
    across0 = swap(keep0, 2)
    diagonal0 = swap(give0, 3)
    near0 = swap(give0, 1)
    across1 = swap(keep1, 2)
    diagonal1 = swap(give1, 3)
    ones = np.kron(np.eye(LANES // SUB_PIX), np.ones((SUB_PIX, SUB_PIX))).astype(np.float32)
    optics_in = (amplitude, jnp.asarray(ones), *[jnp.asarray(table) for table in tables_of(rows)])
    copies = [shape(*array.shape, dtype=array.dtype) for array in (screens, *optics_in, wind)]
    row_weights, cols, *loaded = call(
        functools.partial(weights_kernel, (n_layer, rows_dev, cols_dev * n_layer)),
        [shape(2, layers, pupil_rows, 4 * rows_dev), shape(layers, cols_dev, pupil_cols)]
        + [shape(8, pupil_cols, dtype=dtype) for dtype in (jnp.int32, jnp.int32, f32, f32)]
        + copies,
        (wind, offsets, ratio, screens, *optics_in),
        0,
        "weights",
        in_hbm=range(8),
        scratch=[smem(array.shape, jnp.int32) for array in (wind, offsets, ratio)]
        + [sem((9,))],
        brief=True,
    )
    tables, (own, *optics_in, wind) = loaded[:4], loaded[4:]
    give1, own = lax.optimization_barrier((give1, own))
    near1 = swap(give1, 1)
    across0, diagonal0, row_weights, cols = lax.optimization_barrier((across0, diagonal0, row_weights, cols))

    projected = shape(layers, half, width)
    mine0, sibling0, other0, sibling_other0 = call(
        first_rows_kernel,
        [projected] * 4,
        (row_weights, across0, diagonal0, near0, keep0),
        0,
        "rows_first",
        brief=True,
    )
    came0 = partner(other0)
    sibling_came0 = partner(sibling_other0, 1)

    wind, mine0 = lax.optimization_barrier((wind, mine0))
    others, strip, sibling_strip = call(
        strips_kernel,
        [shape(layers, cols_dev, pupil_cols)] + [shape(STRIP, rows_dev)] * 2,
        (wind, *tables, across0, diagonal0, near0, keep0),
        0,
        "strips",
        scratch=wind_scratch,
        brief=True,
    )
    steps = strip_steps(pairs)
    far = len(steps) * rows
    message = shape(layers * far + STRIP * rows_dev // LANES, width)
    remainder = shape(layers * (half - far), width)
    mine1, give, far1, sibling_far1, rest1, sibling_rest1 = call(
        later_rows_kernel,
        [projected, shape(layers, half + 64, 2 * width), message, message, remainder, remainder],
        (row_weights, across1, diagonal1, near1, keep1, across0, diagonal0, near0, keep0, sibling0, strip, sibling_strip),
        0,
        "rows_later",
        brief=True,
    )
    far1, sibling_far1 = partner(far1), partner(sibling_far1, 1)
    taken = swap(give, 1)
    phase = call(
        phase_kernel,
        shape(half, pupil_cols, dtype=f32),
        (cols, others, mine0, mine1, came0, sibling_came0),
        10_000_000_000,
        "phase",
    )

    rest1, sibling_rest1, phase = lax.optimization_barrier((rest1, sibling_rest1, phase))
    rest1, sibling_rest1 = partner(rest1), partner(sibling_rest1, 1)
    *far_sums, strips = call(
        far_kernel,
        [shape(rows, pupil_cols + rows_dev)] * len(steps) + [shape(2 * STRIP, rows_dev)],
        (cols, others, phase, taken, far1, sibling_far1),
        300_000_000,
        "far",
    )
    rest_sums = call(
        rest_kernel,
        [shape(rows, pupil_cols)] * (pairs - len(steps)),
        (cols, others, phase, taken, rest1, sibling_rest1),
        0,
        "rest",
        brief=True,
    )
    received = dict(zip(send_order(pairs), [*rest_sums, *far_sums]))
    for k in range(1, pairs):
        received[k] = lax.ppermute(received[k], "layer", [(i, i ^ (2 * k)) for i in range(n_layer)])
    received = [received[k] for k in range(pairs)]

    optics_in, received[1] = lax.optimization_barrier((optics_in, received[1]))
    optics = call(
        optics_kernel,
        (
            shape(rows, pupil_cols, dtype=f32),
            shape(*optics_in[2].shape),
            shape(*optics_in[3].shape),
        ),
        optics_in,
        0,
        "optics",
        brief=True,
    )
    received[-1], optics = lax.optimization_barrier((received[-1], optics))
    shifted = call(
        shift_kernel,
        shape(layers, rows_dev, cols_dev),
        (wind, own, near0, near1, diagonal0, diagonal1, taken, strips, *[received[k] for k in steps]),
        0,
        "shift",
        scratch=wind_scratch,
        brief=True,
    )
    spots_shape = shape(2 * rows, 2 * pupil_cols, dtype=f32)
    spots, new_screens = call(
        functools.partial(imaging_kernel, pairs),
        [spots_shape, shape(layers, rows_dev, cols_dev)],
        (*received, *optics, shifted),
        400_000_000,
        "imaging",
        out_hbm=(0, 1),
        scratch=[pltpu.VMEM(spots_shape.shape, f32), sem((1 + pupil_cols // (2 * LANES),))],
    )
    return (new_screens, spots[None])


def solution(mesh):
    return jax.shard_map(
        per_device,
        mesh=mesh,
        in_specs=(P(None, "dir", "layer"), P("layer", None), P(), P(), P()),
        out_specs=(P(None, "dir", "layer"), P("dir", "layer", None)),
        check_vma=False,
    )
```

```python
import functools

import jax
import jax.numpy as jnp
import numpy as np
from jax import lax
from jax.experimental import pallas as pl
from jax.experimental.pallas import tpu as pltpu
from jax.sharding import PartitionSpec as P

SUB_PIX = 16
SPOT_PIX = 32
WIND_MAX = 8
LANES = 128
STRIP = 32

HBM_SPEC = pl.BlockSpec(memory_space=pltpu.HBM)
VMEM_SPEC = pl.BlockSpec(memory_space=pltpu.VMEM)


def params(*arrays):
    held = sum(array.size * array.dtype.itemsize for array in jax.tree.leaves(arrays))
    return pltpu.CompilerParams(vmem_limit_bytes=held + 8 * 1024 * 1024)


def call(kernel, out_shape, operands, flops, name, in_hbm=(), out_hbm=(), scratch=(), brief=False):
    def spec(k, array):
        return HBM_SPEC if k in in_hbm else VMEM_SPEC

    if out_hbm:
        out_specs = [HBM_SPEC if k in out_hbm else VMEM_SPEC for k in range(len(out_shape))]
    else:
        out_specs = jax.tree.map(lambda _: VMEM_SPEC, out_shape)
    size = sum(array.size * array.dtype.itemsize for array in jax.tree.leaves((operands, out_shape)))
    if brief:
        flops = size = 0
    in_specs = [spec(k, array) for k, array in enumerate(operands)]
    operands = [
        pltpu.with_memory_space_constraint(array, pltpu.HBM) if space is HBM_SPEC else array
        for array, space in zip(operands, in_specs)
    ]
    return pl.pallas_call(
        kernel,
        out_shape=out_shape,
        in_specs=in_specs,
        out_specs=out_specs,
        scratch_shapes=list(scratch),
        compiler_params=params(operands, out_shape),
        cost_estimate=pl.CostEstimate(flops=flops, bytes_accessed=size, transcendentals=0),
        name=name,
    )(*operands)


def fetch(*pairs):
    copies = [pltpu.make_async_copy(source, target, sem) for source, target, sem in pairs]
    for copy in copies:
        copy.start()
    return copies


def wrap(value, length):
    value = jnp.where(value < 0, value + length, value)
    return jnp.where(value >= length, value - length, value)


def stack(*blocks):
    return jnp.concatenate(blocks, axis=0)


def beside(*blocks):
    return jnp.concatenate(blocks, axis=1)


def dot(left, right):
    return jnp.dot(left, right, preferred_element_type=jnp.float32)


def spans(pixel, anchor, num, den, length):
    stretched = (pixel * num).astype(jnp.float32)
    den = (jnp.zeros_like(pixel) + den).astype(jnp.float32)
    whole = jnp.floor((stretched + 0.5) / den)
    fraction = (stretched - whole * den) / den
    base = wrap(anchor + whole.astype(jnp.int32), length)
    upper = wrap(base + 1, length)
    return base, upper, 1.0 - fraction, fraction


def chunk_start(half, chunk):
    return 3 * half + chunk * (1 - 2 * half)


def split_kernel(screens, *refs):
    ints, outs, held, sems = refs[:3], refs[3:7], refs[7:10], refs[-1]
    width = outs[0].shape[2]
    core = lax.rem(lax.axis_index("dir"), 2)
    pairs = []
    for k, out in enumerate(outs):
        half = core if k < 2 else 1 - core
        start = pl.multiple_of(chunk_start(half, k % 2) * width, LANES)
        pairs.append((screens.at[:, :, pl.ds(start, width)], out, sems.at[k]))
    pairs += [(source, copy, sems.at[4 + k]) for k, (source, copy) in enumerate(zip(ints, held))]
    for load in fetch(*pairs):
        load.wait()


def weights_kernel(geometry, wind_held, offsets_held, ratio_held, *refs):
    n_layer, rows_dev, screen_cols = geometry
    sources, (rows_out, cols_out, *tables), refs = refs[:5], refs[5:11], refs[11:]
    copies, (wind, offsets, ratio, sems) = refs[:5], refs[5:]
    pupil_cols = cols_out.shape[2]
    loads = fetch(
        (wind_held, wind, sems.at[0]),
        (offsets_held, offsets, sems.at[1]),
        (ratio_held, ratio, sems.at[2]),
    )
    pairs = [*zip(sources, copies)]
    others = fetch(*[(source, copy, sems.at[3 + k]) for k, (source, copy) in enumerate(pairs)])
    _, layers, pupil_rows, screen_rows = rows_out.shape
    half = pupil_rows // 2
    direction = lax.axis_index("dir")
    column = lax.axis_index("layer")
    block = pupil_rows // n_layer
    row = lax.broadcasted_iota(jnp.int32, (half, LANES), 0)
    step = row // block
    for at, value in enumerate(send_order(n_layer // 2)):
        step = jnp.where(row // block == at, value, step)
    pair = jnp.bitwise_xor(step, column // 2)
    parity = lax.rem(column, 2)
    inside = lax.rem(row, block) + pair * (2 * block)
    pixel_rows = stack(inside + parity * block, inside + (1 - parity) * block)
    lane = lax.broadcasted_iota(jnp.int32, (pupil_rows, LANES), 1)
    for load in loads:
        load.wait()
    for side in range(2):
        target = jnp.bitwise_xor(direction, side)
        for level in range(layers):
            anchor = wrap(offsets[level, 0, target] - wind[0, level], screen_rows)
            num, den = ratio[level, 0, target], ratio[level, 1, target]
            base, upper, low, high = spans(pixel_rows, anchor, num, den, screen_rows)
            for peer in range(4):
                for part in range(rows_dev // LANES):
                    index = lane + (jnp.bitwise_xor(direction, peer) * rows_dev + part * LANES)
                    weight = jnp.where(index == base, low, 0.0)
                    weight = jnp.where(index == upper, high, weight)
                    start = peer * rows_dev + part * LANES
                    rows_out[side, level, :, start : start + LANES] = weight.astype(jnp.bfloat16)
    sub = lax.broadcasted_iota(jnp.int32, (8, LANES), 0)
    anchor, num, den = jnp.zeros_like(sub), jnp.zeros_like(sub), jnp.ones_like(sub)
    for level in range(layers):
        start = wrap(offsets[level, 1, direction] - wind[1, level], screen_cols)
        anchor = jnp.where(sub == level, start, anchor)
        num = jnp.where(sub == level, ratio[level, 0, direction], num)
        den = jnp.where(sub == level, ratio[level, 1, direction], den)
    for at in range(0, pupil_cols, LANES):
        pixel = lax.broadcasted_iota(jnp.int32, (8, LANES), 1) + at
        values = spans(pixel, anchor, num, den, screen_cols)
        for table, value in zip(tables, values):
            table[:, at : at + LANES] = value
    column_weights(*tables, column * cols_out.shape[1], cols_out)
    for load in others:
        load.wait()


def column_weights(base_ref, upper_ref, low_ref, high_ref, first, out):
    layers, cols_dev, pupil_cols = out.shape
    width = cols_dev // 4
    core = lax.rem(lax.axis_index("dir"), 2)
    sub = lax.broadcasted_iota(jnp.int32, (width, LANES), 0).astype(jnp.float32).astype(jnp.bfloat16)
    zero = jnp.zeros((width, LANES), jnp.bfloat16)
    for level in range(layers):

        def tile(step, carry):
            start = pl.multiple_of(step * LANES, LANES)
            cut = (slice(level, level + 1), pl.ds(start, LANES))
            base, upper = base_ref[cut], upper_ref[cut]
            low, high = [
                jnp.broadcast_to(ref[cut].astype(jnp.bfloat16), (width, LANES)) for ref in (low_ref, high_ref)
            ]
            for k in range(4):
                shift = first + chunk_start(jnp.bitwise_xor(core, k // 2), k % 2) * width
                base_at, upper_at = [
                    jnp.broadcast_to(
                        jnp.clip(value - shift, -1, width).astype(jnp.float32).astype(jnp.bfloat16), (width, LANES)
                    )
                    for value in (base, upper)
                ]
                weight = jnp.where(sub == base_at, low, zero)
                weight = jnp.where(sub == upper_at, high, weight)
                out[level, k * width : (k + 1) * width, pl.ds(start, LANES)] = weight
            return carry

        lax.fori_loop(0, pupil_cols // LANES, tile, 0)


def strips_kernel(wind_held, *refs):
    tables, (across, diagonal, near, keep, cols_out, strip, sibling_strip, wind, sem) = refs[:4], refs[4:]
    load = fetch((wind_held, wind, sem))[0]
    column_weights(*tables, jnp.bitwise_xor(lax.axis_index("layer"), 1) * cols_out.shape[1], cols_out)
    layers, rows, _ = keep.shape
    core = lax.rem(lax.axis_index("dir"), 2)
    odd = core == 1
    lane = lax.broadcasted_iota(jnp.int32, (rows + 32, LANES), 1)

    def wide(own, near, far, odd, level):
        own, near, far = [block[level].astype(jnp.float32) for block in (own, near, far)]
        before = jnp.where(odd, near[rows - 16 :], far[rows - 16 :])
        return stack(before, own, jnp.where(odd, far[:16], near[:16]))

    packed = jnp.zeros((rows + 32, LANES), jnp.float32)
    for level in range(layers):
        blocks = (keep, near, diagonal, odd), (near, keep, across, core == 0)
        for at, block in zip((WIND_MAX * level, STRIP + WIND_MAX * level), blocks):
            block = pltpu.roll(wide(*block, level), at + WIND_MAX * core, 1)
            packed = jnp.where((lane >= at) & (lane < at + WIND_MAX), block, packed)
    load.wait()
    strips = jnp.zeros((rows, LANES), jnp.float32)
    for level in range(layers):
        shift = wind[0, level]
        shift = jnp.where(shift < 0, shift + rows + 32, shift)
        moved = pltpu.roll(packed, shift, 0)[16 : 16 + rows]
        mine = lax.rem(lane[:rows], STRIP)
        strips = jnp.where((mine >= WIND_MAX * level) & (mine < WIND_MAX * (level + 1)), moved, strips)
    strips = strips.T.astype(jnp.bfloat16)
    strip[...] = strips[:STRIP]
    sibling_strip[...] = strips[STRIP : 2 * STRIP]


def project_rows(rows_ref, keep, near, across, diagonal, level):
    screen = stack(keep[level], near[level], across[level], diagonal[level])
    rows = stack(rows_ref[0, level], rows_ref[1, level])
    return dot(rows, screen).astype(jnp.bfloat16)


def first_rows_kernel(rows_ref, across, diagonal, near, keep, mine, sibling, other, sibling_other):
    layers, half, _ = mine.shape
    for level in range(layers):
        part = project_rows(rows_ref, keep, near, across, diagonal, level)
        for k, out in enumerate((mine, other, sibling, sibling_other)):
            out[level] = part[k * half : (k + 1) * half]


def put_strip(out, at, strip):
    for k in range(strip.shape[1] // LANES):
        out[at + k * STRIP : at + (k + 1) * STRIP, :] = strip[:, k * LANES : (k + 1) * LANES]


def get_strip(ref, at):
    return beside(*[ref[start : start + STRIP, :] for start in range(at, ref.shape[0], STRIP)])


def later_rows_kernel(rows_ref, *refs):
    chunks, refs = refs[:8], refs[8:]
    sibling0, strip, sibling_strip, mine, give, far, sibling_far, rest, sibling_rest = refs
    across, diagonal, near, keep, across0, diagonal0, near0, keep0 = chunks
    layers, half, width = mine.shape
    rows = near.shape[1]
    size = (far.shape[0] - STRIP * rows // LANES) // layers
    start = half - size
    for level in range(layers):
        part = project_rows(rows_ref, keep, near, across, diagonal, level)
        mine[level] = part[:half]
        for k, out, remainder in ((1, far, rest), (3, sibling_far, sibling_rest)):
            piece = part[k * half : (k + 1) * half]
            out[level * size : (level + 1) * size] = piece[start:]
            remainder[level * start : (level + 1) * start] = piece[:start]
        give[level, :half, :width] = sibling0[level]
        give[level, :half, width:] = part[2 * half : 3 * half]
        for k, blocks in enumerate(((across0, keep0), (across, keep))):
            cut = slice(k * width, (k + 1) * width)
            edges = [block[level, at : at + 16] for block in blocks for at in (0, rows - 16)]
            give[level, half:, cut] = stack(*edges)
    put_strip(far, layers * size, strip)
    put_strip(sibling_far, layers * size, sibling_strip)


def project(parts, cols_refs, at):
    cols = stack(*[ref[level, start:stop, at : at + 256] for ref, level, start, stop in cols_refs])
    return dot(beside(*parts), cols)


def phase_kernel(mine_ref, other_ref, mine0, mine1, came, sibling_came, phase):
    layers, _, width = mine0.shape
    parts, cuts = [], []
    for level in range(layers):
        parts += [mine0[level], mine1[level], came[level], sibling_came[level]]
        cuts += [(mine_ref, level, 0, 2 * width)]
        cuts += [(other_ref, level, 0, width), (other_ref, level, 2 * width, 3 * width)]
    for at in range(0, phase.shape[1], 256):
        phase[:, at : at + 256] = project(parts, cuts, at)


def taken_kernel(mine_ref, phase, taken, out):
    half, pupil_cols = phase.shape
    layers, cols_dev, _ = mine_ref.shape
    parts = [taken[level, :half] for level in range(layers)]
    cuts = [(mine_ref, level, cols_dev // 2, cols_dev) for level in range(layers)]
    for at in range(0, pupil_cols, 256):
        out[:, at : at + 256] = phase[:, at : at + 256] + project(parts, cuts, at)


def sum_up(start, cols_ref, phase, came, sibling_came, outs):
    layers, cols_dev, _ = cols_ref.shape
    width = cols_dev // 4
    block = outs[0].shape[0]
    size = block * len(outs)
    rows = slice(start, start + size)
    parts, cuts = [], []
    for level in range(layers):
        cut = slice(level * size, (level + 1) * size)
        parts += [came[cut], sibling_came[cut]]
        cuts += [(cols_ref, level, width, 2 * width), (cols_ref, level, 3 * width, 4 * width)]
    pupil_cols = phase.shape[1]
    for at in range(0, pupil_cols, 256):
        total = (phase[rows, at : at + 256] + project(parts, cuts, at)).astype(jnp.bfloat16)
        for k, out in enumerate(outs):
            out[:, at : at + 256] = total[k * block : (k + 1) * block]


def strip_steps(pairs):
    return [2**k - 1 for k in range(1, pairs.bit_length())]


def send_order(pairs):
    steps = strip_steps(pairs)
    return [k for k in range(pairs) if k not in steps] + steps


def add_strip(pairs, step, strips, out):
    pair = lax.axis_index("layer") // 2
    after = lax.rem(pair + 1, pairs) == jnp.bitwise_xor(pair, step)
    at = out.shape[1] - strips.shape[1]
    last, first = strips[:STRIP].astype(jnp.float32), strips[STRIP:].astype(jnp.float32)
    out[:, at:] = jnp.where(after, last, first).astype(jnp.bfloat16)


def far_kernel(cols_ref, phase, came, sibling_came, *outs):
    *outs, strips = outs
    half = phase.shape[0]
    size = outs[0].shape[0] * len(outs)
    sum_up(half - size, cols_ref, phase, came, sibling_came, outs)
    layers = cols_ref.shape[0]
    odd = lax.rem(lax.axis_index("dir"), 2) == 1
    here = get_strip(came, layers * size).astype(jnp.float32)
    there = get_strip(sibling_came, layers * size).astype(jnp.float32)
    strips[:STRIP] = jnp.where(odd, here, there).astype(jnp.bfloat16)
    strips[STRIP:] = jnp.where(odd, there, here).astype(jnp.bfloat16)
    pairs = half // outs[0].shape[0]
    for out, step in zip(outs, strip_steps(pairs)):
        add_strip(pairs, step, strips, out)


def rest_kernel(cols_ref, phase, came, sibling_came, *outs):
    sum_up(0, cols_ref, phase, came, sibling_came, outs)


def shifted_rows(shift, odd, own, near, far):
    own, near, far = [block.astype(jnp.float32) for block in (own, near, far)]
    rows = own.shape[0]
    before = jnp.where(odd, near[16:], far[16:])
    after = jnp.where(odd, far[:16], near[:16])
    shift = jnp.where(shift < 0, shift + rows + 32, shift)
    return pltpu.roll(stack(before, own, after), shift, 0)[16 : 16 + rows]


def shift_kernel(wind_held, own, near0, near1, diagonal0, diagonal1, taken, partner_strips, *refs):
    messages, (out, wind, sem) = refs[:-3], refs[-3:]
    load = fetch((wind_held, wind, sem))[0]
    layers, rows, cols = own.shape
    odd = lax.rem(lax.axis_index("dir"), 2) == 1
    half = taken.shape[1] - 64
    pairs = 2 ** len(messages)
    pair, second = lax.axis_index("layer") // 2, lax.rem(lax.axis_index("layer"), 2) == 1
    before = jnp.bitwise_xor(pair, lax.rem(pair + pairs - 1, pairs))
    after = jnp.bitwise_xor(pair, lax.rem(pair + 1, pairs))
    left = partner_strips[:STRIP].astype(jnp.float32)
    right = partner_strips[STRIP:].astype(jnp.float32)
    for step, message in zip(strip_steps(pairs), messages):
        strip = message[:, message.shape[1] - rows :].astype(jnp.float32)
        left = jnp.where(jnp.logical_and(before == step, jnp.logical_not(second)), strip, left)
        right = jnp.where(jnp.logical_and(after == step, second), strip, right)
    strips = stack(left, right, jnp.zeros((LANES - 2 * STRIP, rows), jnp.float32)).T
    lane = lax.broadcasted_iota(jnp.int32, (rows, LANES), 1)
    load.wait()
    for level in range(layers):
        last = pltpu.roll(strips, LANES - WIND_MAX * (level + 1), 1)
        first = pltpu.roll(strips, LANES - STRIP - WIND_MAX * level, 1)
        extra = jnp.where(lane < WIND_MAX, first, last)
        pair = []
        for at, parts in ((half, (diagonal0, diagonal1)), (half + 32, (near0, near1))):
            here = [stack(part[level, :16], part[level, rows - 16 :]).astype(jnp.float32) for part in parts]
            there = taken[level, at : at + 32].astype(jnp.float32)
            width = there.shape[1] // 2
            quarters = [*here, there[:, width:], there[:, :width]]
            pair.append(beside(*[jnp.where(odd, quarters[3 - k], quarters[k]) for k in range(4)]))
        far, near = pair
        moved = shifted_rows(wind[0, level], odd, own[level], near, far)
        shift = wind[1, level]
        shift = jnp.where(shift < 0, shift + cols + LANES, shift)
        out[level] = pltpu.roll(beside(moved, extra), shift, 1)[:, :cols].astype(jnp.bfloat16)


def optics_kernel(amplitude, ones, columns, lines, amp_out, columns_out, lines_out):
    rows, pupil_cols = amplitude.shape
    for step in range(pupil_cols // LANES):
        cut = slice(step * LANES, (step + 1) * LANES)
        amp = amplitude[:, cut]
        energy = (amp * amp).reshape(rows // SUB_PIX, SUB_PIX, LANES).sum(axis=1)
        energy = jnp.broadcast_to(energy[:, None], (rows // SUB_PIX, SUB_PIX, LANES)).reshape(rows, LANES)
        total = jnp.dot(energy, ones[...], precision=lax.Precision.HIGHEST, preferred_element_type=jnp.float32)
        amp_out[:, cut] = amp * lax.rsqrt(total)
    columns_out[...] = columns[...].astype(jnp.bfloat16)
    lines_out[...] = lines[...].astype(jnp.bfloat16)


def sin_cos(phase):
    turns = jnp.floor(phase * (1.0 / np.pi) + 0.5)
    rest = phase - turns * 3.140625
    rest = rest - turns * 9.67653589793e-4
    odd = turns - 2.0 * jnp.floor(turns * 0.5)
    sign = 1.0 - 2.0 * odd
    square = rest * rest
    sine = -1.0 / 39916800.0
    for term in (1.0 / 362880.0, -1.0 / 5040.0, 1.0 / 120.0, -1.0 / 6.0, 1.0):
        sine = sine * square + term
    cosine = 1.0 / 479001600.0
    for term in (-1.0 / 3628800.0, 1.0 / 40320.0, -1.0 / 720.0, 1.0 / 24.0, -0.5, 1.0):
        cosine = cosine * square + term
    return sine * rest * sign, cosine * sign


def imaging_kernel(count, *refs):
    parts, (amp_ref, columns, lines, shifted, spots, screens, out, sems) = refs[:count], refs[count:]
    copies = fetch((shifted, screens, sems.at[0]))
    rows, cols = amp_ref.shape
    tiles = cols // LANES
    phase = parts[0][:, :cols].astype(jnp.float32)
    for part in parts[1:]:
        phase = phase + part[:, :cols].astype(jnp.float32)
    sine, cosine = sin_cos(phase)
    amp = amp_ref[...]
    real, imag = (amp * cosine).astype(jnp.bfloat16), (amp * sine).astype(jnp.bfloat16)
    cuts = [slice(t * LANES, (t + 1) * LANES) for t in range(tiles)]
    field = stack(*[beside(real[:, cut], imag[:, cut]) for cut in cuts])
    half = dot(field, columns[...]).astype(jnp.bfloat16)
    wide = 2 * LANES
    out_rows = 2 * rows
    for t in range(tiles):
        mine = half[t * rows : (t + 1) * rows]
        full = dot(lines[...], stack(mine[:, :wide], mine[:, wide:]))
        real, imag = full[:out_rows], full[out_rows:]
        out[:, t * wide : (t + 1) * wide] = real * real + imag * imag
        if t % 2:
            cut = slice((t - 1) * wide, (t + 1) * wide)
            copies += fetch((out.at[:, cut], spots.at[:, cut], sems.at[1 + t // 2]))
    for copy in copies:
        copy.wait()


def tables_of(rows):
    freq = np.arange(SPOT_PIX)[:, None] - SPOT_PIX // 2
    angle = ((freq * np.arange(SUB_PIX)[None, :]) % SPOT_PIX) * (2.0 * np.pi / SPOT_PIX)
    cos, sin = np.cos(angle), np.sin(angle)

    def blocks(table, count):
        return np.kron(np.eye(count), table)

    per_tile = LANES // SUB_PIX
    col_cos, col_sin = blocks(cos.T, per_tile), blocks(sin.T, per_tile)
    columns = np.block([[col_cos, -col_sin], [col_sin, col_cos]])
    count = rows // SUB_PIX
    row_cos, row_sin = blocks(cos, count), blocks(sin, count)
    lines = np.block([[row_cos, row_sin], [-row_sin, row_cos]])

    return columns.astype(np.float32), lines.astype(np.float32)


def per_device(screens, amplitude, wind, offsets, ratio):
    layers, rows_dev, cols_dev = screens.shape
    n_layer = lax.axis_size("layer")
    n_dir = lax.axis_size("dir")
    rows, pupil_cols = amplitude.shape
    pairs = n_layer // 2
    half = pairs * rows
    pupil_rows = 2 * half
    assert n_dir == 4 and rows == STRIP and pairs > 2
    bf16, f32 = jnp.bfloat16, jnp.float32
    wind = jnp.transpose(wind, (1, 0))
    offsets = jnp.transpose(offsets, (1, 2, 0))
    ratio = jnp.transpose(ratio, (1, 2, 0))
    smem, sem = pltpu.SMEM, pltpu.SemaphoreType.DMA
    wind_scratch = [smem(wind.shape, jnp.int32), sem]

    def shape(*dims, dtype=bf16):
        return jax.ShapeDtypeStruct(dims, dtype)

    def swap(value, bits):
        return lax.ppermute(value, "dir", [(i, i ^ bits) for i in range(n_dir)])

    def partner(value, bits=0):
        count = n_layer * n_dir
        return lax.ppermute(value, ("layer", "dir"), [(i, i ^ n_dir ^ bits) for i in range(count)])

    def turn(value, step):
        return lax.ppermute(value, "layer", [(i, (i + step) % n_layer) for i in range(n_layer)])

    width = cols_dev // 4
    chunk = shape(layers, rows_dev, width)
    ints = (wind, offsets, ratio)
    keep0, keep1, give0, give1, *ints = call(
        split_kernel,
        [chunk] * 4 + [shape(*array.shape, dtype=jnp.int32) for array in ints],
        (screens, *ints),
        0,
        "split",
        in_hbm=range(4),
        scratch=[sem((7,))],
        brief=True,
    )
    across0 = swap(keep0, 2)
    diagonal0 = swap(give0, 3)
    near0 = swap(give0, 1)
    across1 = swap(keep1, 2)
    diagonal1 = swap(give1, 3)
    ones = np.kron(np.eye(LANES // SUB_PIX), np.ones((SUB_PIX, SUB_PIX))).astype(np.float32)
    optics_in = (amplitude, jnp.asarray(ones), *[jnp.asarray(table) for table in tables_of(rows)])
    copies = [shape(*array.shape, dtype=array.dtype) for array in (screens, *optics_in)]
    row_weights, cols, *loaded = call(
        functools.partial(weights_kernel, (n_layer, rows_dev, cols_dev * n_layer)),
        [shape(2, layers, pupil_rows, 4 * rows_dev), shape(layers, cols_dev, pupil_cols)]
        + [shape(8, pupil_cols, dtype=dtype) for dtype in (jnp.int32, jnp.int32, f32, f32)]
        + copies,
        (*ints, screens, *optics_in),
        0,
        "weights",
        in_hbm=range(3, 8),
        scratch=[smem(array.shape, jnp.int32) for array in (wind, offsets, ratio)]
        + [sem((8,))],
        brief=True,
    )
    tables, (own, *optics_in) = loaded[:4], loaded[4:]
    wind = ints[0]
    give1, own = lax.optimization_barrier((give1, own))
    near1 = swap(give1, 1)
    across0, diagonal0, row_weights, cols = lax.optimization_barrier((across0, diagonal0, row_weights, cols))

    projected = shape(layers, half, width)
    mine0, sibling0, other0, sibling_other0 = call(
        first_rows_kernel,
        [projected] * 4,
        (row_weights, across0, diagonal0, near0, keep0),
        0,
        "rows_first",
        brief=True,
    )
    came0 = partner(other0)
    sibling_came0 = partner(sibling_other0, 1)

    wind, mine0 = lax.optimization_barrier((wind, mine0))
    others, strip, sibling_strip = call(
        strips_kernel,
        [shape(layers, cols_dev, pupil_cols)] + [shape(STRIP, rows_dev)] * 2,
        (wind, *tables, across0, diagonal0, near0, keep0),
        0,
        "strips",
        scratch=wind_scratch,
        brief=True,
    )
    steps = strip_steps(pairs)
    far = len(steps) * rows
    message = shape(layers * far + STRIP * rows_dev // LANES, width)
    remainder = shape(layers * (half - far), width)
    mine1, give, far1, sibling_far1, rest1, sibling_rest1 = call(
        later_rows_kernel,
        [projected, shape(layers, half + 64, 2 * width), message, message, remainder, remainder],
        (row_weights, across1, diagonal1, near1, keep1, across0, diagonal0, near0, keep0, sibling0, strip, sibling_strip),
        0,
        "rows_later",
        brief=True,
    )
    far1, sibling_far1 = partner(far1), partner(sibling_far1, 1)
    taken = swap(give, 1)
    phase = call(
        phase_kernel,
        shape(half, pupil_cols, dtype=f32),
        (cols, others, mine0, mine1, came0, sibling_came0),
        10_000_000_000,
        "phase",
    )

    rest1, sibling_rest1, phase = lax.optimization_barrier((rest1, sibling_rest1, phase))
    rest1, sibling_rest1 = partner(rest1), partner(sibling_rest1, 1)
    phase = call(
        taken_kernel,
        shape(half, pupil_cols, dtype=f32),
        (cols, phase, taken),
        0,
        "taken",
        brief=True,
    )
    *far_sums, strips = call(
        far_kernel,
        [shape(rows, pupil_cols + rows_dev)] * len(steps) + [shape(2 * STRIP, rows_dev)],
        (others, phase, far1, sibling_far1),
        300_000_000,
        "far",
    )
    rest_sums = call(
        rest_kernel,
        [shape(rows, pupil_cols)] * (pairs - len(steps)),
        (others, phase, rest1, sibling_rest1),
        0,
        "rest",
        brief=True,
    )
    received = dict(zip(send_order(pairs), [*rest_sums, *far_sums]))
    for k in range(1, pairs):
        received[k] = lax.ppermute(received[k], "layer", [(i, i ^ (2 * k)) for i in range(n_layer)])
    received = [received[k] for k in range(pairs)]

    optics_in, received[-1] = lax.optimization_barrier((optics_in, received[-1]))
    optics = call(
        optics_kernel,
        (
            shape(rows, pupil_cols, dtype=f32),
            shape(*optics_in[2].shape),
            shape(*optics_in[3].shape),
        ),
        optics_in,
        0,
        "optics",
        brief=True,
    )
    received[1], optics = lax.optimization_barrier((received[1], optics))
    shifted = call(
        shift_kernel,
        shape(layers, rows_dev, cols_dev),
        (wind, own, near0, near1, diagonal0, diagonal1, taken, strips, *[received[k] for k in steps]),
        0,
        "shift",
        scratch=wind_scratch,
        brief=True,
    )
    spots_shape = shape(2 * rows, 2 * pupil_cols, dtype=f32)
    spots, new_screens = call(
        functools.partial(imaging_kernel, pairs),
        [spots_shape, shape(layers, rows_dev, cols_dev)],
        (*received, *optics, shifted),
        400_000_000,
        "imaging",
        out_hbm=(0, 1),
        scratch=[pltpu.VMEM(spots_shape.shape, f32), sem((1 + pupil_cols // (2 * LANES),))],
    )
    return (new_screens, spots[None])


def solution(mesh):
    return jax.shard_map(
        per_device,
        mesh=mesh,
        in_specs=(P(None, "dir", "layer"), P("layer", None), P(), P(), P()),
        out_specs=(P(None, "dir", "layer"), P("dir", "layer", None)),
        check_vma=False,
    )
```

```python
import functools

import jax
import jax.numpy as jnp
import numpy as np
from jax import lax
from jax.experimental import pallas as pl
from jax.experimental.pallas import tpu as pltpu
from jax.sharding import PartitionSpec as P

SUB_PIX = 16
SPOT_PIX = 32
WIND_MAX = 8
LANES = 128
STRIP = 32

HBM_SPEC = pl.BlockSpec(memory_space=pltpu.HBM)
VMEM_SPEC = pl.BlockSpec(memory_space=pltpu.VMEM)


def params(*arrays):
    held = sum(array.size * array.dtype.itemsize for array in jax.tree.leaves(arrays))
    return pltpu.CompilerParams(vmem_limit_bytes=held + 8 * 1024 * 1024)


def call(kernel, out_shape, operands, flops, name, in_hbm=(), out_hbm=(), scratch=(), brief=False):
    def spec(k, array):
        return HBM_SPEC if k in in_hbm else VMEM_SPEC

    if out_hbm:
        out_specs = [HBM_SPEC if k in out_hbm else VMEM_SPEC for k in range(len(out_shape))]
    else:
        out_specs = jax.tree.map(lambda _: VMEM_SPEC, out_shape)
    size = sum(array.size * array.dtype.itemsize for array in jax.tree.leaves((operands, out_shape)))
    if brief:
        flops = size = 0
    in_specs = [spec(k, array) for k, array in enumerate(operands)]
    operands = [
        pltpu.with_memory_space_constraint(array, pltpu.HBM) if space is HBM_SPEC else array
        for array, space in zip(operands, in_specs)
    ]
    return pl.pallas_call(
        kernel,
        out_shape=out_shape,
        in_specs=in_specs,
        out_specs=out_specs,
        scratch_shapes=list(scratch),
        compiler_params=params(operands, out_shape),
        cost_estimate=pl.CostEstimate(flops=flops, bytes_accessed=size, transcendentals=0),
        name=name,
    )(*operands)


def fetch(*pairs):
    copies = [pltpu.make_async_copy(source, target, sem) for source, target, sem in pairs]
    for copy in copies:
        copy.start()
    return copies


def wrap(value, length):
    value = jnp.where(value < 0, value + length, value)
    return jnp.where(value >= length, value - length, value)


def stack(*blocks):
    return jnp.concatenate(blocks, axis=0)


def beside(*blocks):
    return jnp.concatenate(blocks, axis=1)


def dot(left, right):
    return jnp.dot(left, right, preferred_element_type=jnp.float32)


def spans(pixel, anchor, num, den, length):
    stretched = (pixel * num).astype(jnp.float32)
    den = (jnp.zeros_like(pixel) + den).astype(jnp.float32)
    whole = jnp.floor((stretched + 0.5) / den)
    fraction = (stretched - whole * den) / den
    base = wrap(anchor + whole.astype(jnp.int32), length)
    upper = wrap(base + 1, length)
    return base, upper, 1.0 - fraction, fraction


def chunk_start(half, chunk):
    return 3 * half + chunk * (1 - 2 * half)


def split_kernel(screens, *refs):
    ints, outs, held, sems = refs[:3], refs[3:7], refs[7:10], refs[-1]
    width = outs[0].shape[2]
    core = lax.rem(lax.axis_index("dir"), 2)
    pairs = []
    for k, out in enumerate(outs):
        half = core if k < 2 else 1 - core
        start = pl.multiple_of(chunk_start(half, k % 2) * width, LANES)
        pairs.append((screens.at[:, :, pl.ds(start, width)], out, sems.at[k]))
    pairs += [(source, copy, sems.at[4 + k]) for k, (source, copy) in enumerate(zip(ints, held))]
    for load in fetch(*pairs):
        load.wait()


def weights_kernel(geometry, wind_held, offsets_held, ratio_held, *refs):
    n_layer, rows_dev, screen_cols = geometry
    sources, (rows_out, cols_out, *tables), refs = refs[:5], refs[5:11], refs[11:]
    copies, (wind, offsets, ratio, sems) = refs[:5], refs[5:]
    pupil_cols = cols_out.shape[2]
    loads = fetch(
        (wind_held, wind, sems.at[0]),
        (offsets_held, offsets, sems.at[1]),
        (ratio_held, ratio, sems.at[2]),
    )
    pairs = [*zip(sources, copies)]
    others = fetch(*[(source, copy, sems.at[3 + k]) for k, (source, copy) in enumerate(pairs)])
    _, layers, pupil_rows, screen_rows = rows_out.shape
    half = pupil_rows // 2
    direction = lax.axis_index("dir")
    column = lax.axis_index("layer")
    block = pupil_rows // n_layer
    row = lax.broadcasted_iota(jnp.int32, (half, LANES), 0)
    step = row // block
    for at, value in enumerate(send_order(n_layer // 2)):
        step = jnp.where(row // block == at, value, step)
    pair = step + column // 2
    pair = jnp.where(pair >= n_layer // 2, pair - n_layer // 2, pair)
    parity = lax.rem(column, 2)
    inside = lax.rem(row, block) + pair * (2 * block)
    pixel_rows = stack(inside + parity * block, inside + (1 - parity) * block)
    lane = lax.broadcasted_iota(jnp.int32, (pupil_rows, LANES), 1)
    for load in loads:
        load.wait()
    for side in range(2):
        target = jnp.bitwise_xor(direction, side)
        for level in range(layers):
            anchor = wrap(offsets[level, 0, target] - wind[0, level], screen_rows)
            num, den = ratio[level, 0, target], ratio[level, 1, target]
            base, upper, low, high = spans(pixel_rows, anchor, num, den, screen_rows)
            for peer in range(4):
                for part in range(rows_dev // LANES):
                    index = lane + (jnp.bitwise_xor(direction, peer) * rows_dev + part * LANES)
                    weight = jnp.where(index == base, low, 0.0)
                    weight = jnp.where(index == upper, high, weight)
                    start = peer * rows_dev + part * LANES
                    rows_out[side, level, :, start : start + LANES] = weight.astype(jnp.bfloat16)
    sub = lax.broadcasted_iota(jnp.int32, (8, LANES), 0)
    anchor, num, den = jnp.zeros_like(sub), jnp.zeros_like(sub), jnp.ones_like(sub)
    for level in range(layers):
        start = wrap(offsets[level, 1, direction] - wind[1, level], screen_cols)
        anchor = jnp.where(sub == level, start, anchor)
        num = jnp.where(sub == level, ratio[level, 0, direction], num)
        den = jnp.where(sub == level, ratio[level, 1, direction], den)
    for at in range(0, pupil_cols, LANES):
        pixel = lax.broadcasted_iota(jnp.int32, (8, LANES), 1) + at
        values = spans(pixel, anchor, num, den, screen_cols)
        for table, value in zip(tables, values):
            table[:, at : at + LANES] = value
    column_weights(*tables, column * cols_out.shape[1], cols_out)
    for load in others:
        load.wait()


def column_weights(base_ref, upper_ref, low_ref, high_ref, first, out):
    layers, cols_dev, pupil_cols = out.shape
    width = cols_dev // 4
    core = lax.rem(lax.axis_index("dir"), 2)
    sub = lax.broadcasted_iota(jnp.int32, (width, LANES), 0).astype(jnp.float32).astype(jnp.bfloat16)
    zero = jnp.zeros((width, LANES), jnp.bfloat16)
    for level in range(layers):

        def tile(step, carry):
            start = pl.multiple_of(step * LANES, LANES)
            cut = (slice(level, level + 1), pl.ds(start, LANES))
            base, upper = base_ref[cut], upper_ref[cut]
            low, high = [
                jnp.broadcast_to(ref[cut].astype(jnp.bfloat16), (width, LANES)) for ref in (low_ref, high_ref)
            ]
            for k in range(4):
                shift = first + chunk_start(jnp.bitwise_xor(core, k // 2), k % 2) * width
                base_at, upper_at = [
                    jnp.broadcast_to(
                        jnp.clip(value - shift, -1, width).astype(jnp.float32).astype(jnp.bfloat16), (width, LANES)
                    )
                    for value in (base, upper)
                ]
                weight = jnp.where(sub == base_at, low, zero)
                weight = jnp.where(sub == upper_at, high, weight)
                out[level, k * width : (k + 1) * width, pl.ds(start, LANES)] = weight
            return carry

        lax.fori_loop(0, pupil_cols // LANES, tile, 0)


def strips_kernel(wind_held, *refs):
    tables, (across, diagonal, near, keep, cols_out, strip, sibling_strip, wind, sem) = refs[:4], refs[4:]
    load = fetch((wind_held, wind, sem))[0]
    column_weights(*tables, jnp.bitwise_xor(lax.axis_index("layer"), 1) * cols_out.shape[1], cols_out)
    layers, rows, _ = keep.shape
    core = lax.rem(lax.axis_index("dir"), 2)
    odd = core == 1
    lane = lax.broadcasted_iota(jnp.int32, (rows + 32, LANES), 1)

    def wide(own, near, far, odd, level):
        own, near, far = [block[level].astype(jnp.float32) for block in (own, near, far)]
        before = jnp.where(odd, near[rows - 16 :], far[rows - 16 :])
        return stack(before, own, jnp.where(odd, far[:16], near[:16]))

    packed = jnp.zeros((rows + 32, LANES), jnp.float32)
    for level in range(layers):
        blocks = (keep, near, diagonal, odd), (near, keep, across, core == 0)
        for at, block in zip((WIND_MAX * level, STRIP + WIND_MAX * level), blocks):
            block = pltpu.roll(wide(*block, level), at + WIND_MAX * core, 1)
            packed = jnp.where((lane >= at) & (lane < at + WIND_MAX), block, packed)
    load.wait()
    strips = jnp.zeros((rows, LANES), jnp.float32)
    for level in range(layers):
        shift = wind[0, level]
        shift = jnp.where(shift < 0, shift + rows + 32, shift)
        moved = pltpu.roll(packed, shift, 0)[16 : 16 + rows]
        mine = lax.rem(lane[:rows], STRIP)
        strips = jnp.where((mine >= WIND_MAX * level) & (mine < WIND_MAX * (level + 1)), moved, strips)
    strips = strips.T.astype(jnp.bfloat16)
    strip[...] = strips[:STRIP]
    sibling_strip[...] = strips[STRIP : 2 * STRIP]


def project_rows(rows_ref, keep, near, across, diagonal, level):
    screen = stack(keep[level], near[level], across[level], diagonal[level])
    rows = stack(rows_ref[0, level], rows_ref[1, level])
    return dot(rows, screen).astype(jnp.bfloat16)


def first_rows_kernel(rows_ref, across, diagonal, near, keep, mine, sibling, other, sibling_other):
    layers, half, _ = mine.shape
    for level in range(layers):
        part = project_rows(rows_ref, keep, near, across, diagonal, level)
        for k, out in enumerate((mine, other, sibling, sibling_other)):
            out[level] = part[k * half : (k + 1) * half]


def put_strip(out, at, strip):
    for k in range(strip.shape[1] // LANES):
        out[at + k * STRIP : at + (k + 1) * STRIP, :] = strip[:, k * LANES : (k + 1) * LANES]


def get_strip(ref, at):
    return beside(*[ref[start : start + STRIP, :] for start in range(at, ref.shape[0], STRIP)])


def later_rows_kernel(rows_ref, *refs):
    chunks, refs = refs[:8], refs[8:]
    sibling0, strip, sibling_strip, mine, give, far, sibling_far, rest, sibling_rest = refs
    across, diagonal, near, keep, across0, diagonal0, near0, keep0 = chunks
    layers, half, width = mine.shape
    rows = near.shape[1]
    size = (far.shape[0] - STRIP * rows // LANES) // layers
    start = half - size
    for level in range(layers):
        part = project_rows(rows_ref, keep, near, across, diagonal, level)
        mine[level] = part[:half]
        for k, out, remainder in ((1, far, rest), (3, sibling_far, sibling_rest)):
            piece = part[k * half : (k + 1) * half]
            out[level * size : (level + 1) * size] = piece[start:]
            remainder[level * start : (level + 1) * start] = piece[:start]
        give[level, :half, :width] = sibling0[level]
        give[level, :half, width:] = part[2 * half : 3 * half]
        for k, blocks in enumerate(((across0, keep0), (across, keep))):
            cut = slice(k * width, (k + 1) * width)
            edges = [block[level, at : at + 16] for block in blocks for at in (0, rows - 16)]
            give[level, half:, cut] = stack(*edges)
    put_strip(far, layers * size, strip)
    put_strip(sibling_far, layers * size, sibling_strip)


def project(parts, cols_refs, at):
    cols = stack(*[ref[level, start:stop, at : at + 256] for ref, level, start, stop in cols_refs])
    return dot(beside(*parts), cols)


def phase_kernel(mine_ref, other_ref, mine0, mine1, came, sibling_came, phase):
    layers, _, width = mine0.shape
    parts, cuts = [], []
    for level in range(layers):
        parts += [mine0[level], mine1[level], came[level], sibling_came[level]]
        cuts += [(mine_ref, level, 0, 2 * width)]
        cuts += [(other_ref, level, 0, width), (other_ref, level, 2 * width, 3 * width)]
    for at in range(0, phase.shape[1], 256):
        phase[:, at : at + 256] = project(parts, cuts, at)


def taken_kernel(mine_ref, phase, taken, out):
    half, pupil_cols = phase.shape
    layers, cols_dev, _ = mine_ref.shape
    parts = [taken[level, :half] for level in range(layers)]
    cuts = [(mine_ref, level, cols_dev // 2, cols_dev) for level in range(layers)]
    for at in range(0, pupil_cols, 256):
        out[:, at : at + 256] = phase[:, at : at + 256] + project(parts, cuts, at)


def sum_up(start, cols_ref, phase, came, sibling_came, outs):
    layers, cols_dev, _ = cols_ref.shape
    width = cols_dev // 4
    block = outs[0].shape[0]
    size = block * len(outs)
    rows = slice(start, start + size)
    parts, cuts = [], []
    for level in range(layers):
        cut = slice(level * size, (level + 1) * size)
        parts += [came[cut], sibling_came[cut]]
        cuts += [(cols_ref, level, width, 2 * width), (cols_ref, level, 3 * width, 4 * width)]
    pupil_cols = phase.shape[1]
    for at in range(0, pupil_cols, 256):
        total = (phase[rows, at : at + 256] + project(parts, cuts, at)).astype(jnp.bfloat16)
        for k, out in enumerate(outs):
            out[:, at : at + 256] = total[k * block : (k + 1) * block]


def send_order(pairs):
    return [0, *range(2, pairs - 1), 1, pairs - 1]


def far_kernel(cols_ref, phase, came, sibling_came, *outs):
    *outs, strips = outs
    half = phase.shape[0]
    size = outs[0].shape[0] * len(outs)
    sum_up(half - size, cols_ref, phase, came, sibling_came, outs)
    layers = cols_ref.shape[0]
    odd = lax.rem(lax.axis_index("dir"), 2) == 1
    here = get_strip(came, layers * size).astype(jnp.float32)
    there = get_strip(sibling_came, layers * size).astype(jnp.float32)
    last = jnp.where(odd, here, there).astype(jnp.bfloat16)
    first = jnp.where(odd, there, here).astype(jnp.bfloat16)
    strips[:STRIP], strips[STRIP:] = last, first
    for out, strip in zip(outs, (last, first)):
        out[:, phase.shape[1] :] = strip


def rest_kernel(cols_ref, phase, came, sibling_came, *outs):
    sum_up(0, cols_ref, phase, came, sibling_came, outs)


def shifted_rows(shift, odd, own, near, far):
    own, near, far = [block.astype(jnp.float32) for block in (own, near, far)]
    rows = own.shape[0]
    before = jnp.where(odd, near[16:], far[16:])
    after = jnp.where(odd, far[:16], near[:16])
    shift = jnp.where(shift < 0, shift + rows + 32, shift)
    return pltpu.roll(stack(before, own, after), shift, 0)[16 : 16 + rows]


def shift_kernel(wind_held, own, near0, near1, diagonal0, diagonal1, taken, partner_strips, before, after, out, wind, sem):
    load = fetch((wind_held, wind, sem))[0]
    layers, rows, cols = own.shape
    odd = lax.rem(lax.axis_index("dir"), 2) == 1
    half = taken.shape[1] - 64
    second = lax.rem(lax.axis_index("layer"), 2) == 1
    at = before.shape[1] - rows
    left = jnp.where(second, partner_strips[:STRIP].astype(jnp.float32), before[:, at:].astype(jnp.float32))
    right = jnp.where(second, after[:, at:].astype(jnp.float32), partner_strips[STRIP:].astype(jnp.float32))
    strips = stack(left, right, jnp.zeros((LANES - 2 * STRIP, rows), jnp.float32)).T
    lane = lax.broadcasted_iota(jnp.int32, (rows, LANES), 1)
    load.wait()
    for level in range(layers):
        last = pltpu.roll(strips, LANES - WIND_MAX * (level + 1), 1)
        first = pltpu.roll(strips, LANES - STRIP - WIND_MAX * level, 1)
        extra = jnp.where(lane < WIND_MAX, first, last)
        pair = []
        for at, parts in ((half, (diagonal0, diagonal1)), (half + 32, (near0, near1))):
            here = [stack(part[level, :16], part[level, rows - 16 :]).astype(jnp.float32) for part in parts]
            there = taken[level, at : at + 32].astype(jnp.float32)
            width = there.shape[1] // 2
            quarters = [*here, there[:, width:], there[:, :width]]
            pair.append(beside(*[jnp.where(odd, quarters[3 - k], quarters[k]) for k in range(4)]))
        far, near = pair
        moved = shifted_rows(wind[0, level], odd, own[level], near, far)
        shift = wind[1, level]
        shift = jnp.where(shift < 0, shift + cols + LANES, shift)
        out[level] = pltpu.roll(beside(moved, extra), shift, 1)[:, :cols].astype(jnp.bfloat16)


def optics_kernel(amplitude, ones, columns, lines, amp_out, columns_out, lines_out):
    rows, pupil_cols = amplitude.shape
    for step in range(pupil_cols // LANES):
        cut = slice(step * LANES, (step + 1) * LANES)
        amp = amplitude[:, cut]
        energy = (amp * amp).reshape(rows // SUB_PIX, SUB_PIX, LANES).sum(axis=1)
        energy = jnp.broadcast_to(energy[:, None], (rows // SUB_PIX, SUB_PIX, LANES)).reshape(rows, LANES)
        total = jnp.dot(energy, ones[...], precision=lax.Precision.HIGHEST, preferred_element_type=jnp.float32)
        amp_out[:, cut] = amp * lax.rsqrt(total)
    columns_out[...] = columns[...].astype(jnp.bfloat16)
    lines_out[...] = lines[...].astype(jnp.bfloat16)


def sin_cos(phase):
    turns = jnp.floor(phase * (1.0 / np.pi) + 0.5)
    rest = phase - turns * 3.140625
    rest = rest - turns * 9.67653589793e-4
    odd = turns - 2.0 * jnp.floor(turns * 0.5)
    sign = 1.0 - 2.0 * odd
    square = rest * rest
    sine = -1.0 / 39916800.0
    for term in (1.0 / 362880.0, -1.0 / 5040.0, 1.0 / 120.0, -1.0 / 6.0, 1.0):
        sine = sine * square + term
    cosine = 1.0 / 479001600.0
    for term in (-1.0 / 3628800.0, 1.0 / 40320.0, -1.0 / 720.0, 1.0 / 24.0, -0.5, 1.0):
        cosine = cosine * square + term
    return sine * rest * sign, cosine * sign


def imaging_kernel(count, *refs):
    parts, (amp_ref, columns, lines, shifted, spots, screens, out, sems) = refs[:count], refs[count:]
    copies = fetch((shifted, screens, sems.at[0]))
    rows, cols = amp_ref.shape
    tiles = cols // LANES
    phase = parts[0][:, :cols].astype(jnp.float32)
    for part in parts[1:]:
        phase = phase + part[:, :cols].astype(jnp.float32)
    sine, cosine = sin_cos(phase)
    amp = amp_ref[...]
    real, imag = (amp * cosine).astype(jnp.bfloat16), (amp * sine).astype(jnp.bfloat16)
    cuts = [slice(t * LANES, (t + 1) * LANES) for t in range(tiles)]
    field = stack(*[beside(real[:, cut], imag[:, cut]) for cut in cuts])
    half = dot(field, columns[...]).astype(jnp.bfloat16)
    wide = 2 * LANES
    out_rows = 2 * rows
    for t in range(tiles):
        mine = half[t * rows : (t + 1) * rows]
        full = dot(lines[...], stack(mine[:, :wide], mine[:, wide:]))
        real, imag = full[:out_rows], full[out_rows:]
        out[:, t * wide : (t + 1) * wide] = real * real + imag * imag
        if t % 2:
            cut = slice((t - 1) * wide, (t + 1) * wide)
            copies += fetch((out.at[:, cut], spots.at[:, cut], sems.at[1 + t // 2]))
    for copy in copies:
        copy.wait()


def tables_of(rows):
    freq = np.arange(SPOT_PIX)[:, None] - SPOT_PIX // 2
    angle = ((freq * np.arange(SUB_PIX)[None, :]) % SPOT_PIX) * (2.0 * np.pi / SPOT_PIX)
    cos, sin = np.cos(angle), np.sin(angle)

    def blocks(table, count):
        return np.kron(np.eye(count), table)

    per_tile = LANES // SUB_PIX
    col_cos, col_sin = blocks(cos.T, per_tile), blocks(sin.T, per_tile)
    columns = np.block([[col_cos, -col_sin], [col_sin, col_cos]])
    count = rows // SUB_PIX
    row_cos, row_sin = blocks(cos, count), blocks(sin, count)
    lines = np.block([[row_cos, row_sin], [-row_sin, row_cos]])

    return columns.astype(np.float32), lines.astype(np.float32)


def per_device(screens, amplitude, wind, offsets, ratio):
    layers, rows_dev, cols_dev = screens.shape
    n_layer = lax.axis_size("layer")
    n_dir = lax.axis_size("dir")
    rows, pupil_cols = amplitude.shape
    pairs = n_layer // 2
    half = pairs * rows
    pupil_rows = 2 * half
    assert n_dir == 4 and rows == STRIP and pairs > 2
    bf16, f32 = jnp.bfloat16, jnp.float32
    wind = jnp.transpose(wind, (1, 0))
    offsets = jnp.transpose(offsets, (1, 2, 0))
    ratio = jnp.transpose(ratio, (1, 2, 0))
    smem, sem = pltpu.SMEM, pltpu.SemaphoreType.DMA
    wind_scratch = [smem(wind.shape, jnp.int32), sem]

    def shape(*dims, dtype=bf16):
        return jax.ShapeDtypeStruct(dims, dtype)

    def swap(value, bits):
        return lax.ppermute(value, "dir", [(i, i ^ bits) for i in range(n_dir)])

    def partner(value, bits=0):
        count = n_layer * n_dir
        return lax.ppermute(value, ("layer", "dir"), [(i, i ^ n_dir ^ bits) for i in range(count)])

    def turn(value, step):
        return lax.ppermute(value, "layer", [(i, (i + step) % n_layer) for i in range(n_layer)])

    width = cols_dev // 4
    chunk = shape(layers, rows_dev, width)
    ints = (wind, offsets, ratio)
    keep0, keep1, give0, give1, *ints = call(
        split_kernel,
        [chunk] * 4 + [shape(*array.shape, dtype=jnp.int32) for array in ints],
        (screens, *ints),
        0,
        "split",
        in_hbm=range(4),
        scratch=[sem((7,))],
        brief=True,
    )
    across0 = swap(keep0, 2)
    diagonal0 = swap(give0, 3)
    near0 = swap(give0, 1)
    across1 = swap(keep1, 2)
    diagonal1 = swap(give1, 3)
    ones = np.kron(np.eye(LANES // SUB_PIX), np.ones((SUB_PIX, SUB_PIX))).astype(np.float32)
    optics_in = (amplitude, jnp.asarray(ones), *[jnp.asarray(table) for table in tables_of(rows)])
    copies = [shape(*array.shape, dtype=array.dtype) for array in (screens, *optics_in)]
    row_weights, cols, *loaded = call(
        functools.partial(weights_kernel, (n_layer, rows_dev, cols_dev * n_layer)),
        [shape(2, layers, pupil_rows, 4 * rows_dev), shape(layers, cols_dev, pupil_cols)]
        + [shape(8, pupil_cols, dtype=dtype) for dtype in (jnp.int32, jnp.int32, f32, f32)]
        + copies,
        (*ints, screens, *optics_in),
        0,
        "weights",
        in_hbm=range(3, 8),
        scratch=[smem(array.shape, jnp.int32) for array in (wind, offsets, ratio)]
        + [sem((8,))],
        brief=True,
    )
    tables, (own, *optics_in) = loaded[:4], loaded[4:]
    wind = ints[0]
    give1, own = lax.optimization_barrier((give1, own))
    near1 = swap(give1, 1)
    across0, diagonal0, row_weights, cols = lax.optimization_barrier((across0, diagonal0, row_weights, cols))

    projected = shape(layers, half, width)
    mine0, sibling0, other0, sibling_other0 = call(
        first_rows_kernel,
        [projected] * 4,
        (row_weights, across0, diagonal0, near0, keep0),
        0,
        "rows_first",
        brief=True,
    )
    came0 = partner(other0)
    sibling_came0 = partner(sibling_other0, 1)

    wind, mine0 = lax.optimization_barrier((wind, mine0))
    others, strip, sibling_strip = call(
        strips_kernel,
        [shape(layers, cols_dev, pupil_cols)] + [shape(STRIP, rows_dev)] * 2,
        (wind, *tables, across0, diagonal0, near0, keep0),
        0,
        "strips",
        scratch=wind_scratch,
        brief=True,
    )
    far = 2 * rows
    message = shape(layers * far + STRIP * rows_dev // LANES, width)
    remainder = shape(layers * (half - far), width)
    mine1, give, far1, sibling_far1, rest1, sibling_rest1 = call(
        later_rows_kernel,
        [projected, shape(layers, half + 64, 2 * width), message, message, remainder, remainder],
        (row_weights, across1, diagonal1, near1, keep1, across0, diagonal0, near0, keep0, sibling0, strip, sibling_strip),
        0,
        "rows_later",
        brief=True,
    )
    far1, sibling_far1 = partner(far1), partner(sibling_far1, 1)
    taken = swap(give, 1)
    phase = call(
        phase_kernel,
        shape(half, pupil_cols, dtype=f32),
        (cols, others, mine0, mine1, came0, sibling_came0),
        10_000_000_000,
        "phase",
    )

    rest1, sibling_rest1, phase = lax.optimization_barrier((rest1, sibling_rest1, phase))
    rest1, sibling_rest1 = partner(rest1), partner(sibling_rest1, 1)
    phase = call(
        taken_kernel,
        shape(half, pupil_cols, dtype=f32),
        (cols, phase, taken),
        0,
        "taken",
        brief=True,
    )
    *far_sums, strips = call(
        far_kernel,
        [shape(rows, pupil_cols + rows_dev)] * 2 + [shape(2 * STRIP, rows_dev)],
        (others, phase, far1, sibling_far1),
        300_000_000,
        "far",
    )
    rest_sums = call(
        rest_kernel,
        [shape(rows, pupil_cols)] * (pairs - 2),
        (others, phase, rest1, sibling_rest1),
        0,
        "rest",
        brief=True,
    )
    received = dict(zip(send_order(pairs), [*rest_sums, *far_sums]))
    for k in range(1, pairs):
        received[k] = turn(received[k], 2 * k)
    received = [received[k] for k in range(pairs)]

    optics_in, received[1] = lax.optimization_barrier((optics_in, received[1]))
    optics = call(
        optics_kernel,
        (
            shape(rows, pupil_cols, dtype=f32),
            shape(*optics_in[2].shape),
            shape(*optics_in[3].shape),
        ),
        optics_in,
        0,
        "optics",
        brief=True,
    )
    received[-1], optics = lax.optimization_barrier((received[-1], optics))
    shifted = call(
        shift_kernel,
        shape(layers, rows_dev, cols_dev),
        (wind, own, near0, near1, diagonal0, diagonal1, taken, strips, received[1], received[-1]),
        0,
        "shift",
        scratch=wind_scratch,
        brief=True,
    )
    spots_shape = shape(2 * rows, 2 * pupil_cols, dtype=f32)
    spots, new_screens = call(
        functools.partial(imaging_kernel, pairs),
        [spots_shape, shape(layers, rows_dev, cols_dev)],
        (*received, *optics, shifted),
        400_000_000,
        "imaging",
        out_hbm=(0, 1),
        scratch=[pltpu.VMEM(spots_shape.shape, f32), sem((1 + pupil_cols // (2 * LANES),))],
    )
    return (new_screens, spots[None])


def solution(mesh):
    return jax.shard_map(
        per_device,
        mesh=mesh,
        in_specs=(P(None, "dir", "layer"), P("layer", None), P(), P(), P()),
        out_specs=(P(None, "dir", "layer"), P("dir", "layer", None)),
        check_vma=False,
    )
```

```python
import functools

import jax
import jax.numpy as jnp
import numpy as np
from jax import lax
from jax.experimental import pallas as pl
from jax.experimental.pallas import tpu as pltpu
from jax.sharding import PartitionSpec as P

SUB_PIX = 16
SPOT_PIX = 32
WIND_MAX = 8
LANES = 128
STRIP = 32

HBM_SPEC = pl.BlockSpec(memory_space=pltpu.HBM)
VMEM_SPEC = pl.BlockSpec(memory_space=pltpu.VMEM)


def params(*arrays):
    held = sum(array.size * array.dtype.itemsize for array in jax.tree.leaves(arrays))
    return pltpu.CompilerParams(vmem_limit_bytes=held + 8 * 1024 * 1024)


def call(kernel, out_shape, operands, flops, name, in_hbm=(), out_hbm=(), scratch=(), brief=False):
    def spec(k, array):
        return HBM_SPEC if k in in_hbm else VMEM_SPEC

    if out_hbm:
        out_specs = [HBM_SPEC if k in out_hbm else VMEM_SPEC for k in range(len(out_shape))]
    else:
        out_specs = jax.tree.map(lambda _: VMEM_SPEC, out_shape)
    size = sum(array.size * array.dtype.itemsize for array in jax.tree.leaves((operands, out_shape)))
    if brief:
        flops = size = 0
    in_specs = [spec(k, array) for k, array in enumerate(operands)]
    operands = [
        pltpu.with_memory_space_constraint(array, pltpu.HBM) if space is HBM_SPEC else array
        for array, space in zip(operands, in_specs)
    ]
    return pl.pallas_call(
        kernel,
        out_shape=out_shape,
        in_specs=in_specs,
        out_specs=out_specs,
        scratch_shapes=list(scratch),
        compiler_params=params(operands, out_shape),
        cost_estimate=pl.CostEstimate(flops=flops, bytes_accessed=size, transcendentals=0),
        name=name,
    )(*operands)


def fetch(*pairs):
    copies = [pltpu.make_async_copy(source, target, sem) for source, target, sem in pairs]
    for copy in copies:
        copy.start()
    return copies


def wrap(value, length):
    value = jnp.where(value < 0, value + length, value)
    return jnp.where(value >= length, value - length, value)


def stack(*blocks):
    return jnp.concatenate(blocks, axis=0)


def beside(*blocks):
    return jnp.concatenate(blocks, axis=1)


def dot(left, right):
    return jnp.dot(left, right, preferred_element_type=jnp.float32)


def spans(pixel, anchor, num, den, length):
    stretched = (pixel * num).astype(jnp.float32)
    den = (jnp.zeros_like(pixel) + den).astype(jnp.float32)
    whole = jnp.floor((stretched + 0.5) / den)
    fraction = (stretched - whole * den) / den
    base = wrap(anchor + whole.astype(jnp.int32), length)
    upper = wrap(base + 1, length)
    return base, upper, 1.0 - fraction, fraction


def chunk_start(half, chunk):
    return 3 * half + chunk * (1 - 2 * half)


def split_kernel(screens, *refs):
    ints, outs, held, sems = refs[:3], refs[3:7], refs[7:10], refs[-1]
    width = outs[0].shape[2]
    core = lax.rem(lax.axis_index("dir"), 2)
    pairs = []
    for k, out in enumerate(outs):
        half = core if k < 2 else 1 - core
        start = pl.multiple_of(chunk_start(half, k % 2) * width, LANES)
        pairs.append((screens.at[:, :, pl.ds(start, width)], out, sems.at[k]))
    pairs += [(source, copy, sems.at[4 + k]) for k, (source, copy) in enumerate(zip(ints, held))]
    for load in fetch(*pairs):
        load.wait()


def weights_kernel(geometry, wind_held, offsets_held, ratio_held, *refs):
    n_layer, rows_dev, screen_cols = geometry
    sources, (rows_out, cols_out, *tables), refs = refs[:5], refs[5:11], refs[11:]
    copies, (wind, offsets, ratio, sems) = refs[:5], refs[5:]
    pupil_cols = cols_out.shape[2]
    loads = fetch(
        (wind_held, wind, sems.at[0]),
        (offsets_held, offsets, sems.at[1]),
        (ratio_held, ratio, sems.at[2]),
    )
    pairs = [*zip(sources, copies)]
    others = fetch(*[(source, copy, sems.at[3 + k]) for k, (source, copy) in enumerate(pairs)])
    _, layers, pupil_rows, screen_rows = rows_out.shape
    half = pupil_rows // 2
    direction = lax.axis_index("dir")
    column = lax.axis_index("layer")
    block = pupil_rows // n_layer
    row = lax.broadcasted_iota(jnp.int32, (half, LANES), 0)
    step = row // block
    for at, value in enumerate(send_order(n_layer // 2)):
        step = jnp.where(row // block == at, value, step)
    pair = jnp.bitwise_xor(step, column // 2)
    parity = lax.rem(column, 2)
    inside = lax.rem(row, block) + pair * (2 * block)
    pixel_rows = stack(inside + parity * block, inside + (1 - parity) * block)
    lane = lax.broadcasted_iota(jnp.int32, (pupil_rows, LANES), 1)
    for load in loads:
        load.wait()
    for side in range(2):
        target = jnp.bitwise_xor(direction, side)
        for level in range(layers):
            anchor = wrap(offsets[level, 0, target] - wind[0, level], screen_rows)
            num, den = ratio[level, 0, target], ratio[level, 1, target]
            base, upper, low, high = spans(pixel_rows, anchor, num, den, screen_rows)
            for peer in range(4):
                for part in range(rows_dev // LANES):
                    index = lane + (jnp.bitwise_xor(direction, peer) * rows_dev + part * LANES)
                    weight = jnp.where(index == base, low, 0.0)
                    weight = jnp.where(index == upper, high, weight)
                    start = peer * rows_dev + part * LANES
                    rows_out[side, level, :, start : start + LANES] = weight.astype(jnp.bfloat16)
    sub = lax.broadcasted_iota(jnp.int32, (8, LANES), 0)
    anchor, num, den = jnp.zeros_like(sub), jnp.zeros_like(sub), jnp.ones_like(sub)
    for level in range(layers):
        start = wrap(offsets[level, 1, direction] - wind[1, level], screen_cols)
        anchor = jnp.where(sub == level, start, anchor)
        num = jnp.where(sub == level, ratio[level, 0, direction], num)
        den = jnp.where(sub == level, ratio[level, 1, direction], den)
    for at in range(0, pupil_cols, LANES):
        pixel = lax.broadcasted_iota(jnp.int32, (8, LANES), 1) + at
        values = spans(pixel, anchor, num, den, screen_cols)
        for table, value in zip(tables, values):
            table[:, at : at + LANES] = value
    column_weights(*tables, column * cols_out.shape[1], cols_out)
    for load in others:
        load.wait()


def column_weights(base_ref, upper_ref, low_ref, high_ref, first, out):
    layers, cols_dev, pupil_cols = out.shape
    width = cols_dev // 4
    core = lax.rem(lax.axis_index("dir"), 2)
    sub = lax.broadcasted_iota(jnp.int32, (width, LANES), 0).astype(jnp.float32).astype(jnp.bfloat16)
    zero = jnp.zeros((width, LANES), jnp.bfloat16)
    for level in range(layers):

        def tile(step, carry):
            start = pl.multiple_of(step * LANES, LANES)
            cut = (slice(level, level + 1), pl.ds(start, LANES))
            base, upper = base_ref[cut], upper_ref[cut]
            low, high = [
                jnp.broadcast_to(ref[cut].astype(jnp.bfloat16), (width, LANES)) for ref in (low_ref, high_ref)
            ]
            for k in range(4):
                shift = first + chunk_start(jnp.bitwise_xor(core, k // 2), k % 2) * width
                base_at, upper_at = [
                    jnp.broadcast_to(
                        jnp.clip(value - shift, -1, width).astype(jnp.float32).astype(jnp.bfloat16), (width, LANES)
                    )
                    for value in (base, upper)
                ]
                weight = jnp.where(sub == base_at, low, zero)
                weight = jnp.where(sub == upper_at, high, weight)
                out[level, k * width : (k + 1) * width, pl.ds(start, LANES)] = weight
            return carry

        lax.fori_loop(0, pupil_cols // LANES, tile, 0)


def strips_kernel(wind_held, *refs):
    tables, rows_ref, blocks, refs = refs[:4], refs[4], refs[5:9], refs[9:]
    across, diagonal, near, keep = blocks
    cols_out, mine, sibling, strip, sibling_strip, wind, sem = refs
    load = fetch((wind_held, wind, sem))[0]
    half = mine.shape[1]
    for level in range(mine.shape[0]):
        part = project_rows(rows_ref, keep, near, across, diagonal, level, slice(0, half))
        mine[level] = part[:half]
        sibling[level] = part[half:]
    column_weights(*tables, jnp.bitwise_xor(lax.axis_index("layer"), 1) * cols_out.shape[1], cols_out)
    layers, rows, _ = keep.shape
    core = lax.rem(lax.axis_index("dir"), 2)
    odd = core == 1
    lane = lax.broadcasted_iota(jnp.int32, (rows + 32, LANES), 1)

    def wide(own, near, far, odd, level):
        own, near, far = [block[level].astype(jnp.float32) for block in (own, near, far)]
        before = jnp.where(odd, near[rows - 16 :], far[rows - 16 :])
        return stack(before, own, jnp.where(odd, far[:16], near[:16]))

    packed = jnp.zeros((rows + 32, LANES), jnp.float32)
    for level in range(layers):
        blocks = (keep, near, diagonal, odd), (near, keep, across, core == 0)
        for at, block in zip((WIND_MAX * level, STRIP + WIND_MAX * level), blocks):
            block = pltpu.roll(wide(*block, level), at + WIND_MAX * core, 1)
            packed = jnp.where((lane >= at) & (lane < at + WIND_MAX), block, packed)
    load.wait()
    strips = jnp.zeros((rows, LANES), jnp.float32)
    for level in range(layers):
        shift = wind[0, level]
        shift = jnp.where(shift < 0, shift + rows + 32, shift)
        moved = pltpu.roll(packed, shift, 0)[16 : 16 + rows]
        mine = lax.rem(lane[:rows], STRIP)
        strips = jnp.where((mine >= WIND_MAX * level) & (mine < WIND_MAX * (level + 1)), moved, strips)
    strips = strips.T.astype(jnp.bfloat16)
    strip[...] = strips[:STRIP]
    sibling_strip[...] = strips[STRIP : 2 * STRIP]


def project_rows(rows_ref, keep, near, across, diagonal, level, cut=slice(None)):
    screen = stack(keep[level], near[level], across[level], diagonal[level])
    rows = stack(rows_ref[0, level, cut], rows_ref[1, level, cut])
    return dot(rows, screen).astype(jnp.bfloat16)


def first_rows_kernel(rows_ref, across, diagonal, near, keep, other, sibling_other):
    layers, half, _ = other.shape
    for level in range(layers):
        part = project_rows(rows_ref, keep, near, across, diagonal, level, slice(half, 2 * half))
        other[level] = part[:half]
        sibling_other[level] = part[half:]


def put_strip(out, at, strip):
    for k in range(strip.shape[1] // LANES):
        out[at + k * STRIP : at + (k + 1) * STRIP, :] = strip[:, k * LANES : (k + 1) * LANES]


def get_strip(ref, at):
    return beside(*[ref[start : start + STRIP, :] for start in range(at, ref.shape[0], STRIP)])


def later_rows_kernel(rows_ref, *refs):
    chunks, refs = refs[:8], refs[8:]
    sibling0, strip, sibling_strip, mine, give, far, sibling_far, rest, sibling_rest = refs
    across, diagonal, near, keep, across0, diagonal0, near0, keep0 = chunks
    layers, half, width = mine.shape
    rows = near.shape[1]
    size = (far.shape[0] - STRIP * rows // LANES) // layers
    start = half - size
    for level in range(layers):
        part = project_rows(rows_ref, keep, near, across, diagonal, level)
        mine[level] = part[:half]
        for k, out, remainder in ((1, far, rest), (3, sibling_far, sibling_rest)):
            piece = part[k * half : (k + 1) * half]
            out[level * size : (level + 1) * size] = piece[start:]
            remainder[level * start : (level + 1) * start] = piece[:start]
        give[level, :half, :width] = sibling0[level]
        give[level, :half, width:] = part[2 * half : 3 * half]
        for k, blocks in enumerate(((across0, keep0), (across, keep))):
            cut = slice(k * width, (k + 1) * width)
            edges = [block[level, at : at + 16] for block in blocks for at in (0, rows - 16)]
            give[level, half:, cut] = stack(*edges)
    put_strip(far, layers * size, strip)
    put_strip(sibling_far, layers * size, sibling_strip)


def project(parts, cols_refs, at):
    cols = stack(*[ref[level, start:stop, at : at + 256] for ref, level, start, stop in cols_refs])
    return dot(beside(*parts), cols)


def phase_kernel(mine_ref, other_ref, mine0, mine1, came, sibling_came, phase):
    layers, _, width = mine0.shape
    parts, cuts = [], []
    for level in range(layers):
        parts += [mine0[level], mine1[level], came[level], sibling_came[level]]
        cuts += [(mine_ref, level, 0, 2 * width)]
        cuts += [(other_ref, level, 0, width), (other_ref, level, 2 * width, 3 * width)]
    for at in range(0, phase.shape[1], 256):
        phase[:, at : at + 256] = project(parts, cuts, at)


def taken_kernel(mine_ref, phase, taken, out):
    half, pupil_cols = phase.shape
    layers, cols_dev, _ = mine_ref.shape
    parts = [taken[level, :half] for level in range(layers)]
    cuts = [(mine_ref, level, cols_dev // 2, cols_dev) for level in range(layers)]
    for at in range(0, pupil_cols, 256):
        out[:, at : at + 256] = phase[:, at : at + 256] + project(parts, cuts, at)


def sum_up(start, cols_ref, phase, came, sibling_came, outs):
    layers, cols_dev, _ = cols_ref.shape
    width = cols_dev // 4
    block = outs[0].shape[0]
    size = block * len(outs)
    rows = slice(start, start + size)
    parts, cuts = [], []
    for level in range(layers):
        cut = slice(level * size, (level + 1) * size)
        parts += [came[cut], sibling_came[cut]]
        cuts += [(cols_ref, level, width, 2 * width), (cols_ref, level, 3 * width, 4 * width)]
    pupil_cols = phase.shape[1]
    for at in range(0, pupil_cols, 256):
        total = (phase[rows, at : at + 256] + project(parts, cuts, at)).astype(jnp.bfloat16)
        for k, out in enumerate(outs):
            out[:, at : at + 256] = total[k * block : (k + 1) * block]


def strip_steps(pairs):
    return [2**k - 1 for k in range(1, pairs.bit_length())]


def send_order(pairs):
    steps = strip_steps(pairs)
    return [k for k in range(pairs) if k not in steps] + steps


def add_strip(pairs, step, strips, out):
    pair = lax.axis_index("layer") // 2
    after = lax.rem(pair + 1, pairs) == jnp.bitwise_xor(pair, step)
    at = out.shape[1] - strips.shape[1]
    last, first = strips[:STRIP].astype(jnp.float32), strips[STRIP:].astype(jnp.float32)
    out[:, at:] = jnp.where(after, last, first).astype(jnp.bfloat16)


def far_kernel(cols_ref, phase, came, sibling_came, *outs):
    *outs, strips = outs
    half = phase.shape[0]
    size = outs[0].shape[0] * len(outs)
    sum_up(half - size, cols_ref, phase, came, sibling_came, outs)
    layers = cols_ref.shape[0]
    odd = lax.rem(lax.axis_index("dir"), 2) == 1
    here = get_strip(came, layers * size).astype(jnp.float32)
    there = get_strip(sibling_came, layers * size).astype(jnp.float32)
    strips[:STRIP] = jnp.where(odd, here, there).astype(jnp.bfloat16)
    strips[STRIP:] = jnp.where(odd, there, here).astype(jnp.bfloat16)
    pairs = half // outs[0].shape[0]
    for out, step in zip(outs, strip_steps(pairs)):
        add_strip(pairs, step, strips, out)


def rest_kernel(cols_ref, phase, came, sibling_came, *outs):
    sum_up(0, cols_ref, phase, came, sibling_came, outs)


def shifted_rows(shift, odd, own, near, far):
    own, near, far = [block.astype(jnp.float32) for block in (own, near, far)]
    rows = own.shape[0]
    before = jnp.where(odd, near[16:], far[16:])
    after = jnp.where(odd, far[:16], near[:16])
    shift = jnp.where(shift < 0, shift + rows + 32, shift)
    return pltpu.roll(stack(before, own, after), shift, 0)[16 : 16 + rows]


def shift_kernel(wind_held, own, near0, near1, diagonal0, diagonal1, taken, partner_strips, *refs):
    messages, (out, wind, sem) = refs[:-3], refs[-3:]
    load = fetch((wind_held, wind, sem))[0]
    layers, rows, cols = own.shape
    odd = lax.rem(lax.axis_index("dir"), 2) == 1
    half = taken.shape[1] - 64
    pairs = 2 ** len(messages)
    pair, second = lax.axis_index("layer") // 2, lax.rem(lax.axis_index("layer"), 2) == 1
    before = jnp.bitwise_xor(pair, lax.rem(pair + pairs - 1, pairs))
    after = jnp.bitwise_xor(pair, lax.rem(pair + 1, pairs))
    left = partner_strips[:STRIP].astype(jnp.float32)
    right = partner_strips[STRIP:].astype(jnp.float32)
    for step, message in zip(strip_steps(pairs), messages):
        strip = message[:, message.shape[1] - rows :].astype(jnp.float32)
        left = jnp.where(jnp.logical_and(before == step, jnp.logical_not(second)), strip, left)
        right = jnp.where(jnp.logical_and(after == step, second), strip, right)
    strips = stack(left, right, jnp.zeros((LANES - 2 * STRIP, rows), jnp.float32)).T
    lane = lax.broadcasted_iota(jnp.int32, (rows, LANES), 1)
    load.wait()
    for level in range(layers):
        last = pltpu.roll(strips, LANES - WIND_MAX * (level + 1), 1)
        first = pltpu.roll(strips, LANES - STRIP - WIND_MAX * level, 1)
        extra = jnp.where(lane < WIND_MAX, first, last)
        pair = []
        for at, parts in ((half, (diagonal0, diagonal1)), (half + 32, (near0, near1))):
            here = [stack(part[level, :16], part[level, rows - 16 :]).astype(jnp.float32) for part in parts]
            there = taken[level, at : at + 32].astype(jnp.float32)
            width = there.shape[1] // 2
            quarters = [*here, there[:, width:], there[:, :width]]
            pair.append(beside(*[jnp.where(odd, quarters[3 - k], quarters[k]) for k in range(4)]))
        far, near = pair
        moved = shifted_rows(wind[0, level], odd, own[level], near, far)
        shift = wind[1, level]
        shift = jnp.where(shift < 0, shift + cols + LANES, shift)
        out[level] = pltpu.roll(beside(moved, extra), shift, 1)[:, :cols].astype(jnp.bfloat16)


def optics_kernel(amplitude, ones, columns, lines, amp_out, columns_out, lines_out):
    rows, pupil_cols = amplitude.shape
    for step in range(pupil_cols // LANES):
        cut = slice(step * LANES, (step + 1) * LANES)
        amp = amplitude[:, cut]
        energy = (amp * amp).reshape(rows // SUB_PIX, SUB_PIX, LANES).sum(axis=1)
        energy = jnp.broadcast_to(energy[:, None], (rows // SUB_PIX, SUB_PIX, LANES)).reshape(rows, LANES)
        total = jnp.dot(energy, ones[...], precision=lax.Precision.HIGHEST, preferred_element_type=jnp.float32)
        amp_out[:, cut] = amp * lax.rsqrt(total)
    columns_out[...] = columns[...].astype(jnp.bfloat16)
    lines_out[...] = lines[...].astype(jnp.bfloat16)


def sin_cos(phase):
    turns = jnp.floor(phase * (1.0 / np.pi) + 0.5)
    rest = phase - turns * 3.140625
    rest = rest - turns * 9.67653589793e-4
    odd = turns - 2.0 * jnp.floor(turns * 0.5)
    sign = 1.0 - 2.0 * odd
    square = rest * rest
    sine = -1.0 / 39916800.0
    for term in (1.0 / 362880.0, -1.0 / 5040.0, 1.0 / 120.0, -1.0 / 6.0, 1.0):
        sine = sine * square + term
    cosine = 1.0 / 479001600.0
    for term in (-1.0 / 3628800.0, 1.0 / 40320.0, -1.0 / 720.0, 1.0 / 24.0, -0.5, 1.0):
        cosine = cosine * square + term
    return sine * rest * sign, cosine * sign


def imaging_kernel(count, *refs):
    parts, (amp_ref, columns, lines, shifted, spots, screens, out, sems) = refs[:count], refs[count:]
    copies = fetch((shifted, screens, sems.at[0]))
    rows, cols = amp_ref.shape
    tiles = cols // LANES
    phase = parts[0][:, :cols].astype(jnp.float32)
    for part in parts[1:]:
        phase = phase + part[:, :cols].astype(jnp.float32)
    sine, cosine = sin_cos(phase)
    amp = amp_ref[...]
    real, imag = (amp * cosine).astype(jnp.bfloat16), (amp * sine).astype(jnp.bfloat16)
    cuts = [slice(t * LANES, (t + 1) * LANES) for t in range(tiles)]
    field = stack(*[beside(real[:, cut], imag[:, cut]) for cut in cuts])
    half = dot(field, columns[...]).astype(jnp.bfloat16)
    wide = 2 * LANES
    out_rows = 2 * rows
    for t in range(tiles):
        mine = half[t * rows : (t + 1) * rows]
        full = dot(lines[...], stack(mine[:, :wide], mine[:, wide:]))
        real, imag = full[:out_rows], full[out_rows:]
        out[:, t * wide : (t + 1) * wide] = real * real + imag * imag
        if t % 2:
            cut = slice((t - 1) * wide, (t + 1) * wide)
            copies += fetch((out.at[:, cut], spots.at[:, cut], sems.at[1 + t // 2]))
    for copy in copies:
        copy.wait()


def tables_of(rows):
    freq = np.arange(SPOT_PIX)[:, None] - SPOT_PIX // 2
    angle = ((freq * np.arange(SUB_PIX)[None, :]) % SPOT_PIX) * (2.0 * np.pi / SPOT_PIX)
    cos, sin = np.cos(angle), np.sin(angle)

    def blocks(table, count):
        return np.kron(np.eye(count), table)

    per_tile = LANES // SUB_PIX
    col_cos, col_sin = blocks(cos.T, per_tile), blocks(sin.T, per_tile)
    columns = np.block([[col_cos, -col_sin], [col_sin, col_cos]])
    count = rows // SUB_PIX
    row_cos, row_sin = blocks(cos, count), blocks(sin, count)
    lines = np.block([[row_cos, row_sin], [-row_sin, row_cos]])

    return columns.astype(np.float32), lines.astype(np.float32)


def per_device(screens, amplitude, wind, offsets, ratio):
    layers, rows_dev, cols_dev = screens.shape
    n_layer = lax.axis_size("layer")
    n_dir = lax.axis_size("dir")
    rows, pupil_cols = amplitude.shape
    pairs = n_layer // 2
    half = pairs * rows
    pupil_rows = 2 * half
    assert n_dir == 4 and rows == STRIP and pairs > 2
    bf16, f32 = jnp.bfloat16, jnp.float32
    wind = jnp.transpose(wind, (1, 0))
    offsets = jnp.transpose(offsets, (1, 2, 0))
    ratio = jnp.transpose(ratio, (1, 2, 0))
    smem, sem = pltpu.SMEM, pltpu.SemaphoreType.DMA
    wind_scratch = [smem(wind.shape, jnp.int32), sem]

    def shape(*dims, dtype=bf16):
        return jax.ShapeDtypeStruct(dims, dtype)

    def swap(value, bits):
        return lax.ppermute(value, "dir", [(i, i ^ bits) for i in range(n_dir)])

    def partner(value, bits=0):
        count = n_layer * n_dir
        return lax.ppermute(value, ("layer", "dir"), [(i, i ^ n_dir ^ bits) for i in range(count)])

    def turn(value, step):
        return lax.ppermute(value, "layer", [(i, (i + step) % n_layer) for i in range(n_layer)])

    width = cols_dev // 4
    chunk = shape(layers, rows_dev, width)
    ints = (wind, offsets, ratio)
    keep0, keep1, give0, give1, *ints = call(
        split_kernel,
        [chunk] * 4 + [shape(*array.shape, dtype=jnp.int32) for array in ints],
        (screens, *ints),
        0,
        "split",
        in_hbm=range(4),
        scratch=[sem((7,))],
        brief=True,
    )
    across0 = swap(keep0, 2)
    diagonal0 = swap(give0, 3)
    near0 = swap(give0, 1)
    across1 = swap(keep1, 2)
    diagonal1 = swap(give1, 3)
    ones = np.kron(np.eye(LANES // SUB_PIX), np.ones((SUB_PIX, SUB_PIX))).astype(np.float32)
    optics_in = (amplitude, jnp.asarray(ones), *[jnp.asarray(table) for table in tables_of(rows)])
    copies = [shape(*array.shape, dtype=array.dtype) for array in (screens, *optics_in)]
    row_weights, cols, *loaded = call(
        functools.partial(weights_kernel, (n_layer, rows_dev, cols_dev * n_layer)),
        [shape(2, layers, pupil_rows, 4 * rows_dev), shape(layers, cols_dev, pupil_cols)]
        + [shape(8, pupil_cols, dtype=dtype) for dtype in (jnp.int32, jnp.int32, f32, f32)]
        + copies,
        (*ints, screens, *optics_in),
        0,
        "weights",
        in_hbm=range(3, 8),
        scratch=[smem(array.shape, jnp.int32) for array in (wind, offsets, ratio)]
        + [sem((8,))],
        brief=True,
    )
    tables, (own, *optics_in) = loaded[:4], loaded[4:]
    wind = ints[0]
    give1, own = lax.optimization_barrier((give1, own))
    near1 = swap(give1, 1)
    across0, diagonal0, row_weights, cols = lax.optimization_barrier((across0, diagonal0, row_weights, cols))

    projected = shape(layers, half, width)
    other0, sibling_other0 = call(
        first_rows_kernel,
        [projected] * 2,
        (row_weights, across0, diagonal0, near0, keep0),
        0,
        "rows_first",
        brief=True,
    )
    sends = other0, sibling_other0
    came0 = partner(sends[0])
    sibling_came0 = partner(sends[1], 1)

    wind, other0 = lax.optimization_barrier((wind, other0))
    others, mine0, sibling0, strip, sibling_strip = call(
        strips_kernel,
        [shape(layers, cols_dev, pupil_cols)] + [projected] * 2 + [shape(STRIP, rows_dev)] * 2,
        (wind, *tables, row_weights, across0, diagonal0, near0, keep0),
        0,
        "strips",
        scratch=wind_scratch,
        brief=True,
    )
    steps = strip_steps(pairs)
    far = len(steps) * rows
    message = shape(layers * far + STRIP * rows_dev // LANES, width)
    remainder = shape(layers * (half - far), width)
    mine1, give, far1, sibling_far1, rest1, sibling_rest1 = call(
        later_rows_kernel,
        [projected, shape(layers, half + 64, 2 * width), message, message, remainder, remainder],
        (row_weights, across1, diagonal1, near1, keep1, across0, diagonal0, near0, keep0, sibling0, strip, sibling_strip),
        0,
        "rows_later",
        brief=True,
    )
    far1, sibling_far1 = partner(far1), partner(sibling_far1, 1)
    taken = swap(give, 1)
    phase = call(
        phase_kernel,
        shape(half, pupil_cols, dtype=f32),
        (cols, others, mine0, mine1, came0, sibling_came0),
        10_000_000_000,
        "phase",
    )

    rest1, sibling_rest1, phase = lax.optimization_barrier((rest1, sibling_rest1, phase))
    rest1, sibling_rest1 = partner(rest1), partner(sibling_rest1, 1)
    phase = call(
        taken_kernel,
        shape(half, pupil_cols, dtype=f32),
        (cols, phase, taken),
        0,
        "taken",
        brief=True,
    )
    *far_sums, strips = call(
        far_kernel,
        [shape(rows, pupil_cols + rows_dev)] * len(steps) + [shape(2 * STRIP, rows_dev)],
        (others, phase, far1, sibling_far1),
        300_000_000,
        "far",
    )
    rest_sums = call(
        rest_kernel,
        [shape(rows, pupil_cols)] * (pairs - len(steps)),
        (others, phase, rest1, sibling_rest1),
        0,
        "rest",
        brief=True,
    )
    received = dict(zip(send_order(pairs), [*rest_sums, *far_sums]))
    for k in range(1, pairs):
        received[k] = lax.ppermute(received[k], "layer", [(i, i ^ (2 * k)) for i in range(n_layer)])
    received = [received[k] for k in range(pairs)]

    optics_in, received[-1] = lax.optimization_barrier((optics_in, received[-1]))
    optics = call(
        optics_kernel,
        (
            shape(rows, pupil_cols, dtype=f32),
            shape(*optics_in[2].shape),
            shape(*optics_in[3].shape),
        ),
        optics_in,
        0,
        "optics",
        brief=True,
    )
    received[1], optics = lax.optimization_barrier((received[1], optics))
    shifted = call(
        shift_kernel,
        shape(layers, rows_dev, cols_dev),
        (wind, own, near0, near1, diagonal0, diagonal1, taken, strips, *[received[k] for k in steps]),
        0,
        "shift",
        scratch=wind_scratch,
        brief=True,
    )
    spots_shape = shape(2 * rows, 2 * pupil_cols, dtype=f32)
    spots, new_screens = call(
        functools.partial(imaging_kernel, pairs),
        [spots_shape, shape(layers, rows_dev, cols_dev)],
        (*received, *optics, shifted),
        400_000_000,
        "imaging",
        out_hbm=(0, 1),
        scratch=[pltpu.VMEM(spots_shape.shape, f32), sem((1 + pupil_cols // (2 * LANES),))],
    )
    return (new_screens, spots[None])


def solution(mesh):
    return jax.shard_map(
        per_device,
        mesh=mesh,
        in_specs=(P(None, "dir", "layer"), P("layer", None), P(), P(), P()),
        out_specs=(P(None, "dir", "layer"), P("dir", "layer", None)),
        check_vma=False,
    )
```

```python
import functools

import jax
import jax.numpy as jnp
import numpy as np
from jax import lax
from jax.experimental import pallas as pl
from jax.experimental.pallas import tpu as pltpu
from jax.sharding import PartitionSpec as P

SUB_PIX = 16
SPOT_PIX = 32
WIND_MAX = 8
LANES = 128
STRIP = 32

HBM_SPEC = pl.BlockSpec(memory_space=pltpu.HBM)
VMEM_SPEC = pl.BlockSpec(memory_space=pltpu.VMEM)


def params(*arrays):
    held = sum(array.size * array.dtype.itemsize for array in jax.tree.leaves(arrays))
    return pltpu.CompilerParams(vmem_limit_bytes=held + 8 * 1024 * 1024)


def call(kernel, out_shape, operands, flops, name, in_hbm=(), out_hbm=(), scratch=(), brief=False):
    def spec(k, array):
        return HBM_SPEC if k in in_hbm else VMEM_SPEC

    if out_hbm:
        out_specs = [HBM_SPEC if k in out_hbm else VMEM_SPEC for k in range(len(out_shape))]
    else:
        out_specs = jax.tree.map(lambda _: VMEM_SPEC, out_shape)
    size = sum(array.size * array.dtype.itemsize for array in jax.tree.leaves((operands, out_shape)))
    if brief:
        flops = size = 0
    in_specs = [spec(k, array) for k, array in enumerate(operands)]
    operands = [
        pltpu.with_memory_space_constraint(array, pltpu.HBM) if space is HBM_SPEC else array
        for array, space in zip(operands, in_specs)
    ]
    return pl.pallas_call(
        kernel,
        out_shape=out_shape,
        in_specs=in_specs,
        out_specs=out_specs,
        scratch_shapes=list(scratch),
        compiler_params=params(operands, out_shape),
        cost_estimate=pl.CostEstimate(flops=flops, bytes_accessed=size, transcendentals=0),
        name=name,
    )(*operands)


def fetch(*pairs):
    copies = [pltpu.make_async_copy(source, target, sem) for source, target, sem in pairs]
    for copy in copies:
        copy.start()
    return copies


def wrap(value, length):
    value = jnp.where(value < 0, value + length, value)
    return jnp.where(value >= length, value - length, value)


def stack(*blocks):
    return jnp.concatenate(blocks, axis=0)


def beside(*blocks):
    return jnp.concatenate(blocks, axis=1)


def dot(left, right):
    return jnp.dot(left, right, preferred_element_type=jnp.float32)


def spans(pixel, anchor, num, den, length):
    stretched = (pixel * num).astype(jnp.float32)
    den = (jnp.zeros_like(pixel) + den).astype(jnp.float32)
    whole = jnp.floor((stretched + 0.5) / den)
    fraction = (stretched - whole * den) / den
    base = wrap(anchor + whole.astype(jnp.int32), length)
    upper = wrap(base + 1, length)
    return base, upper, 1.0 - fraction, fraction


def chunk_start(half, chunk):
    return 3 * half + chunk * (1 - 2 * half)


def split_kernel(screens, *refs):
    ints, outs, held, sems = refs[:3], refs[3:7], refs[7:10], refs[-1]
    width = outs[0].shape[2]
    core = lax.rem(lax.axis_index("dir"), 2)
    pairs = []
    for k, out in enumerate(outs):
        half = core if k < 2 else 1 - core
        start = pl.multiple_of(chunk_start(half, k % 2) * width, LANES)
        pairs.append((screens.at[:, :, pl.ds(start, width)], out, sems.at[k]))
    pairs += [(source, copy, sems.at[4 + k]) for k, (source, copy) in enumerate(zip(ints, held))]
    for load in fetch(*pairs):
        load.wait()


def weights_kernel(geometry, wind_held, offsets_held, ratio_held, *refs):
    n_layer, rows_dev, screen_cols = geometry
    sources, (rows_out, cols_out, *tables), refs = refs[:5], refs[5:11], refs[11:]
    copies, (wind, offsets, ratio, sems) = refs[:5], refs[5:]
    pupil_cols = cols_out.shape[2]
    loads = fetch(
        (wind_held, wind, sems.at[0]),
        (offsets_held, offsets, sems.at[1]),
        (ratio_held, ratio, sems.at[2]),
    )
    pairs = [*zip(sources, copies)]
    others = fetch(*[(source, copy, sems.at[3 + k]) for k, (source, copy) in enumerate(pairs)])
    _, layers, pupil_rows, screen_rows = rows_out.shape
    half = pupil_rows // 2
    direction = lax.axis_index("dir")
    column = lax.axis_index("layer")
    block = pupil_rows // n_layer
    row = lax.broadcasted_iota(jnp.int32, (half, LANES), 0)
    step = row // block
    for at, value in enumerate(send_order(n_layer // 2)):
        step = jnp.where(row // block == at, value, step)
    pair = jnp.bitwise_xor(step, column // 2)
    parity = lax.rem(column, 2)
    inside = lax.rem(row, block) + pair * (2 * block)
    pixel_rows = stack(inside + parity * block, inside + (1 - parity) * block)
    lane = lax.broadcasted_iota(jnp.int32, (pupil_rows, LANES), 1)
    for load in loads:
        load.wait()
    for side in range(2):
        target = jnp.bitwise_xor(direction, side)
        for level in range(layers):
            anchor = wrap(offsets[level, 0, target] - wind[0, level], screen_rows)
            num, den = ratio[level, 0, target], ratio[level, 1, target]
            base, upper, low, high = spans(pixel_rows, anchor, num, den, screen_rows)
            for peer in range(4):
                for part in range(rows_dev // LANES):
                    index = lane + (jnp.bitwise_xor(direction, peer) * rows_dev + part * LANES)
                    weight = jnp.where(index == base, low, 0.0)
                    weight = jnp.where(index == upper, high, weight)
                    start = peer * rows_dev + part * LANES
                    rows_out[side, level, :, start : start + LANES] = weight.astype(jnp.bfloat16)
    sub = lax.broadcasted_iota(jnp.int32, (8, LANES), 0)
    anchor, num, den = jnp.zeros_like(sub), jnp.zeros_like(sub), jnp.ones_like(sub)
    for level in range(layers):
        start = wrap(offsets[level, 1, direction] - wind[1, level], screen_cols)
        anchor = jnp.where(sub == level, start, anchor)
        num = jnp.where(sub == level, ratio[level, 0, direction], num)
        den = jnp.where(sub == level, ratio[level, 1, direction], den)
    for at in range(0, pupil_cols, LANES):
        pixel = lax.broadcasted_iota(jnp.int32, (8, LANES), 1) + at
        values = spans(pixel, anchor, num, den, screen_cols)
        for table, value in zip(tables, values):
            table[:, at : at + LANES] = value
    column_weights(*tables, column * cols_out.shape[1], cols_out)
    for load in others:
        load.wait()


def column_weights(base_ref, upper_ref, low_ref, high_ref, first, out):
    layers, cols_dev, pupil_cols = out.shape
    width = cols_dev // 4
    core = lax.rem(lax.axis_index("dir"), 2)
    sub = lax.broadcasted_iota(jnp.int32, (width, LANES), 0).astype(jnp.float32).astype(jnp.bfloat16)
    zero = jnp.zeros((width, LANES), jnp.bfloat16)
    for level in range(layers):

        def tile(step, carry):
            start = pl.multiple_of(step * LANES, LANES)
            cut = (slice(level, level + 1), pl.ds(start, LANES))
            base, upper = base_ref[cut], upper_ref[cut]
            low, high = [
                jnp.broadcast_to(ref[cut].astype(jnp.bfloat16), (width, LANES)) for ref in (low_ref, high_ref)
            ]
            for k in range(4):
                shift = first + chunk_start(jnp.bitwise_xor(core, k // 2), k % 2) * width
                base_at, upper_at = [
                    jnp.broadcast_to(
                        jnp.clip(value - shift, -1, width).astype(jnp.float32).astype(jnp.bfloat16), (width, LANES)
                    )
                    for value in (base, upper)
                ]
                weight = jnp.where(sub == base_at, low, zero)
                weight = jnp.where(sub == upper_at, high, weight)
                out[level, k * width : (k + 1) * width, pl.ds(start, LANES)] = weight
            return carry

        lax.fori_loop(0, pupil_cols // LANES, tile, 0)


def strips_kernel(wind_held, *refs):
    tables, (across, diagonal, near, keep, cols_out, strip, sibling_strip, wind, sem) = refs[:4], refs[4:]
    load = fetch((wind_held, wind, sem))[0]
    column_weights(*tables, jnp.bitwise_xor(lax.axis_index("layer"), 1) * cols_out.shape[1], cols_out)
    layers, rows, _ = keep.shape
    core = lax.rem(lax.axis_index("dir"), 2)
    odd = core == 1
    lane = lax.broadcasted_iota(jnp.int32, (rows + 32, LANES), 1)

    def wide(own, near, far, odd, level):
        own, near, far = [block[level].astype(jnp.float32) for block in (own, near, far)]
        before = jnp.where(odd, near[rows - 16 :], far[rows - 16 :])
        return stack(before, own, jnp.where(odd, far[:16], near[:16]))

    packed = jnp.zeros((rows + 32, LANES), jnp.float32)
    for level in range(layers):
        blocks = (keep, near, diagonal, odd), (near, keep, across, core == 0)
        for at, block in zip((WIND_MAX * level, STRIP + WIND_MAX * level), blocks):
            block = pltpu.roll(wide(*block, level), at + WIND_MAX * core, 1)
            packed = jnp.where((lane >= at) & (lane < at + WIND_MAX), block, packed)
    load.wait()
    strips = jnp.zeros((rows, LANES), jnp.float32)
    for level in range(layers):
        shift = wind[0, level]
        shift = jnp.where(shift < 0, shift + rows + 32, shift)
        moved = pltpu.roll(packed, shift, 0)[16 : 16 + rows]
        mine = lax.rem(lane[:rows], STRIP)
        strips = jnp.where((mine >= WIND_MAX * level) & (mine < WIND_MAX * (level + 1)), moved, strips)
    strips = strips.T.astype(jnp.bfloat16)
    strip[...] = strips[:STRIP]
    sibling_strip[...] = strips[STRIP : 2 * STRIP]


def project_rows(rows_ref, keep, near, across, diagonal, level):
    screen = stack(keep[level], near[level], across[level], diagonal[level])
    rows = stack(rows_ref[0, level], rows_ref[1, level])
    return dot(rows, screen).astype(jnp.bfloat16)


def first_rows_kernel(rows_ref, across, diagonal, near, keep, mine, sibling, other, sibling_other):
    layers, half, _ = mine.shape
    for level in range(layers):
        part = project_rows(rows_ref, keep, near, across, diagonal, level)
        for k, out in enumerate((mine, other, sibling, sibling_other)):
            out[level] = part[k * half : (k + 1) * half]


def put_strip(out, at, strip):
    for k in range(strip.shape[1] // LANES):
        out[at + k * STRIP : at + (k + 1) * STRIP, :] = strip[:, k * LANES : (k + 1) * LANES]


def get_strip(ref, at):
    return beside(*[ref[start : start + STRIP, :] for start in range(at, ref.shape[0], STRIP)])


def later_rows_kernel(rows_ref, *refs):
    chunks, refs = refs[:8], refs[8:]
    sibling0, strip, sibling_strip, mine, give, far, sibling_far, rest, sibling_rest = refs
    across, diagonal, near, keep, across0, diagonal0, near0, keep0 = chunks
    layers, half, width = mine.shape
    rows = near.shape[1]
    size = (far.shape[0] - STRIP * rows // LANES) // layers
    start = half - size
    for level in range(layers):
        part = project_rows(rows_ref, keep, near, across, diagonal, level)
        mine[level] = part[:half]
        for k, out, remainder in ((1, far, rest), (3, sibling_far, sibling_rest)):
            piece = part[k * half : (k + 1) * half]
            out[level * size : (level + 1) * size] = piece[start:]
            remainder[level * start : (level + 1) * start] = piece[:start]
        give[level, :half, :width] = sibling0[level]
        give[level, :half, width:] = part[2 * half : 3 * half]
        for k, blocks in enumerate(((across0, keep0), (across, keep))):
            cut = slice(k * width, (k + 1) * width)
            edges = [block[level, at : at + 16] for block in blocks for at in (0, rows - 16)]
            give[level, half:, cut] = stack(*edges)
    put_strip(far, layers * size, strip)
    put_strip(sibling_far, layers * size, sibling_strip)


def project(parts, cols_refs, at):
    cols = stack(*[ref[level, start:stop, at : at + 256] for ref, level, start, stop in cols_refs])
    return dot(beside(*parts), cols)


def phase_kernel(mine_ref, other_ref, mine0, mine1, came, sibling_came, phase):
    layers, _, width = mine0.shape
    parts, cuts = [], []
    for level in range(layers):
        parts += [mine0[level], mine1[level], came[level], sibling_came[level]]
        cuts += [(mine_ref, level, 0, 2 * width)]
        cuts += [(other_ref, level, 0, width), (other_ref, level, 2 * width, 3 * width)]
    for at in range(0, phase.shape[1], 256):
        phase[:, at : at + 256] = project(parts, cuts, at)


def taken_kernel(mine_ref, phase, taken, out):
    half, pupil_cols = phase.shape
    layers, cols_dev, _ = mine_ref.shape
    parts = [taken[level, :half] for level in range(layers)]
    cuts = [(mine_ref, level, cols_dev // 2, cols_dev) for level in range(layers)]
    for at in range(0, pupil_cols, 256):
        out[:, at : at + 256] = phase[:, at : at + 256] + project(parts, cuts, at)


def sum_up(start, cols_ref, phase, came, sibling_came, outs):
    layers, cols_dev, _ = cols_ref.shape
    width = cols_dev // 4
    block = outs[0].shape[0]
    size = block * len(outs)
    rows = slice(start, start + size)
    parts, cuts = [], []
    for level in range(layers):
        cut = slice(level * size, (level + 1) * size)
        parts += [came[cut], sibling_came[cut]]
        cuts += [(cols_ref, level, width, 2 * width), (cols_ref, level, 3 * width, 4 * width)]
    pupil_cols = phase.shape[1]
    for at in range(0, pupil_cols, 256):
        total = (phase[rows, at : at + 256] + project(parts, cuts, at)).astype(jnp.bfloat16)
        for k, out in enumerate(outs):
            out[:, at : at + 256] = total[k * block : (k + 1) * block]


def strip_steps(pairs):
    return [2**k - 1 for k in range(1, pairs.bit_length())]


def send_order(pairs):
    steps = strip_steps(pairs)
    return [k for k in range(pairs) if k not in steps] + steps


def add_strip(pairs, step, strips, out):
    pair = lax.axis_index("layer") // 2
    after = lax.rem(pair + 1, pairs) == jnp.bitwise_xor(pair, step)
    at = out.shape[1] - strips.shape[1]
    last, first = strips[:STRIP].astype(jnp.float32), strips[STRIP:].astype(jnp.float32)
    out[:, at:] = jnp.where(after, last, first).astype(jnp.bfloat16)


def far_kernel(cols_ref, phase, came, sibling_came, *outs):
    *outs, strips = outs
    half = phase.shape[0]
    size = outs[0].shape[0] * len(outs)
    sum_up(half - size, cols_ref, phase, came, sibling_came, outs)
    layers = cols_ref.shape[0]
    odd = lax.rem(lax.axis_index("dir"), 2) == 1
    here = get_strip(came, layers * size).astype(jnp.float32)
    there = get_strip(sibling_came, layers * size).astype(jnp.float32)
    strips[:STRIP] = jnp.where(odd, here, there).astype(jnp.bfloat16)
    strips[STRIP:] = jnp.where(odd, there, here).astype(jnp.bfloat16)
    pairs = half // outs[0].shape[0]
    for out, step in zip(outs, strip_steps(pairs)):
        add_strip(pairs, step, strips, out)


def rest_kernel(cols_ref, phase, came, sibling_came, *outs):
    sum_up(0, cols_ref, phase, came, sibling_came, outs)


def shifted_rows(shift, odd, own, near, far):
    own, near, far = [block.astype(jnp.float32) for block in (own, near, far)]
    rows = own.shape[0]
    before = jnp.where(odd, near[16:], far[16:])
    after = jnp.where(odd, far[:16], near[:16])
    shift = jnp.where(shift < 0, shift + rows + 32, shift)
    return pltpu.roll(stack(before, own, after), shift, 0)[16 : 16 + rows]


def shift_kernel(wind_held, own, near0, near1, diagonal0, diagonal1, taken, partner_strips, *refs):
    messages, (out, wind, sem) = refs[:-3], refs[-3:]
    load = fetch((wind_held, wind, sem))[0]
    layers, rows, cols = own.shape
    odd = lax.rem(lax.axis_index("dir"), 2) == 1
    half = taken.shape[1] - 64
    pairs = 2 ** len(messages)
    pair, second = lax.axis_index("layer") // 2, lax.rem(lax.axis_index("layer"), 2) == 1
    before = jnp.bitwise_xor(pair, lax.rem(pair + pairs - 1, pairs))
    after = jnp.bitwise_xor(pair, lax.rem(pair + 1, pairs))
    left = partner_strips[:STRIP].astype(jnp.float32)
    right = partner_strips[STRIP:].astype(jnp.float32)
    for step, message in zip(strip_steps(pairs), messages):
        strip = message[:, message.shape[1] - rows :].astype(jnp.float32)
        left = jnp.where(jnp.logical_and(before == step, jnp.logical_not(second)), strip, left)
        right = jnp.where(jnp.logical_and(after == step, second), strip, right)
    strips = stack(left, right, jnp.zeros((LANES - 2 * STRIP, rows), jnp.float32)).T
    lane = lax.broadcasted_iota(jnp.int32, (rows, LANES), 1)
    load.wait()
    for level in range(layers):
        last = pltpu.roll(strips, LANES - WIND_MAX * (level + 1), 1)
        first = pltpu.roll(strips, LANES - STRIP - WIND_MAX * level, 1)
        extra = jnp.where(lane < WIND_MAX, first, last)
        pair = []
        for at, parts in ((half, (diagonal0, diagonal1)), (half + 32, (near0, near1))):
            here = [stack(part[level, :16], part[level, rows - 16 :]).astype(jnp.float32) for part in parts]
            there = taken[level, at : at + 32].astype(jnp.float32)
            width = there.shape[1] // 2
            quarters = [*here, there[:, width:], there[:, :width]]
            pair.append(beside(*[jnp.where(odd, quarters[3 - k], quarters[k]) for k in range(4)]))
        far, near = pair
        moved = shifted_rows(wind[0, level], odd, own[level], near, far)
        shift = wind[1, level]
        shift = jnp.where(shift < 0, shift + cols + LANES, shift)
        out[level] = pltpu.roll(beside(moved, extra), shift, 1)[:, :cols].astype(jnp.bfloat16)


def optics_kernel(amplitude, ones, columns, lines, amp_out, columns_out, lines_out):
    rows, pupil_cols = amplitude.shape
    for step in range(pupil_cols // LANES):
        cut = slice(step * LANES, (step + 1) * LANES)
        amp = amplitude[:, cut]
        energy = (amp * amp).reshape(rows // SUB_PIX, SUB_PIX, LANES).sum(axis=1)
        energy = jnp.broadcast_to(energy[:, None], (rows // SUB_PIX, SUB_PIX, LANES)).reshape(rows, LANES)
        total = jnp.dot(energy, ones[...], precision=lax.Precision.HIGHEST, preferred_element_type=jnp.float32)
        amp_out[:, cut] = amp * lax.rsqrt(total)
    columns_out[...] = columns[...].astype(jnp.bfloat16)
    lines_out[...] = lines[...].astype(jnp.bfloat16)


def sin_cos(phase):
    turns = jnp.floor(phase * (1.0 / np.pi) + 0.5)
    rest = phase - turns * 3.140625
    rest = rest - turns * 9.67653589793e-4
    odd = turns - 2.0 * jnp.floor(turns * 0.5)
    sign = 1.0 - 2.0 * odd
    square = rest * rest
    sine = -1.0 / 39916800.0
    for term in (1.0 / 362880.0, -1.0 / 5040.0, 1.0 / 120.0, -1.0 / 6.0, 1.0):
        sine = sine * square + term
    cosine = 1.0 / 479001600.0
    for term in (-1.0 / 3628800.0, 1.0 / 40320.0, -1.0 / 720.0, 1.0 / 24.0, -0.5, 1.0):
        cosine = cosine * square + term
    return sine * rest * sign, cosine * sign


def imaging_kernel(count, *refs):
    parts, (amp_ref, columns, lines, shifted, spots, screens, out, sems) = refs[:count], refs[count:]
    copies = fetch((shifted, screens, sems.at[0]))
    rows, cols = amp_ref.shape
    tiles = cols // LANES
    phase = parts[0][:, :cols].astype(jnp.float32)
    for part in parts[1:]:
        phase = phase + part[:, :cols].astype(jnp.float32)
    sine, cosine = sin_cos(phase)
    amp = amp_ref[...]
    real, imag = (amp * cosine).astype(jnp.bfloat16), (amp * sine).astype(jnp.bfloat16)
    cuts = [slice(t * LANES, (t + 1) * LANES) for t in range(tiles)]
    field = stack(*[beside(real[:, cut], imag[:, cut]) for cut in cuts])
    half = dot(field, columns[...]).astype(jnp.bfloat16)
    wide = 2 * LANES
    out_rows = 2 * rows
    for t in range(tiles):
        mine = half[t * rows : (t + 1) * rows]
        full = dot(lines[...], stack(mine[:, :wide], mine[:, wide:]))
        real, imag = full[:out_rows], full[out_rows:]
        out[:, t * wide : (t + 1) * wide] = real * real + imag * imag
        if t % 2:
            cut = slice((t - 1) * wide, (t + 1) * wide)
            copies += fetch((out.at[:, cut], spots.at[:, cut], sems.at[1 + t // 2]))
    for copy in copies:
        copy.wait()


def tables_of(rows):
    freq = np.arange(SPOT_PIX)[:, None] - SPOT_PIX // 2
    angle = ((freq * np.arange(SUB_PIX)[None, :]) % SPOT_PIX) * (2.0 * np.pi / SPOT_PIX)
    cos, sin = np.cos(angle), np.sin(angle)

    def blocks(table, count):
        return np.kron(np.eye(count), table)

    per_tile = LANES // SUB_PIX
    col_cos, col_sin = blocks(cos.T, per_tile), blocks(sin.T, per_tile)
    columns = np.block([[col_cos, -col_sin], [col_sin, col_cos]])
    count = rows // SUB_PIX
    row_cos, row_sin = blocks(cos, count), blocks(sin, count)
    lines = np.block([[row_cos, row_sin], [-row_sin, row_cos]])

    return columns.astype(np.float32), lines.astype(np.float32)


def per_device(screens, amplitude, wind, offsets, ratio):
    layers, rows_dev, cols_dev = screens.shape
    n_layer = lax.axis_size("layer")
    n_dir = lax.axis_size("dir")
    rows, pupil_cols = amplitude.shape
    pairs = n_layer // 2
    half = pairs * rows
    pupil_rows = 2 * half
    assert n_dir == 4 and rows == STRIP and pairs > 2
    bf16, f32 = jnp.bfloat16, jnp.float32
    wind = jnp.transpose(wind, (1, 0))
    offsets = jnp.transpose(offsets, (1, 2, 0))
    ratio = jnp.transpose(ratio, (1, 2, 0))
    smem, sem = pltpu.SMEM, pltpu.SemaphoreType.DMA
    wind_scratch = [smem(wind.shape, jnp.int32), sem]

    def shape(*dims, dtype=bf16):
        return jax.ShapeDtypeStruct(dims, dtype)

    def swap(value, bits):
        return lax.ppermute(value, "dir", [(i, i ^ bits) for i in range(n_dir)])

    def partner(value, bits=0):
        count = n_layer * n_dir
        return lax.ppermute(value, ("layer", "dir"), [(i, i ^ n_dir ^ bits) for i in range(count)])

    def turn(value, step):
        return lax.ppermute(value, "layer", [(i, (i + step) % n_layer) for i in range(n_layer)])

    width = cols_dev // 4
    chunk = shape(layers, rows_dev, width)
    ints = (wind, offsets, ratio)
    keep0, keep1, give0, give1, *ints = call(
        split_kernel,
        [chunk] * 4 + [shape(*array.shape, dtype=jnp.int32) for array in ints],
        (screens, *ints),
        0,
        "split",
        in_hbm=range(4),
        scratch=[sem((7,))],
        brief=True,
    )
    across0 = swap(keep0, 2)
    diagonal0 = swap(give0, 3)
    near0 = swap(give0, 1)
    near1 = swap(give1, 1)
    ones = np.kron(np.eye(LANES // SUB_PIX), np.ones((SUB_PIX, SUB_PIX))).astype(np.float32)
    optics_in = (amplitude, jnp.asarray(ones), *[jnp.asarray(table) for table in tables_of(rows)])
    copies = [shape(*array.shape, dtype=array.dtype) for array in (screens, *optics_in)]
    row_weights, cols, *loaded = call(
        functools.partial(weights_kernel, (n_layer, rows_dev, cols_dev * n_layer)),
        [shape(2, layers, pupil_rows, 4 * rows_dev), shape(layers, cols_dev, pupil_cols)]
        + [shape(8, pupil_cols, dtype=dtype) for dtype in (jnp.int32, jnp.int32, f32, f32)]
        + copies,
        (*ints, screens, *optics_in),
        0,
        "weights",
        in_hbm=range(3, 8),
        scratch=[smem(array.shape, jnp.int32) for array in (wind, offsets, ratio)]
        + [sem((8,))],
        brief=True,
    )
    tables, (own, *optics_in) = loaded[:4], loaded[4:]
    wind = ints[0]
    keep1, give1, own = lax.optimization_barrier((keep1, give1, own))
    across1 = swap(keep1, 2)
    diagonal1 = swap(give1, 3)
    across0, diagonal0, row_weights, cols = lax.optimization_barrier((across0, diagonal0, row_weights, cols))

    projected = shape(layers, half, width)
    mine0, sibling0, other0, sibling_other0 = call(
        first_rows_kernel,
        [projected] * 4,
        (row_weights, across0, diagonal0, near0, keep0),
        0,
        "rows_first",
        brief=True,
    )
    came0 = partner(other0)
    sibling_came0 = partner(sibling_other0, 1)

    wind, mine0 = lax.optimization_barrier((wind, mine0))
    others, strip, sibling_strip = call(
        strips_kernel,
        [shape(layers, cols_dev, pupil_cols)] + [shape(STRIP, rows_dev)] * 2,
        (wind, *tables, across0, diagonal0, near0, keep0),
        0,
        "strips",
        scratch=wind_scratch,
        brief=True,
    )
    steps = strip_steps(pairs)
    far = len(steps) * rows
    message = shape(layers * far + STRIP * rows_dev // LANES, width)
    remainder = shape(layers * (half - far), width)
    mine1, give, far1, sibling_far1, rest1, sibling_rest1 = call(
        later_rows_kernel,
        [projected, shape(layers, half + 64, 2 * width), message, message, remainder, remainder],
        (row_weights, across1, diagonal1, near1, keep1, across0, diagonal0, near0, keep0, sibling0, strip, sibling_strip),
        0,
        "rows_later",
        brief=True,
    )
    far1, sibling_far1 = partner(far1), partner(sibling_far1, 1)
    taken = swap(give, 1)
    phase = call(
        phase_kernel,
        shape(half, pupil_cols, dtype=f32),
        (cols, others, mine0, mine1, came0, sibling_came0),
        10_000_000_000,
        "phase",
    )

    rest1, sibling_rest1, phase = lax.optimization_barrier((rest1, sibling_rest1, phase))
    rest1, sibling_rest1 = partner(rest1), partner(sibling_rest1, 1)
    phase = call(
        taken_kernel,
        shape(half, pupil_cols, dtype=f32),
        (cols, phase, taken),
        0,
        "taken",
        brief=True,
    )
    *far_sums, strips = call(
        far_kernel,
        [shape(rows, pupil_cols + rows_dev)] * len(steps) + [shape(2 * STRIP, rows_dev)],
        (others, phase, far1, sibling_far1),
        300_000_000,
        "far",
    )
    rest_sums = call(
        rest_kernel,
        [shape(rows, pupil_cols)] * (pairs - len(steps)),
        (others, phase, rest1, sibling_rest1),
        0,
        "rest",
        brief=True,
    )
    received = dict(zip(send_order(pairs), [*rest_sums, *far_sums]))
    for k in range(1, pairs):
        received[k] = lax.ppermute(received[k], "layer", [(i, i ^ (2 * k)) for i in range(n_layer)])
    received = [received[k] for k in range(pairs)]

    optics_in, received[-1] = lax.optimization_barrier((optics_in, received[-1]))
    optics = call(
        optics_kernel,
        (
            shape(rows, pupil_cols, dtype=f32),
            shape(*optics_in[2].shape),
            shape(*optics_in[3].shape),
        ),
        optics_in,
        0,
        "optics",
        brief=True,
    )
    received[1], optics = lax.optimization_barrier((received[1], optics))
    shifted = call(
        shift_kernel,
        shape(layers, rows_dev, cols_dev),
        (wind, own, near0, near1, diagonal0, diagonal1, taken, strips, *[received[k] for k in steps]),
        0,
        "shift",
        scratch=wind_scratch,
        brief=True,
    )
    spots_shape = shape(2 * rows, 2 * pupil_cols, dtype=f32)
    spots, new_screens = call(
        functools.partial(imaging_kernel, pairs),
        [spots_shape, shape(layers, rows_dev, cols_dev)],
        (*received, *optics, shifted),
        400_000_000,
        "imaging",
        out_hbm=(0, 1),
        scratch=[pltpu.VMEM(spots_shape.shape, f32), sem((1 + pupil_cols // (2 * LANES),))],
    )
    return (new_screens, spots[None])


def solution(mesh):
    return jax.shard_map(
        per_device,
        mesh=mesh,
        in_specs=(P(None, "dir", "layer"), P("layer", None), P(), P(), P()),
        out_specs=(P(None, "dir", "layer"), P("dir", "layer", None)),
        check_vma=False,
    )
```

```python
import functools

import jax
import jax.numpy as jnp
import numpy as np
from jax import lax
from jax.experimental import pallas as pl
from jax.experimental.pallas import tpu as pltpu
from jax.sharding import PartitionSpec as P

SUB_PIX = 16
SPOT_PIX = 32
WIND_MAX = 8
LANES = 128
STRIP = 32

HBM_SPEC = pl.BlockSpec(memory_space=pltpu.HBM)
VMEM_SPEC = pl.BlockSpec(memory_space=pltpu.VMEM)


def params(*arrays):
    held = sum(array.size * array.dtype.itemsize for array in jax.tree.leaves(arrays))
    return pltpu.CompilerParams(vmem_limit_bytes=held + 8 * 1024 * 1024)


def call(kernel, out_shape, operands, flops, name, in_hbm=(), out_hbm=(), scratch=(), brief=False):
    def spec(k, array):
        return HBM_SPEC if k in in_hbm else VMEM_SPEC

    if out_hbm:
        out_specs = [HBM_SPEC if k in out_hbm else VMEM_SPEC for k in range(len(out_shape))]
    else:
        out_specs = jax.tree.map(lambda _: VMEM_SPEC, out_shape)
    size = sum(array.size * array.dtype.itemsize for array in jax.tree.leaves((operands, out_shape)))
    if brief:
        flops = size = 0
    in_specs = [spec(k, array) for k, array in enumerate(operands)]
    operands = [
        pltpu.with_memory_space_constraint(array, pltpu.HBM) if space is HBM_SPEC else array
        for array, space in zip(operands, in_specs)
    ]
    return pl.pallas_call(
        kernel,
        out_shape=out_shape,
        in_specs=in_specs,
        out_specs=out_specs,
        scratch_shapes=list(scratch),
        compiler_params=params(operands, out_shape),
        cost_estimate=pl.CostEstimate(flops=flops, bytes_accessed=size, transcendentals=0),
        name=name,
    )(*operands)


def fetch(*pairs):
    copies = [pltpu.make_async_copy(source, target, sem) for source, target, sem in pairs]
    for copy in copies:
        copy.start()
    return copies


def wrap(value, length):
    value = jnp.where(value < 0, value + length, value)
    return jnp.where(value >= length, value - length, value)


def stack(*blocks):
    return jnp.concatenate(blocks, axis=0)


def beside(*blocks):
    return jnp.concatenate(blocks, axis=1)


def dot(left, right):
    return jnp.dot(left, right, preferred_element_type=jnp.float32)


def spans(pixel, anchor, num, den, length):
    stretched = (pixel * num).astype(jnp.float32)
    den = (jnp.zeros_like(pixel) + den).astype(jnp.float32)
    whole = jnp.floor((stretched + 0.5) / den)
    fraction = (stretched - whole * den) / den
    base = wrap(anchor + whole.astype(jnp.int32), length)
    upper = wrap(base + 1, length)
    return base, upper, 1.0 - fraction, fraction


def chunk_start(half, chunk):
    return 3 * half + chunk * (1 - 2 * half)


def split_kernel(screens, *refs):
    ints, outs, held, sems = refs[:3], refs[3:7], refs[7:10], refs[-1]
    width = outs[0].shape[2]
    core = lax.rem(lax.axis_index("dir"), 2)
    pairs = []
    for k, out in enumerate(outs):
        half = core if k < 2 else 1 - core
        start = pl.multiple_of(chunk_start(half, k % 2) * width, LANES)
        pairs.append((screens.at[:, :, pl.ds(start, width)], out, sems.at[k]))
    pairs += [(source, copy, sems.at[4 + k]) for k, (source, copy) in enumerate(zip(ints, held))]
    for load in fetch(*pairs):
        load.wait()


def weights_kernel(geometry, wind_held, offsets_held, ratio_held, *refs):
    n_layer, rows_dev, screen_cols = geometry
    sources, (rows_out, cols_out, *tables), refs = refs[:5], refs[5:11], refs[11:]
    copies, (wind, offsets, ratio, sems) = refs[:5], refs[5:]
    pupil_cols = cols_out.shape[2]
    loads = fetch(
        (wind_held, wind, sems.at[0]),
        (offsets_held, offsets, sems.at[1]),
        (ratio_held, ratio, sems.at[2]),
    )
    pairs = [*zip(sources, copies)]
    others = fetch(*[(source, copy, sems.at[3 + k]) for k, (source, copy) in enumerate(pairs)])
    _, layers, pupil_rows, screen_rows = rows_out.shape
    half = pupil_rows // 2
    direction = lax.axis_index("dir")
    column = lax.axis_index("layer")
    block = pupil_rows // n_layer
    row = lax.broadcasted_iota(jnp.int32, (half, LANES), 0)
    step = row // block
    for at, value in enumerate(send_order(n_layer // 2)):
        step = jnp.where(row // block == at, value, step)
    pair = jnp.bitwise_xor(step, column // 2)
    parity = lax.rem(column, 2)
    inside = lax.rem(row, block) + pair * (2 * block)
    pixel_rows = stack(inside + parity * block, inside + (1 - parity) * block)
    lane = lax.broadcasted_iota(jnp.int32, (pupil_rows, LANES), 1)
    for load in loads:
        load.wait()
    for side in range(2):
        target = jnp.bitwise_xor(direction, side)
        for level in range(layers):
            anchor = wrap(offsets[level, 0, target] - wind[0, level], screen_rows)
            num, den = ratio[level, 0, target], ratio[level, 1, target]
            base, upper, low, high = spans(pixel_rows, anchor, num, den, screen_rows)
            for peer in range(4):
                for part in range(rows_dev // LANES):
                    index = lane + (jnp.bitwise_xor(direction, peer) * rows_dev + part * LANES)
                    weight = jnp.where(index == base, low, 0.0)
                    weight = jnp.where(index == upper, high, weight)
                    start = peer * rows_dev + part * LANES
                    rows_out[side, level, :, start : start + LANES] = weight.astype(jnp.bfloat16)
    sub = lax.broadcasted_iota(jnp.int32, (8, LANES), 0)
    anchor, num, den = jnp.zeros_like(sub), jnp.zeros_like(sub), jnp.ones_like(sub)
    for level in range(layers):
        start = wrap(offsets[level, 1, direction] - wind[1, level], screen_cols)
        anchor = jnp.where(sub == level, start, anchor)
        num = jnp.where(sub == level, ratio[level, 0, direction], num)
        den = jnp.where(sub == level, ratio[level, 1, direction], den)
    for at in range(0, pupil_cols, LANES):
        pixel = lax.broadcasted_iota(jnp.int32, (8, LANES), 1) + at
        values = spans(pixel, anchor, num, den, screen_cols)
        for table, value in zip(tables, values):
            table[:, at : at + LANES] = value
    column_weights(*tables, column * cols_out.shape[1], cols_out)
    for load in others:
        load.wait()


def column_weights(base_ref, upper_ref, low_ref, high_ref, first, out):
    layers, cols_dev, pupil_cols = out.shape
    width = cols_dev // 4
    core = lax.rem(lax.axis_index("dir"), 2)
    sub = lax.broadcasted_iota(jnp.int32, (width, LANES), 0).astype(jnp.float32).astype(jnp.bfloat16)
    zero = jnp.zeros((width, LANES), jnp.bfloat16)
    for level in range(layers):

        def tile(step, carry):
            start = pl.multiple_of(step * LANES, LANES)
            cut = (slice(level, level + 1), pl.ds(start, LANES))
            base, upper = base_ref[cut], upper_ref[cut]
            low, high = [
                jnp.broadcast_to(ref[cut].astype(jnp.bfloat16), (width, LANES)) for ref in (low_ref, high_ref)
            ]
            for k in range(4):
                shift = first + chunk_start(jnp.bitwise_xor(core, k // 2), k % 2) * width
                base_at, upper_at = [
                    jnp.broadcast_to(
                        jnp.clip(value - shift, -1, width).astype(jnp.float32).astype(jnp.bfloat16), (width, LANES)
                    )
                    for value in (base, upper)
                ]
                weight = jnp.where(sub == base_at, low, zero)
                weight = jnp.where(sub == upper_at, high, weight)
                out[level, k * width : (k + 1) * width, pl.ds(start, LANES)] = weight
            return carry

        lax.fori_loop(0, pupil_cols // LANES, tile, 0)


def strips_kernel(wind_held, *refs):
    tables, (across, diagonal, near, keep, cols_out, strip, sibling_strip, wind, sem) = refs[:4], refs[4:]
    load = fetch((wind_held, wind, sem))[0]
    column_weights(*tables, jnp.bitwise_xor(lax.axis_index("layer"), 1) * cols_out.shape[1], cols_out)
    layers, rows, _ = keep.shape
    core = lax.rem(lax.axis_index("dir"), 2)
    odd = core == 1
    lane = lax.broadcasted_iota(jnp.int32, (rows + 32, LANES), 1)

    def wide(own, near, far, odd, level):
        own, near, far = [block[level].astype(jnp.float32) for block in (own, near, far)]
        before = jnp.where(odd, near[rows - 16 :], far[rows - 16 :])
        return stack(before, own, jnp.where(odd, far[:16], near[:16]))

    packed = jnp.zeros((rows + 32, LANES), jnp.float32)
    for level in range(layers):
        blocks = (keep, near, diagonal, odd), (near, keep, across, core == 0)
        for at, block in zip((WIND_MAX * level, STRIP + WIND_MAX * level), blocks):
            block = pltpu.roll(wide(*block, level), at + WIND_MAX * core, 1)
            packed = jnp.where((lane >= at) & (lane < at + WIND_MAX), block, packed)
    load.wait()
    strips = jnp.zeros((rows, LANES), jnp.float32)
    for level in range(layers):
        shift = wind[0, level]
        shift = jnp.where(shift < 0, shift + rows + 32, shift)
        moved = pltpu.roll(packed, shift, 0)[16 : 16 + rows]
        mine = lax.rem(lane[:rows], STRIP)
        strips = jnp.where((mine >= WIND_MAX * level) & (mine < WIND_MAX * (level + 1)), moved, strips)
    strips = strips.T.astype(jnp.bfloat16)
    strip[...] = strips[:STRIP]
    sibling_strip[...] = strips[STRIP : 2 * STRIP]


def project_rows(rows_ref, keep, near, across, diagonal, level):
    screen = stack(keep[level], near[level], across[level], diagonal[level])
    rows = stack(rows_ref[0, level], rows_ref[1, level])
    return dot(rows, screen).astype(jnp.bfloat16)


def first_rows_kernel(rows_ref, across, diagonal, near, keep, mine, sibling, other, sibling_other):
    layers, half, _ = mine.shape
    for level in range(layers):
        part = project_rows(rows_ref, keep, near, across, diagonal, level)
        for k, out in enumerate((mine, other, sibling, sibling_other)):
            out[level] = part[k * half : (k + 1) * half]


def put_strip(out, at, strip):
    for k in range(strip.shape[1] // LANES):
        out[at + k * STRIP : at + (k + 1) * STRIP, :] = strip[:, k * LANES : (k + 1) * LANES]


def get_strip(ref, at):
    return beside(*[ref[start : start + STRIP, :] for start in range(at, ref.shape[0], STRIP)])


def later_rows_kernel(rows_ref, *refs):
    chunks, refs = refs[:8], refs[8:]
    sibling0, strip, sibling_strip, mine, give, far, sibling_far, rest, sibling_rest = refs
    across, diagonal, near, keep, across0, diagonal0, near0, keep0 = chunks
    layers, half, width = mine.shape
    rows = near.shape[1]
    size = (far.shape[0] - STRIP * rows // LANES) // layers
    start = half - size
    for level in range(layers):
        part = project_rows(rows_ref, keep, near, across, diagonal, level)
        mine[level] = part[:half]
        for k, out, remainder in ((1, far, rest), (3, sibling_far, sibling_rest)):
            piece = part[k * half : (k + 1) * half]
            out[level * size : (level + 1) * size] = piece[start:]
            remainder[level * start : (level + 1) * start] = piece[:start]
        give[level, :half, :width] = sibling0[level]
        give[level, :half, width:] = part[2 * half : 3 * half]
        for k, blocks in enumerate(((across0, keep0), (across, keep))):
            cut = slice(k * width, (k + 1) * width)
            edges = [block[level, at : at + 16] for block in blocks for at in (0, rows - 16)]
            give[level, half:, cut] = stack(*edges)
    put_strip(far, layers * size, strip)
    put_strip(sibling_far, layers * size, sibling_strip)


def project(parts, cols_refs, at):
    cols = stack(*[ref[level, start:stop, at : at + 256] for ref, level, start, stop in cols_refs])
    return dot(beside(*parts), cols)


def phase_kernel(mine_ref, other_ref, mine0, mine1, came, sibling_came, phase):
    layers, _, width = mine0.shape
    parts, cuts = [], []
    for level in range(layers):
        parts += [mine0[level], mine1[level], came[level], sibling_came[level]]
        cuts += [(mine_ref, level, 0, 2 * width)]
        cuts += [(other_ref, level, 0, width), (other_ref, level, 2 * width, 3 * width)]
    for at in range(0, phase.shape[1], 256):
        phase[:, at : at + 256] = project(parts, cuts, at)


def taken_kernel(mine_ref, phase, taken, out):
    half, pupil_cols = phase.shape
    layers, cols_dev, _ = mine_ref.shape
    parts = [taken[level, :half] for level in range(layers)]
    cuts = [(mine_ref, level, cols_dev // 2, cols_dev) for level in range(layers)]
    for at in range(0, pupil_cols, 256):
        out[:, at : at + 256] = phase[:, at : at + 256] + project(parts, cuts, at)


def sum_up(start, cols_ref, phase, came, sibling_came, outs):
    layers, cols_dev, _ = cols_ref.shape
    width = cols_dev // 4
    block = outs[0].shape[0]
    size = block * len(outs)
    rows = slice(start, start + size)
    parts, cuts = [], []
    for level in range(layers):
        cut = slice(level * size, (level + 1) * size)
        parts += [came[cut], sibling_came[cut]]
        cuts += [(cols_ref, level, width, 2 * width), (cols_ref, level, 3 * width, 4 * width)]
    pupil_cols = phase.shape[1]
    for at in range(0, pupil_cols, 256):
        total = (phase[rows, at : at + 256] + project(parts, cuts, at)).astype(jnp.bfloat16)
        for k, out in enumerate(outs):
            out[:, at : at + 256] = total[k * block : (k + 1) * block]


def strip_steps(pairs):
    return [2**k - 1 for k in range(1, pairs.bit_length())]


def send_order(pairs):
    steps = strip_steps(pairs)
    return [k for k in range(pairs) if k not in steps] + steps


def add_strip(pairs, step, strips, out):
    pair = lax.axis_index("layer") // 2
    after = lax.rem(pair + 1, pairs) == jnp.bitwise_xor(pair, step)
    at = out.shape[1] - strips.shape[1]
    last, first = strips[:STRIP].astype(jnp.float32), strips[STRIP:].astype(jnp.float32)
    out[:, at:] = jnp.where(after, last, first).astype(jnp.bfloat16)


def far_kernel(cols_ref, phase, came, sibling_came, *outs):
    *outs, strips = outs
    half = phase.shape[0]
    size = outs[0].shape[0] * len(outs)
    sum_up(half - size, cols_ref, phase, came, sibling_came, outs)
    layers = cols_ref.shape[0]
    odd = lax.rem(lax.axis_index("dir"), 2) == 1
    here = get_strip(came, layers * size).astype(jnp.float32)
    there = get_strip(sibling_came, layers * size).astype(jnp.float32)
    strips[:STRIP] = jnp.where(odd, here, there).astype(jnp.bfloat16)
    strips[STRIP:] = jnp.where(odd, there, here).astype(jnp.bfloat16)
    pairs = half // outs[0].shape[0]
    for out, step in zip(outs, strip_steps(pairs)):
        add_strip(pairs, step, strips, out)


def rest_kernel(cols_ref, phase, came, sibling_came, *outs):
    sum_up(0, cols_ref, phase, came, sibling_came, outs)


def shifted_rows(shift, odd, own, near, far):
    own, near, far = [block.astype(jnp.float32) for block in (own, near, far)]
    rows = own.shape[0]
    before = jnp.where(odd, near[16:], far[16:])
    after = jnp.where(odd, far[:16], near[:16])
    shift = jnp.where(shift < 0, shift + rows + 32, shift)
    return pltpu.roll(stack(before, own, after), shift, 0)[16 : 16 + rows]


def shift_kernel(wind_held, own, near0, near1, diagonal0, diagonal1, taken, partner_strips, *refs):
    messages, (out, wind, sem) = refs[:-3], refs[-3:]
    load = fetch((wind_held, wind, sem))[0]
    layers, rows, cols = own.shape
    odd = lax.rem(lax.axis_index("dir"), 2) == 1
    half = taken.shape[1] - 64
    pairs = 2 ** len(messages)
    pair, second = lax.axis_index("layer") // 2, lax.rem(lax.axis_index("layer"), 2) == 1
    before = jnp.bitwise_xor(pair, lax.rem(pair + pairs - 1, pairs))
    after = jnp.bitwise_xor(pair, lax.rem(pair + 1, pairs))
    left = partner_strips[:STRIP].astype(jnp.float32)
    right = partner_strips[STRIP:].astype(jnp.float32)
    for step, message in zip(strip_steps(pairs), messages):
        strip = message[:, message.shape[1] - rows :].astype(jnp.float32)
        left = jnp.where(jnp.logical_and(before == step, jnp.logical_not(second)), strip, left)
        right = jnp.where(jnp.logical_and(after == step, second), strip, right)
    strips = stack(left, right, jnp.zeros((LANES - 2 * STRIP, rows), jnp.float32)).T
    lane = lax.broadcasted_iota(jnp.int32, (rows, LANES), 1)
    load.wait()
    for level in range(layers):
        last = pltpu.roll(strips, LANES - WIND_MAX * (level + 1), 1)
        first = pltpu.roll(strips, LANES - STRIP - WIND_MAX * level, 1)
        extra = jnp.where(lane < WIND_MAX, first, last)
        pair = []
        for at, parts in ((half, (diagonal0, diagonal1)), (half + 32, (near0, near1))):
            here = [stack(part[level, :16], part[level, rows - 16 :]).astype(jnp.float32) for part in parts]
            there = taken[level, at : at + 32].astype(jnp.float32)
            width = there.shape[1] // 2
            quarters = [*here, there[:, width:], there[:, :width]]
            pair.append(beside(*[jnp.where(odd, quarters[3 - k], quarters[k]) for k in range(4)]))
        far, near = pair
        moved = shifted_rows(wind[0, level], odd, own[level], near, far)
        shift = wind[1, level]
        shift = jnp.where(shift < 0, shift + cols + LANES, shift)
        out[level] = pltpu.roll(beside(moved, extra), shift, 1)[:, :cols].astype(jnp.bfloat16)


def optics_kernel(amplitude, ones, columns, lines, amp_out, columns_out, lines_out):
    rows, pupil_cols = amplitude.shape
    for step in range(pupil_cols // LANES):
        cut = slice(step * LANES, (step + 1) * LANES)
        amp = amplitude[:, cut]
        energy = (amp * amp).reshape(rows // SUB_PIX, SUB_PIX, LANES).sum(axis=1)
        energy = jnp.broadcast_to(energy[:, None], (rows // SUB_PIX, SUB_PIX, LANES)).reshape(rows, LANES)
        total = jnp.dot(energy, ones[...], precision=lax.Precision.HIGHEST, preferred_element_type=jnp.float32)
        amp_out[:, cut] = amp * lax.rsqrt(total)
    columns_out[...] = columns[...].astype(jnp.bfloat16)
    lines_out[...] = lines[...].astype(jnp.bfloat16)


def sin_cos(phase):
    turns = jnp.floor(phase * (1.0 / np.pi) + 0.5)
    rest = phase - turns * 3.140625
    rest = rest - turns * 9.67653589793e-4
    odd = turns - 2.0 * jnp.floor(turns * 0.5)
    sign = 1.0 - 2.0 * odd
    square = rest * rest
    sine = -1.0 / 39916800.0
    for term in (1.0 / 362880.0, -1.0 / 5040.0, 1.0 / 120.0, -1.0 / 6.0, 1.0):
        sine = sine * square + term
    cosine = 1.0 / 479001600.0
    for term in (-1.0 / 3628800.0, 1.0 / 40320.0, -1.0 / 720.0, 1.0 / 24.0, -0.5, 1.0):
        cosine = cosine * square + term
    return sine * rest * sign, cosine * sign


def imaging_kernel(count, *refs):
    parts, (amp_ref, columns, lines, shifted, spots, screens, out, sems) = refs[:count], refs[count:]
    copies = fetch((shifted, screens, sems.at[0]))
    rows, cols = amp_ref.shape
    tiles = cols // LANES
    phase = parts[0][:, :cols].astype(jnp.float32)
    for part in parts[1:]:
        phase = phase + part[:, :cols].astype(jnp.float32)
    sine, cosine = sin_cos(phase)
    amp = amp_ref[...]
    real, imag = (amp * cosine).astype(jnp.bfloat16), (amp * sine).astype(jnp.bfloat16)
    cuts = [slice(t * LANES, (t + 1) * LANES) for t in range(tiles)]
    field = stack(*[beside(real[:, cut], imag[:, cut]) for cut in cuts])
    half = dot(field, columns[...]).astype(jnp.bfloat16)
    wide = 2 * LANES
    out_rows = 2 * rows
    for t in range(tiles):
        mine = half[t * rows : (t + 1) * rows]
        full = dot(lines[...], stack(mine[:, :wide], mine[:, wide:]))
        real, imag = full[:out_rows], full[out_rows:]
        out[:, t * wide : (t + 1) * wide] = real * real + imag * imag
        if t % 2:
            cut = slice((t - 1) * wide, (t + 1) * wide)
            copies += fetch((out.at[:, cut], spots.at[:, cut], sems.at[1 + t // 2]))
    for copy in copies:
        copy.wait()


def tables_of(rows):
    freq = np.arange(SPOT_PIX)[:, None] - SPOT_PIX // 2
    angle = ((freq * np.arange(SUB_PIX)[None, :]) % SPOT_PIX) * (2.0 * np.pi / SPOT_PIX)
    cos, sin = np.cos(angle), np.sin(angle)

    def blocks(table, count):
        return np.kron(np.eye(count), table)

    per_tile = LANES // SUB_PIX
    col_cos, col_sin = blocks(cos.T, per_tile), blocks(sin.T, per_tile)
    columns = np.block([[col_cos, -col_sin], [col_sin, col_cos]])
    count = rows // SUB_PIX
    row_cos, row_sin = blocks(cos, count), blocks(sin, count)
    lines = np.block([[row_cos, row_sin], [-row_sin, row_cos]])

    return columns.astype(np.float32), lines.astype(np.float32)


def per_device(screens, amplitude, wind, offsets, ratio):
    layers, rows_dev, cols_dev = screens.shape
    n_layer = lax.axis_size("layer")
    n_dir = lax.axis_size("dir")
    rows, pupil_cols = amplitude.shape
    pairs = n_layer // 2
    half = pairs * rows
    pupil_rows = 2 * half
    assert n_dir == 4 and rows == STRIP and pairs > 2
    bf16, f32 = jnp.bfloat16, jnp.float32
    wind = jnp.transpose(wind, (1, 0))
    offsets = jnp.transpose(offsets, (1, 2, 0))
    ratio = jnp.transpose(ratio, (1, 2, 0))
    smem, sem = pltpu.SMEM, pltpu.SemaphoreType.DMA
    wind_scratch = [smem(wind.shape, jnp.int32), sem]

    def shape(*dims, dtype=bf16):
        return jax.ShapeDtypeStruct(dims, dtype)

    def swap(value, bits):
        return lax.ppermute(value, "dir", [(i, i ^ bits) for i in range(n_dir)])

    def partner(value, bits=0):
        count = n_layer * n_dir
        return lax.ppermute(value, ("layer", "dir"), [(i, i ^ n_dir ^ bits) for i in range(count)])

    def turn(value, step):
        return lax.ppermute(value, "layer", [(i, (i + step) % n_layer) for i in range(n_layer)])

    width = cols_dev // 4
    chunk = shape(layers, rows_dev, width)
    ints = (wind, offsets, ratio)
    keep0, keep1, give0, give1, *ints = call(
        split_kernel,
        [chunk] * 4 + [shape(*array.shape, dtype=jnp.int32) for array in ints],
        (screens, *ints),
        0,
        "split",
        in_hbm=range(4),
        scratch=[sem((7,))],
        brief=True,
    )
    across0 = swap(keep0, 2)
    diagonal0 = swap(give0, 3)
    near0 = swap(give0, 1)
    near1 = swap(give1, 1)
    diagonal1 = swap(give1, 3)
    ones = np.kron(np.eye(LANES // SUB_PIX), np.ones((SUB_PIX, SUB_PIX))).astype(np.float32)
    optics_in = (amplitude, jnp.asarray(ones), *[jnp.asarray(table) for table in tables_of(rows)])
    copies = [shape(*array.shape, dtype=array.dtype) for array in (screens, *optics_in)]
    row_weights, cols, *loaded = call(
        functools.partial(weights_kernel, (n_layer, rows_dev, cols_dev * n_layer)),
        [shape(2, layers, pupil_rows, 4 * rows_dev), shape(layers, cols_dev, pupil_cols)]
        + [shape(8, pupil_cols, dtype=dtype) for dtype in (jnp.int32, jnp.int32, f32, f32)]
        + copies,
        (*ints, screens, *optics_in),
        0,
        "weights",
        in_hbm=range(3, 8),
        scratch=[smem(array.shape, jnp.int32) for array in (wind, offsets, ratio)]
        + [sem((8,))],
        brief=True,
    )
    tables, (own, *optics_in) = loaded[:4], loaded[4:]
    wind = ints[0]
    keep1, own = lax.optimization_barrier((keep1, own))
    across1 = swap(keep1, 2)
    across0, diagonal0, row_weights, cols = lax.optimization_barrier((across0, diagonal0, row_weights, cols))

    projected = shape(layers, half, width)
    mine0, sibling0, other0, sibling_other0 = call(
        first_rows_kernel,
        [projected] * 4,
        (row_weights, across0, diagonal0, near0, keep0),
        0,
        "rows_first",
        brief=True,
    )
    came0 = partner(other0)
    sibling_came0 = partner(sibling_other0, 1)

    wind, mine0 = lax.optimization_barrier((wind, mine0))
    others, strip, sibling_strip = call(
        strips_kernel,
        [shape(layers, cols_dev, pupil_cols)] + [shape(STRIP, rows_dev)] * 2,
        (wind, *tables, across0, diagonal0, near0, keep0),
        0,
        "strips",
        scratch=wind_scratch,
        brief=True,
    )
    steps = strip_steps(pairs)
    far = len(steps) * rows
    message = shape(layers * far + STRIP * rows_dev // LANES, width)
    remainder = shape(layers * (half - far), width)
    mine1, give, far1, sibling_far1, rest1, sibling_rest1 = call(
        later_rows_kernel,
        [projected, shape(layers, half + 64, 2 * width), message, message, remainder, remainder],
        (row_weights, across1, diagonal1, near1, keep1, across0, diagonal0, near0, keep0, sibling0, strip, sibling_strip),
        0,
        "rows_later",
        brief=True,
    )
    far1, sibling_far1 = partner(far1), partner(sibling_far1, 1)
    taken = swap(give, 1)
    phase = call(
        phase_kernel,
        shape(half, pupil_cols, dtype=f32),
        (cols, others, mine0, mine1, came0, sibling_came0),
        10_000_000_000,
        "phase",
    )

    rest1, sibling_rest1, phase = lax.optimization_barrier((rest1, sibling_rest1, phase))
    rest1, sibling_rest1 = partner(rest1), partner(sibling_rest1, 1)
    phase = call(
        taken_kernel,
        shape(half, pupil_cols, dtype=f32),
        (cols, phase, taken),
        0,
        "taken",
        brief=True,
    )
    *far_sums, strips = call(
        far_kernel,
        [shape(rows, pupil_cols + rows_dev)] * len(steps) + [shape(2 * STRIP, rows_dev)],
        (others, phase, far1, sibling_far1),
        300_000_000,
        "far",
    )
    rest_sums = call(
        rest_kernel,
        [shape(rows, pupil_cols)] * (pairs - len(steps)),
        (others, phase, rest1, sibling_rest1),
        0,
        "rest",
        brief=True,
    )
    received = dict(zip(send_order(pairs), [*rest_sums, *far_sums]))
    for k in range(1, pairs):
        received[k] = lax.ppermute(received[k], "layer", [(i, i ^ (2 * k)) for i in range(n_layer)])
    received = [received[k] for k in range(pairs)]

    optics_in, received[-1] = lax.optimization_barrier((optics_in, received[-1]))
    optics = call(
        optics_kernel,
        (
            shape(rows, pupil_cols, dtype=f32),
            shape(*optics_in[2].shape),
            shape(*optics_in[3].shape),
        ),
        optics_in,
        0,
        "optics",
        brief=True,
    )
    received[1], optics = lax.optimization_barrier((received[1], optics))
    shifted = call(
        shift_kernel,
        shape(layers, rows_dev, cols_dev),
        (wind, own, near0, near1, diagonal0, diagonal1, taken, strips, *[received[k] for k in steps]),
        0,
        "shift",
        scratch=wind_scratch,
        brief=True,
    )
    spots_shape = shape(2 * rows, 2 * pupil_cols, dtype=f32)
    spots, new_screens = call(
        functools.partial(imaging_kernel, pairs),
        [spots_shape, shape(layers, rows_dev, cols_dev)],
        (*received, *optics, shifted),
        400_000_000,
        "imaging",
        out_hbm=(0, 1),
        scratch=[pltpu.VMEM(spots_shape.shape, f32), sem((1 + pupil_cols // (2 * LANES),))],
    )
    return (new_screens, spots[None])


def solution(mesh):
    return jax.shard_map(
        per_device,
        mesh=mesh,
        in_specs=(P(None, "dir", "layer"), P("layer", None), P(), P(), P()),
        out_specs=(P(None, "dir", "layer"), P("dir", "layer", None)),
        check_vma=False,
    )
```

```python
import functools

import jax
import jax.numpy as jnp
import numpy as np
from jax import lax
from jax.experimental import pallas as pl
from jax.experimental.pallas import tpu as pltpu
from jax.sharding import PartitionSpec as P

SUB_PIX = 16
SPOT_PIX = 32
WIND_MAX = 8
LANES = 128
STRIP = 32

HBM_SPEC = pl.BlockSpec(memory_space=pltpu.HBM)
VMEM_SPEC = pl.BlockSpec(memory_space=pltpu.VMEM)


def params(*arrays):
    held = sum(array.size * array.dtype.itemsize for array in jax.tree.leaves(arrays))
    return pltpu.CompilerParams(vmem_limit_bytes=held + 8 * 1024 * 1024)


def call(kernel, out_shape, operands, flops, name, in_hbm=(), out_hbm=(), scratch=(), brief=False):
    def spec(k, array):
        return HBM_SPEC if k in in_hbm else VMEM_SPEC

    if out_hbm:
        out_specs = [HBM_SPEC if k in out_hbm else VMEM_SPEC for k in range(len(out_shape))]
    else:
        out_specs = jax.tree.map(lambda _: VMEM_SPEC, out_shape)
    size = sum(array.size * array.dtype.itemsize for array in jax.tree.leaves((operands, out_shape)))
    if brief:
        flops = size = 0
    in_specs = [spec(k, array) for k, array in enumerate(operands)]
    operands = [
        pltpu.with_memory_space_constraint(array, pltpu.HBM) if space is HBM_SPEC else array
        for array, space in zip(operands, in_specs)
    ]
    return pl.pallas_call(
        kernel,
        out_shape=out_shape,
        in_specs=in_specs,
        out_specs=out_specs,
        scratch_shapes=list(scratch),
        compiler_params=params(operands, out_shape),
        cost_estimate=pl.CostEstimate(flops=flops, bytes_accessed=size, transcendentals=0),
        name=name,
    )(*operands)


def fetch(*pairs):
    copies = [pltpu.make_async_copy(source, target, sem) for source, target, sem in pairs]
    for copy in copies:
        copy.start()
    return copies


def wrap(value, length):
    value = jnp.where(value < 0, value + length, value)
    return jnp.where(value >= length, value - length, value)


def stack(*blocks):
    return jnp.concatenate(blocks, axis=0)


def beside(*blocks):
    return jnp.concatenate(blocks, axis=1)


def dot(left, right):
    return jnp.dot(left, right, preferred_element_type=jnp.float32)


def spans(pixel, anchor, num, den, length):
    stretched = (pixel * num).astype(jnp.float32)
    den = (jnp.zeros_like(pixel) + den).astype(jnp.float32)
    whole = jnp.floor((stretched + 0.5) / den)
    fraction = (stretched - whole * den) / den
    base = wrap(anchor + whole.astype(jnp.int32), length)
    upper = wrap(base + 1, length)
    return base, upper, 1.0 - fraction, fraction


def chunk_start(half, chunk):
    return 3 * half + chunk * (1 - 2 * half)


def split_kernel(screens, *refs):
    ints, outs, held, sems = refs[:3], refs[3:7], refs[7:10], refs[-1]
    width = outs[0].shape[2]
    core = lax.rem(lax.axis_index("dir"), 2)
    pairs = []
    for k, out in enumerate(outs):
        half = core if k < 2 else 1 - core
        start = pl.multiple_of(chunk_start(half, k % 2) * width, LANES)
        pairs.append((screens.at[:, :, pl.ds(start, width)], out, sems.at[k]))
    pairs += [(source, copy, sems.at[4 + k]) for k, (source, copy) in enumerate(zip(ints, held))]
    for load in fetch(*pairs):
        load.wait()


def weights_kernel(geometry, wind_held, offsets_held, ratio_held, *refs):
    n_layer, rows_dev, screen_cols = geometry
    sources, (rows_out, cols_out, *tables), refs = refs[:5], refs[5:11], refs[11:]
    copies, (wind, offsets, ratio, sems) = refs[:5], refs[5:]
    pupil_cols = cols_out.shape[2]
    loads = fetch(
        (wind_held, wind, sems.at[0]),
        (offsets_held, offsets, sems.at[1]),
        (ratio_held, ratio, sems.at[2]),
    )
    pairs = [*zip(sources, copies)]
    others = fetch(*[(source, copy, sems.at[3 + k]) for k, (source, copy) in enumerate(pairs)])
    _, layers, pupil_rows, screen_rows = rows_out.shape
    half = pupil_rows // 2
    direction = lax.axis_index("dir")
    column = lax.axis_index("layer")
    block = pupil_rows // n_layer
    row = lax.broadcasted_iota(jnp.int32, (half, LANES), 0)
    step = row // block
    for at, value in enumerate(send_order(n_layer // 2)):
        step = jnp.where(row // block == at, value, step)
    pair = jnp.bitwise_xor(step, column // 2)
    parity = lax.rem(column, 2)
    inside = lax.rem(row, block) + pair * (2 * block)
    pixel_rows = stack(inside + parity * block, inside + (1 - parity) * block)
    lane = lax.broadcasted_iota(jnp.int32, (pupil_rows, LANES), 1)
    for load in loads:
        load.wait()
    for side in range(2):
        target = jnp.bitwise_xor(direction, side)
        for level in range(layers):
            anchor = wrap(offsets[level, 0, target] - wind[0, level], screen_rows)
            num, den = ratio[level, 0, target], ratio[level, 1, target]
            base, upper, low, high = spans(pixel_rows, anchor, num, den, screen_rows)
            for peer in range(4):
                for part in range(rows_dev // LANES):
                    index = lane + (jnp.bitwise_xor(direction, peer) * rows_dev + part * LANES)
                    weight = jnp.where(index == base, low, 0.0)
                    weight = jnp.where(index == upper, high, weight)
                    start = peer * rows_dev + part * LANES
                    rows_out[side, level, :, start : start + LANES] = weight.astype(jnp.bfloat16)
    sub = lax.broadcasted_iota(jnp.int32, (8, LANES), 0)
    anchor, num, den = jnp.zeros_like(sub), jnp.zeros_like(sub), jnp.ones_like(sub)
    for level in range(layers):
        start = wrap(offsets[level, 1, direction] - wind[1, level], screen_cols)
        anchor = jnp.where(sub == level, start, anchor)
        num = jnp.where(sub == level, ratio[level, 0, direction], num)
        den = jnp.where(sub == level, ratio[level, 1, direction], den)
    for at in range(0, pupil_cols, LANES):
        pixel = lax.broadcasted_iota(jnp.int32, (8, LANES), 1) + at
        values = spans(pixel, anchor, num, den, screen_cols)
        for table, value in zip(tables, values):
            table[:, at : at + LANES] = value
    column_weights(*tables, column * cols_out.shape[1], cols_out)
    for load in others:
        load.wait()


def column_weights(base_ref, upper_ref, low_ref, high_ref, first, out):
    layers, cols_dev, pupil_cols = out.shape
    width = cols_dev // 4
    core = lax.rem(lax.axis_index("dir"), 2)
    sub = lax.broadcasted_iota(jnp.int32, (width, LANES), 0).astype(jnp.float32).astype(jnp.bfloat16)
    zero = jnp.zeros((width, LANES), jnp.bfloat16)
    for level in range(layers):

        def tile(step, carry):
            start = pl.multiple_of(step * LANES, LANES)
            cut = (slice(level, level + 1), pl.ds(start, LANES))
            base, upper = base_ref[cut], upper_ref[cut]
            low, high = [
                jnp.broadcast_to(ref[cut].astype(jnp.bfloat16), (width, LANES)) for ref in (low_ref, high_ref)
            ]
            for k in range(4):
                shift = first + chunk_start(jnp.bitwise_xor(core, k // 2), k % 2) * width
                base_at, upper_at = [
                    jnp.broadcast_to(
                        jnp.clip(value - shift, -1, width).astype(jnp.float32).astype(jnp.bfloat16), (width, LANES)
                    )
                    for value in (base, upper)
                ]
                weight = jnp.where(sub == base_at, low, zero)
                weight = jnp.where(sub == upper_at, high, weight)
                out[level, k * width : (k + 1) * width, pl.ds(start, LANES)] = weight
            return carry

        lax.fori_loop(0, pupil_cols // LANES, tile, 0)


def strips_kernel(wind_held, *refs):
    tables, (across, diagonal, near, keep, cols_out, strip, sibling_strip, wind, sem) = refs[:4], refs[4:]
    load = fetch((wind_held, wind, sem))[0]
    column_weights(*tables, jnp.bitwise_xor(lax.axis_index("layer"), 1) * cols_out.shape[1], cols_out)
    layers, rows, _ = keep.shape
    core = lax.rem(lax.axis_index("dir"), 2)
    odd = core == 1
    lane = lax.broadcasted_iota(jnp.int32, (rows + 32, LANES), 1)

    def wide(own, near, far, odd, level):
        own, near, far = [block[level].astype(jnp.float32) for block in (own, near, far)]
        before = jnp.where(odd, near[rows - 16 :], far[rows - 16 :])
        return stack(before, own, jnp.where(odd, far[:16], near[:16]))

    packed = jnp.zeros((rows + 32, LANES), jnp.float32)
    for level in range(layers):
        blocks = (keep, near, diagonal, odd), (near, keep, across, core == 0)
        for at, block in zip((WIND_MAX * level, STRIP + WIND_MAX * level), blocks):
            block = pltpu.roll(wide(*block, level), at + WIND_MAX * core, 1)
            packed = jnp.where((lane >= at) & (lane < at + WIND_MAX), block, packed)
    load.wait()
    strips = jnp.zeros((rows, LANES), jnp.float32)
    for level in range(layers):
        shift = wind[0, level]
        shift = jnp.where(shift < 0, shift + rows + 32, shift)
        moved = pltpu.roll(packed, shift, 0)[16 : 16 + rows]
        mine = lax.rem(lane[:rows], STRIP)
        strips = jnp.where((mine >= WIND_MAX * level) & (mine < WIND_MAX * (level + 1)), moved, strips)
    strips = strips.T.astype(jnp.bfloat16)
    strip[...] = strips[:STRIP]
    sibling_strip[...] = strips[STRIP : 2 * STRIP]


def project_rows(rows_ref, keep, near, across, diagonal, level):
    screen = stack(keep[level], near[level], across[level], diagonal[level])
    rows = stack(rows_ref[0, level], rows_ref[1, level])
    return dot(rows, screen).astype(jnp.bfloat16)


def first_rows_kernel(rows_ref, across, diagonal, near, keep, mine, sibling, other, sibling_other):
    layers, half, _ = mine.shape
    for level in range(layers):
        part = project_rows(rows_ref, keep, near, across, diagonal, level)
        for k, out in enumerate((mine, other, sibling, sibling_other)):
            out[level] = part[k * half : (k + 1) * half]


def put_strip(out, at, strip):
    for k in range(strip.shape[1] // LANES):
        out[at + k * STRIP : at + (k + 1) * STRIP, :] = strip[:, k * LANES : (k + 1) * LANES]


def get_strip(ref, at):
    return beside(*[ref[start : start + STRIP, :] for start in range(at, ref.shape[0], STRIP)])


def later_rows_kernel(rows_ref, *refs):
    chunks, refs = refs[:8], refs[8:]
    sibling0, strip, sibling_strip, mine, give, far, sibling_far, rest, sibling_rest = refs
    across, diagonal, near, keep, across0, diagonal0, near0, keep0 = chunks
    layers, half, width = mine.shape
    rows = near.shape[1]
    size = (far.shape[0] - STRIP * rows // LANES) // layers
    start = half - size
    for level in range(layers):
        part = project_rows(rows_ref, keep, near, across, diagonal, level)
        mine[level] = part[:half]
        for k, out, remainder in ((1, far, rest), (3, sibling_far, sibling_rest)):
            piece = part[k * half : (k + 1) * half]
            out[level * size : (level + 1) * size] = piece[start:]
            remainder[level * start : (level + 1) * start] = piece[:start]
        give[level, :half, :width] = sibling0[level]
        give[level, :half, width:] = part[2 * half : 3 * half]
        for k, blocks in enumerate(((across0, keep0), (across, keep))):
            cut = slice(k * width, (k + 1) * width)
            edges = [block[level, at : at + 16] for block in blocks for at in (0, rows - 16)]
            give[level, half:, cut] = stack(*edges)
    put_strip(far, layers * size, strip)
    put_strip(sibling_far, layers * size, sibling_strip)


def project(parts, cols_refs, at):
    cols = stack(*[ref[level, start:stop, at : at + 256] for ref, level, start, stop in cols_refs])
    return dot(beside(*parts), cols)


def phase_kernel(mine_ref, other_ref, mine0, mine1, came, sibling_came, phase):
    layers, _, width = mine0.shape
    parts, cuts = [], []
    for level in range(layers):
        parts += [mine0[level], mine1[level], came[level], sibling_came[level]]
        cuts += [(mine_ref, level, 0, 2 * width)]
        cuts += [(other_ref, level, 0, width), (other_ref, level, 2 * width, 3 * width)]
    for at in range(0, phase.shape[1], 256):
        phase[:, at : at + 256] = project(parts, cuts, at)


def taken_kernel(mine_ref, phase, taken, out):
    half, pupil_cols = phase.shape
    layers, cols_dev, _ = mine_ref.shape
    parts = [taken[level, :half] for level in range(layers)]
    cuts = [(mine_ref, level, cols_dev // 2, cols_dev) for level in range(layers)]
    for at in range(0, pupil_cols, 256):
        out[:, at : at + 256] = phase[:, at : at + 256] + project(parts, cuts, at)


def sum_up(start, cols_ref, phase, came, sibling_came, outs):
    layers, cols_dev, _ = cols_ref.shape
    width = cols_dev // 4
    block = outs[0].shape[0]
    size = block * len(outs)
    rows = slice(start, start + size)
    parts, cuts = [], []
    for level in range(layers):
        cut = slice(level * size, (level + 1) * size)
        parts += [came[cut], sibling_came[cut]]
        cuts += [(cols_ref, level, width, 2 * width), (cols_ref, level, 3 * width, 4 * width)]
    pupil_cols = phase.shape[1]
    for at in range(0, pupil_cols, 256):
        total = (phase[rows, at : at + 256] + project(parts, cuts, at)).astype(jnp.bfloat16)
        for k, out in enumerate(outs):
            out[:, at : at + 256] = total[k * block : (k + 1) * block]


def strip_steps(pairs):
    return [2**k - 1 for k in range(1, pairs.bit_length())]


def send_order(pairs):
    steps = strip_steps(pairs)
    return [k for k in range(pairs) if k not in steps] + steps


def add_strip(pairs, step, strips, out):
    pair = lax.axis_index("layer") // 2
    after = lax.rem(pair + 1, pairs) == jnp.bitwise_xor(pair, step)
    at = out.shape[1] - strips.shape[1]
    last, first = strips[:STRIP].astype(jnp.float32), strips[STRIP:].astype(jnp.float32)
    out[:, at:] = jnp.where(after, last, first).astype(jnp.bfloat16)


def far_kernel(cols_ref, phase, came, sibling_came, *outs):
    *outs, strips = outs
    half = phase.shape[0]
    size = outs[0].shape[0] * len(outs)
    sum_up(half - size, cols_ref, phase, came, sibling_came, outs)
    layers = cols_ref.shape[0]
    odd = lax.rem(lax.axis_index("dir"), 2) == 1
    here = get_strip(came, layers * size).astype(jnp.float32)
    there = get_strip(sibling_came, layers * size).astype(jnp.float32)
    strips[:STRIP] = jnp.where(odd, here, there).astype(jnp.bfloat16)
    strips[STRIP:] = jnp.where(odd, there, here).astype(jnp.bfloat16)
    pairs = half // outs[0].shape[0]
    for out, step in zip(outs, strip_steps(pairs)):
        add_strip(pairs, step, strips, out)


def rest_kernel(cols_ref, phase, came, sibling_came, *outs):
    sum_up(0, cols_ref, phase, came, sibling_came, outs)


def shifted_rows(shift, odd, own, near, far):
    own, near, far = [block.astype(jnp.float32) for block in (own, near, far)]
    rows = own.shape[0]
    before = jnp.where(odd, near[16:], far[16:])
    after = jnp.where(odd, far[:16], near[:16])
    shift = jnp.where(shift < 0, shift + rows + 32, shift)
    return pltpu.roll(stack(before, own, after), shift, 0)[16 : 16 + rows]


def shift_kernel(wind_held, own, near0, near1, diagonal0, diagonal1, taken, partner_strips, *refs):
    messages, (out, wind, sem) = refs[:-3], refs[-3:]
    load = fetch((wind_held, wind, sem))[0]
    layers, rows, cols = own.shape
    odd = lax.rem(lax.axis_index("dir"), 2) == 1
    half = taken.shape[1] - 64
    pairs = 2 ** len(messages)
    pair, second = lax.axis_index("layer") // 2, lax.rem(lax.axis_index("layer"), 2) == 1
    before = jnp.bitwise_xor(pair, lax.rem(pair + pairs - 1, pairs))
    after = jnp.bitwise_xor(pair, lax.rem(pair + 1, pairs))
    left = partner_strips[:STRIP].astype(jnp.float32)
    right = partner_strips[STRIP:].astype(jnp.float32)
    for step, message in zip(strip_steps(pairs), messages):
        strip = message[:, message.shape[1] - rows :].astype(jnp.float32)
        left = jnp.where(jnp.logical_and(before == step, jnp.logical_not(second)), strip, left)
        right = jnp.where(jnp.logical_and(after == step, second), strip, right)
    strips = stack(left, right, jnp.zeros((LANES - 2 * STRIP, rows), jnp.float32)).T
    lane = lax.broadcasted_iota(jnp.int32, (rows, LANES), 1)
    load.wait()
    for level in range(layers):
        last = pltpu.roll(strips, LANES - WIND_MAX * (level + 1), 1)
        first = pltpu.roll(strips, LANES - STRIP - WIND_MAX * level, 1)
        extra = jnp.where(lane < WIND_MAX, first, last)
        pair = []
        for at, parts in ((half, (diagonal0, diagonal1)), (half + 32, (near0, near1))):
            here = [stack(part[level, :16], part[level, rows - 16 :]).astype(jnp.float32) for part in parts]
            there = taken[level, at : at + 32].astype(jnp.float32)
            width = there.shape[1] // 2
            quarters = [*here, there[:, width:], there[:, :width]]
            pair.append(beside(*[jnp.where(odd, quarters[3 - k], quarters[k]) for k in range(4)]))
        far, near = pair
        moved = shifted_rows(wind[0, level], odd, own[level], near, far)
        shift = wind[1, level]
        shift = jnp.where(shift < 0, shift + cols + LANES, shift)
        out[level] = pltpu.roll(beside(moved, extra), shift, 1)[:, :cols].astype(jnp.bfloat16)


def optics_kernel(amplitude, ones, columns, lines, amp_out, columns_out, lines_out):
    rows, pupil_cols = amplitude.shape
    for step in range(pupil_cols // LANES):
        cut = slice(step * LANES, (step + 1) * LANES)
        amp = amplitude[:, cut]
        energy = (amp * amp).reshape(rows // SUB_PIX, SUB_PIX, LANES).sum(axis=1)
        energy = jnp.broadcast_to(energy[:, None], (rows // SUB_PIX, SUB_PIX, LANES)).reshape(rows, LANES)
        total = jnp.dot(energy, ones[...], precision=lax.Precision.HIGHEST, preferred_element_type=jnp.float32)
        amp_out[:, cut] = amp * lax.rsqrt(total)
    columns_out[...] = columns[...].astype(jnp.bfloat16)
    lines_out[...] = lines[...].astype(jnp.bfloat16)


def sin_cos(phase):
    turns = jnp.floor(phase * (1.0 / np.pi) + 0.5)
    rest = phase - turns * 3.140625
    rest = rest - turns * 9.67653589793e-4
    odd = turns - 2.0 * jnp.floor(turns * 0.5)
    sign = 1.0 - 2.0 * odd
    square = rest * rest
    sine = -1.0 / 39916800.0
    for term in (1.0 / 362880.0, -1.0 / 5040.0, 1.0 / 120.0, -1.0 / 6.0, 1.0):
        sine = sine * square + term
    cosine = 1.0 / 479001600.0
    for term in (-1.0 / 3628800.0, 1.0 / 40320.0, -1.0 / 720.0, 1.0 / 24.0, -0.5, 1.0):
        cosine = cosine * square + term
    return sine * rest * sign, cosine * sign


def imaging_kernel(count, *refs):
    parts, (amp_ref, columns, lines, shifted, spots, screens, out, sems) = refs[:count], refs[count:]
    copies = fetch((shifted, screens, sems.at[0]))
    rows, cols = amp_ref.shape
    tiles = cols // LANES
    phase = parts[0][:, :cols].astype(jnp.float32)
    for part in parts[1:]:
        phase = phase + part[:, :cols].astype(jnp.float32)
    sine, cosine = sin_cos(phase)
    amp = amp_ref[...]
    real, imag = (amp * cosine).astype(jnp.bfloat16), (amp * sine).astype(jnp.bfloat16)
    lined = dot(lines[...], stack(real, imag)).astype(jnp.bfloat16)
    out_rows, wide, group = 2 * rows, 2 * LANES, tiles // 2
    for part in range(2):
        cuts = [slice(t * LANES, (t + 1) * LANES) for t in range(part * group, (part + 1) * group)]
        field = stack(*[beside(lined[:out_rows, cut], lined[out_rows:, cut]) for cut in cuts])
        full = dot(field, columns[...])
        for k in range(group):
            mine = full[k * out_rows : (k + 1) * out_rows]
            real, imag = mine[:, :wide], mine[:, wide:]
            at = (part * group + k) * wide
            out[:, at : at + wide] = real * real + imag * imag
        cut = slice(part * group * wide, (part + 1) * group * wide)
        copies += fetch((out.at[:, cut], spots.at[:, cut], sems.at[1 + part]))
    for copy in copies:
        copy.wait()


def tables_of(rows):
    freq = np.arange(SPOT_PIX)[:, None] - SPOT_PIX // 2
    angle = ((freq * np.arange(SUB_PIX)[None, :]) % SPOT_PIX) * (2.0 * np.pi / SPOT_PIX)
    cos, sin = np.cos(angle), np.sin(angle)

    def blocks(table, count):
        return np.kron(np.eye(count), table)

    per_tile = LANES // SUB_PIX
    col_cos, col_sin = blocks(cos.T, per_tile), blocks(sin.T, per_tile)
    columns = np.block([[col_cos, -col_sin], [col_sin, col_cos]])
    count = rows // SUB_PIX
    row_cos, row_sin = blocks(cos, count), blocks(sin, count)
    lines = np.block([[row_cos, row_sin], [-row_sin, row_cos]])

    return columns.astype(np.float32), lines.astype(np.float32)


def per_device(screens, amplitude, wind, offsets, ratio):
    layers, rows_dev, cols_dev = screens.shape
    n_layer = lax.axis_size("layer")
    n_dir = lax.axis_size("dir")
    rows, pupil_cols = amplitude.shape
    pairs = n_layer // 2
    half = pairs * rows
    pupil_rows = 2 * half
    assert n_dir == 4 and rows == STRIP and pairs > 2
    bf16, f32 = jnp.bfloat16, jnp.float32
    wind = jnp.transpose(wind, (1, 0))
    offsets = jnp.transpose(offsets, (1, 2, 0))
    ratio = jnp.transpose(ratio, (1, 2, 0))
    smem, sem = pltpu.SMEM, pltpu.SemaphoreType.DMA
    wind_scratch = [smem(wind.shape, jnp.int32), sem]

    def shape(*dims, dtype=bf16):
        return jax.ShapeDtypeStruct(dims, dtype)

    def swap(value, bits):
        return lax.ppermute(value, "dir", [(i, i ^ bits) for i in range(n_dir)])

    def partner(value, bits=0):
        count = n_layer * n_dir
        return lax.ppermute(value, ("layer", "dir"), [(i, i ^ n_dir ^ bits) for i in range(count)])

    def turn(value, step):
        return lax.ppermute(value, "layer", [(i, (i + step) % n_layer) for i in range(n_layer)])

    width = cols_dev // 4
    chunk = shape(layers, rows_dev, width)
    ints = (wind, offsets, ratio)
    keep0, keep1, give0, give1, *ints = call(
        split_kernel,
        [chunk] * 4 + [shape(*array.shape, dtype=jnp.int32) for array in ints],
        (screens, *ints),
        0,
        "split",
        in_hbm=range(4),
        scratch=[sem((7,))],
        brief=True,
    )
    across0 = swap(keep0, 2)
    diagonal0 = swap(give0, 3)
    near0 = swap(give0, 1)
    near1 = swap(give1, 1)
    diagonal1 = swap(give1, 3)
    ones = np.kron(np.eye(LANES // SUB_PIX), np.ones((SUB_PIX, SUB_PIX))).astype(np.float32)
    optics_in = (amplitude, jnp.asarray(ones), *[jnp.asarray(table) for table in tables_of(rows)])
    copies = [shape(*array.shape, dtype=array.dtype) for array in (screens, *optics_in)]
    row_weights, cols, *loaded = call(
        functools.partial(weights_kernel, (n_layer, rows_dev, cols_dev * n_layer)),
        [shape(2, layers, pupil_rows, 4 * rows_dev), shape(layers, cols_dev, pupil_cols)]
        + [shape(8, pupil_cols, dtype=dtype) for dtype in (jnp.int32, jnp.int32, f32, f32)]
        + copies,
        (*ints, screens, *optics_in),
        0,
        "weights",
        in_hbm=range(3, 8),
        scratch=[smem(array.shape, jnp.int32) for array in (wind, offsets, ratio)]
        + [sem((8,))],
        brief=True,
    )
    tables, (own, *optics_in) = loaded[:4], loaded[4:]
    wind = ints[0]
    keep1, own = lax.optimization_barrier((keep1, own))
    across1 = swap(keep1, 2)
    across0, diagonal0, row_weights, cols = lax.optimization_barrier((across0, diagonal0, row_weights, cols))

    projected = shape(layers, half, width)
    mine0, sibling0, other0, sibling_other0 = call(
        first_rows_kernel,
        [projected] * 4,
        (row_weights, across0, diagonal0, near0, keep0),
        0,
        "rows_first",
        brief=True,
    )
    came0 = partner(other0)
    sibling_came0 = partner(sibling_other0, 1)

    wind, mine0 = lax.optimization_barrier((wind, mine0))
    others, strip, sibling_strip = call(
        strips_kernel,
        [shape(layers, cols_dev, pupil_cols)] + [shape(STRIP, rows_dev)] * 2,
        (wind, *tables, across0, diagonal0, near0, keep0),
        0,
        "strips",
        scratch=wind_scratch,
        brief=True,
    )
    steps = strip_steps(pairs)
    far = len(steps) * rows
    message = shape(layers * far + STRIP * rows_dev // LANES, width)
    remainder = shape(layers * (half - far), width)
    mine1, give, far1, sibling_far1, rest1, sibling_rest1 = call(
        later_rows_kernel,
        [projected, shape(layers, half + 64, 2 * width), message, message, remainder, remainder],
        (row_weights, across1, diagonal1, near1, keep1, across0, diagonal0, near0, keep0, sibling0, strip, sibling_strip),
        0,
        "rows_later",
        brief=True,
    )
    far1, sibling_far1 = partner(far1), partner(sibling_far1, 1)
    taken = swap(give, 1)
    phase = call(
        phase_kernel,
        shape(half, pupil_cols, dtype=f32),
        (cols, others, mine0, mine1, came0, sibling_came0),
        10_000_000_000,
        "phase",
    )

    rest1, sibling_rest1, phase = lax.optimization_barrier((rest1, sibling_rest1, phase))
    rest1, sibling_rest1 = partner(rest1), partner(sibling_rest1, 1)
    phase = call(
        taken_kernel,
        shape(half, pupil_cols, dtype=f32),
        (cols, phase, taken),
        0,
        "taken",
        brief=True,
    )
    *far_sums, strips = call(
        far_kernel,
        [shape(rows, pupil_cols + rows_dev)] * len(steps) + [shape(2 * STRIP, rows_dev)],
        (others, phase, far1, sibling_far1),
        300_000_000,
        "far",
    )
    rest_sums = call(
        rest_kernel,
        [shape(rows, pupil_cols)] * (pairs - len(steps)),
        (others, phase, rest1, sibling_rest1),
        0,
        "rest",
        brief=True,
    )
    received = dict(zip(send_order(pairs), [*rest_sums, *far_sums]))
    for k in range(1, pairs):
        received[k] = lax.ppermute(received[k], "layer", [(i, i ^ (2 * k)) for i in range(n_layer)])
    received = [received[k] for k in range(pairs)]

    optics_in, received[-1] = lax.optimization_barrier((optics_in, received[-1]))
    optics = call(
        optics_kernel,
        (
            shape(rows, pupil_cols, dtype=f32),
            shape(*optics_in[2].shape),
            shape(*optics_in[3].shape),
        ),
        optics_in,
        0,
        "optics",
        brief=True,
    )
    received[1], optics = lax.optimization_barrier((received[1], optics))
    shifted = call(
        shift_kernel,
        shape(layers, rows_dev, cols_dev),
        (wind, own, near0, near1, diagonal0, diagonal1, taken, strips, *[received[k] for k in steps]),
        0,
        "shift",
        scratch=wind_scratch,
        brief=True,
    )
    spots_shape = shape(2 * rows, 2 * pupil_cols, dtype=f32)
    spots, new_screens = call(
        functools.partial(imaging_kernel, pairs),
        [spots_shape, shape(layers, rows_dev, cols_dev)],
        (*received, *optics, shifted),
        400_000_000,
        "imaging",
        out_hbm=(0, 1),
        scratch=[pltpu.VMEM(spots_shape.shape, f32), sem((3,))],
    )
    return (new_screens, spots[None])


def solution(mesh):
    return jax.shard_map(
        per_device,
        mesh=mesh,
        in_specs=(P(None, "dir", "layer"), P("layer", None), P(), P(), P()),
        out_specs=(P(None, "dir", "layer"), P("dir", "layer", None)),
        check_vma=False,
    )
```

```python
import functools

import jax
import jax.numpy as jnp
import numpy as np
from jax import lax
from jax.experimental import pallas as pl
from jax.experimental.pallas import tpu as pltpu
from jax.sharding import PartitionSpec as P

SUB_PIX = 16
SPOT_PIX = 32
WIND_MAX = 8
LANES = 128
STRIP = 32

HBM_SPEC = pl.BlockSpec(memory_space=pltpu.HBM)
VMEM_SPEC = pl.BlockSpec(memory_space=pltpu.VMEM)


def params(*arrays):
    held = sum(array.size * array.dtype.itemsize for array in jax.tree.leaves(arrays))
    return pltpu.CompilerParams(vmem_limit_bytes=held + 8 * 1024 * 1024)


def call(kernel, out_shape, operands, flops, name, in_hbm=(), out_hbm=(), scratch=(), brief=False):
    def spec(k, array):
        return HBM_SPEC if k in in_hbm else VMEM_SPEC

    if out_hbm:
        out_specs = [HBM_SPEC if k in out_hbm else VMEM_SPEC for k in range(len(out_shape))]
    else:
        out_specs = jax.tree.map(lambda _: VMEM_SPEC, out_shape)
    size = sum(array.size * array.dtype.itemsize for array in jax.tree.leaves((operands, out_shape)))
    if brief:
        flops = size = 0
    in_specs = [spec(k, array) for k, array in enumerate(operands)]
    operands = [
        pltpu.with_memory_space_constraint(array, pltpu.HBM) if space is HBM_SPEC else array
        for array, space in zip(operands, in_specs)
    ]
    return pl.pallas_call(
        kernel,
        out_shape=out_shape,
        in_specs=in_specs,
        out_specs=out_specs,
        scratch_shapes=list(scratch),
        compiler_params=params(operands, out_shape),
        cost_estimate=pl.CostEstimate(flops=flops, bytes_accessed=size, transcendentals=0),
        name=name,
    )(*operands)


def fetch(*pairs):
    copies = [pltpu.make_async_copy(source, target, sem) for source, target, sem in pairs]
    for copy in copies:
        copy.start()
    return copies


def wrap(value, length):
    value = jnp.where(value < 0, value + length, value)
    return jnp.where(value >= length, value - length, value)


def stack(*blocks):
    return jnp.concatenate(blocks, axis=0)


def beside(*blocks):
    return jnp.concatenate(blocks, axis=1)


def dot(left, right):
    return jnp.dot(left, right, preferred_element_type=jnp.float32)


def spans(pixel, anchor, num, den, length):
    stretched = (pixel * num).astype(jnp.float32)
    den = (jnp.zeros_like(pixel) + den).astype(jnp.float32)
    whole = jnp.floor((stretched + 0.5) / den)
    fraction = (stretched - whole * den) / den
    base = wrap(anchor + whole.astype(jnp.int32), length)
    upper = wrap(base + 1, length)
    return base, upper, 1.0 - fraction, fraction


def chunk_start(half, chunk):
    return 3 * half + chunk * (1 - 2 * half)


def split_kernel(screens, *refs):
    ints, outs, held, sems = refs[:3], refs[3:7], refs[7:10], refs[-1]
    width = outs[0].shape[2]
    core = lax.rem(lax.axis_index("dir"), 2)
    pairs = []
    for k, out in enumerate(outs):
        half = core if k < 2 else 1 - core
        start = pl.multiple_of(chunk_start(half, k % 2) * width, LANES)
        pairs.append((screens.at[:, :, pl.ds(start, width)], out, sems.at[k]))
    pairs += [(source, copy, sems.at[4 + k]) for k, (source, copy) in enumerate(zip(ints, held))]
    for load in fetch(*pairs):
        load.wait()


def weights_kernel(geometry, wind_held, offsets_held, ratio_held, *refs):
    n_layer, rows_dev, screen_cols = geometry
    sources, (rows_out, cols_out, *tables), refs = refs[:5], refs[5:11], refs[11:]
    copies, (wind, offsets, ratio, sems) = refs[:5], refs[5:]
    pupil_cols = cols_out.shape[2]
    loads = fetch(
        (wind_held, wind, sems.at[0]),
        (offsets_held, offsets, sems.at[1]),
        (ratio_held, ratio, sems.at[2]),
    )
    pairs = [*zip(sources, copies)]
    others = fetch(*[(source, copy, sems.at[3 + k]) for k, (source, copy) in enumerate(pairs)])
    _, layers, pupil_rows, screen_rows = rows_out.shape
    half = pupil_rows // 2
    direction = lax.axis_index("dir")
    column = lax.axis_index("layer")
    block = pupil_rows // n_layer
    row = lax.broadcasted_iota(jnp.int32, (half, LANES), 0)
    step = row // block
    for at, value in enumerate(send_order(n_layer // 2)):
        step = jnp.where(row // block == at, value, step)
    pair = jnp.bitwise_xor(step, column // 2)
    parity = lax.rem(column, 2)
    inside = lax.rem(row, block) + pair * (2 * block)
    pixel_rows = stack(inside + parity * block, inside + (1 - parity) * block)
    lane = lax.broadcasted_iota(jnp.int32, (pupil_rows, LANES), 1)
    for load in loads:
        load.wait()
    for side in range(2):
        target = jnp.bitwise_xor(direction, side)
        for level in range(layers):
            anchor = wrap(offsets[level, 0, target] - wind[0, level], screen_rows)
            num, den = ratio[level, 0, target], ratio[level, 1, target]
            base, upper, low, high = spans(pixel_rows, anchor, num, den, screen_rows)
            for peer in range(4):
                for part in range(rows_dev // LANES):
                    index = lane + (jnp.bitwise_xor(direction, peer) * rows_dev + part * LANES)
                    weight = jnp.where(index == base, low, 0.0)
                    weight = jnp.where(index == upper, high, weight)
                    start = peer * rows_dev + part * LANES
                    rows_out[side, level, :, start : start + LANES] = weight.astype(jnp.bfloat16)
    sub = lax.broadcasted_iota(jnp.int32, (8, LANES), 0)
    anchor, num, den = jnp.zeros_like(sub), jnp.zeros_like(sub), jnp.ones_like(sub)
    for level in range(layers):
        start = wrap(offsets[level, 1, direction] - wind[1, level], screen_cols)
        anchor = jnp.where(sub == level, start, anchor)
        num = jnp.where(sub == level, ratio[level, 0, direction], num)
        den = jnp.where(sub == level, ratio[level, 1, direction], den)
    for at in range(0, pupil_cols, LANES):
        pixel = lax.broadcasted_iota(jnp.int32, (8, LANES), 1) + at
        values = spans(pixel, anchor, num, den, screen_cols)
        for table, value in zip(tables, values):
            table[:, at : at + LANES] = value
    column_weights(*tables, column * cols_out.shape[1], cols_out)
    for load in others:
        load.wait()


def column_weights(base_ref, upper_ref, low_ref, high_ref, first, out):
    layers, cols_dev, pupil_cols = out.shape
    width = cols_dev // 4
    core = lax.rem(lax.axis_index("dir"), 2)
    sub = lax.broadcasted_iota(jnp.int32, (width, LANES), 0).astype(jnp.float32).astype(jnp.bfloat16)
    zero = jnp.zeros((width, LANES), jnp.bfloat16)
    for level in range(layers):

        def tile(step, carry):
            start = pl.multiple_of(step * LANES, LANES)
            cut = (slice(level, level + 1), pl.ds(start, LANES))
            base, upper = base_ref[cut], upper_ref[cut]
            low, high = [
                jnp.broadcast_to(ref[cut].astype(jnp.bfloat16), (width, LANES)) for ref in (low_ref, high_ref)
            ]
            for k in range(4):
                shift = first + chunk_start(jnp.bitwise_xor(core, k // 2), k % 2) * width
                base_at, upper_at = [
                    jnp.broadcast_to(
                        jnp.clip(value - shift, -1, width).astype(jnp.float32).astype(jnp.bfloat16), (width, LANES)
                    )
                    for value in (base, upper)
                ]
                weight = jnp.where(sub == base_at, low, zero)
                weight = jnp.where(sub == upper_at, high, weight)
                out[level, k * width : (k + 1) * width, pl.ds(start, LANES)] = weight
            return carry

        lax.fori_loop(0, pupil_cols // LANES, tile, 0)


def strips_kernel(wind_held, *refs):
    tables, (across, diagonal, near, keep, cols_out, strip, sibling_strip, wind, sem) = refs[:4], refs[4:]
    load = fetch((wind_held, wind, sem))[0]
    column_weights(*tables, jnp.bitwise_xor(lax.axis_index("layer"), 1) * cols_out.shape[1], cols_out)
    layers, rows, _ = keep.shape
    core = lax.rem(lax.axis_index("dir"), 2)
    odd = core == 1
    lane = lax.broadcasted_iota(jnp.int32, (rows + 32, LANES), 1)

    def wide(own, near, far, odd, level):
        own, near, far = [block[level].astype(jnp.float32) for block in (own, near, far)]
        before = jnp.where(odd, near[rows - 16 :], far[rows - 16 :])
        return stack(before, own, jnp.where(odd, far[:16], near[:16]))

    packed = jnp.zeros((rows + 32, LANES), jnp.float32)
    for level in range(layers):
        blocks = (keep, near, diagonal, odd), (near, keep, across, core == 0)
        for at, block in zip((WIND_MAX * level, STRIP + WIND_MAX * level), blocks):
            block = pltpu.roll(wide(*block, level), at + WIND_MAX * core, 1)
            packed = jnp.where((lane >= at) & (lane < at + WIND_MAX), block, packed)
    load.wait()
    strips = jnp.zeros((rows, LANES), jnp.float32)
    for level in range(layers):
        shift = wind[0, level]
        shift = jnp.where(shift < 0, shift + rows + 32, shift)
        moved = pltpu.roll(packed, shift, 0)[16 : 16 + rows]
        mine = lax.rem(lane[:rows], STRIP)
        strips = jnp.where((mine >= WIND_MAX * level) & (mine < WIND_MAX * (level + 1)), moved, strips)
    strips = strips.T.astype(jnp.bfloat16)
    strip[...] = strips[:STRIP]
    sibling_strip[...] = strips[STRIP : 2 * STRIP]


def project_rows(rows_ref, keep, near, across, diagonal, level):
    screen = stack(keep[level], near[level], across[level], diagonal[level])
    rows = stack(rows_ref[0, level], rows_ref[1, level])
    return dot(rows, screen).astype(jnp.bfloat16)


def first_rows_kernel(rows_ref, across, diagonal, near, keep, mine, sibling, other, sibling_other):
    layers, half, _ = mine.shape
    for level in range(layers):
        part = project_rows(rows_ref, keep, near, across, diagonal, level)
        for k, out in enumerate((mine, other, sibling, sibling_other)):
            out[level] = part[k * half : (k + 1) * half]


def put_strip(out, at, strip):
    for k in range(strip.shape[1] // LANES):
        out[at + k * STRIP : at + (k + 1) * STRIP, :] = strip[:, k * LANES : (k + 1) * LANES]


def get_strip(ref, at):
    return beside(*[ref[start : start + STRIP, :] for start in range(at, ref.shape[0], STRIP)])


def later_rows_kernel(rows_ref, *refs):
    chunks, refs = refs[:8], refs[8:]
    sibling0, strip, sibling_strip, mine, give, far, sibling_far, rest, sibling_rest = refs
    across, diagonal, near, keep, across0, diagonal0, near0, keep0 = chunks
    layers, half, width = mine.shape
    rows = near.shape[1]
    size = (far.shape[0] - STRIP * rows // LANES) // layers
    start = half - size
    for level in range(layers):
        part = project_rows(rows_ref, keep, near, across, diagonal, level)
        mine[level] = part[:half]
        for k, out, remainder in ((1, far, rest), (3, sibling_far, sibling_rest)):
            piece = part[k * half : (k + 1) * half]
            out[level * size : (level + 1) * size] = piece[start:]
            remainder[level * start : (level + 1) * start] = piece[:start]
        give[level, :half, :width] = sibling0[level]
        give[level, :half, width:] = part[2 * half : 3 * half]
        for k, blocks in enumerate(((across0, keep0), (across, keep))):
            cut = slice(k * width, (k + 1) * width)
            edges = [block[level, at : at + 16] for block in blocks for at in (0, rows - 16)]
            give[level, half:, cut] = stack(*edges)
    put_strip(far, layers * size, strip)
    put_strip(sibling_far, layers * size, sibling_strip)


def project(parts, cols_refs, at):
    cols = stack(*[ref[level, start:stop, at : at + 256] for ref, level, start, stop in cols_refs])
    return dot(beside(*parts), cols)


def phase_kernel(mine_ref, other_ref, mine0, mine1, came, sibling_came, phase):
    layers, _, width = mine0.shape
    parts, cuts = [], []
    for level in range(layers):
        parts += [mine0[level], mine1[level], came[level], sibling_came[level]]
        cuts += [(mine_ref, level, 0, 2 * width)]
        cuts += [(other_ref, level, 0, width), (other_ref, level, 2 * width, 3 * width)]
    for at in range(0, phase.shape[1], 256):
        phase[:, at : at + 256] = project(parts, cuts, at)


def taken_kernel(mine_ref, phase, taken, out):
    half, pupil_cols = phase.shape
    layers, cols_dev, _ = mine_ref.shape
    parts = [taken[level, :half] for level in range(layers)]
    cuts = [(mine_ref, level, cols_dev // 2, cols_dev) for level in range(layers)]
    for at in range(0, pupil_cols, 256):
        out[:, at : at + 256] = phase[:, at : at + 256] + project(parts, cuts, at)


def sum_up(start, cols_ref, phase, came, sibling_came, outs):
    layers, cols_dev, _ = cols_ref.shape
    width = cols_dev // 4
    block = outs[0].shape[0]
    size = block * len(outs)
    rows = slice(start, start + size)
    parts, cuts = [], []
    for level in range(layers):
        cut = slice(level * size, (level + 1) * size)
        parts += [came[cut], sibling_came[cut]]
        cuts += [(cols_ref, level, width, 2 * width), (cols_ref, level, 3 * width, 4 * width)]
    pupil_cols = phase.shape[1]
    for at in range(0, pupil_cols, 256):
        total = (phase[rows, at : at + 256] + project(parts, cuts, at)).astype(jnp.bfloat16)
        for k, out in enumerate(outs):
            out[:, at : at + 256] = total[k * block : (k + 1) * block]


def strip_steps(pairs):
    return [2**k - 1 for k in range(1, pairs.bit_length())]


def send_order(pairs):
    steps = strip_steps(pairs)
    return [k for k in range(pairs) if k not in steps] + steps


def add_strip(pairs, step, strips, out):
    pair = lax.axis_index("layer") // 2
    after = lax.rem(pair + 1, pairs) == jnp.bitwise_xor(pair, step)
    at = out.shape[1] - strips.shape[1]
    last, first = strips[:STRIP].astype(jnp.float32), strips[STRIP:].astype(jnp.float32)
    out[:, at:] = jnp.where(after, last, first).astype(jnp.bfloat16)


def far_kernel(cols_ref, phase, came, sibling_came, *outs):
    *outs, strips = outs
    half = phase.shape[0]
    size = outs[0].shape[0] * len(outs)
    sum_up(half - size, cols_ref, phase, came, sibling_came, outs)
    layers = cols_ref.shape[0]
    odd = lax.rem(lax.axis_index("dir"), 2) == 1
    here = get_strip(came, layers * size).astype(jnp.float32)
    there = get_strip(sibling_came, layers * size).astype(jnp.float32)
    strips[:STRIP] = jnp.where(odd, here, there).astype(jnp.bfloat16)
    strips[STRIP:] = jnp.where(odd, there, here).astype(jnp.bfloat16)
    pairs = half // outs[0].shape[0]
    add_strip(pairs, strip_steps(pairs)[-1], strips, outs[0])


def rest_kernel(cols_ref, phase, came, sibling_came, strips, *outs):
    sum_up(0, cols_ref, phase, came, sibling_came, outs)
    pairs = len(outs) + 1
    for out, step in zip(outs, send_order(pairs)):
        if step in strip_steps(pairs):
            add_strip(pairs, step, strips, out)


def shifted_rows(shift, odd, own, near, far):
    own, near, far = [block.astype(jnp.float32) for block in (own, near, far)]
    rows = own.shape[0]
    before = jnp.where(odd, near[16:], far[16:])
    after = jnp.where(odd, far[:16], near[:16])
    shift = jnp.where(shift < 0, shift + rows + 32, shift)
    return pltpu.roll(stack(before, own, after), shift, 0)[16 : 16 + rows]


def shift_kernel(wind_held, own, near0, near1, diagonal0, diagonal1, taken, partner_strips, *refs):
    messages, (out, wind, sem) = refs[:-3], refs[-3:]
    load = fetch((wind_held, wind, sem))[0]
    layers, rows, cols = own.shape
    odd = lax.rem(lax.axis_index("dir"), 2) == 1
    half = taken.shape[1] - 64
    pairs = 2 ** len(messages)
    pair, second = lax.axis_index("layer") // 2, lax.rem(lax.axis_index("layer"), 2) == 1
    before = jnp.bitwise_xor(pair, lax.rem(pair + pairs - 1, pairs))
    after = jnp.bitwise_xor(pair, lax.rem(pair + 1, pairs))
    left = partner_strips[:STRIP].astype(jnp.float32)
    right = partner_strips[STRIP:].astype(jnp.float32)
    for step, message in zip(strip_steps(pairs), messages):
        strip = message[:, message.shape[1] - rows :].astype(jnp.float32)
        left = jnp.where(jnp.logical_and(before == step, jnp.logical_not(second)), strip, left)
        right = jnp.where(jnp.logical_and(after == step, second), strip, right)
    strips = stack(left, right, jnp.zeros((LANES - 2 * STRIP, rows), jnp.float32)).T
    lane = lax.broadcasted_iota(jnp.int32, (rows, LANES), 1)
    load.wait()
    for level in range(layers):
        last = pltpu.roll(strips, LANES - WIND_MAX * (level + 1), 1)
        first = pltpu.roll(strips, LANES - STRIP - WIND_MAX * level, 1)
        extra = jnp.where(lane < WIND_MAX, first, last)
        pair = []
        for at, parts in ((half, (diagonal0, diagonal1)), (half + 32, (near0, near1))):
            here = [stack(part[level, :16], part[level, rows - 16 :]).astype(jnp.float32) for part in parts]
            there = taken[level, at : at + 32].astype(jnp.float32)
            width = there.shape[1] // 2
            quarters = [*here, there[:, width:], there[:, :width]]
            pair.append(beside(*[jnp.where(odd, quarters[3 - k], quarters[k]) for k in range(4)]))
        far, near = pair
        moved = shifted_rows(wind[0, level], odd, own[level], near, far)
        shift = wind[1, level]
        shift = jnp.where(shift < 0, shift + cols + LANES, shift)
        out[level] = pltpu.roll(beside(moved, extra), shift, 1)[:, :cols].astype(jnp.bfloat16)


def optics_kernel(amplitude, ones, columns, lines, amp_out, columns_out, lines_out):
    rows, pupil_cols = amplitude.shape
    for step in range(pupil_cols // LANES):
        cut = slice(step * LANES, (step + 1) * LANES)
        amp = amplitude[:, cut]
        energy = (amp * amp).reshape(rows // SUB_PIX, SUB_PIX, LANES).sum(axis=1)
        energy = jnp.broadcast_to(energy[:, None], (rows // SUB_PIX, SUB_PIX, LANES)).reshape(rows, LANES)
        total = jnp.dot(energy, ones[...], precision=lax.Precision.HIGHEST, preferred_element_type=jnp.float32)
        amp_out[:, cut] = amp * lax.rsqrt(total)
    columns_out[...] = columns[...].astype(jnp.bfloat16)
    lines_out[...] = lines[...].astype(jnp.bfloat16)


def sin_cos(phase):
    turns = jnp.floor(phase * (1.0 / np.pi) + 0.5)
    rest = phase - turns * 3.140625
    rest = rest - turns * 9.67653589793e-4
    odd = turns - 2.0 * jnp.floor(turns * 0.5)
    sign = 1.0 - 2.0 * odd
    square = rest * rest
    sine = -1.0 / 39916800.0
    for term in (1.0 / 362880.0, -1.0 / 5040.0, 1.0 / 120.0, -1.0 / 6.0, 1.0):
        sine = sine * square + term
    cosine = 1.0 / 479001600.0
    for term in (-1.0 / 3628800.0, 1.0 / 40320.0, -1.0 / 720.0, 1.0 / 24.0, -0.5, 1.0):
        cosine = cosine * square + term
    return sine * rest * sign, cosine * sign


def imaging_kernel(count, *refs):
    parts, (amp_ref, columns, lines, shifted, spots, screens, out, sems) = refs[:count], refs[count:]
    copies = fetch((shifted, screens, sems.at[0]))
    rows, cols = amp_ref.shape
    tiles = cols // LANES
    phase = parts[0][:, :cols].astype(jnp.float32)
    for part in parts[1:]:
        phase = phase + part[:, :cols].astype(jnp.float32)
    sine, cosine = sin_cos(phase)
    amp = amp_ref[...]
    real, imag = (amp * cosine).astype(jnp.bfloat16), (amp * sine).astype(jnp.bfloat16)
    cuts = [slice(t * LANES, (t + 1) * LANES) for t in range(tiles)]
    field = stack(*[beside(real[:, cut], imag[:, cut]) for cut in cuts])
    half = dot(field, columns[...]).astype(jnp.bfloat16)
    wide = 2 * LANES
    out_rows = 2 * rows
    for t in range(tiles):
        mine = half[t * rows : (t + 1) * rows]
        full = dot(lines[...], stack(mine[:, :wide], mine[:, wide:]))
        real, imag = full[:out_rows], full[out_rows:]
        out[:, t * wide : (t + 1) * wide] = real * real + imag * imag
        if t % 2:
            cut = slice((t - 1) * wide, (t + 1) * wide)
            copies += fetch((out.at[:, cut], spots.at[:, cut], sems.at[1 + t // 2]))
    for copy in copies:
        copy.wait()


def tables_of(rows):
    freq = np.arange(SPOT_PIX)[:, None] - SPOT_PIX // 2
    angle = ((freq * np.arange(SUB_PIX)[None, :]) % SPOT_PIX) * (2.0 * np.pi / SPOT_PIX)
    cos, sin = np.cos(angle), np.sin(angle)

    def blocks(table, count):
        return np.kron(np.eye(count), table)

    per_tile = LANES // SUB_PIX
    col_cos, col_sin = blocks(cos.T, per_tile), blocks(sin.T, per_tile)
    columns = np.block([[col_cos, -col_sin], [col_sin, col_cos]])
    count = rows // SUB_PIX
    row_cos, row_sin = blocks(cos, count), blocks(sin, count)
    lines = np.block([[row_cos, row_sin], [-row_sin, row_cos]])

    return columns.astype(np.float32), lines.astype(np.float32)


def per_device(screens, amplitude, wind, offsets, ratio):
    layers, rows_dev, cols_dev = screens.shape
    n_layer = lax.axis_size("layer")
    n_dir = lax.axis_size("dir")
    rows, pupil_cols = amplitude.shape
    pairs = n_layer // 2
    half = pairs * rows
    pupil_rows = 2 * half
    assert n_dir == 4 and rows == STRIP and pairs > 2
    bf16, f32 = jnp.bfloat16, jnp.float32
    wind = jnp.transpose(wind, (1, 0))
    offsets = jnp.transpose(offsets, (1, 2, 0))
    ratio = jnp.transpose(ratio, (1, 2, 0))
    smem, sem = pltpu.SMEM, pltpu.SemaphoreType.DMA
    wind_scratch = [smem(wind.shape, jnp.int32), sem]

    def shape(*dims, dtype=bf16):
        return jax.ShapeDtypeStruct(dims, dtype)

    def swap(value, bits):
        return lax.ppermute(value, "dir", [(i, i ^ bits) for i in range(n_dir)])

    def partner(value, bits=0):
        count = n_layer * n_dir
        return lax.ppermute(value, ("layer", "dir"), [(i, i ^ n_dir ^ bits) for i in range(count)])

    def turn(value, step):
        return lax.ppermute(value, "layer", [(i, (i + step) % n_layer) for i in range(n_layer)])

    width = cols_dev // 4
    chunk = shape(layers, rows_dev, width)
    ints = (wind, offsets, ratio)
    keep0, keep1, give0, give1, *ints = call(
        split_kernel,
        [chunk] * 4 + [shape(*array.shape, dtype=jnp.int32) for array in ints],
        (screens, *ints),
        0,
        "split",
        in_hbm=range(4),
        scratch=[sem((7,))],
        brief=True,
    )
    across0 = swap(keep0, 2)
    diagonal0 = swap(give0, 3)
    near0 = swap(give0, 1)
    across1 = swap(keep1, 2)
    diagonal1 = swap(give1, 3)
    ones = np.kron(np.eye(LANES // SUB_PIX), np.ones((SUB_PIX, SUB_PIX))).astype(np.float32)
    optics_in = (amplitude, jnp.asarray(ones), *[jnp.asarray(table) for table in tables_of(rows)])
    copies = [shape(*array.shape, dtype=array.dtype) for array in (screens, *optics_in)]
    row_weights, cols, *loaded = call(
        functools.partial(weights_kernel, (n_layer, rows_dev, cols_dev * n_layer)),
        [shape(2, layers, pupil_rows, 4 * rows_dev), shape(layers, cols_dev, pupil_cols)]
        + [shape(8, pupil_cols, dtype=dtype) for dtype in (jnp.int32, jnp.int32, f32, f32)]
        + copies,
        (*ints, screens, *optics_in),
        0,
        "weights",
        in_hbm=range(3, 8),
        scratch=[smem(array.shape, jnp.int32) for array in (wind, offsets, ratio)]
        + [sem((8,))],
        brief=True,
    )
    tables, (own, *optics_in) = loaded[:4], loaded[4:]
    wind = ints[0]
    give1, own = lax.optimization_barrier((give1, own))
    near1 = swap(give1, 1)
    across0, diagonal0, row_weights, cols = lax.optimization_barrier((across0, diagonal0, row_weights, cols))

    projected = shape(layers, half, width)
    mine0, sibling0, other0, sibling_other0 = call(
        first_rows_kernel,
        [projected] * 4,
        (row_weights, across0, diagonal0, near0, keep0),
        0,
        "rows_first",
        brief=True,
    )
    came0 = partner(other0)
    sibling_came0 = partner(sibling_other0, 1)

    wind, mine0 = lax.optimization_barrier((wind, mine0))
    others, strip, sibling_strip = call(
        strips_kernel,
        [shape(layers, cols_dev, pupil_cols)] + [shape(STRIP, rows_dev)] * 2,
        (wind, *tables, across0, diagonal0, near0, keep0),
        0,
        "strips",
        scratch=wind_scratch,
        brief=True,
    )
    steps = strip_steps(pairs)
    far = rows
    message = shape(layers * far + STRIP * rows_dev // LANES, width)
    remainder = shape(layers * (half - far), width)
    mine1, give, far1, sibling_far1, rest1, sibling_rest1 = call(
        later_rows_kernel,
        [projected, shape(layers, half + 64, 2 * width), message, message, remainder, remainder],
        (row_weights, across1, diagonal1, near1, keep1, across0, diagonal0, near0, keep0, sibling0, strip, sibling_strip),
        0,
        "rows_later",
        brief=True,
    )
    far1, sibling_far1 = partner(far1), partner(sibling_far1, 1)
    rest1, sibling_rest1 = partner(rest1), partner(sibling_rest1, 1)
    taken = swap(give, 1)
    phase = call(
        phase_kernel,
        shape(half, pupil_cols, dtype=f32),
        (cols, others, mine0, mine1, came0, sibling_came0),
        10_000_000_000,
        "phase",
    )

    phase = call(
        taken_kernel,
        shape(half, pupil_cols, dtype=f32),
        (cols, phase, taken),
        0,
        "taken",
        brief=True,
    )
    *far_sums, strips = call(
        far_kernel,
        [shape(rows, pupil_cols + rows_dev), shape(2 * STRIP, rows_dev)],
        (others, phase, far1, sibling_far1),
        300_000_000,
        "far",
    )
    rest_sums = call(
        rest_kernel,
        [shape(rows, pupil_cols + (rows_dev if k in steps else 0)) for k in send_order(pairs)[:-1]],
        (others, phase, rest1, sibling_rest1, strips),
        0,
        "rest",
        brief=True,
    )
    received = dict(zip(send_order(pairs), [*rest_sums, *far_sums]))
    for k in range(1, pairs):
        received[k] = lax.ppermute(received[k], "layer", [(i, i ^ (2 * k)) for i in range(n_layer)])
    received = [received[k] for k in range(pairs)]

    optics_in, received[-1] = lax.optimization_barrier((optics_in, received[-1]))
    optics = call(
        optics_kernel,
        (
            shape(rows, pupil_cols, dtype=f32),
            shape(*optics_in[2].shape),
            shape(*optics_in[3].shape),
        ),
        optics_in,
        0,
        "optics",
        brief=True,
    )
    received[1], optics = lax.optimization_barrier((received[1], optics))
    shifted = call(
        shift_kernel,
        shape(layers, rows_dev, cols_dev),
        (wind, own, near0, near1, diagonal0, diagonal1, taken, strips, *[received[k] for k in steps]),
        0,
        "shift",
        scratch=wind_scratch,
        brief=True,
    )
    spots_shape = shape(2 * rows, 2 * pupil_cols, dtype=f32)
    spots, new_screens = call(
        functools.partial(imaging_kernel, pairs),
        [spots_shape, shape(layers, rows_dev, cols_dev)],
        (*received, *optics, shifted),
        400_000_000,
        "imaging",
        out_hbm=(0, 1),
        scratch=[pltpu.VMEM(spots_shape.shape, f32), sem((1 + pupil_cols // (2 * LANES),))],
    )
    return (new_screens, spots[None])


def solution(mesh):
    return jax.shard_map(
        per_device,
        mesh=mesh,
        in_specs=(P(None, "dir", "layer"), P("layer", None), P(), P(), P()),
        out_specs=(P(None, "dir", "layer"), P("dir", "layer", None)),
        check_vma=False,
    )
```

```python
import functools

import jax
import jax.numpy as jnp
import numpy as np
from jax import lax
from jax.experimental import pallas as pl
from jax.experimental.pallas import tpu as pltpu
from jax.sharding import PartitionSpec as P

SUB_PIX = 16
SPOT_PIX = 32
WIND_MAX = 8
LANES = 128
STRIP = 32

HBM_SPEC = pl.BlockSpec(memory_space=pltpu.HBM)
VMEM_SPEC = pl.BlockSpec(memory_space=pltpu.VMEM)


def params(*arrays):
    held = sum(array.size * array.dtype.itemsize for array in jax.tree.leaves(arrays))
    return pltpu.CompilerParams(vmem_limit_bytes=held + 8 * 1024 * 1024)


def call(kernel, out_shape, operands, flops, name, in_hbm=(), out_hbm=(), scratch=(), brief=False):
    def spec(k, array):
        return HBM_SPEC if k in in_hbm else VMEM_SPEC

    if out_hbm:
        out_specs = [HBM_SPEC if k in out_hbm else VMEM_SPEC for k in range(len(out_shape))]
    else:
        out_specs = jax.tree.map(lambda _: VMEM_SPEC, out_shape)
    size = sum(array.size * array.dtype.itemsize for array in jax.tree.leaves((operands, out_shape)))
    if brief:
        flops = size = 0
    in_specs = [spec(k, array) for k, array in enumerate(operands)]
    operands = [
        pltpu.with_memory_space_constraint(array, pltpu.HBM) if space is HBM_SPEC else array
        for array, space in zip(operands, in_specs)
    ]
    return pl.pallas_call(
        kernel,
        out_shape=out_shape,
        in_specs=in_specs,
        out_specs=out_specs,
        scratch_shapes=list(scratch),
        compiler_params=params(operands, out_shape),
        cost_estimate=pl.CostEstimate(flops=flops, bytes_accessed=size, transcendentals=0),
        name=name,
    )(*operands)


def fetch(*pairs):
    copies = [pltpu.make_async_copy(source, target, sem) for source, target, sem in pairs]
    for copy in copies:
        copy.start()
    return copies


def wrap(value, length):
    value = jnp.where(value < 0, value + length, value)
    return jnp.where(value >= length, value - length, value)


def stack(*blocks):
    return jnp.concatenate(blocks, axis=0)


def beside(*blocks):
    return jnp.concatenate(blocks, axis=1)


def dot(left, right):
    return jnp.dot(left, right, preferred_element_type=jnp.float32)


def spans(pixel, anchor, num, den, length):
    stretched = (pixel * num).astype(jnp.float32)
    den = (jnp.zeros_like(pixel) + den).astype(jnp.float32)
    whole = jnp.floor((stretched + 0.5) / den)
    fraction = (stretched - whole * den) / den
    base = wrap(anchor + whole.astype(jnp.int32), length)
    upper = wrap(base + 1, length)
    return base, upper, 1.0 - fraction, fraction


def chunk_start(half, chunk):
    return 3 * half + chunk * (1 - 2 * half)


def split_kernel(screens, *refs):
    ints, outs, held, sems = refs[:3], refs[3:7], refs[7:10], refs[-1]
    width = outs[0].shape[2]
    core = lax.rem(lax.axis_index("dir"), 2)
    pairs = []
    for k, out in enumerate(outs):
        half = core if k < 2 else 1 - core
        start = pl.multiple_of(chunk_start(half, k % 2) * width, LANES)
        pairs.append((screens.at[:, :, pl.ds(start, width)], out, sems.at[k]))
    pairs += [(source, copy, sems.at[4 + k]) for k, (source, copy) in enumerate(zip(ints, held))]
    for load in fetch(*pairs):
        load.wait()


def weights_kernel(geometry, wind_held, offsets_held, ratio_held, *refs):
    n_layer, rows_dev, screen_cols = geometry
    sources, (rows_out, cols_out, *tables), refs = refs[:5], refs[5:11], refs[11:]
    copies, (wind, offsets, ratio, sems) = refs[:5], refs[5:]
    pupil_cols = cols_out.shape[2]
    loads = fetch(
        (wind_held, wind, sems.at[0]),
        (offsets_held, offsets, sems.at[1]),
        (ratio_held, ratio, sems.at[2]),
    )
    pairs = [*zip(sources, copies)]
    others = fetch(*[(source, copy, sems.at[3 + k]) for k, (source, copy) in enumerate(pairs)])
    _, layers, pupil_rows, screen_rows = rows_out.shape
    half = pupil_rows // 2
    direction = lax.axis_index("dir")
    column = lax.axis_index("layer")
    block = pupil_rows // n_layer
    row = lax.broadcasted_iota(jnp.int32, (half, LANES), 0)
    step = row // block
    for at, value in enumerate(send_order(n_layer // 2)):
        step = jnp.where(row // block == at, value, step)
    pair = jnp.bitwise_xor(step, column // 2)
    parity = lax.rem(column, 2)
    inside = lax.rem(row, block) + pair * (2 * block)
    pixel_rows = stack(inside + parity * block, inside + (1 - parity) * block)
    lane = lax.broadcasted_iota(jnp.int32, (pupil_rows, LANES), 1)
    for load in loads:
        load.wait()
    for side in range(2):
        target = jnp.bitwise_xor(direction, side)
        for level in range(layers):
            anchor = wrap(offsets[level, 0, target] - wind[0, level], screen_rows)
            num, den = ratio[level, 0, target], ratio[level, 1, target]
            base, upper, low, high = spans(pixel_rows, anchor, num, den, screen_rows)
            for peer in range(4):
                for part in range(rows_dev // LANES):
                    index = lane + (jnp.bitwise_xor(direction, peer) * rows_dev + part * LANES)
                    weight = jnp.where(index == base, low, 0.0)
                    weight = jnp.where(index == upper, high, weight)
                    start = peer * rows_dev + part * LANES
                    rows_out[side, level, :, start : start + LANES] = weight.astype(jnp.bfloat16)
    sub = lax.broadcasted_iota(jnp.int32, (8, LANES), 0)
    anchor, num, den = jnp.zeros_like(sub), jnp.zeros_like(sub), jnp.ones_like(sub)
    for level in range(layers):
        start = wrap(offsets[level, 1, direction] - wind[1, level], screen_cols)
        anchor = jnp.where(sub == level, start, anchor)
        num = jnp.where(sub == level, ratio[level, 0, direction], num)
        den = jnp.where(sub == level, ratio[level, 1, direction], den)
    for at in range(0, pupil_cols, LANES):
        pixel = lax.broadcasted_iota(jnp.int32, (8, LANES), 1) + at
        values = spans(pixel, anchor, num, den, screen_cols)
        for table, value in zip(tables, values):
            table[:, at : at + LANES] = value
    column_weights(*tables, column * cols_out.shape[1], cols_out)
    for load in others:
        load.wait()


def column_weights(base_ref, upper_ref, low_ref, high_ref, first, out):
    layers, cols_dev, pupil_cols = out.shape
    width = cols_dev // 4
    core = lax.rem(lax.axis_index("dir"), 2)
    sub = lax.broadcasted_iota(jnp.int32, (width, LANES), 0).astype(jnp.float32).astype(jnp.bfloat16)
    zero = jnp.zeros((width, LANES), jnp.bfloat16)
    for level in range(layers):

        def tile(step, carry):
            start = pl.multiple_of(step * LANES, LANES)
            cut = (slice(level, level + 1), pl.ds(start, LANES))
            base, upper = base_ref[cut], upper_ref[cut]
            low, high = [
                jnp.broadcast_to(ref[cut].astype(jnp.bfloat16), (width, LANES)) for ref in (low_ref, high_ref)
            ]
            for k in range(4):
                shift = first + chunk_start(jnp.bitwise_xor(core, k // 2), k % 2) * width
                base_at, upper_at = [
                    jnp.broadcast_to(
                        jnp.clip(value - shift, -1, width).astype(jnp.float32).astype(jnp.bfloat16), (width, LANES)
                    )
                    for value in (base, upper)
                ]
                weight = jnp.where(sub == base_at, low, zero)
                weight = jnp.where(sub == upper_at, high, weight)
                out[level, k * width : (k + 1) * width, pl.ds(start, LANES)] = weight
            return carry

        lax.fori_loop(0, pupil_cols // LANES, tile, 0)


def strips_kernel(wind_held, *refs):
    tables, (across, diagonal, near, keep, cols_out, strip, sibling_strip, wind, sem) = refs[:4], refs[4:]
    load = fetch((wind_held, wind, sem))[0]
    column_weights(*tables, jnp.bitwise_xor(lax.axis_index("layer"), 1) * cols_out.shape[1], cols_out)
    layers, rows, _ = keep.shape
    core = lax.rem(lax.axis_index("dir"), 2)
    odd = core == 1
    lane = lax.broadcasted_iota(jnp.int32, (rows + 32, LANES), 1)

    def wide(own, near, far, odd, level):
        own, near, far = [block[level].astype(jnp.float32) for block in (own, near, far)]
        before = jnp.where(odd, near[rows - 16 :], far[rows - 16 :])
        return stack(before, own, jnp.where(odd, far[:16], near[:16]))

    packed = jnp.zeros((rows + 32, LANES), jnp.float32)
    for level in range(layers):
        blocks = (keep, near, diagonal, odd), (near, keep, across, core == 0)
        for at, block in zip((WIND_MAX * level, STRIP + WIND_MAX * level), blocks):
            block = pltpu.roll(wide(*block, level), at + WIND_MAX * core, 1)
            packed = jnp.where((lane >= at) & (lane < at + WIND_MAX), block, packed)
    load.wait()
    strips = jnp.zeros((rows, LANES), jnp.float32)
    for level in range(layers):
        shift = wind[0, level]
        shift = jnp.where(shift < 0, shift + rows + 32, shift)
        moved = pltpu.roll(packed, shift, 0)[16 : 16 + rows]
        mine = lax.rem(lane[:rows], STRIP)
        strips = jnp.where((mine >= WIND_MAX * level) & (mine < WIND_MAX * (level + 1)), moved, strips)
    strips = strips.T.astype(jnp.bfloat16)
    strip[...] = strips[:STRIP]
    sibling_strip[...] = strips[STRIP : 2 * STRIP]


def project_rows(rows_ref, keep, near, across, diagonal, level):
    screen = stack(keep[level], near[level], across[level], diagonal[level])
    rows = stack(rows_ref[0, level], rows_ref[1, level])
    return dot(rows, screen).astype(jnp.bfloat16)


def first_rows_kernel(rows_ref, across, diagonal, near, keep, mine, sibling, other, sibling_other):
    layers, half, _ = mine.shape
    for level in range(layers):
        part = project_rows(rows_ref, keep, near, across, diagonal, level)
        for k, out in enumerate((mine, other, sibling, sibling_other)):
            out[level] = part[k * half : (k + 1) * half]


def put_strip(out, at, strip):
    for k in range(strip.shape[1] // LANES):
        out[at + k * STRIP : at + (k + 1) * STRIP, :] = strip[:, k * LANES : (k + 1) * LANES]


def get_strip(ref, at):
    return beside(*[ref[start : start + STRIP, :] for start in range(at, ref.shape[0], STRIP)])


def later_rows_kernel(rows_ref, *refs):
    chunks, refs = refs[:8], refs[8:]
    sibling0, strip, sibling_strip, mine, give, far, sibling_far, rest, sibling_rest = refs
    across, diagonal, near, keep, across0, diagonal0, near0, keep0 = chunks
    layers, half, width = mine.shape
    rows = near.shape[1]
    size = (far.shape[0] - STRIP * rows // LANES) // layers
    start = half - size
    for level in range(layers):
        part = project_rows(rows_ref, keep, near, across, diagonal, level)
        mine[level] = part[:half]
        for k, out, remainder in ((1, far, rest), (3, sibling_far, sibling_rest)):
            piece = part[k * half : (k + 1) * half]
            out[level * size : (level + 1) * size] = piece[start:]
            remainder[level * start : (level + 1) * start] = piece[:start]
        give[level, :half, :width] = sibling0[level]
        give[level, :half, width:] = part[2 * half : 3 * half]
        for k, blocks in enumerate(((across0, keep0), (across, keep))):
            cut = slice(k * width, (k + 1) * width)
            edges = [block[level, at : at + 16] for block in blocks for at in (0, rows - 16)]
            give[level, half:, cut] = stack(*edges)
    put_strip(far, layers * size, strip)
    put_strip(sibling_far, layers * size, sibling_strip)


def project(parts, cols_refs, at):
    cols = stack(*[ref[level, start:stop, at : at + 256] for ref, level, start, stop in cols_refs])
    return dot(beside(*parts), cols)


def phase_kernel(mine_ref, other_ref, mine0, mine1, came, sibling_came, phase):
    layers, _, width = mine0.shape
    parts, cuts = [], []
    for level in range(layers):
        parts += [mine0[level], mine1[level], came[level], sibling_came[level]]
        cuts += [(mine_ref, level, 0, 2 * width)]
        cuts += [(other_ref, level, 0, width), (other_ref, level, 2 * width, 3 * width)]
    for at in range(0, phase.shape[1], 256):
        phase[:, at : at + 256] = project(parts, cuts, at)


def taken_kernel(mine_ref, phase, taken, out):
    half, pupil_cols = phase.shape
    layers, cols_dev, _ = mine_ref.shape
    parts = [taken[level, :half] for level in range(layers)]
    cuts = [(mine_ref, level, cols_dev // 2, cols_dev) for level in range(layers)]
    for at in range(0, pupil_cols, 256):
        out[:, at : at + 256] = phase[:, at : at + 256] + project(parts, cuts, at)


def sum_up(start, cols_ref, phase, came, sibling_came, outs):
    layers, cols_dev, _ = cols_ref.shape
    width = cols_dev // 4
    block = outs[0].shape[0]
    size = block * len(outs)
    rows = slice(start, start + size)
    parts, cuts = [], []
    for level in range(layers):
        cut = slice(level * size, (level + 1) * size)
        parts += [came[cut], sibling_came[cut]]
        cuts += [(cols_ref, level, width, 2 * width), (cols_ref, level, 3 * width, 4 * width)]
    pupil_cols = phase.shape[1]
    for at in range(0, pupil_cols, 256):
        total = (phase[rows, at : at + 256] + project(parts, cuts, at)).astype(jnp.bfloat16)
        for k, out in enumerate(outs):
            out[:, at : at + 256] = total[k * block : (k + 1) * block]


def strip_steps(pairs):
    return [2**k - 1 for k in range(1, pairs.bit_length())]


def send_order(pairs):
    steps = strip_steps(pairs)
    return [k for k in range(pairs) if k not in steps] + steps


def add_strip(pairs, step, strips, out):
    pair = lax.axis_index("layer") // 2
    after = lax.rem(pair + 1, pairs) == jnp.bitwise_xor(pair, step)
    at = out.shape[1] - strips.shape[1]
    last, first = strips[:STRIP].astype(jnp.float32), strips[STRIP:].astype(jnp.float32)
    out[:, at:] = jnp.where(after, last, first).astype(jnp.bfloat16)


def far_kernel(cols_ref, phase, came, sibling_came, *outs):
    *outs, strips = outs
    half = phase.shape[0]
    size = outs[0].shape[0] * len(outs)
    sum_up(half - size, cols_ref, phase, came, sibling_came, outs)
    layers = cols_ref.shape[0]
    odd = lax.rem(lax.axis_index("dir"), 2) == 1
    here = get_strip(came, layers * size).astype(jnp.float32)
    there = get_strip(sibling_came, layers * size).astype(jnp.float32)
    strips[:STRIP] = jnp.where(odd, here, there).astype(jnp.bfloat16)
    strips[STRIP:] = jnp.where(odd, there, here).astype(jnp.bfloat16)
    pairs = half // outs[0].shape[0]
    add_strip(pairs, strip_steps(pairs)[-1], strips, outs[0])


def rest_kernel(cols_ref, phase, came, sibling_came, strips, *outs):
    sum_up(0, cols_ref, phase, came, sibling_came, outs)
    pairs = len(outs) + 1
    for out, step in zip(outs, send_order(pairs)):
        if step in strip_steps(pairs):
            add_strip(pairs, step, strips, out)


def shifted_rows(shift, odd, own, near, far):
    own, near, far = [block.astype(jnp.float32) for block in (own, near, far)]
    rows = own.shape[0]
    before = jnp.where(odd, near[16:], far[16:])
    after = jnp.where(odd, far[:16], near[:16])
    shift = jnp.where(shift < 0, shift + rows + 32, shift)
    return pltpu.roll(stack(before, own, after), shift, 0)[16 : 16 + rows]


def shift_kernel(wind_held, own, near0, near1, diagonal0, diagonal1, taken, partner_strips, *refs):
    messages, (out, wind, sem) = refs[:-3], refs[-3:]
    load = fetch((wind_held, wind, sem))[0]
    layers, rows, cols = own.shape
    odd = lax.rem(lax.axis_index("dir"), 2) == 1
    half = taken.shape[1] - 64
    pairs = 2 ** len(messages)
    pair, second = lax.axis_index("layer") // 2, lax.rem(lax.axis_index("layer"), 2) == 1
    before = jnp.bitwise_xor(pair, lax.rem(pair + pairs - 1, pairs))
    after = jnp.bitwise_xor(pair, lax.rem(pair + 1, pairs))
    left = partner_strips[:STRIP].astype(jnp.float32)
    right = partner_strips[STRIP:].astype(jnp.float32)
    for step, message in zip(strip_steps(pairs), messages):
        strip = message[:, message.shape[1] - rows :].astype(jnp.float32)
        left = jnp.where(jnp.logical_and(before == step, jnp.logical_not(second)), strip, left)
        right = jnp.where(jnp.logical_and(after == step, second), strip, right)
    strips = stack(left, right, jnp.zeros((LANES - 2 * STRIP, rows), jnp.float32)).T
    lane = lax.broadcasted_iota(jnp.int32, (rows, LANES), 1)
    load.wait()
    for level in range(layers):
        last = pltpu.roll(strips, LANES - WIND_MAX * (level + 1), 1)
        first = pltpu.roll(strips, LANES - STRIP - WIND_MAX * level, 1)
        extra = jnp.where(lane < WIND_MAX, first, last)
        pair = []
        for at, parts in ((half, (diagonal0, diagonal1)), (half + 32, (near0, near1))):
            here = [stack(part[level, :16], part[level, rows - 16 :]).astype(jnp.float32) for part in parts]
            there = taken[level, at : at + 32].astype(jnp.float32)
            width = there.shape[1] // 2
            quarters = [*here, there[:, width:], there[:, :width]]
            pair.append(beside(*[jnp.where(odd, quarters[3 - k], quarters[k]) for k in range(4)]))
        far, near = pair
        moved = shifted_rows(wind[0, level], odd, own[level], near, far)
        shift = wind[1, level]
        shift = jnp.where(shift < 0, shift + cols + LANES, shift)
        out[level] = pltpu.roll(beside(moved, extra), shift, 1)[:, :cols].astype(jnp.bfloat16)


def optics_kernel(amplitude, ones, columns, lines, amp_out, columns_out, lines_out):
    rows, pupil_cols = amplitude.shape
    for step in range(pupil_cols // LANES):
        cut = slice(step * LANES, (step + 1) * LANES)
        amp = amplitude[:, cut]
        energy = (amp * amp).reshape(rows // SUB_PIX, SUB_PIX, LANES).sum(axis=1)
        energy = jnp.broadcast_to(energy[:, None], (rows // SUB_PIX, SUB_PIX, LANES)).reshape(rows, LANES)
        total = jnp.dot(energy, ones[...], precision=lax.Precision.HIGHEST, preferred_element_type=jnp.float32)
        amp_out[:, cut] = amp * lax.rsqrt(total)
    columns_out[...] = columns[...].astype(jnp.bfloat16)
    lines_out[...] = lines[...].astype(jnp.bfloat16)


def sin_cos(phase):
    turns = jnp.floor(phase * (1.0 / np.pi) + 0.5)
    rest = phase - turns * 3.140625
    rest = rest - turns * 9.67653589793e-4
    odd = turns - 2.0 * jnp.floor(turns * 0.5)
    sign = 1.0 - 2.0 * odd
    square = rest * rest
    sine = -1.0 / 39916800.0
    for term in (1.0 / 362880.0, -1.0 / 5040.0, 1.0 / 120.0, -1.0 / 6.0, 1.0):
        sine = sine * square + term
    cosine = 1.0 / 479001600.0
    for term in (-1.0 / 3628800.0, 1.0 / 40320.0, -1.0 / 720.0, 1.0 / 24.0, -0.5, 1.0):
        cosine = cosine * square + term
    return sine * rest * sign, cosine * sign


def imaging_kernel(count, *refs):
    parts, (amp_ref, columns, lines, shifted, spots, screens, out, sems) = refs[:count], refs[count:]
    copies = fetch((shifted, screens, sems.at[0]))
    rows, cols = amp_ref.shape
    tiles = cols // LANES
    phase = parts[0][:, :cols].astype(jnp.float32)
    for part in parts[1:]:
        phase = phase + part[:, :cols].astype(jnp.float32)
    sine, cosine = sin_cos(phase)
    amp = amp_ref[...]
    real, imag = (amp * cosine).astype(jnp.bfloat16), (amp * sine).astype(jnp.bfloat16)
    cuts = [slice(t * LANES, (t + 1) * LANES) for t in range(tiles)]
    field = stack(*[beside(real[:, cut], imag[:, cut]) for cut in cuts])
    half = dot(field, columns[...]).astype(jnp.bfloat16)
    wide = 2 * LANES
    out_rows = 2 * rows
    for t in range(tiles):
        mine = half[t * rows : (t + 1) * rows]
        full = dot(lines[...], stack(mine[:, :wide], mine[:, wide:]))
        real, imag = full[:out_rows], full[out_rows:]
        out[:, t * wide : (t + 1) * wide] = real * real + imag * imag
        if t % 2:
            cut = slice((t - 1) * wide, (t + 1) * wide)
            copies += fetch((out.at[:, cut], spots.at[:, cut], sems.at[1 + t // 2]))
    for copy in copies:
        copy.wait()


def tables_of(rows):
    freq = np.arange(SPOT_PIX)[:, None] - SPOT_PIX // 2
    angle = ((freq * np.arange(SUB_PIX)[None, :]) % SPOT_PIX) * (2.0 * np.pi / SPOT_PIX)
    cos, sin = np.cos(angle), np.sin(angle)

    def blocks(table, count):
        return np.kron(np.eye(count), table)

    per_tile = LANES // SUB_PIX
    col_cos, col_sin = blocks(cos.T, per_tile), blocks(sin.T, per_tile)
    columns = np.block([[col_cos, -col_sin], [col_sin, col_cos]])
    count = rows // SUB_PIX
    row_cos, row_sin = blocks(cos, count), blocks(sin, count)
    lines = np.block([[row_cos, row_sin], [-row_sin, row_cos]])

    return columns.astype(np.float32), lines.astype(np.float32)


def per_device(screens, amplitude, wind, offsets, ratio):
    layers, rows_dev, cols_dev = screens.shape
    n_layer = lax.axis_size("layer")
    n_dir = lax.axis_size("dir")
    rows, pupil_cols = amplitude.shape
    pairs = n_layer // 2
    half = pairs * rows
    pupil_rows = 2 * half
    assert n_dir == 4 and rows == STRIP and pairs > 2
    bf16, f32 = jnp.bfloat16, jnp.float32
    wind = jnp.transpose(wind, (1, 0))
    offsets = jnp.transpose(offsets, (1, 2, 0))
    ratio = jnp.transpose(ratio, (1, 2, 0))
    smem, sem = pltpu.SMEM, pltpu.SemaphoreType.DMA
    wind_scratch = [smem(wind.shape, jnp.int32), sem]

    def shape(*dims, dtype=bf16):
        return jax.ShapeDtypeStruct(dims, dtype)

    def swap(value, bits):
        return lax.ppermute(value, "dir", [(i, i ^ bits) for i in range(n_dir)])

    def partner(value, bits=0):
        count = n_layer * n_dir
        return lax.ppermute(value, ("layer", "dir"), [(i, i ^ n_dir ^ bits) for i in range(count)])

    def turn(value, step):
        return lax.ppermute(value, "layer", [(i, (i + step) % n_layer) for i in range(n_layer)])

    width = cols_dev // 4
    chunk = shape(layers, rows_dev, width)
    ints = (wind, offsets, ratio)
    keep0, keep1, give0, give1, *ints = call(
        split_kernel,
        [chunk] * 4 + [shape(*array.shape, dtype=jnp.int32) for array in ints],
        (screens, *ints),
        0,
        "split",
        in_hbm=range(4),
        scratch=[sem((7,))],
        brief=True,
    )
    across0 = swap(keep0, 2)
    diagonal0 = swap(give0, 3)
    near0 = swap(give0, 1)
    across1 = swap(keep1, 2)
    diagonal1 = swap(give1, 3)
    ones = np.kron(np.eye(LANES // SUB_PIX), np.ones((SUB_PIX, SUB_PIX))).astype(np.float32)
    optics_in = (amplitude, jnp.asarray(ones), *[jnp.asarray(table) for table in tables_of(rows)])
    copies = [shape(*array.shape, dtype=array.dtype) for array in (screens, *optics_in)]
    row_weights, cols, *loaded = call(
        functools.partial(weights_kernel, (n_layer, rows_dev, cols_dev * n_layer)),
        [shape(2, layers, pupil_rows, 4 * rows_dev), shape(layers, cols_dev, pupil_cols)]
        + [shape(8, pupil_cols, dtype=dtype) for dtype in (jnp.int32, jnp.int32, f32, f32)]
        + copies,
        (*ints, screens, *optics_in),
        0,
        "weights",
        in_hbm=range(3, 8),
        scratch=[smem(array.shape, jnp.int32) for array in (wind, offsets, ratio)]
        + [sem((8,))],
        brief=True,
    )
    tables, (own, *optics_in) = loaded[:4], loaded[4:]
    wind = ints[0]
    give1, own = lax.optimization_barrier((give1, own))
    near1 = swap(give1, 1)
    across0, diagonal0, row_weights, cols = lax.optimization_barrier((across0, diagonal0, row_weights, cols))

    projected = shape(layers, half, width)
    mine0, sibling0, other0, sibling_other0 = call(
        first_rows_kernel,
        [projected] * 4,
        (row_weights, across0, diagonal0, near0, keep0),
        0,
        "rows_first",
        brief=True,
    )
    came0 = partner(other0)
    sibling_came0 = partner(sibling_other0, 1)

    wind, mine0 = lax.optimization_barrier((wind, mine0))
    others, strip, sibling_strip = call(
        strips_kernel,
        [shape(layers, cols_dev, pupil_cols)] + [shape(STRIP, rows_dev)] * 2,
        (wind, *tables, across0, diagonal0, near0, keep0),
        0,
        "strips",
        scratch=wind_scratch,
        brief=True,
    )
    steps = strip_steps(pairs)
    far = rows
    message = shape(layers * far + STRIP * rows_dev // LANES, width)
    remainder = shape(layers * (half - far), width)
    mine1, give, far1, sibling_far1, rest1, sibling_rest1 = call(
        later_rows_kernel,
        [projected, shape(layers, half + 64, 2 * width), message, message, remainder, remainder],
        (row_weights, across1, diagonal1, near1, keep1, across0, diagonal0, near0, keep0, sibling0, strip, sibling_strip),
        0,
        "rows_later",
        brief=True,
    )
    far1, sibling_far1 = partner(far1), partner(sibling_far1, 1)
    rest1, sibling_rest1, sibling_came0 = lax.optimization_barrier((rest1, sibling_rest1, sibling_came0))
    rest1, sibling_rest1 = partner(rest1), partner(sibling_rest1, 1)
    taken = swap(give, 1)
    phase = call(
        phase_kernel,
        shape(half, pupil_cols, dtype=f32),
        (cols, others, mine0, mine1, came0, sibling_came0),
        10_000_000_000,
        "phase",
    )

    phase = call(
        taken_kernel,
        shape(half, pupil_cols, dtype=f32),
        (cols, phase, taken),
        0,
        "taken",
        brief=True,
    )
    *far_sums, strips = call(
        far_kernel,
        [shape(rows, pupil_cols + rows_dev), shape(2 * STRIP, rows_dev)],
        (others, phase, far1, sibling_far1),
        300_000_000,
        "far",
    )
    rest_sums = call(
        rest_kernel,
        [shape(rows, pupil_cols + (rows_dev if k in steps else 0)) for k in send_order(pairs)[:-1]],
        (others, phase, rest1, sibling_rest1, strips),
        0,
        "rest",
        brief=True,
    )
    received = dict(zip(send_order(pairs), [*rest_sums, *far_sums]))
    for k in range(1, pairs):
        received[k] = lax.ppermute(received[k], "layer", [(i, i ^ (2 * k)) for i in range(n_layer)])
    received = [received[k] for k in range(pairs)]

    optics_in, received[-1] = lax.optimization_barrier((optics_in, received[-1]))
    optics = call(
        optics_kernel,
        (
            shape(rows, pupil_cols, dtype=f32),
            shape(*optics_in[2].shape),
            shape(*optics_in[3].shape),
        ),
        optics_in,
        0,
        "optics",
        brief=True,
    )
    received[1], optics = lax.optimization_barrier((received[1], optics))
    shifted = call(
        shift_kernel,
        shape(layers, rows_dev, cols_dev),
        (wind, own, near0, near1, diagonal0, diagonal1, taken, strips, *[received[k] for k in steps]),
        0,
        "shift",
        scratch=wind_scratch,
        brief=True,
    )
    spots_shape = shape(2 * rows, 2 * pupil_cols, dtype=f32)
    spots, new_screens = call(
        functools.partial(imaging_kernel, pairs),
        [spots_shape, shape(layers, rows_dev, cols_dev)],
        (*received, *optics, shifted),
        400_000_000,
        "imaging",
        out_hbm=(0, 1),
        scratch=[pltpu.VMEM(spots_shape.shape, f32), sem((1 + pupil_cols // (2 * LANES),))],
    )
    return (new_screens, spots[None])


def solution(mesh):
    return jax.shard_map(
        per_device,
        mesh=mesh,
        in_specs=(P(None, "dir", "layer"), P("layer", None), P(), P(), P()),
        out_specs=(P(None, "dir", "layer"), P("dir", "layer", None)),
        check_vma=False,
    )
```
